32 devices in a mesh: dp: 16 (over z, x, core), fsdp: 2 (over y).
Axes of the slice: x: 2, y: 2, z: 4, core: 2. Of those that a mesh axis runs over, the one named last changes fastest.
Arguments:
- tokens: bfloat16 [32768, 1024], P(('dp', 'fsdp')), may hold values from -6 to 6
- doc_split: int32 [32], P(('dp', 'fsdp')), may hold values from 512 to 1024, as said below
- head_scale: float32 [16], replicated, may hold values from 0.5 to 1.5
- query_key_value_weight: bfloat16 [1024, 3072], P(('dp', 'fsdp')), may hold values from -0.25 to 0.25
- output_weight: bfloat16 [1024, 1024], P(('dp', 'fsdp')), may hold values from -0.1875 to 0.1875
- first_weight: bfloat16 [1024, 4096], P(('dp', 'fsdp')), may hold values from -0.1875 to 0.1875
- second_weight: bfloat16 [4096, 1024], P(('dp', 'fsdp')), may hold values from -0.09375 to 0.09375
- model_vectors: bfloat16 [10, 1024], P(None, ('dp', 'fsdp')), may hold values from -0.59375 to 1.5, as said below
- hidden_vectors: bfloat16 [3, 4096], P(None, ('dp', 'fsdp')), may hold values from -0.59375 to 1.5, as said below
- cotangent: bfloat16 [32768, 1024], P(('dp', 'fsdp')), may hold values from -6 to 6
Outputs:
- output: bfloat16 [32768, 1024], P(('dp', 'fsdp'))
- grad_tokens: float32 [32768, 1024], P(('dp', 'fsdp'))
- grad_head_scale: float32 [16], replicated
- grad_w_qkv: float32 [1024, 3072], P(('dp', 'fsdp'))
- grad_w_out: float32 [1024, 1024], P(('dp', 'fsdp'))
- grad_w_fc1: float32 [1024, 4096], P(('dp', 'fsdp'))
- grad_w_fc2: float32 [4096, 1024], P(('dp', 'fsdp'))
- grad_vec_d: float32 [10, 1024], P(None, ('dp', 'fsdp'))
- grad_vec_ff: float32 [3, 4096], P(None, ('dp', 'fsdp'))
The draws below stay inside these ranges and needn't reach their ends.
Inputs may be any that keep to these rules, and one draw needn't show every extreme that they name: Every row holds one or two documents; some row has doc_split 1024 (one document) and some 1024 // 2. `model_vectors`: gains and biases. `hidden_vectors`: gains and biases.
All inputs are finite; a program needn't handle non-finite values.
Results may differ from the reference program's by a relative error of at most 0.015.
Values may be sent and summed in bfloat16 or wider, within the bound.
No kernel may reach another device: no remote copies, remote signals or barrier semaphores. Data moves between devices by JAX's collectives and lax.ppermute only.
A program may use at most 256 MiB of HBM per device.

```python
import jax
import jax.numpy as jnp
from jax import lax

D = 1024
FF = 4096
HEADS = 16
HEAD_DIM = 64
TOK_DEV = 1024
TOKENS = 32768


def gains_biases(key, shape, gain_mask):
    key_gain, key_bias = jax.random.split(key)
    gains = jax.random.uniform(key_gain, shape, jnp.float32, 0.5, 1.5)
    biases = jnp.clip(0.3 * jax.random.normal(key_bias, shape, jnp.float32), -0.59375, 0.59375)
    return jnp.where(gain_mask, gains, biases)


def draw_model_vectors(key, part):
    key = jax.random.fold_in(key, 11)
    row_ids = jnp.arange(10)[:, None]
    gain_mask = (row_ids == 0) | (row_ids == 5) | (row_ids == 7)
    return gains_biases(key, (10, D), gain_mask).astype(jnp.bfloat16)


def draw_hidden_vectors(key, part):
    key = jax.random.fold_in(key, 17)
    row_ids = jnp.arange(3)[:, None]
    return gains_biases(key, (3, FF), row_ids == 1).astype(jnp.bfloat16)


def draw_doc_split(key, part):
    key = jax.random.fold_in(key, 23)
    key_base, key_pick = jax.random.split(key)
    row_total = TOKENS // TOK_DEV
    splits = jax.random.randint(key_base, (row_total,), TOK_DEV // 2, TOK_DEV + 1)
    order = jax.random.permutation(key_pick, row_total)
    splits = splits.at[order[0]].set(TOK_DEV)
    splits = splits.at[order[1]].set(TOK_DEV // 2)
    return splits.astype(jnp.int32)


def steps_of(own_key, dims, pieces, low, high):
    def one(position, shards_of):
        heights = jax.random.uniform(jax.random.fold_in(jax.random.fold_in(own_key, 6), position), (shards_of,), jnp.float32, low / len(pieces), high / len(pieces))
        return jnp.repeat(jnp.exp(heights), dims[position] // shards_of).reshape((-1,) + (1,) * (len(dims) - position - 1))

    level = one(*pieces[0])
    for cut in pieces[1:]:
        level = level * one(*cut)
    return level


def scatter_about(own_key, dims, scale, bound, cuts=(), kind=jnp.bfloat16):
    array = scale * jax.random.normal(own_key, dims, jnp.float32)
    if cuts:
        array = array * steps_of(own_key, dims, cuts, -0.22, 0.18)
    return jnp.clip(array, -bound, bound).astype(kind)


def setup_inputs(seed: int = 0) -> dict:
    key_of = jax.random.split(jax.random.key(seed), 11)
    tokens = scatter_about(key_of[0], (TOKENS, D), 1.0, 6.0, ((0, 32),))
    doc_split = draw_doc_split(jax.random.fold_in(key_of[10], 71), 0)
    head_scale = jnp.clip(jax.random.uniform(key_of[2], (HEADS,), jnp.float32, 0.5, 1.5), 0.5, 1.5)
    query_key_value_weight = scatter_about(key_of[3], (D, 3 * D), (D // 2) ** -0.5, 0.25, ((0, 32),))
    output_weight = scatter_about(key_of[4], (D, D), D ** -0.5, 0.1875, ((0, 32),))
    first_weight = scatter_about(key_of[5], (D, FF), D ** -0.5, 0.1875, ((0, 32),))
    second_weight = scatter_about(key_of[6], (FF, D), FF ** -0.5, 0.09375, ((0, 32),))
    model_vectors = draw_model_vectors(jax.random.fold_in(key_of[10], 71), 0)
    hidden_vectors = draw_hidden_vectors(jax.random.fold_in(key_of[10], 71), 0)
    cotangent = scatter_about(key_of[9], (TOKENS, D), 1.0, 6.0, ((0, 32),))
    return {"tokens": tokens, "doc_split": doc_split, "head_scale": head_scale, "query_key_value_weight": query_key_value_weight, "output_weight": output_weight, "first_weight": first_weight, "second_weight": second_weight, "model_vectors": model_vectors, "hidden_vectors": hidden_vectors, "cotangent": cotangent}


@jax.custom_vjp
def low(v):
    return lax.optimization_barrier(v.astype(jnp.bfloat16)).astype(jnp.float32)

@jax.custom_vjp
def reduced_backward(v):
    return v

def low_keep(v):
    return (low(v), None)

def low_pass(kept, grad):
    return (grad,)

def back_keep(v):
    return (v, None)

def back_low(kept, grad):
    return (low(grad),)
low.defvjp(low_keep, low_pass)
reduced_backward.defvjp(back_keep, back_low)
precise_result = lax.Precision.HIGHEST
epsilon = 1e-05

def lowered(values):
    return low(reduced_backward(values))

def norm_rows(values, norm_gain, norm_shift):
    center = values - lax.optimization_barrier(jnp.mean(values, axis=-1, keepdims=True))
    spread = lax.optimization_barrier(jnp.mean(center * center, axis=-1, keepdims=True))
    return center * lax.rsqrt(spread + epsilon) * norm_gain + norm_shift

def layer(params, head_gain, resid, split_at):
    query_key_value_weight, output_weight, first_weight, second_weight, model_vectors, hidden_vectors = params
    seq_count, seq_length, model_width = resid.shape
    normed_first = norm_rows(resid, model_vectors[0], model_vectors[1])
    first_activation = low(normed_first)
    projected_rows = jnp.einsum('cgk,ku->cgu', first_activation, query_key_value_weight, precision=precise_result)
    head_shape = (seq_count, seq_length, HEADS, HEAD_DIM)
    queries = lowered(projected_rows[..., :D] + model_vectors[2]).reshape(head_shape)
    keys_all = lowered(projected_rows[..., D:2 * D]).reshape(head_shape)
    values_all = lowered(projected_rows[..., 2 * D:] + model_vectors[3]).reshape(head_shape)
    scores = reduced_backward(jnp.einsum('sqhe,skhe->shqk', queries, keys_all, precision=precise_result) * HEAD_DIM ** (-0.5))
    positions = jnp.arange(seq_length)
    doc_ids = positions[None, :] >= split_at[:, None]
    allowed = (doc_ids[:, :, None] == doc_ids[:, None, :]) & (positions[None, None, :] <= positions[None, :, None])
    masked_scores = jnp.where(allowed[:, None], scores, -1e+30)
    row_peak = lax.optimization_barrier(jnp.max(masked_scores, axis=-1, keepdims=True))
    exponent = jnp.exp(masked_scores - row_peak)
    softmax_rows = low(exponent / lax.optimization_barrier(jnp.sum(exponent, axis=-1, keepdims=True)))
    attended = reduced_backward(jnp.einsum('shqk,skhe->sqhe', softmax_rows, values_all, precision=precise_result))
    scaled_rows = lowered((attended * head_gain[:, None]).reshape(seq_count, seq_length, D))
    branch_output = reduced_backward(jnp.einsum('cgk,ku->cgu', scaled_rows, output_weight, precision=precise_result) + model_vectors[4])
    middle_state = resid + norm_rows(branch_output, model_vectors[5], model_vectors[6])
    second_activation = low(norm_rows(middle_state, model_vectors[7], model_vectors[8]))
    before_gate = reduced_backward(jnp.einsum('yma,ar->ymr', second_activation, first_weight, precision=precise_result) + hidden_vectors[0])
    gated = jax.nn.gelu(before_gate, approximate=True)
    hidden_activation = lowered(norm_rows(gated, hidden_vectors[1], hidden_vectors[2]))
    return middle_state + (jnp.einsum('cmu,ue->cme', hidden_activation, second_weight, precision=precise_result) + model_vectors[9])

def reference(tokens, doc_split, head_scale, query_key_value_weight, output_weight, first_weight, second_weight, model_vectors, hidden_vectors, cotangent):
    params = (query_key_value_weight.astype(jnp.float32), output_weight.astype(jnp.float32), first_weight.astype(jnp.float32), second_weight.astype(jnp.float32), model_vectors.astype(jnp.float32), hidden_vectors.astype(jnp.float32))
    head_gain = head_scale.astype(jnp.float32)
    steps_total = TOKENS // (2 * TOK_DEV)
    inputs_all = tokens.astype(jnp.float32).reshape(steps_total, 2, TOK_DEV, D)
    cots_all = cotangent.astype(jnp.float32).reshape(steps_total, 2, TOK_DEV, D)
    splits_all = doc_split.astype(jnp.int32).reshape(steps_total, 2)

    def one_step(carried, block_item):
        resid, cot_rows, split_at = block_item

        def forward(param_set, gain_set, resid_set):
            return layer(param_set, gain_set, resid_set, split_at)
        result, pullback = jax.vjp(forward, params, head_gain, resid)
        grad_params, grad_gain, grad_resid = pullback(cot_rows)
        summed = tuple((acc + new for acc, new in zip(carried[0], grad_params)))
        return ((summed, carried[1] + grad_gain), (result, grad_resid))
    start_state = (tuple((jnp.zeros(p.shape, jnp.float32) for p in params)), jnp.zeros((HEADS,), jnp.float32))
    final_state, stacked = lax.scan(one_step, start_state, (inputs_all, cots_all, splits_all))
    grad_params, grad_gain = final_state
    results, grad_resid = stacked
    return (results.reshape(TOKENS, D).astype(jnp.bfloat16), grad_resid.reshape(TOKENS, D), grad_gain, grad_params[0], grad_params[1], grad_params[2], grad_params[3], grad_params[4], grad_params[5])
```

```python
import functools

import jax
import jax.numpy as jnp
from jax import lax
from jax.experimental import pallas as pl
from jax.experimental.pallas import tpu as pltpu
from jax.sharding import PartitionSpec as P

epsilon = 1e-05
AXES = ("dp", "fsdp")
f32 = jnp.float32
bf16 = jnp.bfloat16
NEG = -1e30
VMEM_LIMIT = 56 << 20


class Plan:
    def __init__(self, mesh):
        n_dp, n_fs = mesh.shape["dp"], mesh.shape["fsdp"]
        self.count = n_dp * n_fs
        self.ways = min(self.count, 32)
        self.low = self.count // self.ways
        self.core = max(1, n_fs // self.low)
        dims = [1 << b for b in range(self.ways.bit_length() - 1) if 1 << b != self.core]
        if len(dims) >= 2:
            dims[-1] |= dims[-2]
        self.dims = dims
        self.half = self.ways // 2
        self.steps = len(dims)

    def order(self, core_bit, part):
        shift = (core_bit + 2 * part) % self.steps
        return self.dims[shift:] + self.dims[:shift]

    def pairs(self, part, step):
        out = []
        for i in range(self.count):
            group = i // self.low
            mask = self.order(int(bool(group & self.core)), part)[step]
            out.append((i, i ^ (mask * self.low)))
        return out

    def core_pairs(self):
        return [(i, i ^ (self.core * self.low)) for i in range(self.count)]

    def low_groups(self):
        return [[g * self.low + i for i in range(self.low)] for g in range(self.ways)]

    def table(self, part, msb_first):
        me = (lax.axis_index("dp") * lax.axis_size("fsdp") + lax.axis_index("fsdp")) // self.low
        rows = []
        for core_bit in (0, 1):
            row = []
            for other in (0, 1):
                masks = self.order(core_bit ^ other, part)
                for r in range(self.half):
                    x = self.core if other else 0
                    for k in range(self.steps):
                        bit = self.steps - 1 - k if msb_first else k
                        if (r >> bit) & 1:
                            x ^= masks[k]
                    row.append(x)
            rows.append(row)
        mine = ((me & self.core) != 0).astype(jnp.int32)
        masks = jnp.where(mine == 1, jnp.array(rows[1], jnp.int32), jnp.array(rows[0], jnp.int32))
        return jnp.bitwise_xor(me.astype(jnp.int32), masks)


def gather_part(plan, piece, part):
    held = piece[None]
    fresh = held
    for step in range(plan.steps):
        fresh = lax.ppermute(held, AXES, plan.pairs(part, step))
        if step < plan.steps - 1:
            held = jnp.concatenate([held, fresh], 0)
    far_held = lax.ppermute(held, AXES, plan.core_pairs())
    far_fresh = lax.ppermute(fresh, AXES, plan.core_pairs())
    return [held, fresh, far_held, far_fresh]


def join_low(plan, piece):
    if plan.low == 1:
        return piece
    return lax.all_gather(piece, AXES, axis=0, tiled=True, axis_index_groups=plan.low_groups())


def assemble_kernel(table_ref, *refs, quarter, parts, layout):
    sources, rest = refs[: 4 * parts], refs[4 * parts :]
    outs, sem = rest[:-1], rest[-1]
    copies = []
    for line, (part, src_col, out, out_col, width) in enumerate(layout):
        for r in range(4 * quarter):
            src = sources[4 * part + r // quarter]
            rows = src.shape[1]
            at = pl.multiple_of(table_ref[part, r] * rows, rows)
            copy = pltpu.make_async_copy(
                src.at[r % quarter, :, pl.ds(src_col, width)],
                outs[out].at[pl.ds(at, rows), pl.ds(out_col, width)],
                sem.at[line, r],
            )
            copy.start()
            copies.append(copy)
    for copy in copies:
        copy.wait()


def assemble(plan, blocks, out_shapes, layout):
    table = jnp.stack([plan.table(part, False) for part in range(len(blocks))])
    flat = [b for part in blocks for b in part]
    anywhere = pl.BlockSpec(memory_space=pl.ANY)
    moved = sum(2 * b.size * b.dtype.itemsize for b in flat)
    return pl.pallas_call(
        functools.partial(
            assemble_kernel, quarter=plan.half // 2, parts=len(blocks), layout=layout
        ),
        in_specs=[pl.BlockSpec(memory_space=pltpu.SMEM)] + [anywhere] * len(flat),
        out_specs=[anywhere] * len(out_shapes),
        out_shape=[jax.ShapeDtypeStruct(s, bf16) for s in out_shapes],
        scratch_shapes=[pltpu.SemaphoreType.DMA((len(layout), plan.ways))],
        compiler_params=pltpu.CompilerParams(vmem_limit_bytes=VMEM_LIMIT),
        cost_estimate=pl.CostEstimate(flops=0, bytes_accessed=moved, transcendentals=0),
        name="assemble",
    )(table, *flat)


def scatter_part(plan, keep, send, part):
    def plus(a, b):
        return a.astype(f32) + b.astype(f32)

    got = lax.ppermute(send, AXES, plan.core_pairs())
    for step in range(plan.steps):
        half = keep.shape[0] // 2
        going = plus(keep[half:], got[half:]).astype(bf16)
        arriving = lax.ppermute(going, AXES, plan.pairs(part, step))
        keep = plus(keep[:half], got[:half]).astype(bf16)
        got = arriving
    total = plus(keep[0], got[0])
    if plan.low > 1:
        total = lax.psum_scatter(
            total, AXES, scatter_dimension=0, tiled=True, axis_index_groups=plan.low_groups()
        )
    return total


def dot_nt(a, b):
    return lax.dot_general(a, b, (((1,), (1,)), ((), ())), preferred_element_type=f32)


def dot_nn(a, b):
    return lax.dot_general(a, b, (((1,), (0,)), ((), ())), preferred_element_type=f32)


def transposed(a):
    return a.astype(f32).T.astype(a.dtype)


def allowed_block(i, j, split, blk):
    key_pos = j * blk + lax.broadcasted_iota(jnp.int32, (blk, blk), 0)
    query_row = i * blk + lax.broadcasted_iota(jnp.int32, (1, blk), 1)
    allowed = key_pos >= jnp.where(query_row >= split, split, 0)
    if i == j:
        allowed &= key_pos <= i * blk + lax.broadcasted_iota(jnp.int32, (blk, blk), 1)
    return allowed


def attention_kernel(split_ref, q_ref, k_ref, v_ref, o_ref, lse_ref, *, seq, hd, blk):
    split = split_ref[0]
    v_t = transposed(v_ref[...])
    lane = lax.broadcasted_iota(jnp.int32, (blk, 2 * hd), 1)
    for i in range(seq // blk):
        rows = slice(i * blk, (i + 1) * blk)
        outs = []
        for h in (0, 1):
            q = jnp.where((lane >= hd) if h else (lane < hd), q_ref[rows, :], 0) * bf16(hd**-0.5)
            scores = []
            for j in range(i + 1):
                s = dot_nt(k_ref[j * blk : (j + 1) * blk, :], q)
                scores.append(jnp.where(allowed_block(i, j, split, blk), s, NEG))
            peak = scores[0].max(0, keepdims=True)
            for s in scores[1:]:
                peak = jnp.maximum(peak, s.max(0, keepdims=True))
            total = jnp.zeros((1, blk), f32)
            mixed = jnp.zeros((hd, blk), f32)
            for j, s in enumerate(scores):
                e = jnp.exp(s - peak)
                total += e.sum(0, keepdims=True)
                mixed += dot_nn(
                    v_t[h * hd : (h + 1) * hd, j * blk : (j + 1) * blk], e.astype(bf16)
                )
            outs.append(mixed / total)
            lse_ref[0, h : h + 1, rows] = peak + jnp.log(total)
        o_ref[rows, :] = jnp.concatenate(outs, 0).T


def attention(split, qkv, heads, blk):
    seq, width = qkv.shape[0], qkv.shape[1] // 3
    hd, pairs = width // heads, heads // 2
    w = 2 * hd
    return pl.pallas_call(
        functools.partial(attention_kernel, seq=seq, hd=hd, blk=blk),
        grid=(pairs,),
        in_specs=[
            pl.BlockSpec(memory_space=pltpu.SMEM),
            pl.BlockSpec((seq, w), lambda p: (0, p)),
            pl.BlockSpec((seq, w), lambda p: (0, p + pairs)),
            pl.BlockSpec((seq, w), lambda p: (0, p + 2 * pairs)),
        ],
        out_specs=[
            pl.BlockSpec((seq, w), lambda p: (0, p)),
            pl.BlockSpec((1, 2, seq), lambda p: (p, 0, 0)),
        ],
        out_shape=[
            jax.ShapeDtypeStruct((seq, width), f32),
            jax.ShapeDtypeStruct((pairs, 2, seq), f32),
        ],
        compiler_params=pltpu.CompilerParams(vmem_limit_bytes=VMEM_LIMIT),
        cost_estimate=pl.CostEstimate(
            flops=12 * seq * seq * width,
            bytes_accessed=seq * width * 10,
            transcendentals=heads * seq * seq,
        ),
        name="attention",
    )(split, qkv, qkv, qkv)


def attention_back_kernel(
    split_ref, q_ref, k_ref, v_ref, da_ref, o_ref, lse_ref, dq_ref, dk_ref, dv_ref, dk_acc, dv_acc,
    *, seq, hd, blk,
):
    split = split_ref[0]
    k_t = transposed(k_ref[...])
    lane = lax.broadcasted_iota(jnp.int32, (blk, 2 * hd), 1)
    for i in range(seq // blk):
        rows = slice(i * blk, (i + 1) * blk)
        q_full, da_full = q_ref[rows, :], da_ref[rows, :]
        inner = (da_full.astype(f32) * o_ref[rows, :]).T
        dqs = []
        for h in (0, 1):
            mine = (lane >= hd) if h else (lane < hd)
            q = jnp.where(mine, q_full, 0) * bf16(hd**-0.5)
            da = jnp.where(mine, da_full, 0)
            row_inner = inner[h * hd : (h + 1) * hd].sum(0, keepdims=True)
            lse = lse_ref[0, h : h + 1, rows]
            dq = jnp.zeros((hd, blk), f32)
            for j in range(i + 1):
                keys = slice(j * blk, (j + 1) * blk)
                s = dot_nt(k_ref[keys, :], q)
                s = jnp.where(allowed_block(i, j, split, blk), s, NEG)
                p = jnp.exp(s - lse)
                dp = dot_nt(v_ref[keys, :], da)
                ds = (p * (dp - row_inner)).astype(bf16)
                dv = dot_nn(p.astype(bf16), da)
                dk = dot_nn(ds, q)
                if i == j and h == 0:
                    dv_acc[keys, :] = dv
                    dk_acc[keys, :] = dk
                else:
                    dv_acc[keys, :] += dv
                    dk_acc[keys, :] += dk
                dq += dot_nn(k_t[h * hd : (h + 1) * hd, keys], ds)
            dqs.append(dq)
        dq_ref[rows, :] = (jnp.concatenate(dqs, 0).T * (hd**-0.5)).astype(bf16)
    dk_ref[...] = dk_acc[...].astype(bf16)
    dv_ref[...] = dv_acc[...].astype(bf16)


def attention_back(split, qkv, da, attended, lse, heads, blk):
    seq, width = qkv.shape[0], qkv.shape[1] // 3
    hd, pairs = width // heads, heads // 2
    w = 2 * hd
    column = pl.BlockSpec((seq, w), lambda p: (0, p))
    return pl.pallas_call(
        functools.partial(attention_back_kernel, seq=seq, hd=hd, blk=blk),
        grid=(pairs,),
        in_specs=[
            pl.BlockSpec(memory_space=pltpu.SMEM),
            column,
            pl.BlockSpec((seq, w), lambda p: (0, p + pairs)),
            pl.BlockSpec((seq, w), lambda p: (0, p + 2 * pairs)),
            column,
            column,
            pl.BlockSpec((1, 2, seq), lambda p: (p, 0, 0)),
        ],
        out_specs=[column, column, column],
        out_shape=[jax.ShapeDtypeStruct((seq, width), bf16)] * 3,
        scratch_shapes=[pltpu.VMEM((seq, w), f32)] * 2,
        compiler_params=pltpu.CompilerParams(vmem_limit_bytes=VMEM_LIMIT),
        cost_estimate=pl.CostEstimate(
            flops=20 * seq * seq * width,
            bytes_accessed=seq * width * 20,
            transcendentals=heads * seq * seq,
        ),
        name="attention_back",
    )(split, qkv, qkv, qkv, da, attended, lse)


def grad_rows_kernel(table_ref, left_ref, right_ref, send_ref, keep_ref, left_t, acc, *, ways):
    @pl.when(pl.program_id(0) == 0)
    def _():
        left_t[...] = transposed(left_ref[...])

    acc[...] = dot_nn(left_t[...], right_ref[...])
    rows = acc.shape[0] // ways
    for r in range(ways // 2):
        at = pl.multiple_of(table_ref[r] * rows, rows)
        keep_ref[r] = acc[pl.ds(at, rows), :].astype(bf16)
        at = pl.multiple_of(table_ref[ways // 2 + r] * rows, rows)
        send_ref[r] = acc[pl.ds(at, rows), :].astype(bf16)


def grad_rows(table, left, right, tile):
    tokens, m = left.shape
    n = right.shape[1]
    ways = table.shape[0]
    block = pl.BlockSpec((ways // 2, m // ways, tile), lambda i: (0, 0, i))
    shape = jax.ShapeDtypeStruct((ways // 2, m // ways, n), bf16)
    send, keep = pl.pallas_call(
        functools.partial(grad_rows_kernel, ways=ways),
        grid=(n // tile,),
        in_specs=[
            pl.BlockSpec(memory_space=pltpu.SMEM),
            pl.BlockSpec((tokens, m), lambda i: (0, 0)),
            pl.BlockSpec((tokens, tile), lambda i: (0, i)),
        ],
        out_specs=[block, block],
        out_shape=[shape, shape],
        scratch_shapes=[pltpu.VMEM((m, tokens), bf16), pltpu.VMEM((m, tile), f32)],
        compiler_params=pltpu.CompilerParams(vmem_limit_bytes=VMEM_LIMIT),
        cost_estimate=pl.CostEstimate(
            flops=2 * tokens * m * n,
            bytes_accessed=2 * (tokens * (m + n) + m * n),
            transcendentals=0,
        ),
        name="grad_rows",
    )(table, left, right)
    return keep, send


def grad_tall_kernel(table_ref, *refs, per_step, sends):
    lefts, (right_ref, send_ref, keep_ref) = refs[:per_step], refs[per_step:]
    left_t = jnp.concatenate([transposed(ref[...]) for ref in lefts], 0)
    out = dot_nn(left_t, right_ref[...]).astype(bf16)
    out = out.reshape(per_step, out.shape[0] // per_step, out.shape[1])

    @pl.when(pl.program_id(0) < sends)
    def _():
        send_ref[...] = out

    @pl.when(pl.program_id(0) >= sends)
    def _():
        keep_ref[...] = out


def grad_tall(table, left, right, per_step=4):
    tokens, m = left.shape
    n = right.shape[1]
    ways = table.shape[0]
    rows = m // ways
    sends = ways // 2 // per_step

    def left_spec(k):
        def place(i, table_ref):
            r = lax.rem(i * per_step + k + ways // 2, ways)
            return (0, table_ref[r])

        return pl.BlockSpec((tokens, rows), place)

    shape = jax.ShapeDtypeStruct((ways // 2, rows, n), bf16)
    send, keep = pl.pallas_call(
        functools.partial(grad_tall_kernel, per_step=per_step, sends=sends),
        grid_spec=pltpu.PrefetchScalarGridSpec(
            num_scalar_prefetch=1,
            grid=(ways // per_step,),
            in_specs=[left_spec(k) for k in range(per_step)]
            + [pl.BlockSpec((tokens, n), lambda i, t: (0, 0))],
            out_specs=[
                pl.BlockSpec((per_step, rows, n), lambda i, t: (jnp.minimum(i, sends - 1), 0, 0)),
                pl.BlockSpec((per_step, rows, n), lambda i, t: (jnp.maximum(i - sends, 0), 0, 0)),
            ],
        ),
        out_shape=[shape, shape],
        compiler_params=pltpu.CompilerParams(vmem_limit_bytes=VMEM_LIMIT),
        cost_estimate=pl.CostEstimate(
            flops=2 * tokens * m * n,
            bytes_accessed=2 * (tokens * (m + n) + m * n),
            transcendentals=0,
        ),
        name="grad_tall",
    )(table, *([left] * per_step), right)
    return keep, send


def norm_rows(values, norm_gain, norm_shift):
    center = values - jnp.mean(values, axis=-1, keepdims=True)
    spread = jnp.mean(center * center, axis=-1, keepdims=True)
    return center * lax.rsqrt(spread + epsilon) * norm_gain + norm_shift


def smooth_gate(values):
    return jax.nn.gelu(values, approximate=True)


def rounded(values):
    return lax.optimization_barrier(values.astype(bf16)).astype(f32)


def local(
    plan,
    tokens,
    doc_split,
    head_scale,
    query_key_value_weight,
    output_weight,
    first_weight,
    second_weight,
    model_vectors,
    hidden_vectors,
    cotangent,
):
    seq, width = tokens.shape
    hidden = first_weight.shape[1]
    heads = head_scale.shape[0]
    head_shape = (seq, heads, width // heads)
    blk = min(256, seq)
    shard = query_key_value_weight.shape[0]

    per_row = hidden_vectors.shape[1] // shard
    n_vec = model_vectors.shape[0]
    n_hid = hidden_vectors.shape[0]
    vec_cols = jnp.concatenate(
        [
            model_vectors.T,
            hidden_vectors.reshape(n_hid, shard, per_row)
            .transpose(1, 0, 2)
            .reshape(shard, n_hid * per_row),
        ],
        1,
    )
    vec_cols = jnp.pad(vec_cols, ((0, 0), (0, 128 - vec_cols.shape[1])))
    cut = 2 * width
    piece_a = join_low(plan, jnp.concatenate([query_key_value_weight[:, :cut], vec_cols], 1))
    piece_b = join_low(
        plan, jnp.concatenate([query_key_value_weight[:, cut:], output_weight], 1)
    )
    blocks = [gather_part(plan, piece_a, 0), gather_part(plan, piece_b, 1)]
    w_qkv, w_out, vec_all = assemble(
        plan,
        blocks,
        [(width, 3 * width), (width, width), (width, 128)],
        [(0, 0, 0, 0, cut), (0, cut, 2, 0, 128), (1, 0, 0, cut, width), (1, width, 1, 0, width)],
    )
    blocks = [
        gather_part(plan, join_low(plan, first_weight), 0),
        gather_part(plan, join_low(plan, second_weight), 1),
    ]
    w_fc1, w_fc2 = assemble(
        plan, blocks, [(width, hidden), (hidden, width)], [(0, 0, 0, 0, hidden), (1, 0, 1, 0, width)]
    )
    vecd = vec_all[:, :n_vec].T.astype(f32)
    vecff = (
        vec_all[:, n_vec : n_vec + n_hid * per_row]
        .reshape(width, n_hid, per_row)
        .transpose(1, 0, 2)
        .reshape(n_hid, hidden)
        .astype(f32)
    )

    resid = tokens.astype(f32)
    normed_first, first_back = jax.vjp(norm_rows, resid, vecd[0], vecd[1])
    first_activation = normed_first.astype(bf16)
    projected = jnp.dot(first_activation, w_qkv, preferred_element_type=f32)
    qkv_bias = jnp.concatenate([vecd[2], jnp.zeros((width,), f32), vecd[3]])
    qkv = (projected + qkv_bias).astype(bf16)
    attended, lse = attention(doc_split, qkv, heads, blk)
    scale_row = jnp.repeat(head_scale, width // heads)
    scaled_heads = (attended * scale_row).astype(bf16)
    branch_output = jnp.dot(scaled_heads, w_out, preferred_element_type=f32) + vecd[4]
    normed_attn, attn_norm_back = jax.vjp(norm_rows, branch_output, vecd[5], vecd[6])
    middle_state = resid + normed_attn
    normed_second, second_back = jax.vjp(norm_rows, middle_state, vecd[7], vecd[8])
    second_activation = normed_second.astype(bf16)
    before_gate = jnp.dot(second_activation, w_fc1, preferred_element_type=f32) + vecff[0]
    gated, gate_back = jax.vjp(smooth_gate, before_gate)
    normed_hidden, hidden_back = jax.vjp(norm_rows, gated, vecff[1], vecff[2])
    hidden_activation = normed_hidden.astype(bf16)
    result = middle_state + (
        jnp.dot(hidden_activation, w_fc2, preferred_element_type=f32) + vecd[9]
    )
    output = result.astype(bf16)

    tables = [plan.table(part, True) for part in (0, 1)]
    upstream = cotangent.astype(f32)
    grad_fc2 = grad_tall(tables[1], hidden_activation, cotangent)
    sent_fc2 = scatter_part(plan, *grad_fc2, 1)
    grad_bias_two = jnp.sum(upstream, axis=0)
    grad_hidden_act = rounded(dot_nt(cotangent, w_fc2))
    grad_gated, grad_gain_hidden, grad_shift_hidden = hidden_back(grad_hidden_act)
    grad_pre = gate_back(grad_gated)[0].astype(bf16)
    grad_fc1 = grad_rows(tables[0], second_activation, grad_pre, 512)
    sent_fc1 = scatter_part(plan, *grad_fc1, 0)
    grad_bias_one = jnp.sum(grad_pre.astype(f32), axis=0)
    grad_second_act = dot_nt(grad_pre, w_fc1)
    grad_middle_norm, grad_gain_second, grad_shift_second = second_back(grad_second_act)
    grad_middle = upstream + grad_middle_norm
    grad_branch, grad_gain_attn, grad_shift_attn = attn_norm_back(grad_middle)
    grad_branch_low = grad_branch.astype(bf16)
    grad_bias_out = jnp.sum(grad_branch_low.astype(f32), axis=0)
    grad_scaled = rounded(dot_nt(grad_branch_low, w_out))
    head_products = jnp.sum(grad_scaled * attended, axis=0)
    grad_heads_local = jnp.sum(head_products.reshape(heads, -1), axis=1)
    grad_attended = (grad_scaled * scale_row).astype(bf16)
    dq, dk, dv = attention_back(doc_split, qkv, grad_attended, attended, lse, heads, blk)
    grad_projected = jnp.concatenate([dq, dk, dv], axis=1)
    grad_bias_query = jnp.sum(dq.astype(f32), axis=0)
    grad_bias_value = jnp.sum(dv.astype(f32), axis=0)
    grad_first_act = dot_nt(grad_projected, w_qkv)
    grad_resid_norm, grad_gain_first, grad_shift_first = first_back(grad_first_act)
    grad_tokens = grad_middle + grad_resid_norm
    vec_grads = jnp.stack(
        [
            grad_gain_first,
            grad_shift_first,
            grad_bias_query,
            grad_bias_value,
            grad_bias_out,
            grad_gain_attn,
            grad_shift_attn,
            grad_gain_second,
            grad_shift_second,
            grad_bias_two,
        ]
    )
    hid_grads = jnp.stack([grad_bias_one, grad_gain_hidden, grad_shift_hidden])
    vec_cols = jnp.concatenate(
        [
            vec_grads.T,
            hid_grads.reshape(n_hid, width, per_row)
            .transpose(1, 0, 2)
            .reshape(width, n_hid * per_row),
            jnp.broadcast_to(grad_heads_local, (width, heads)),
        ],
        1,
    )
    used = vec_cols.shape[1]
    vec_cols = jnp.pad(vec_cols, ((0, 0), (0, 128 - used))).astype(bf16)
    vec_blocks = vec_cols.reshape(plan.ways, width // plan.ways, 128)[tables[0]]
    keep_a, send_a = grad_rows(tables[0], first_activation, grad_projected[:, :cut], 512)
    keep_a = jnp.concatenate([keep_a, vec_blocks[: plan.half]], 2)
    send_a = jnp.concatenate([send_a, vec_blocks[plan.half :]], 2)
    keep_b, send_b = grad_rows(tables[1], first_activation, dv, 512)
    keep_o, send_o = grad_rows(tables[1], scaled_heads, grad_branch_low, 512)
    keep_b = jnp.concatenate([keep_b, keep_o], 2)
    send_b = jnp.concatenate([send_b, send_o], 2)
    sent_a = scatter_part(plan, keep_a, send_a, 0)
    sent_b = scatter_part(plan, keep_b, send_b, 1)
    sent_qkv = jnp.concatenate([sent_a[:, :cut], sent_b[:, :width]], 1)
    sent_out = sent_b[:, width:]
    sent_vecd = sent_a[:, cut : cut + n_vec].T
    mid = cut + n_vec + n_hid * per_row
    sent_vecff = (
        sent_a[:, cut + n_vec : mid]
        .reshape(shard, n_hid, per_row)
        .transpose(1, 0, 2)
        .reshape(n_hid, shard * per_row)
    )
    grad_heads = sent_a[0, mid : mid + heads]
    return (
        output,
        grad_tokens,
        grad_heads,
        sent_qkv,
        sent_out,
        sent_fc1,
        sent_fc2,
        sent_vecd,
        sent_vecff,
    )


def solution(mesh):
    rows = P(AXES, None)
    columns = P(None, AXES)
    return jax.shard_map(
        functools.partial(local, Plan(mesh)),
        mesh=mesh,
        in_specs=(rows, P(AXES), P(), rows, rows, rows, rows, columns, columns, rows),
        out_specs=(rows, rows, P(), rows, rows, rows, rows, columns, columns),
        check_vma=False,
    )
```

```python
import functools

import jax
import jax.numpy as jnp
from jax import lax
from jax.experimental import pallas as pl
from jax.experimental.pallas import tpu as pltpu
from jax.sharding import PartitionSpec as P

epsilon = 1e-05
AXES = ("dp", "fsdp")
f32 = jnp.float32
bf16 = jnp.bfloat16
NEG = -1e30
VMEM_LIMIT = 56 << 20


class Plan:
    def __init__(self, mesh):
        n_dp, n_fs = mesh.shape["dp"], mesh.shape["fsdp"]
        self.count = n_dp * n_fs
        self.ways = min(self.count, 32)
        self.low = self.count // self.ways
        self.core = max(1, n_fs // self.low)
        dims = [1 << b for b in range(self.ways.bit_length() - 1) if 1 << b != self.core]
        if len(dims) >= 2:
            dims[-1] |= dims[-2]
        self.dims = dims
        self.half = self.ways // 2
        self.steps = len(dims)

    def order(self, core_bit, part):
        shift = (core_bit + 2 * part) % self.steps
        return self.dims[shift:] + self.dims[:shift]

    def pairs(self, part, step):
        out = []
        for i in range(self.count):
            group = i // self.low
            mask = self.order(int(bool(group & self.core)), part)[step]
            out.append((i, i ^ (mask * self.low)))
        return out

    def core_pairs(self):
        return [(i, i ^ (self.core * self.low)) for i in range(self.count)]

    def low_groups(self):
        return [[g * self.low + i for i in range(self.low)] for g in range(self.ways)]

    def table(self, part, msb_first):
        me = (lax.axis_index("dp") * lax.axis_size("fsdp") + lax.axis_index("fsdp")) // self.low
        rows = []
        for core_bit in (0, 1):
            row = []
            for other in (0, 1):
                masks = self.order(core_bit ^ other, part)
                for r in range(self.half):
                    x = self.core if other else 0
                    for k in range(self.steps):
                        bit = self.steps - 1 - k if msb_first else k
                        if (r >> bit) & 1:
                            x ^= masks[k]
                    row.append(x)
            rows.append(row)
        mine = ((me & self.core) != 0).astype(jnp.int32)
        masks = jnp.where(mine == 1, jnp.array(rows[1], jnp.int32), jnp.array(rows[0], jnp.int32))
        return jnp.bitwise_xor(me.astype(jnp.int32), masks)


def tied(*values):
    return lax.optimization_barrier(values)


class Gather:
    def __init__(self, plan, pieces):
        self.plan = plan
        self.held = [piece[None] for piece in pieces]
        self.fresh = None
        self.at = 0

    def step(self):
        if self.fresh is not None:
            self.held = [jnp.concatenate(pair, 0) for pair in zip(self.held, self.fresh)]
        self.fresh = [
            lax.ppermute(h, AXES, self.plan.pairs(part, self.at)) for part, h in enumerate(self.held)
        ]
        self.at += 1

    def after(self, other):
        if self.fresh is None:
            *self.held, _ = tied(*self.held, other)
        else:
            *self.fresh, _ = tied(*self.fresh, other)

    def cross_held(self):
        self.far_held = [lax.ppermute(h, AXES, self.plan.core_pairs()) for h in self.held]

    def cross_fresh(self):
        self.far_fresh = [lax.ppermute(h, AXES, self.plan.core_pairs()) for h in self.fresh]

    def blocks(self):
        return [list(b) for b in zip(self.held, self.fresh, self.far_held, self.far_fresh)]


def join_low(plan, piece):
    if plan.low == 1:
        return piece
    return lax.all_gather(piece, AXES, axis=0, tiled=True, axis_index_groups=plan.low_groups())


def assemble_kernel(table_ref, *refs, quarter, parts, layout):
    sources, rest = refs[: 4 * parts], refs[4 * parts :]
    outs, sem = rest[:-1], rest[-1]
    copies = []
    for line, (part, src_col, out, out_col, width) in enumerate(layout):
        for r in range(4 * quarter):
            src = sources[4 * part + r // quarter]
            rows = src.shape[1]
            at = pl.multiple_of(table_ref[part, r] * rows, rows)
            copy = pltpu.make_async_copy(
                src.at[r % quarter, :, pl.ds(src_col, width)],
                outs[out].at[pl.ds(at, rows), pl.ds(out_col, width)],
                sem.at[line, r],
            )
            copy.start()
            copies.append(copy)
    for copy in copies:
        copy.wait()


def assemble(plan, blocks, out_shapes, layout):
    table = jnp.stack([plan.table(part, False) for part in range(len(blocks))])
    flat = [b for part in blocks for b in part]
    anywhere = pl.BlockSpec(memory_space=pl.ANY)
    moved = sum(2 * b.size * b.dtype.itemsize for b in flat)
    return pl.pallas_call(
        functools.partial(
            assemble_kernel, quarter=plan.half // 2, parts=len(blocks), layout=layout
        ),
        in_specs=[pl.BlockSpec(memory_space=pltpu.SMEM)] + [anywhere] * len(flat),
        out_specs=[pl.BlockSpec(memory_space=pltpu.VMEM)] * len(out_shapes),
        out_shape=[jax.ShapeDtypeStruct(s, bf16) for s in out_shapes],
        scratch_shapes=[pltpu.SemaphoreType.DMA((len(layout), plan.ways))],
        compiler_params=pltpu.CompilerParams(vmem_limit_bytes=VMEM_LIMIT),
        cost_estimate=pl.CostEstimate(flops=0, bytes_accessed=moved, transcendentals=0),
        name="assemble",
    )(table, *flat)


def plus(a, b):
    return a.astype(f32) + b.astype(f32)


class Scatter:
    def __init__(self, plan, parts, keep, send):
        self.plan, self.parts, self.keep = plan, parts, keep
        self.got = [lax.ppermute(s, AXES, plan.core_pairs()) for s in send]
        self.at = 0

    def step(self):
        half = self.keep[0].shape[0] // 2
        going = [plus(k[half:], g[half:]).astype(bf16) for k, g in zip(self.keep, self.got)]
        arriving = [
            lax.ppermute(g, AXES, self.plan.pairs(part, self.at))
            for g, part in zip(going, self.parts)
        ]
        self.keep = [plus(k[:half], g[:half]).astype(bf16) for k, g in zip(self.keep, self.got)]
        self.got = arriving
        self.at += 1

    def finish(self):
        while self.at < self.plan.steps:
            self.step()
        totals = [plus(k[0], g[0]) for k, g in zip(self.keep, self.got)]
        if self.plan.low > 1:
            groups = self.plan.low_groups()
            totals = [
                lax.psum_scatter(
                    t, AXES, scatter_dimension=0, tiled=True, axis_index_groups=groups
                )
                for t in totals
            ]
        return totals


def dot_nt(a, b):
    return lax.dot_general(a, b, (((1,), (1,)), ((), ())), preferred_element_type=f32)


def dot_nn(a, b):
    return lax.dot_general(a, b, (((1,), (0,)), ((), ())), preferred_element_type=f32)


def transposed(a):
    return a.astype(f32).T.astype(a.dtype)


def allowed_block(i, j, split, blk):
    key_pos = j * blk + lax.broadcasted_iota(jnp.int32, (blk, blk), 0)
    query_row = i * blk + lax.broadcasted_iota(jnp.int32, (1, blk), 1)
    allowed = key_pos >= jnp.where(query_row >= split, split, 0)
    if i == j:
        allowed &= key_pos <= i * blk + lax.broadcasted_iota(jnp.int32, (blk, blk), 1)
    return allowed


def attention_kernel(split_ref, q_ref, k_ref, v_ref, o_ref, lse_ref, *, seq, hd, blk):
    split = split_ref[0]
    v_t = transposed(v_ref[...])
    lane = lax.broadcasted_iota(jnp.int32, (blk, 2 * hd), 1)
    for i in range(seq // blk):
        rows = slice(i * blk, (i + 1) * blk)
        outs = []
        for h in (0, 1):
            q = jnp.where((lane >= hd) if h else (lane < hd), q_ref[rows, :], 0) * bf16(hd**-0.5)
            scores = []
            for j in range(i + 1):
                s = dot_nt(k_ref[j * blk : (j + 1) * blk, :], q)
                scores.append(jnp.where(allowed_block(i, j, split, blk), s, NEG))
            peak = scores[0].max(0, keepdims=True)
            for s in scores[1:]:
                peak = jnp.maximum(peak, s.max(0, keepdims=True))
            total = jnp.zeros((1, blk), f32)
            mixed = jnp.zeros((hd, blk), f32)
            for j, s in enumerate(scores):
                e = jnp.exp(s - peak)
                total += e.sum(0, keepdims=True)
                mixed += dot_nn(
                    v_t[h * hd : (h + 1) * hd, j * blk : (j + 1) * blk], e.astype(bf16)
                )
            outs.append(mixed / total)
            lse_ref[0, h : h + 1, rows] = peak + jnp.log(total)
        o_ref[rows, :] = jnp.concatenate(outs, 0).T


def attention(split, qkv, heads, blk):
    seq, width = qkv.shape[0], qkv.shape[1] // 3
    hd, pairs = width // heads, heads // 2
    w = 2 * hd
    return pl.pallas_call(
        functools.partial(attention_kernel, seq=seq, hd=hd, blk=blk),
        grid=(pairs,),
        in_specs=[
            pl.BlockSpec(memory_space=pltpu.SMEM),
            pl.BlockSpec((seq, w), lambda p: (0, p)),
            pl.BlockSpec((seq, w), lambda p: (0, p + pairs)),
            pl.BlockSpec((seq, w), lambda p: (0, p + 2 * pairs)),
        ],
        out_specs=[
            pl.BlockSpec((seq, w), lambda p: (0, p)),
            pl.BlockSpec((1, 2, seq), lambda p: (p, 0, 0)),
        ],
        out_shape=[
            jax.ShapeDtypeStruct((seq, width), f32),
            jax.ShapeDtypeStruct((pairs, 2, seq), f32),
        ],
        compiler_params=pltpu.CompilerParams(vmem_limit_bytes=VMEM_LIMIT),
        cost_estimate=pl.CostEstimate(
            flops=12 * seq * seq * width,
            bytes_accessed=seq * width * 10,
            transcendentals=heads * seq * seq,
        ),
        name="attention",
    )(split, qkv, qkv, qkv)


def attention_back_kernel(
    split_ref, q_ref, k_ref, v_ref, da_ref, o_ref, lse_ref, dq_ref, dk_ref, dv_ref, dk_acc, dv_acc,
    *, seq, hd, blk,
):
    split = split_ref[0]
    k_t = transposed(k_ref[...])
    lane = lax.broadcasted_iota(jnp.int32, (blk, 2 * hd), 1)
    for i in range(seq // blk):
        rows = slice(i * blk, (i + 1) * blk)
        q_full, da_full = q_ref[rows, :], da_ref[rows, :]
        inner = (da_full.astype(f32) * o_ref[rows, :]).T
        dqs = []
        for h in (0, 1):
            mine = (lane >= hd) if h else (lane < hd)
            q = jnp.where(mine, q_full, 0) * bf16(hd**-0.5)
            da = jnp.where(mine, da_full, 0)
            row_inner = inner[h * hd : (h + 1) * hd].sum(0, keepdims=True)
            lse = lse_ref[0, h : h + 1, rows]
            dq = jnp.zeros((hd, blk), f32)
            for j in range(i + 1):
                keys = slice(j * blk, (j + 1) * blk)
                s = dot_nt(k_ref[keys, :], q)
                s = jnp.where(allowed_block(i, j, split, blk), s, NEG)
                p = jnp.exp(s - lse)
                dp = dot_nt(v_ref[keys, :], da)
                ds = (p * (dp - row_inner)).astype(bf16)
                dv = dot_nn(p.astype(bf16), da)
                dk = dot_nn(ds, q)
                if i == j and h == 0:
                    dv_acc[keys, :] = dv
                    dk_acc[keys, :] = dk
                else:
                    dv_acc[keys, :] += dv
                    dk_acc[keys, :] += dk
                dq += dot_nn(k_t[h * hd : (h + 1) * hd, keys], ds)
            dqs.append(dq)
        dq_ref[rows, :] = (jnp.concatenate(dqs, 0).T * (hd**-0.5)).astype(bf16)
    dk_ref[...] = dk_acc[...].astype(bf16)
    dv_ref[...] = dv_acc[...].astype(bf16)


def attention_back(split, qkv, da, attended, lse, heads, blk, which):
    seq, width = qkv.shape[0], qkv.shape[1] // 3
    hd, pairs = width // heads, heads // 2
    w = 2 * hd
    count = pairs // 2
    start = which * count
    column = pl.BlockSpec((seq, w), lambda p: (0, p + start))
    out = pl.BlockSpec((seq, w), lambda p: (0, p))
    return pl.pallas_call(
        functools.partial(attention_back_kernel, seq=seq, hd=hd, blk=blk),
        grid=(count,),
        in_specs=[
            pl.BlockSpec(memory_space=pltpu.SMEM),
            column,
            pl.BlockSpec((seq, w), lambda p: (0, p + start + pairs)),
            pl.BlockSpec((seq, w), lambda p: (0, p + start + 2 * pairs)),
            column,
            column,
            pl.BlockSpec((1, 2, seq), lambda p: (p + start, 0, 0)),
        ],
        out_specs=[out, out, out],
        out_shape=[jax.ShapeDtypeStruct((seq, width // 2), bf16)] * 3,
        scratch_shapes=[pltpu.VMEM((seq, w), f32)] * 2,
        compiler_params=pltpu.CompilerParams(vmem_limit_bytes=VMEM_LIMIT),
        cost_estimate=pl.CostEstimate(
            flops=10 * seq * seq * width,
            bytes_accessed=seq * width * 10,
            transcendentals=heads * seq * seq // 2,
        ),
        name="attention_back",
    )(split, qkv, qkv, qkv, da, attended, lse)


def grad_rows_kernel(table_ref, left_ref, right_ref, send_ref, keep_ref, left_t, acc, *, ways):
    @pl.when(pl.program_id(0) == 0)
    def _():
        left_t[...] = transposed(left_ref[...])

    acc[...] = dot_nn(left_t[...], right_ref[...])
    rows = acc.shape[0] // ways
    for r in range(ways // 2):
        at = pl.multiple_of(table_ref[r] * rows, rows)
        keep_ref[r] = acc[pl.ds(at, rows), :].astype(bf16)
        at = pl.multiple_of(table_ref[ways // 2 + r] * rows, rows)
        send_ref[r] = acc[pl.ds(at, rows), :].astype(bf16)


def grad_rows(table, left, right, tile):
    tokens, m = left.shape
    n = right.shape[1]
    ways = table.shape[0]
    block = pl.BlockSpec((ways // 2, m // ways, tile), lambda i: (0, 0, i))
    shape = jax.ShapeDtypeStruct((ways // 2, m // ways, n), bf16)
    send, keep = pl.pallas_call(
        functools.partial(grad_rows_kernel, ways=ways),
        grid=(n // tile,),
        in_specs=[
            pl.BlockSpec(memory_space=pltpu.SMEM),
            pl.BlockSpec((tokens, m), lambda i: (0, 0)),
            pl.BlockSpec((tokens, tile), lambda i: (0, i)),
        ],
        out_specs=[block, block],
        out_shape=[shape, shape],
        scratch_shapes=[pltpu.VMEM((m, tokens), bf16), pltpu.VMEM((m, tile), f32)],
        compiler_params=pltpu.CompilerParams(vmem_limit_bytes=VMEM_LIMIT),
        cost_estimate=pl.CostEstimate(
            flops=2 * tokens * m * n,
            bytes_accessed=2 * (tokens * (m + n) + m * n),
            transcendentals=0,
        ),
        name="grad_rows",
    )(table, left, right)
    return keep, send


def grad_tall_kernel(table_ref, *refs, per_step, sends):
    lefts, (right_ref, send_ref, keep_ref) = refs[:per_step], refs[per_step:]
    left_t = jnp.concatenate([transposed(ref[...]) for ref in lefts], 0)
    out = dot_nn(left_t, right_ref[...]).astype(bf16)
    out = out.reshape(per_step, out.shape[0] // per_step, out.shape[1])

    @pl.when(pl.program_id(0) < sends)
    def _():
        send_ref[...] = out

    @pl.when(pl.program_id(0) >= sends)
    def _():
        keep_ref[...] = out


def grad_tall(table, left, right, per_step=4):
    tokens, m = left.shape
    n = right.shape[1]
    ways = table.shape[0]
    rows = m // ways
    sends = ways // 2 // per_step

    def left_spec(k):
        def place(i, table_ref):
            r = lax.rem(i * per_step + k + ways // 2, ways)
            return (0, table_ref[r])

        return pl.BlockSpec((tokens, rows), place)

    shape = jax.ShapeDtypeStruct((ways // 2, rows, n), bf16)
    send, keep = pl.pallas_call(
        functools.partial(grad_tall_kernel, per_step=per_step, sends=sends),
        grid_spec=pltpu.PrefetchScalarGridSpec(
            num_scalar_prefetch=1,
            grid=(ways // per_step,),
            in_specs=[left_spec(k) for k in range(per_step)]
            + [pl.BlockSpec((tokens, n), lambda i, t: (0, 0))],
            out_specs=[
                pl.BlockSpec((per_step, rows, n), lambda i, t: (jnp.minimum(i, sends - 1), 0, 0)),
                pl.BlockSpec((per_step, rows, n), lambda i, t: (jnp.maximum(i - sends, 0), 0, 0)),
            ],
        ),
        out_shape=[shape, shape],
        compiler_params=pltpu.CompilerParams(vmem_limit_bytes=VMEM_LIMIT),
        cost_estimate=pl.CostEstimate(
            flops=2 * tokens * m * n,
            bytes_accessed=2 * (tokens * (m + n) + m * n),
            transcendentals=0,
        ),
        name="grad_tall",
    )(table, *([left] * per_step), right)
    return keep, send


def norm_rows(values, norm_gain, norm_shift):
    center = values - jnp.mean(values, axis=-1, keepdims=True)
    spread = jnp.mean(center * center, axis=-1, keepdims=True)
    return center * lax.rsqrt(spread + epsilon) * norm_gain + norm_shift


def smooth_gate(values):
    return jax.nn.gelu(values, approximate=True)


def rounded(values):
    return lax.optimization_barrier(values.astype(bf16)).astype(f32)


def local(
    plan,
    tokens,
    doc_split,
    head_scale,
    query_key_value_weight,
    output_weight,
    first_weight,
    second_weight,
    model_vectors,
    hidden_vectors,
    cotangent,
):
    seq, width = tokens.shape
    hidden = first_weight.shape[1]
    heads = head_scale.shape[0]
    head_shape = (seq, heads, width // heads)
    blk = min(256, seq)
    shard = query_key_value_weight.shape[0]

    per_row = hidden_vectors.shape[1] // shard
    n_vec = model_vectors.shape[0]
    n_hid = hidden_vectors.shape[0]
    vec_cols = jnp.concatenate(
        [
            model_vectors.T,
            hidden_vectors.reshape(n_hid, shard, per_row)
            .transpose(1, 0, 2)
            .reshape(shard, n_hid * per_row),
        ],
        1,
    )
    vec_cols = jnp.pad(vec_cols, ((0, 0), (0, 128 - vec_cols.shape[1])))
    cut = 2 * width
    piece_a = join_low(plan, jnp.concatenate([query_key_value_weight[:, :cut], vec_cols], 1))
    piece_b = join_low(
        plan, jnp.concatenate([query_key_value_weight[:, cut:], output_weight], 1)
    )
    first = Gather(plan, [piece_a, piece_b])
    second = Gather(plan, [join_low(plan, first_weight), join_low(plan, second_weight)])
    for step in range(plan.steps):
        first.step()
        if step < plan.steps - 2:
            second.after(first.fresh[0])
            second.step()
    first.cross_held()
    first.cross_fresh()
    second.after(first.fresh[0])
    while second.at < plan.steps - 1:
        second.step()
    w_qkv, w_out, vec_all = assemble(
        plan,
        first.blocks(),
        [(width, 3 * width), (width, width), (width, 128)],
        [(0, 0, 0, 0, cut), (0, cut, 2, 0, 128), (1, 0, 0, cut, width), (1, width, 1, 0, width)],
    )
    vecd = vec_all[:, :n_vec].T.astype(f32)
    vecff = (
        vec_all[:, n_vec : n_vec + n_hid * per_row]
        .reshape(width, n_hid, per_row)
        .transpose(1, 0, 2)
        .reshape(n_hid, hidden)
        .astype(f32)
    )

    resid = tokens.astype(f32)
    normed_first, first_back = jax.vjp(norm_rows, resid, vecd[0], vecd[1])
    first_activation = normed_first.astype(bf16)
    projected = jnp.dot(first_activation, w_qkv, preferred_element_type=f32)
    qkv_bias = jnp.concatenate([vecd[2], jnp.zeros((width,), f32), vecd[3]])
    qkv = (projected + qkv_bias).astype(bf16)
    qkv, *second.fresh = tied(qkv, *second.fresh)
    second.step()
    second.cross_held()
    attended, lse = attention(doc_split, qkv, heads, blk)
    attended, *second.fresh = tied(attended, *second.fresh)
    second.cross_fresh()
    scale_row = jnp.repeat(head_scale, width // heads)
    scaled_heads = (attended * scale_row).astype(bf16)
    branch_output = jnp.dot(scaled_heads, w_out, preferred_element_type=f32) + vecd[4]
    normed_attn, attn_norm_back = jax.vjp(norm_rows, branch_output, vecd[5], vecd[6])
    middle_state = resid + normed_attn
    normed_second, second_back = jax.vjp(norm_rows, middle_state, vecd[7], vecd[8])
    second_activation = normed_second.astype(bf16)
    w_fc1, w_fc2 = assemble(
        plan,
        second.blocks(),
        [(width, hidden), (hidden, width)],
        [(0, 0, 0, 0, hidden), (1, 0, 1, 0, width)],
    )
    before_gate = jnp.dot(second_activation, w_fc1, preferred_element_type=f32) + vecff[0]
    gated, gate_back = jax.vjp(smooth_gate, before_gate)
    normed_hidden, hidden_back = jax.vjp(norm_rows, gated, vecff[1], vecff[2])
    hidden_activation = normed_hidden.astype(bf16)
    result = middle_state + (
        jnp.dot(hidden_activation, w_fc2, preferred_element_type=f32) + vecd[9]
    )
    output = result.astype(bf16)

    tables = [plan.table(part, True) for part in (0, 1)]
    upstream = cotangent.astype(f32)
    keep_fc2, send_fc2 = grad_tall(tables[1], hidden_activation, cotangent)
    grad_bias_two = jnp.sum(upstream, axis=0)
    grad_hidden_act = rounded(dot_nt(cotangent, w_fc2))
    grad_gated, grad_gain_hidden, grad_shift_hidden = hidden_back(grad_hidden_act)
    grad_pre = gate_back(grad_gated)[0].astype(bf16)
    keep_fc1, send_fc1 = grad_rows(tables[0], second_activation, grad_pre, 512)
    late = Scatter(plan, [0, 1], [keep_fc1, keep_fc2], [send_fc1, send_fc2])
    grad_bias_one = jnp.sum(grad_pre.astype(f32), axis=0)
    grad_second_act = dot_nt(grad_pre, w_fc1)
    grad_middle_norm, grad_gain_second, grad_shift_second = second_back(grad_second_act)
    grad_middle = upstream + grad_middle_norm
    grad_branch, grad_gain_attn, grad_shift_attn = attn_norm_back(grad_middle)
    grad_branch_low = grad_branch.astype(bf16)
    grad_bias_out = jnp.sum(grad_branch_low.astype(f32), axis=0)
    grad_scaled = rounded(dot_nt(grad_branch_low, w_out))
    head_products = jnp.sum(grad_scaled * attended, axis=0)
    grad_heads_local = jnp.sum(head_products.reshape(heads, -1), axis=1)
    grad_attended = (grad_scaled * scale_row).astype(bf16)
    grad_attended, *late.got = tied(grad_attended, *late.got)
    late.step()
    first_half = attention_back(doc_split, qkv, grad_attended, attended, lse, heads, blk, 0)
    grad_attended, first_half, *late.got = tied(grad_attended, first_half, *late.got)
    late.step()
    last_half = attention_back(doc_split, qkv, grad_attended, attended, lse, heads, blk, 1)
    last_half, *late.got = tied(last_half, *late.got)
    late.step()
    dq, dk, dv = (jnp.concatenate(pair, 1) for pair in zip(first_half, last_half))
    grad_projected = jnp.concatenate([dq, dk, dv], axis=1)
    grad_bias_query = jnp.sum(dq.astype(f32), axis=0)
    grad_bias_value = jnp.sum(dv.astype(f32), axis=0)
    grad_first_act = dot_nt(grad_projected, w_qkv)
    grad_resid_norm, grad_gain_first, grad_shift_first = first_back(grad_first_act)
    grad_tokens = grad_middle + grad_resid_norm
    vec_grads = jnp.stack(
        [
            grad_gain_first,
            grad_shift_first,
            grad_bias_query,
            grad_bias_value,
            grad_bias_out,
            grad_gain_attn,
            grad_shift_attn,
            grad_gain_second,
            grad_shift_second,
            grad_bias_two,
        ]
    )
    hid_grads = jnp.stack([grad_bias_one, grad_gain_hidden, grad_shift_hidden])
    vec_cols = jnp.concatenate(
        [
            vec_grads.T,
            hid_grads.reshape(n_hid, width, per_row)
            .transpose(1, 0, 2)
            .reshape(width, n_hid * per_row),
            jnp.broadcast_to(grad_heads_local, (width, heads)),
        ],
        1,
    )
    used = vec_cols.shape[1]
    vec_cols = jnp.pad(vec_cols, ((0, 0), (0, 128 - used))).astype(bf16)
    vec_blocks = vec_cols.reshape(plan.ways, width // plan.ways, 128)[tables[0]]
    keep_a, send_a = grad_rows(tables[0], first_activation, grad_projected[:, :cut], 512)
    keep_a = jnp.concatenate([keep_a, vec_blocks[: plan.half]], 2)
    send_a = jnp.concatenate([send_a, vec_blocks[plan.half :]], 2)
    keep_b, send_b = grad_rows(tables[1], first_activation, dv, 512)
    keep_o, send_o = grad_rows(tables[1], scaled_heads, grad_branch_low, 512)
    keep_b = jnp.concatenate([keep_b, keep_o], 2)
    send_b = jnp.concatenate([send_b, send_o], 2)
    last = Scatter(plan, [0, 1], [keep_a, keep_b], [send_a, send_b])
    sent_fc1, sent_fc2 = late.finish()
    sent_a, sent_b = last.finish()
    sent_qkv = jnp.concatenate([sent_a[:, :cut], sent_b[:, :width]], 1)
    sent_out = sent_b[:, width:]
    sent_vecd = sent_a[:, cut : cut + n_vec].T
    mid = cut + n_vec + n_hid * per_row
    sent_vecff = (
        sent_a[:, cut + n_vec : mid]
        .reshape(shard, n_hid, per_row)
        .transpose(1, 0, 2)
        .reshape(n_hid, shard * per_row)
    )
    grad_heads = sent_a[0, mid : mid + heads]
    return (
        output,
        grad_tokens,
        grad_heads,
        sent_qkv,
        sent_out,
        sent_fc1,
        sent_fc2,
        sent_vecd,
        sent_vecff,
    )


def solution(mesh):
    rows = P(AXES, None)
    columns = P(None, AXES)
    return jax.shard_map(
        functools.partial(local, Plan(mesh)),
        mesh=mesh,
        in_specs=(rows, P(AXES), P(), rows, rows, rows, rows, columns, columns, rows),
        out_specs=(rows, rows, P(), rows, rows, rows, rows, columns, columns),
        check_vma=False,
    )
```

```python
import functools

import jax
import jax.numpy as jnp
from jax import lax
from jax.experimental import pallas as pl
from jax.experimental.pallas import tpu as pltpu
from jax.sharding import PartitionSpec as P

epsilon = 1e-05
AXES = ("dp", "fsdp")
f32 = jnp.float32
bf16 = jnp.bfloat16
NEG = -1e30
VMEM_LIMIT = 56 << 20


class Plan:
    def __init__(self, mesh):
        n_dp, n_fs = mesh.shape["dp"], mesh.shape["fsdp"]
        self.count = n_dp * n_fs
        self.ways = min(self.count, 32)
        self.low = self.count // self.ways
        self.core = max(1, n_fs // self.low)
        self.dims = [1 << b for b in range(self.ways.bit_length() - 1) if 1 << b != self.core]
        self.half = self.ways // 2
        self.steps = len(self.dims)

    def order(self, core_bit, part, gathers):
        near, far = self.dims[:-1], self.dims[-1:]
        shift = (core_bit if part == 0 else 2) % len(near)
        near = near[shift:] + near[:shift]
        return far + near if gathers else near + far

    def pairs(self, part, step, gathers):
        out = []
        for i in range(self.count):
            group = i // self.low
            mask = self.order(int(bool(group & self.core)), part, gathers)[step]
            out.append((i, i ^ (mask * self.low)))
        return out

    def core_pairs(self):
        return [(i, i ^ (self.core * self.low)) for i in range(self.count)]

    def low_groups(self):
        return [[g * self.low + i for i in range(self.low)] for g in range(self.ways)]

    def table(self, part, gathers):
        me = (lax.axis_index("dp") * lax.axis_size("fsdp") + lax.axis_index("fsdp")) // self.low
        rows = []
        for core_bit in (0, 1):
            row = []
            for other in (0, 1):
                masks = self.order(core_bit ^ other, part, gathers)
                for r in range(self.half):
                    x = self.core if other else 0
                    for k in range(self.steps):
                        bit = k if gathers else self.steps - 1 - k
                        if (r >> bit) & 1:
                            x ^= masks[k]
                    row.append(x)
            rows.append(row)
        mine = ((me & self.core) != 0).astype(jnp.int32)
        masks = jnp.where(mine == 1, jnp.array(rows[1], jnp.int32), jnp.array(rows[0], jnp.int32))
        return jnp.bitwise_xor(me.astype(jnp.int32), masks)


def tied(*values):
    return lax.optimization_barrier(values)


class Gather:
    def __init__(self, plan, pieces):
        self.plan = plan
        self.held = [piece[None] for piece in pieces]
        self.fresh = None
        self.at = 0

    def step(self):
        if self.fresh is not None:
            self.held = [jnp.concatenate(pair, 0) for pair in zip(self.held, self.fresh)]
        self.fresh = [
            lax.ppermute(h, AXES, self.plan.pairs(part, self.at, True)) for part, h in enumerate(self.held)
        ]
        self.at += 1

    def after(self, other):
        if self.fresh is None:
            *self.held, _ = tied(*self.held, other)
        else:
            *self.fresh, _ = tied(*self.fresh, other)

    def cross_held(self):
        self.far_held = [lax.ppermute(h, AXES, self.plan.core_pairs()) for h in self.held]

    def cross_fresh(self):
        self.far_fresh = [lax.ppermute(h, AXES, self.plan.core_pairs()) for h in self.fresh]

    def blocks(self):
        return [list(b) for b in zip(self.held, self.fresh, self.far_held, self.far_fresh)]


def join_low(plan, piece):
    if plan.low == 1:
        return piece
    return lax.all_gather(piece, AXES, axis=0, tiled=True, axis_index_groups=plan.low_groups())


def assemble_kernel(table_ref, *refs, quarter, parts, layout):
    sources, rest = refs[: 4 * parts], refs[4 * parts :]
    outs, sem = rest[:-1], rest[-1]
    copies = []
    for line, (part, src_col, out, out_col, width, stride, row) in enumerate(layout):
        for r in range(4 * quarter):
            src = sources[4 * part + r // quarter]
            rows = src.shape[1]
            at = pl.multiple_of(table_ref[part, r] * stride + row, rows)
            copy = pltpu.make_async_copy(
                src.at[r % quarter, :, pl.ds(src_col, width)],
                outs[out].at[pl.ds(at, rows), pl.ds(out_col, width)],
                sem.at[line, r],
            )
            copy.start()
            copies.append(copy)
    for copy in copies:
        copy.wait()


def assemble(plan, blocks, out_shapes, layout):
    table = jnp.stack([plan.table(part, True) for part in range(len(blocks))])
    flat = [b for part in blocks for b in part]
    anywhere = pl.BlockSpec(memory_space=pl.ANY)
    moved = sum(2 * b.size * b.dtype.itemsize for b in flat)
    return pl.pallas_call(
        functools.partial(
            assemble_kernel, quarter=plan.half // 2, parts=len(blocks), layout=layout
        ),
        in_specs=[pl.BlockSpec(memory_space=pltpu.SMEM)] + [anywhere] * len(flat),
        out_specs=[pl.BlockSpec(memory_space=pltpu.VMEM)] * len(out_shapes),
        out_shape=[jax.ShapeDtypeStruct(s, bf16) for s in out_shapes],
        scratch_shapes=[pltpu.SemaphoreType.DMA((len(layout), plan.ways))],
        compiler_params=pltpu.CompilerParams(vmem_limit_bytes=VMEM_LIMIT),
        cost_estimate=pl.CostEstimate(flops=0, bytes_accessed=moved, transcendentals=0),
        name="assemble",
    )(table, *flat)


def plus(a, b):
    return a.astype(f32) + b.astype(f32)


class Scatter:
    def __init__(self, plan, parts, keep, send):
        self.plan, self.parts, self.keep = plan, parts, keep
        self.got = [lax.ppermute(s, AXES, plan.core_pairs()) for s in send]
        self.at = 0

    def step(self):
        half = self.keep[0].shape[0] // 2
        going = [plus(k[half:], g[half:]).astype(bf16) for k, g in zip(self.keep, self.got)]
        arriving = [
            lax.ppermute(g, AXES, self.plan.pairs(part, self.at, False))
            for g, part in zip(going, self.parts)
        ]
        self.keep = [plus(k[:half], g[:half]).astype(bf16) for k, g in zip(self.keep, self.got)]
        self.got = arriving
        self.at += 1

    def finish(self):
        while self.at < self.plan.steps:
            self.step()
        return [plus(k[0], g[0]) for k, g in zip(self.keep, self.got)]


def split_low(plan, total):
    if plan.low == 1:
        return total
    return lax.psum_scatter(
        total, AXES, scatter_dimension=0, tiled=True, axis_index_groups=plan.low_groups()
    )


def dot_nt(a, b):
    return lax.dot_general(a, b, (((1,), (1,)), ((), ())), preferred_element_type=f32)


def dot_nn(a, b):
    return lax.dot_general(a, b, (((1,), (0,)), ((), ())), preferred_element_type=f32)


def transposed(a):
    return a.astype(f32).T.astype(a.dtype)


def allowed_block(i, j, split, blk):
    key_pos = j * blk + lax.broadcasted_iota(jnp.int32, (blk, blk), 0)
    query_row = i * blk + lax.broadcasted_iota(jnp.int32, (1, blk), 1)
    allowed = key_pos >= jnp.where(query_row >= split, split, 0)
    if i == j:
        allowed &= key_pos <= i * blk + lax.broadcasted_iota(jnp.int32, (blk, blk), 1)
    return allowed


def attention_kernel(split_ref, q_ref, k_ref, v_ref, o_ref, lse_ref, *, seq, hd, blk):
    split = split_ref[0]
    v_t = transposed(v_ref[...])
    lane = lax.broadcasted_iota(jnp.int32, (blk, 2 * hd), 1)
    for i in range(seq // blk):
        rows = slice(i * blk, (i + 1) * blk)
        outs = []
        for h in (0, 1):
            q = jnp.where((lane >= hd) if h else (lane < hd), q_ref[rows, :], 0) * bf16(hd**-0.5)
            scores = []
            for j in range(i + 1):
                s = dot_nt(k_ref[j * blk : (j + 1) * blk, :], q)
                scores.append(jnp.where(allowed_block(i, j, split, blk), s, NEG))
            peak = scores[0].max(0, keepdims=True)
            for s in scores[1:]:
                peak = jnp.maximum(peak, s.max(0, keepdims=True))
            total = jnp.zeros((1, blk), f32)
            mixed = jnp.zeros((hd, blk), f32)
            for j, s in enumerate(scores):
                e = jnp.exp(s - peak)
                total += e.sum(0, keepdims=True)
                mixed += dot_nn(
                    v_t[h * hd : (h + 1) * hd, j * blk : (j + 1) * blk], e.astype(bf16)
                )
            outs.append(mixed / total)
            lse_ref[0, h : h + 1, rows] = peak + jnp.log(total)
        o_ref[rows, :] = jnp.concatenate(outs, 0).T


def attention(split, qkv, heads, blk, which):
    seq, width = qkv.shape[0], qkv.shape[1] // 3
    hd, pairs = width // heads, heads // 2
    w = 2 * hd
    count = pairs // 2
    start = which * count
    return pl.pallas_call(
        functools.partial(attention_kernel, seq=seq, hd=hd, blk=blk),
        grid=(count,),
        in_specs=[
            pl.BlockSpec(memory_space=pltpu.SMEM),
            pl.BlockSpec((seq, w), lambda p: (0, p + start)),
            pl.BlockSpec((seq, w), lambda p: (0, p + start + pairs)),
            pl.BlockSpec((seq, w), lambda p: (0, p + start + 2 * pairs)),
        ],
        out_specs=[
            pl.BlockSpec((seq, w), lambda p: (0, p)),
            pl.BlockSpec((1, 2, seq), lambda p: (p, 0, 0)),
        ],
        out_shape=[
            jax.ShapeDtypeStruct((seq, width // 2), f32),
            jax.ShapeDtypeStruct((count, 2, seq), f32),
        ],
        compiler_params=pltpu.CompilerParams(vmem_limit_bytes=VMEM_LIMIT),
        cost_estimate=pl.CostEstimate(
            flops=6 * seq * seq * width,
            bytes_accessed=seq * width * 5,
            transcendentals=heads * seq * seq // 2,
        ),
        name="attention",
    )(split, qkv, qkv, qkv)


def attention_back_kernel(
    split_ref, q_ref, k_ref, v_ref, da_ref, o_ref, lse_ref, dq_ref, dk_ref, dv_ref, dk_acc, dv_acc,
    *, seq, hd, blk,
):
    split = split_ref[0]
    k_t = transposed(k_ref[...])
    lane = lax.broadcasted_iota(jnp.int32, (blk, 2 * hd), 1)
    for i in range(seq // blk):
        rows = slice(i * blk, (i + 1) * blk)
        q_full, da_full = q_ref[rows, :], da_ref[rows, :]
        inner = (da_full.astype(f32) * o_ref[rows, :]).T
        dqs = []
        for h in (0, 1):
            mine = (lane >= hd) if h else (lane < hd)
            q = jnp.where(mine, q_full, 0) * bf16(hd**-0.5)
            da = jnp.where(mine, da_full, 0)
            row_inner = inner[h * hd : (h + 1) * hd].sum(0, keepdims=True)
            lse = lse_ref[0, h : h + 1, rows]
            dq = jnp.zeros((hd, blk), f32)
            for j in range(i + 1):
                keys = slice(j * blk, (j + 1) * blk)
                s = dot_nt(k_ref[keys, :], q)
                s = jnp.where(allowed_block(i, j, split, blk), s, NEG)
                p = jnp.exp(s - lse)
                dp = dot_nt(v_ref[keys, :], da)
                ds = (p * (dp - row_inner)).astype(bf16)
                dv = dot_nn(p.astype(bf16), da)
                dk = dot_nn(ds, q)
                if i == j and h == 0:
                    dv_acc[keys, :] = dv
                    dk_acc[keys, :] = dk
                else:
                    dv_acc[keys, :] += dv
                    dk_acc[keys, :] += dk
                dq += dot_nn(k_t[h * hd : (h + 1) * hd, keys], ds)
            dqs.append(dq)
        dq_ref[rows, :] = (jnp.concatenate(dqs, 0).T * (hd**-0.5)).astype(bf16)
    dk_ref[...] = dk_acc[...].astype(bf16)
    dv_ref[...] = dv_acc[...].astype(bf16)


def attention_back(split, qkv, da, attended, lse, heads, blk, which):
    seq, width = qkv.shape[0], qkv.shape[1] // 3
    hd, pairs = width // heads, heads // 2
    w = 2 * hd
    count = pairs // 2
    start = which * count
    column = pl.BlockSpec((seq, w), lambda p: (0, p + start))
    out = pl.BlockSpec((seq, w), lambda p: (0, p))
    return pl.pallas_call(
        functools.partial(attention_back_kernel, seq=seq, hd=hd, blk=blk),
        grid=(count,),
        in_specs=[
            pl.BlockSpec(memory_space=pltpu.SMEM),
            column,
            pl.BlockSpec((seq, w), lambda p: (0, p + start + pairs)),
            pl.BlockSpec((seq, w), lambda p: (0, p + start + 2 * pairs)),
            column,
            column,
            pl.BlockSpec((1, 2, seq), lambda p: (p + start, 0, 0)),
        ],
        out_specs=[out, out, out],
        out_shape=[jax.ShapeDtypeStruct((seq, width // 2), bf16)] * 3,
        scratch_shapes=[pltpu.VMEM((seq, w), f32)] * 2,
        compiler_params=pltpu.CompilerParams(vmem_limit_bytes=VMEM_LIMIT),
        cost_estimate=pl.CostEstimate(
            flops=10 * seq * seq * width,
            bytes_accessed=seq * width * 10,
            transcendentals=heads * seq * seq // 2,
        ),
        name="attention_back",
    )(split, qkv, qkv, qkv, da, attended, lse)


def grads_kernel(table_ref, place_ref, *refs, runs, n_left, n_right, tile, extra):
    lefts, rights = refs[:n_left], refs[n_left : n_left + n_right]
    extra_ref = refs[n_left + n_right] if extra else None
    send_ref, keep_ref, left = refs[n_left + n_right + bool(extra) :]
    ways, rows, tokens = left.shape
    step = pl.program_id(0)
    columns = pl.ds(pl.multiple_of(step * tile, tile), tile) if extra else slice(None)
    for first, last, l, r in runs:

        @pl.when(step == first)
        def _():
            for w in range(ways):
                left[w] = lefts[l][table_ref[w], 0]

        @pl.when((step >= first) & (step < last))
        def _():
            product = dot_nn(left[...].reshape(ways * rows, tokens), rights[r][...])
            product = product.astype(bf16).reshape(ways, rows, tile)
            keep_ref[:, :, columns] = product[: ways // 2]
            send_ref[:, :, columns] = product[ways // 2 :]

    if extra:

        @pl.when(step == 0)
        def _():
            width = extra_ref.shape[2]
            at = slice(keep_ref.shape[2] - width, keep_ref.shape[2])
            for w in range(ways // 2):
                keep_ref[w, :, at] = extra_ref[table_ref[w]]
                send_ref[w, :, at] = extra_ref[table_ref[ways // 2 + w]]


def grads(table, jobs, extra=None, tile=512):
    ways, _, rows, tokens = jobs[0][0].shape
    lefts, rights, runs, places = [], [], [], []
    at = 0
    for left, q, right, numbers in jobs:
        for known, one in ((lefts, left), (rights, right)):
            if not any(one is k for k in known):
                known.append(one)
        l = next(i for i, k in enumerate(lefts) if k is left)
        r = next(i for i, k in enumerate(rights) if k is right)
        runs.append((at, at + len(numbers), l, r))
        for n in numbers:
            places.append((l, q, r, n))
        at += len(numbers)

    def held(which, entry, count):
        table = []
        for k in range(count):
            used = [(s, p[entry]) for s, p in enumerate(places) if p[which] == k]
            table.append([next((v for s, v in used if s >= i), used[-1][1]) for i in range(at)])
        return table

    place = jnp.array(held(0, 1, len(lefts)) + held(2, 3, len(rights)), jnp.int32)

    def left_spec(k):
        return pl.BlockSpec((ways, 1, rows, tokens), lambda i, t, p: (0, p[k, i], 0, 0))

    def right_spec(k):
        return pl.BlockSpec((tokens, tile), lambda i, t, p: (0, p[len(lefts) + k, i]))

    width = at * tile
    if extra is None:
        out_spec = pl.BlockSpec((ways // 2, rows, tile), lambda i, t, p: (0, 0, i))
        more, more_spec = [], []
    else:
        width += extra.shape[2]
        out_spec = pl.BlockSpec((ways // 2, rows, width), lambda i, t, p: (0, 0, 0))
        more, more_spec = [extra], [pl.BlockSpec(extra.shape, lambda i, t, p: (0, 0, 0))]
    shape = jax.ShapeDtypeStruct((ways // 2, rows, width), bf16)
    send, keep = pl.pallas_call(
        functools.partial(
            grads_kernel,
            runs=runs,
            n_left=len(lefts),
            n_right=len(rights),
            tile=tile,
            extra=extra is not None,
        ),
        grid_spec=pltpu.PrefetchScalarGridSpec(
            num_scalar_prefetch=2,
            grid=(at,),
            in_specs=[left_spec(k) for k in range(len(lefts))]
            + [right_spec(k) for k in range(len(rights))]
            + more_spec,
            out_specs=[out_spec, out_spec],
            scratch_shapes=[pltpu.VMEM((ways, rows, tokens), bf16)],
        ),
        out_shape=[shape, shape],
        compiler_params=pltpu.CompilerParams(vmem_limit_bytes=VMEM_LIMIT),
        cost_estimate=pl.CostEstimate(
            flops=2 * tokens * ways * rows * tile * at,
            bytes_accessed=2 * ways * rows * (tokens * (len(lefts) + 1) + 2 * width),
            transcendentals=0,
        ),
        name="grads",
    )(table, place, *lefts, *rights, *more)
    return keep, send


def norm_rows(values, norm_gain, norm_shift):
    center = values - jnp.mean(values, axis=-1, keepdims=True)
    spread = jnp.mean(center * center, axis=-1, keepdims=True)
    return center * lax.rsqrt(spread + epsilon) * norm_gain + norm_shift


def smooth_gate(values):
    return jax.nn.gelu(values, approximate=True)


def rounded(values):
    return lax.optimization_barrier(values.astype(bf16)).astype(f32)


def local(
    plan,
    tokens,
    doc_split,
    head_scale,
    query_key_value_weight,
    output_weight,
    first_weight,
    second_weight,
    model_vectors,
    hidden_vectors,
    cotangent,
):
    seq, width = tokens.shape
    hidden = first_weight.shape[1]
    heads = head_scale.shape[0]
    head_shape = (seq, heads, width // heads)
    blk = min(256, seq)
    shard = query_key_value_weight.shape[0]

    per_row = hidden_vectors.shape[1] // shard
    n_vec = model_vectors.shape[0]
    n_hid = hidden_vectors.shape[0]
    vec_cols = jnp.concatenate(
        [
            model_vectors.T,
            hidden_vectors.reshape(n_hid, shard, per_row)
            .transpose(1, 0, 2)
            .reshape(shard, n_hid * per_row),
        ],
        1,
    )
    vec_cols = jnp.pad(vec_cols, ((0, 0), (0, 128 - vec_cols.shape[1])))
    cut = 2 * width
    weight_a = join_low(plan, jnp.concatenate([query_key_value_weight, vec_cols], 1))
    fc1_rows = join_low(plan, first_weight)
    fc2_rows = join_low(plan, second_weight)
    out_rows = join_low(plan, output_weight)
    group = fc1_rows.shape[0]
    quarters = [fc2_rows[q * group : (q + 1) * group] for q in range(hidden // width)]
    half_q = len(quarters) // 2
    first = Gather(
        plan,
        [jnp.concatenate([weight_a[:, :cut], weight_a[:, 3 * width :]], 1), weight_a[:, cut : 3 * width]],
    )
    second = Gather(
        plan,
        [
            jnp.concatenate([fc1_rows, *quarters[:half_q]], 1),
            jnp.concatenate([*quarters[half_q:], out_rows], 1),
        ],
    )
    first.step()
    second.after(first.fresh[0])
    second.step()
    while first.at < plan.steps:
        first.step()
    first.cross_held()
    first.cross_fresh()
    second.after(first.held[0])
    second.step()
    w_qkv, vec_all = assemble(
        plan,
        first.blocks(),
        [(width, 3 * width), (width, 128)],
        [
            (0, 0, 0, 0, cut, group, 0),
            (0, cut, 1, 0, 128, group, 0),
            (1, 0, 0, cut, width, group, 0),
        ],
    )
    vecd = vec_all[:, :n_vec].T.astype(f32)
    vecff = (
        vec_all[:, n_vec : n_vec + n_hid * per_row]
        .reshape(width, n_hid, per_row)
        .transpose(1, 0, 2)
        .reshape(n_hid, hidden)
        .astype(f32)
    )

    resid = tokens.astype(f32)
    normed_first, first_back = jax.vjp(norm_rows, resid, vecd[0], vecd[1])
    first_activation = normed_first.astype(bf16)
    projected = jnp.dot(first_activation, w_qkv, preferred_element_type=f32)
    qkv_bias = jnp.concatenate([vecd[2], jnp.zeros((width,), f32), vecd[3]])
    qkv = (projected + qkv_bias).astype(bf16)
    qkv, *second.fresh = tied(qkv, *second.fresh)
    second.step()
    att_a, lse_a = attention(doc_split, qkv, heads, blk, 0)
    qkv, att_a, *second.fresh = tied(qkv, att_a, *second.fresh)
    second.step()
    second.cross_held()
    att_b, lse_b = attention(doc_split, qkv, heads, blk, 1)
    attended = jnp.concatenate([att_a, att_b], 1)
    lse = jnp.concatenate([lse_a, lse_b], 0)
    second.cross_fresh()
    w_fc1, w_fc2, w_out = assemble(
        plan,
        second.blocks(),
        [(width, hidden), (hidden, width), (width, width)],
        [(0, 0, 0, 0, hidden, group, 0)]
        + [
            (q // half_q, hidden * (q < half_q) + q % half_q * width, 1, 0, width, 4 * group, q * group)
            for q in range(len(quarters))
        ]
        + [(1, half_q * width, 2, 0, width, group, 0)],
    )
    scale_row = jnp.repeat(head_scale, width // heads)
    scaled_heads = (attended * scale_row).astype(bf16)
    branch_output = jnp.dot(scaled_heads, w_out, preferred_element_type=f32) + vecd[4]
    normed_attn, attn_norm_back = jax.vjp(norm_rows, branch_output, vecd[5], vecd[6])
    middle_state = resid + normed_attn
    normed_second, second_back = jax.vjp(norm_rows, middle_state, vecd[7], vecd[8])
    second_activation = normed_second.astype(bf16)
    before_gate = jnp.dot(second_activation, w_fc1, preferred_element_type=f32) + vecff[0]
    gated, gate_back = jax.vjp(smooth_gate, before_gate)
    normed_hidden, hidden_back = jax.vjp(norm_rows, gated, vecff[1], vecff[2])
    hidden_activation = normed_hidden.astype(bf16)
    result = middle_state + (
        jnp.dot(hidden_activation, w_fc2, preferred_element_type=f32) + vecd[9]
    )
    output = result.astype(bf16)

    tables = [plan.table(part, False) for part in (0, 1)]
    upstream = cotangent.astype(f32)

    def by_group(left):
        return left.T.reshape(plan.ways, -1, width // plan.ways, seq)

    hidden_t = by_group(hidden_activation)
    grad_bias_two = jnp.sum(upstream, axis=0)
    grad_hidden_act = rounded(dot_nt(cotangent, w_fc2))
    grad_gated, grad_gain_hidden, grad_shift_hidden = hidden_back(grad_hidden_act)
    grad_pre = gate_back(grad_gated)[0].astype(bf16)
    both, wide = range(width // 512), range(hidden // 512)
    keep_0, send_0 = grads(
        tables[0],
        [(by_group(second_activation), 0, grad_pre, wide)]
        + [(hidden_t, q, cotangent, both) for q in range(half_q)],
    )
    grad_bias_one = jnp.sum(grad_pre.astype(f32), axis=0)
    grad_second_act = dot_nt(grad_pre, w_fc1)
    grad_middle_norm, grad_gain_second, grad_shift_second = second_back(grad_second_act)
    grad_middle = upstream + grad_middle_norm
    grad_branch, grad_gain_attn, grad_shift_attn = attn_norm_back(grad_middle)
    grad_branch_low = grad_branch.astype(bf16)
    grad_bias_out = jnp.sum(grad_branch_low.astype(f32), axis=0)
    grad_scaled = rounded(dot_nt(grad_branch_low, w_out))
    head_products = jnp.sum(grad_scaled * attended, axis=0)
    grad_heads_local = jnp.sum(head_products.reshape(heads, -1), axis=1)
    grad_attended = (grad_scaled * scale_row).astype(bf16)
    keep_1, send_1 = grads(
        tables[1],
        [(hidden_t, q, cotangent, both) for q in range(half_q, 2 * half_q)]
        + [(by_group(scaled_heads), 0, grad_branch_low, both)],
    )
    late = Scatter(plan, [0, 1], [keep_0, keep_1], [send_0, send_1])
    grad_attended, *late.got = tied(grad_attended, *late.got)
    late.step()
    first_half = attention_back(doc_split, qkv, grad_attended, attended, lse, heads, blk, 0)
    grad_attended, first_half, *late.got = tied(grad_attended, first_half, *late.got)
    late.step()
    last_half = attention_back(doc_split, qkv, grad_attended, attended, lse, heads, blk, 1)
    last_half, *late.got = tied(last_half, *late.got)
    late.step()
    dq, dk, dv = (jnp.concatenate(pair, 1) for pair in zip(first_half, last_half))
    grad_projected = jnp.concatenate([dq, dk, dv], axis=1)
    grad_bias_query = jnp.sum(dq.astype(f32), axis=0)
    grad_bias_value = jnp.sum(dv.astype(f32), axis=0)
    grad_first_act = dot_nt(grad_projected, w_qkv)
    grad_resid_norm, grad_gain_first, grad_shift_first = first_back(grad_first_act)
    grad_tokens = grad_middle + grad_resid_norm
    vec_grads = jnp.stack(
        [
            grad_gain_first,
            grad_shift_first,
            grad_bias_query,
            grad_bias_value,
            grad_bias_out,
            grad_gain_attn,
            grad_shift_attn,
            grad_gain_second,
            grad_shift_second,
            grad_bias_two,
        ]
    )
    hid_grads = jnp.stack([grad_bias_one, grad_gain_hidden, grad_shift_hidden])
    vec_cols = jnp.concatenate(
        [
            vec_grads.T,
            hid_grads.reshape(n_hid, width, per_row)
            .transpose(1, 0, 2)
            .reshape(width, n_hid * per_row),
            jnp.broadcast_to(grad_heads_local, (width, heads)),
        ],
        1,
    )
    used = vec_cols.shape[1]
    vec_cols = jnp.pad(vec_cols, ((0, 0), (0, 128 - used))).astype(bf16)
    first_t = by_group(first_activation)
    keep_b, send_b = grads(tables[1], [(first_t, 0, dv, both)])
    keep_a, send_a = grads(
        tables[0],
        [(first_t, 0, dq, both), (first_t, 0, dk, both)],
        vec_cols.reshape(plan.ways, width // plan.ways, 128),
    )
    last = Scatter(plan, [0, 1], [keep_a, keep_b], [send_a, send_b])
    sum_0, sum_1 = late.finish()
    sent_a, sent_b = last.finish()
    sent_qkv = split_low(plan, jnp.concatenate([sent_a[:, :cut], sent_b], 1))
    sent_fc1 = split_low(plan, sum_0[:, :hidden])
    sent_out = split_low(plan, sum_1[:, half_q * width :])
    row_blocks = [sum_0[:, hidden + q * width : hidden + (q + 1) * width] for q in range(half_q)]
    row_blocks += [sum_1[:, q * width : (q + 1) * width] for q in range(half_q)]
    sent_fc2 = split_low(plan, jnp.concatenate(row_blocks, 0))
    sent_vec = split_low(plan, sent_a[:, cut:])
    sent_vecd = sent_vec[:, :n_vec].T
    mid = n_vec + n_hid * per_row
    sent_vecff = (
        sent_vec[:, n_vec:mid]
        .reshape(shard, n_hid, per_row)
        .transpose(1, 0, 2)
        .reshape(n_hid, shard * per_row)
    )
    grad_heads = sent_vec[0, mid : mid + heads]
    return (
        output,
        grad_tokens,
        grad_heads,
        sent_qkv,
        sent_out,
        sent_fc1,
        sent_fc2,
        sent_vecd,
        sent_vecff,
    )


def solution(mesh):
    rows = P(AXES, None)
    columns = P(None, AXES)
    return jax.shard_map(
        functools.partial(local, Plan(mesh)),
        mesh=mesh,
        in_specs=(rows, P(AXES), P(), rows, rows, rows, rows, columns, columns, rows),
        out_specs=(rows, rows, P(), rows, rows, rows, rows, columns, columns),
        check_vma=False,
    )
```

```python
import functools

import jax
import jax.numpy as jnp
from jax import lax
from jax.experimental import pallas as pl
from jax.experimental.pallas import tpu as pltpu
from jax.sharding import PartitionSpec as P

epsilon = 1e-05
AXES = ("dp", "fsdp")
f32 = jnp.float32
bf16 = jnp.bfloat16
NEG = -1e30
VMEM_LIMIT = 56 << 20
MIDDLE_LIMIT = 62 << 20


class Plan:
    def __init__(self, mesh):
        n_dp, n_fs = mesh.shape["dp"], mesh.shape["fsdp"]
        self.count = n_dp * n_fs
        self.ways = min(self.count, 32)
        self.low = self.count // self.ways
        self.core = max(1, n_fs // self.low)
        self.dims = [1 << b for b in range(self.ways.bit_length() - 1) if 1 << b != self.core]
        self.half = self.ways // 2
        self.steps = len(self.dims)

    def order(self, core_bit, part, gathers):
        near, far = self.dims[:-1], self.dims[-1:]
        shift = (core_bit if part == 0 else 2) % len(near)
        near = near[shift:] + near[:shift]
        return far + near if gathers else near + far

    def pairs(self, part, step, gathers):
        out = []
        for i in range(self.count):
            group = i // self.low
            mask = self.order(int(bool(group & self.core)), part, gathers)[step]
            out.append((i, i ^ (mask * self.low)))
        return out

    def core_pairs(self):
        return [(i, i ^ (self.core * self.low)) for i in range(self.count)]

    def low_groups(self):
        return [[g * self.low + i for i in range(self.low)] for g in range(self.ways)]

    def table(self, part, gathers):
        me = (lax.axis_index("dp") * lax.axis_size("fsdp") + lax.axis_index("fsdp")) // self.low
        rows = []
        for core_bit in (0, 1):
            row = []
            for other in (0, 1):
                masks = self.order(core_bit ^ other, part, gathers)
                for r in range(self.half):
                    x = self.core if other else 0
                    for k in range(self.steps):
                        bit = k if gathers else self.steps - 1 - k
                        if (r >> bit) & 1:
                            x ^= masks[k]
                    row.append(x)
            rows.append(row)
        mine = ((me & self.core) != 0).astype(jnp.int32)
        masks = jnp.where(mine == 1, jnp.array(rows[1], jnp.int32), jnp.array(rows[0], jnp.int32))
        return jnp.bitwise_xor(me.astype(jnp.int32), masks)


def tied(*values):
    return lax.optimization_barrier(values)


class Gather:
    def __init__(self, plan, pieces):
        self.plan = plan
        self.held = [piece[None] for piece in pieces]
        self.fresh = None
        self.at = 0

    def step(self):
        if self.fresh is not None:
            self.held = [jnp.concatenate(pair, 0) for pair in zip(self.held, self.fresh)]
        self.fresh = [
            lax.ppermute(h, AXES, self.plan.pairs(part, self.at, True)) for part, h in enumerate(self.held)
        ]
        self.at += 1

    def after(self, other):
        if self.fresh is None:
            *self.held, _ = tied(*self.held, other)
        else:
            *self.fresh, _ = tied(*self.fresh, other)

    def cross_held(self):
        self.far_held = [lax.ppermute(h, AXES, self.plan.core_pairs()) for h in self.held]

    def cross_fresh(self):
        self.far_fresh = [lax.ppermute(h, AXES, self.plan.core_pairs()) for h in self.fresh]

    def blocks(self):
        return [list(b) for b in zip(self.held, self.fresh, self.far_held, self.far_fresh)]


def join_low(plan, piece):
    if plan.low == 1:
        return piece
    return lax.all_gather(piece, AXES, axis=0, tiled=True, axis_index_groups=plan.low_groups())


def assemble_kernel(table_ref, *refs, quarter, parts, layout):
    sources, rest = refs[: 4 * parts], refs[4 * parts :]
    outs, sem = rest[:-1], rest[-1]
    copies = []
    for line, (part, src_col, out, out_col, width, stride, row) in enumerate(layout):
        for r in range(4 * quarter):
            src = sources[4 * part + r // quarter]
            rows = src.shape[1]
            at = pl.multiple_of(table_ref[part, r] * stride + row, rows)
            copy = pltpu.make_async_copy(
                src.at[r % quarter, :, pl.ds(src_col, width)],
                outs[out].at[pl.ds(at, rows), pl.ds(out_col, width)],
                sem.at[line, r],
            )
            copy.start()
            copies.append(copy)
    for copy in copies:
        copy.wait()


def assemble(plan, blocks, out_shapes, layout):
    table = jnp.stack([plan.table(part, True) for part in range(len(blocks))])
    flat = [b for part in blocks for b in part]
    anywhere = pl.BlockSpec(memory_space=pl.ANY)
    moved = sum(2 * b.size * b.dtype.itemsize for b in flat)
    return pl.pallas_call(
        functools.partial(
            assemble_kernel, quarter=plan.half // 2, parts=len(blocks), layout=layout
        ),
        in_specs=[pl.BlockSpec(memory_space=pltpu.SMEM)] + [anywhere] * len(flat),
        out_specs=[pl.BlockSpec(memory_space=pltpu.VMEM)] * len(out_shapes),
        out_shape=[jax.ShapeDtypeStruct(s, bf16) for s in out_shapes],
        scratch_shapes=[pltpu.SemaphoreType.DMA((len(layout), plan.ways))],
        compiler_params=pltpu.CompilerParams(vmem_limit_bytes=VMEM_LIMIT),
        cost_estimate=pl.CostEstimate(flops=0, bytes_accessed=moved, transcendentals=0),
        name="assemble",
    )(table, *flat)


def plus(a, b):
    return a.astype(f32) + b.astype(f32)


class Scatter:
    def __init__(self, plan, parts, keep, send):
        self.plan, self.parts, self.keep = plan, parts, keep
        self.got = [lax.ppermute(s, AXES, plan.core_pairs()) for s in send]
        self.at = 0

    def step(self):
        half = self.keep[0].shape[0] // 2
        going = [plus(k[half:], g[half:]).astype(bf16) for k, g in zip(self.keep, self.got)]
        arriving = [
            lax.ppermute(g, AXES, self.plan.pairs(part, self.at, False))
            for g, part in zip(going, self.parts)
        ]
        self.keep = [plus(k[:half], g[:half]).astype(bf16) for k, g in zip(self.keep, self.got)]
        self.got = arriving
        self.at += 1

    def finish(self):
        while self.at < self.plan.steps:
            self.step()
        return [plus(k[0], g[0]) for k, g in zip(self.keep, self.got)]


def split_low(plan, total):
    if plan.low == 1:
        return total
    return lax.psum_scatter(
        total, AXES, scatter_dimension=0, tiled=True, axis_index_groups=plan.low_groups()
    )


def dot_nt(a, b):
    return lax.dot_general(a, b, (((1,), (1,)), ((), ())), preferred_element_type=f32)


def dot_nn(a, b):
    return lax.dot_general(a, b, (((1,), (0,)), ((), ())), preferred_element_type=f32)


def transposed(a):
    return a.astype(f32).T.astype(a.dtype)


def allowed_block(i, j, split, blk):
    key_pos = j * blk + lax.broadcasted_iota(jnp.int32, (blk, blk), 0)
    query_row = i * blk + lax.broadcasted_iota(jnp.int32, (1, blk), 1)
    allowed = key_pos >= jnp.where(query_row >= split, split, 0)
    if i == j:
        allowed &= key_pos <= i * blk + lax.broadcasted_iota(jnp.int32, (blk, blk), 1)
    return allowed


def attention_kernel(split_ref, q_ref, k_ref, v_ref, o_ref, lse_ref, *, seq, hd, blk):
    split = split_ref[0]
    v_t = transposed(v_ref[...])
    lane = lax.broadcasted_iota(jnp.int32, (blk, 2 * hd), 1)
    for i in range(seq // blk):
        rows = slice(i * blk, (i + 1) * blk)
        outs = []
        for h in (0, 1):
            q = jnp.where((lane >= hd) if h else (lane < hd), q_ref[rows, :], 0) * bf16(hd**-0.5)
            scores = []
            for j in range(i + 1):
                s = dot_nt(k_ref[j * blk : (j + 1) * blk, :], q)
                scores.append(jnp.where(allowed_block(i, j, split, blk), s, NEG))
            peak = scores[0].max(0, keepdims=True)
            for s in scores[1:]:
                peak = jnp.maximum(peak, s.max(0, keepdims=True))
            total = jnp.zeros((1, blk), f32)
            mixed = jnp.zeros((hd, blk), f32)
            for j, s in enumerate(scores):
                e = jnp.exp(s - peak)
                total += e.sum(0, keepdims=True)
                mixed += dot_nn(
                    v_t[h * hd : (h + 1) * hd, j * blk : (j + 1) * blk], e.astype(bf16)
                )
            outs.append(mixed / total)
            lse_ref[0, h : h + 1, rows] = peak + jnp.log(total)
        o_ref[rows, :] = jnp.concatenate(outs, 0).T


def attention(split, qkv, heads, blk, which):
    seq, width = qkv.shape[0], qkv.shape[1] // 3
    hd, pairs = width // heads, heads // 2
    w = 2 * hd
    count = pairs // 2
    start = which * count
    return pl.pallas_call(
        functools.partial(attention_kernel, seq=seq, hd=hd, blk=blk),
        grid=(count,),
        in_specs=[
            pl.BlockSpec(memory_space=pltpu.SMEM),
            pl.BlockSpec((seq, w), lambda p: (0, p + start)),
            pl.BlockSpec((seq, w), lambda p: (0, p + start + pairs)),
            pl.BlockSpec((seq, w), lambda p: (0, p + start + 2 * pairs)),
        ],
        out_specs=[
            pl.BlockSpec((seq, w), lambda p: (0, p)),
            pl.BlockSpec((1, 2, seq), lambda p: (p, 0, 0)),
        ],
        out_shape=[
            jax.ShapeDtypeStruct((seq, width // 2), f32),
            jax.ShapeDtypeStruct((count, 2, seq), f32),
        ],
        compiler_params=pltpu.CompilerParams(vmem_limit_bytes=VMEM_LIMIT),
        cost_estimate=pl.CostEstimate(
            flops=6 * seq * seq * width,
            bytes_accessed=seq * width * 5,
            transcendentals=heads * seq * seq // 2,
        ),
        name="attention",
    )(split, qkv, qkv, qkv)


def attention_back_kernel(
    split_ref, q_ref, k_ref, v_ref, da_ref, o_ref, lse_ref, dq_ref, dk_ref, dv_ref, dk_acc, dv_acc,
    *, seq, hd, blk,
):
    split = split_ref[0]
    k_t = transposed(k_ref[...])
    lane = lax.broadcasted_iota(jnp.int32, (blk, 2 * hd), 1)
    for i in range(seq // blk):
        rows = slice(i * blk, (i + 1) * blk)
        q_full, da_full = q_ref[rows, :], da_ref[rows, :]
        inner = (da_full.astype(f32) * o_ref[rows, :]).T
        dqs = []
        for h in (0, 1):
            mine = (lane >= hd) if h else (lane < hd)
            q = jnp.where(mine, q_full, 0) * bf16(hd**-0.5)
            da = jnp.where(mine, da_full, 0)
            row_inner = inner[h * hd : (h + 1) * hd].sum(0, keepdims=True)
            lse = lse_ref[0, h : h + 1, rows]
            dq = jnp.zeros((hd, blk), f32)
            for j in range(i + 1):
                keys = slice(j * blk, (j + 1) * blk)
                s = dot_nt(k_ref[keys, :], q)
                s = jnp.where(allowed_block(i, j, split, blk), s, NEG)
                p = jnp.exp(s - lse)
                dp = dot_nt(v_ref[keys, :], da)
                ds = (p * (dp - row_inner)).astype(bf16)
                dv = dot_nn(p.astype(bf16), da)
                dk = dot_nn(ds, q)
                if i == j and h == 0:
                    dv_acc[keys, :] = dv
                    dk_acc[keys, :] = dk
                else:
                    dv_acc[keys, :] += dv
                    dk_acc[keys, :] += dk
                dq += dot_nn(k_t[h * hd : (h + 1) * hd, keys], ds)
            dqs.append(dq)
        dq_ref[rows, :] = (jnp.concatenate(dqs, 0).T * (hd**-0.5)).astype(bf16)
    dk_ref[...] = dk_acc[...].astype(bf16)
    dv_ref[...] = dv_acc[...].astype(bf16)


def attention_back(split, qkv, da, attended, lse, heads, blk, which):
    seq, width = qkv.shape[0], qkv.shape[1] // 3
    hd, pairs = width // heads, heads // 2
    w = 2 * hd
    count = pairs // 2
    start = which * count
    column = pl.BlockSpec((seq, w), lambda p: (0, p + start))
    out = pl.BlockSpec((seq, w), lambda p: (0, p))
    return pl.pallas_call(
        functools.partial(attention_back_kernel, seq=seq, hd=hd, blk=blk),
        grid=(count,),
        in_specs=[
            pl.BlockSpec(memory_space=pltpu.SMEM),
            column,
            pl.BlockSpec((seq, w), lambda p: (0, p + start + pairs)),
            pl.BlockSpec((seq, w), lambda p: (0, p + start + 2 * pairs)),
            column,
            column,
            pl.BlockSpec((1, 2, seq), lambda p: (p + start, 0, 0)),
        ],
        out_specs=[out, out, out],
        out_shape=[jax.ShapeDtypeStruct((seq, width // 2), bf16)] * 3,
        scratch_shapes=[pltpu.VMEM((seq, w), f32)] * 2,
        compiler_params=pltpu.CompilerParams(vmem_limit_bytes=VMEM_LIMIT),
        cost_estimate=pl.CostEstimate(
            flops=10 * seq * seq * width,
            bytes_accessed=seq * width * 10,
            transcendentals=heads * seq * seq // 2,
        ),
        name="attention_back",
    )(split, qkv, qkv, qkv, da, attended, lse)


def grads_kernel(table_ref, place_ref, *refs, runs, n_left, n_right, tile, extra):
    lefts, rights = refs[:n_left], refs[n_left : n_left + n_right]
    extra_ref = refs[n_left + n_right] if extra else None
    send_ref, keep_ref, left = refs[n_left + n_right + bool(extra) :]
    ways, rows, tokens = left.shape
    step = pl.program_id(0)
    columns = pl.ds(pl.multiple_of(step * tile, tile), tile) if extra else slice(None)
    for first, last, l, r in runs:

        @pl.when(step == first)
        def _():
            for w in range(ways):
                left[w] = lefts[l][table_ref[w], 0]

        @pl.when((step >= first) & (step < last))
        def _():
            product = dot_nn(left[...].reshape(ways * rows, tokens), rights[r][...])
            product = product.astype(bf16).reshape(ways, rows, tile)
            keep_ref[:, :, columns] = product[: ways // 2]
            send_ref[:, :, columns] = product[ways // 2 :]

    if extra:

        @pl.when(step == 0)
        def _():
            width = extra_ref.shape[2]
            at = slice(keep_ref.shape[2] - width, keep_ref.shape[2])
            for w in range(ways // 2):
                keep_ref[w, :, at] = extra_ref[table_ref[w]]
                send_ref[w, :, at] = extra_ref[table_ref[ways // 2 + w]]


def grads(table, jobs, extra=None, tile=512):
    ways, _, rows, tokens = jobs[0][0].shape
    lefts, rights, runs, places = [], [], [], []
    at = 0
    for left, q, right, numbers in jobs:
        for known, one in ((lefts, left), (rights, right)):
            if not any(one is k for k in known):
                known.append(one)
        l = next(i for i, k in enumerate(lefts) if k is left)
        r = next(i for i, k in enumerate(rights) if k is right)
        runs.append((at, at + len(numbers), l, r))
        for n in numbers:
            places.append((l, q, r, n))
        at += len(numbers)

    def held(which, entry, count):
        table = []
        for k in range(count):
            used = [(s, p[entry]) for s, p in enumerate(places) if p[which] == k]
            table.append([next((v for s, v in used if s >= i), used[-1][1]) for i in range(at)])
        return table

    place = jnp.array(held(0, 1, len(lefts)) + held(2, 3, len(rights)), jnp.int32)

    def left_spec(k):
        return pl.BlockSpec((ways, 1, rows, tokens), lambda i, t, p: (0, p[k, i], 0, 0))

    def right_spec(k):
        return pl.BlockSpec((tokens, tile), lambda i, t, p: (0, p[len(lefts) + k, i]))

    width = at * tile
    if extra is None:
        out_spec = pl.BlockSpec((ways // 2, rows, tile), lambda i, t, p: (0, 0, i))
        more, more_spec = [], []
    else:
        width += extra.shape[2]
        out_spec = pl.BlockSpec((ways // 2, rows, width), lambda i, t, p: (0, 0, 0))
        more, more_spec = [extra], [pl.BlockSpec(extra.shape, lambda i, t, p: (0, 0, 0))]
    shape = jax.ShapeDtypeStruct((ways // 2, rows, width), bf16)
    send, keep = pl.pallas_call(
        functools.partial(
            grads_kernel,
            runs=runs,
            n_left=len(lefts),
            n_right=len(rights),
            tile=tile,
            extra=extra is not None,
        ),
        grid_spec=pltpu.PrefetchScalarGridSpec(
            num_scalar_prefetch=2,
            grid=(at,),
            in_specs=[left_spec(k) for k in range(len(lefts))]
            + [right_spec(k) for k in range(len(rights))]
            + more_spec,
            out_specs=[out_spec, out_spec],
            scratch_shapes=[pltpu.VMEM((ways, rows, tokens), bf16)],
        ),
        out_shape=[shape, shape],
        compiler_params=pltpu.CompilerParams(vmem_limit_bytes=VMEM_LIMIT),
        cost_estimate=pl.CostEstimate(
            flops=2 * tokens * ways * rows * tile * at,
            bytes_accessed=2 * ways * rows * (tokens * (len(lefts) + 1) + 2 * width),
            transcendentals=0,
        ),
        name="grads",
    )(table, place, *lefts, *rights, *more)
    return keep, send


def normalized(values):
    center = values - jnp.mean(values, axis=-1, keepdims=True)
    rate = lax.rsqrt(jnp.mean(center * center, axis=-1, keepdims=True) + epsilon)
    return center * rate, rate


def norm_back(grad, unit, rate):
    inner = jnp.mean(grad * unit, axis=-1, keepdims=True)
    return rate * (grad - jnp.mean(grad, axis=-1, keepdims=True) - unit * inner)


def column_sum(values):
    return jnp.sum(values, axis=0, keepdims=True)


def resident(shape):
    return pl.BlockSpec(shape, lambda i: (0,) * len(shape), pipeline_mode=pl.Buffered(1))


def by_rows(blk, width):
    return pl.BlockSpec((blk, width), lambda i: (i, 0))


def by_columns(height, blk):
    return pl.BlockSpec((height, blk), lambda i: (0, i))


def project_kernel(x_ref, w_ref, vec_ref, qkv_ref, left_t_ref):
    width = x_ref.shape[1]
    unit, _ = normalized(x_ref[...].astype(f32))
    left = (unit * vec_ref[0:1, :] + vec_ref[1:2, :]).astype(bf16)
    left_t_ref[...] = transposed(left)
    for part, bias in ((0, 2), (1, None), (2, 3)):
        cols = slice(part * width, (part + 1) * width)
        rows = dot_nn(left, w_ref[:, cols])
        if bias is not None:
            rows += vec_ref[bias : bias + 1, :]
        qkv_ref[:, cols] = rows.astype(bf16)


def project(tokens, w_qkv, vec, blk=256):
    seq, width = tokens.shape
    blk = min(blk, seq)
    return pl.pallas_call(
        project_kernel,
        grid=(seq // blk,),
        in_specs=[by_rows(blk, width), resident(w_qkv.shape), resident(vec.shape)],
        out_specs=[by_rows(blk, 3 * width), by_columns(width, blk)],
        out_shape=[
            jax.ShapeDtypeStruct((seq, 3 * width), bf16),
            jax.ShapeDtypeStruct((width, seq), bf16),
        ],
        compiler_params=pltpu.CompilerParams(vmem_limit_bytes=VMEM_LIMIT),
        cost_estimate=pl.CostEstimate(
            flops=6 * seq * width * width, bytes_accessed=18 * seq * width, transcendentals=seq
        ),
        name="project",
    )(tokens, w_qkv, vec)


def middle_kernel(
    x_ref, att_ref, c_ref, wo_ref, w1_ref, w2_ref, vec_ref, hid_ref, scale_ref,
    out_ref, z_t_ref, a2_t_ref, m_t_ref, df_ref, dy_ref, da_ref, dx_ref, sums_ref, hid_sums_ref,
    gate, slope, dm_keep, acc, *, chunk,
):
    hidden = w1_ref.shape[1]
    chunks = [slice(k, k + chunk) for k in range(0, hidden, chunk)]

    @pl.when(pl.program_id(0) == 0)
    def _():
        sums_ref[...] = jnp.zeros_like(sums_ref)
        hid_sums_ref[...] = jnp.zeros_like(hid_sums_ref)

    def vec(row):
        return vec_ref[row : row + 1, :]

    def add_sum(row, values):
        sums_ref[row : row + 1, :] += column_sum(values)

    z = (att_ref[...] * scale_ref[...]).astype(bf16)
    z_t_ref[...] = transposed(z)
    unit_1, rate_1 = normalized(dot_nn(z, wo_ref[...]) + vec(4))
    x2 = x_ref[...].astype(f32) + (unit_1 * vec(5) + vec(6))
    unit_2, rate_2 = normalized(x2)
    a2 = (unit_2 * vec(7) + vec(8)).astype(bf16)
    a2_t_ref[...] = transposed(a2)

    total = 0.0
    root = (2.0 / jnp.pi) ** 0.5
    for ch in chunks:
        f = dot_nn(a2, w1_ref[:, ch]) + hid_ref[0:1, ch]
        square = f * f
        t = jnp.tanh(f * (root + (root * 0.044715) * square))
        half = 0.5 + 0.5 * t
        g = f * half
        gate[:, ch] = g
        slope[:, ch] = half + g * (1.0 - t) * (root + (3 * root * 0.044715) * square)
        total += jnp.sum(g, axis=-1, keepdims=True)
    mean = total / hidden
    spread = 0.0
    for ch in chunks:
        center = gate[:, ch] - mean
        spread += jnp.sum(center * center, axis=-1, keepdims=True)
    rate = lax.rsqrt(spread / hidden + epsilon)

    grad_sum = 0.0
    grad_inner = 0.0
    for ch in chunks:
        unit = (gate[:, ch] - mean) * rate
        gate[:, ch] = unit
        gain = hid_ref[1:2, ch]
        m = (unit * gain + hid_ref[2:3, ch]).astype(bf16)
        m_t_ref[ch, :] = transposed(m)
        y = dot_nn(m, w2_ref[ch, :])
        if ch.start == 0:
            acc[...] = y
        else:
            acc[...] += y
        dm = dot_nt(c_ref[...], w2_ref[ch, :]).astype(bf16)
        dm_keep[:, ch] = dm
        dm = dm.astype(f32)
        hid_sums_ref[1:2, ch] += column_sum(dm * unit)
        hid_sums_ref[2:3, ch] += column_sum(dm)
        grad = dm * gain
        grad_sum += jnp.sum(grad, axis=-1, keepdims=True)
        grad_inner += jnp.sum(grad * unit, axis=-1, keepdims=True)
    out_ref[...] = (x2 + (acc[...] + vec(9))).astype(bf16)

    grad_sum = grad_sum / hidden
    grad_inner = grad_inner / hidden
    for ch in chunks:
        grad = dm_keep[:, ch].astype(f32) * hid_ref[1:2, ch]
        grad = rate * (grad - grad_sum - gate[:, ch] * grad_inner)
        df = (slope[:, ch] * grad).astype(bf16)
        df_ref[:, ch] = df
        hid_sums_ref[0:1, ch] += column_sum(df.astype(f32))
        back = dot_nt(df, w1_ref[:, ch])
        if ch.start == 0:
            acc[...] = back
        else:
            acc[...] += back

    upstream = c_ref[...].astype(f32)
    da2 = acc[...]
    add_sum(9, upstream)
    add_sum(7, da2 * unit_2)
    add_sum(8, da2)
    dx2 = upstream + norm_back(da2 * vec(7), unit_2, rate_2)
    dx_ref[...] = dx2
    add_sum(5, dx2 * unit_1)
    add_sum(6, dx2)
    dy = norm_back(dx2 * vec(5), unit_1, rate_1).astype(bf16)
    dy_ref[...] = dy
    add_sum(4, dy.astype(f32))
    dz = dot_nt(dy, wo_ref[...]).astype(bf16).astype(f32)
    add_sum(10, dz * att_ref[...])
    da_ref[...] = (dz * scale_ref[...]).astype(bf16)


def middle(tokens, attended, cotangent, w_out, w_fc1, w_fc2, vec, hid, scale, blk=256, chunk=256):
    seq, width = tokens.shape
    hidden = w_fc1.shape[1]
    blk = min(blk, seq)
    row, col = by_rows(blk, width), by_columns(width, blk)
    sums = pl.BlockSpec((16, width), lambda i: (0, 0))
    hid_sums = pl.BlockSpec((8, hidden), lambda i: (0, 0))
    shape = jax.ShapeDtypeStruct
    return pl.pallas_call(
        functools.partial(middle_kernel, chunk=chunk),
        grid=(seq // blk,),
        in_specs=[row, row, row]
        + [resident(a.shape) for a in (w_out, w_fc1, w_fc2, vec, hid, scale)],
        out_specs=[
            row, col, col, by_columns(hidden, blk), by_rows(blk, hidden), row, row, row, sums, hid_sums,
        ],
        out_shape=[
            shape((seq, width), bf16),
            shape((width, seq), bf16),
            shape((width, seq), bf16),
            shape((hidden, seq), bf16),
            shape((seq, hidden), bf16),
            shape((seq, width), bf16),
            shape((seq, width), bf16),
            shape((seq, width), f32),
            shape((16, width), f32),
            shape((8, hidden), f32),
        ],
        scratch_shapes=[
            pltpu.VMEM((blk, hidden), f32),
            pltpu.VMEM((blk, hidden), f32),
            pltpu.VMEM((blk, hidden), bf16),
            pltpu.VMEM((blk, width), f32),
        ],
        compiler_params=pltpu.CompilerParams(vmem_limit_bytes=MIDDLE_LIMIT),
        cost_estimate=pl.CostEstimate(
            flops=4 * seq * width * (width + 2 * hidden),
            bytes_accessed=2 * width * (width + 2 * hidden) + 40 * seq * width,
            transcendentals=seq * hidden,
        ),
        name="middle",
    )(tokens, attended, cotangent, w_out, w_fc1, w_fc2, vec, hid, scale)


def finish_kernel(x_ref, dq_ref, dk_ref, dv_ref, dx_ref, w_ref, vec_ref, out_ref, sums_ref):
    width = x_ref.shape[1]

    @pl.when(pl.program_id(0) == 0)
    def _():
        sums_ref[...] = jnp.zeros_like(sums_ref)

    da1 = dot_nt(dq_ref[...], w_ref[:, :width])
    da1 += dot_nt(dk_ref[...], w_ref[:, width : 2 * width])
    da1 += dot_nt(dv_ref[...], w_ref[:, 2 * width :])
    unit, rate = normalized(x_ref[...].astype(f32))
    sums = (da1 * unit, da1, dq_ref[...].astype(f32), dv_ref[...].astype(f32))
    for row, values in enumerate(sums):
        sums_ref[row : row + 1, :] += column_sum(values)
    out_ref[...] = dx_ref[...] + norm_back(da1 * vec_ref[0:1, :], unit, rate)


def finish(tokens, dq, dk, dv, dx2, w_qkv, vec, blk=256):
    seq, width = tokens.shape
    blk = min(blk, seq)
    row = by_rows(blk, width)
    return pl.pallas_call(
        finish_kernel,
        grid=(seq // blk,),
        in_specs=[row] * 5 + [resident(w_qkv.shape), resident(vec.shape)],
        out_specs=[row, pl.BlockSpec((8, width), lambda i: (0, 0))],
        out_shape=[
            jax.ShapeDtypeStruct((seq, width), f32),
            jax.ShapeDtypeStruct((8, width), f32),
        ],
        compiler_params=pltpu.CompilerParams(vmem_limit_bytes=VMEM_LIMIT),
        cost_estimate=pl.CostEstimate(
            flops=6 * seq * width * width, bytes_accessed=24 * seq * width, transcendentals=seq
        ),
        name="finish",
    )(tokens, dq, dk, dv, dx2, w_qkv, vec)


def local(
    plan,
    tokens,
    doc_split,
    head_scale,
    query_key_value_weight,
    output_weight,
    first_weight,
    second_weight,
    model_vectors,
    hidden_vectors,
    cotangent,
):
    seq, width = tokens.shape
    hidden = first_weight.shape[1]
    heads = head_scale.shape[0]
    head_shape = (seq, heads, width // heads)
    blk = min(256, seq)
    shard = query_key_value_weight.shape[0]

    per_row = hidden_vectors.shape[1] // shard
    n_vec = model_vectors.shape[0]
    n_hid = hidden_vectors.shape[0]
    vec_cols = jnp.concatenate(
        [
            model_vectors.T,
            hidden_vectors.reshape(n_hid, shard, per_row)
            .transpose(1, 0, 2)
            .reshape(shard, n_hid * per_row),
        ],
        1,
    )
    vec_cols = jnp.pad(vec_cols, ((0, 0), (0, 128 - vec_cols.shape[1])))
    cut = 2 * width
    weight_a = join_low(plan, jnp.concatenate([query_key_value_weight, vec_cols], 1))
    fc1_rows = join_low(plan, first_weight)
    fc2_rows = join_low(plan, second_weight)
    out_rows = join_low(plan, output_weight)
    group = fc1_rows.shape[0]
    quarters = [fc2_rows[q * group : (q + 1) * group] for q in range(hidden // width)]
    half_q = len(quarters) // 2
    first = Gather(
        plan,
        [jnp.concatenate([weight_a[:, :cut], weight_a[:, 3 * width :]], 1), weight_a[:, cut : 3 * width]],
    )
    second = Gather(
        plan,
        [
            jnp.concatenate([fc1_rows, *quarters[:half_q]], 1),
            jnp.concatenate([*quarters[half_q:], out_rows], 1),
        ],
    )
    first.step()
    second.after(first.fresh[0])
    second.step()
    while first.at < plan.steps:
        first.step()
    first.cross_held()
    first.cross_fresh()
    second.after(first.held[0])
    second.step()
    w_qkv, vec_all = assemble(
        plan,
        first.blocks(),
        [(width, 3 * width), (width, 128)],
        [
            (0, 0, 0, 0, cut, group, 0),
            (0, cut, 1, 0, 128, group, 0),
            (1, 0, 0, cut, width, group, 0),
        ],
    )
    vec = jnp.pad(vec_all[:, :n_vec].T.astype(f32), ((0, 16 - n_vec), (0, 0)))
    hid = (
        vec_all[:, n_vec : n_vec + n_hid * per_row]
        .reshape(width, n_hid, per_row)
        .transpose(1, 0, 2)
        .reshape(n_hid, hidden)
        .astype(f32)
    )
    hid = jnp.pad(hid, ((0, 8 - n_hid), (0, 0)))

    qkv, first_t = project(tokens, w_qkv, vec)
    qkv, *second.fresh = tied(qkv, *second.fresh)
    second.step()
    att_a, lse_a = attention(doc_split, qkv, heads, blk, 0)
    qkv, att_a, *second.fresh = tied(qkv, att_a, *second.fresh)
    second.step()
    second.cross_held()
    att_b, lse_b = attention(doc_split, qkv, heads, blk, 1)
    att_b, *second.fresh = tied(att_b, *second.fresh)
    attended = jnp.concatenate([att_a, att_b], 1)
    lse = jnp.concatenate([lse_a, lse_b], 0)
    second.cross_fresh()
    w_fc1, w_fc2, w_out = assemble(
        plan,
        second.blocks(),
        [(width, hidden), (hidden, width), (width, width)],
        [(0, 0, 0, 0, hidden, group, 0)]
        + [
            (q // half_q, hidden * (q < half_q) + q % half_q * width, 1, 0, width, 4 * group, q * group)
            for q in range(len(quarters))
        ]
        + [(1, half_q * width, 2, 0, width, group, 0)],
    )
    scale_row = jnp.repeat(head_scale, width // heads)[None]

    output, scaled_t, second_t, hidden_t, grad_pre, grad_branch, grad_attended, grad_middle, sums, hid_sums = (
        middle(tokens, attended, cotangent, w_out, w_fc1, w_fc2, vec, hid, scale_row)
    )
    tables = [plan.table(part, False) for part in (0, 1)]

    def by_group(left_t):
        return left_t.reshape(plan.ways, -1, width // plan.ways, seq)

    hidden_t = by_group(hidden_t)
    both, wide = range(width // 512), range(hidden // 512)
    keep_0, send_0 = grads(
        tables[0],
        [(by_group(second_t), 0, grad_pre, wide)]
        + [(hidden_t, q, cotangent, both) for q in range(half_q)],
    )
    keep_1, send_1 = grads(
        tables[1],
        [(hidden_t, q, cotangent, both) for q in range(half_q, 2 * half_q)]
        + [(by_group(scaled_t), 0, grad_branch, both)],
    )
    late = Scatter(plan, [0, 1], [keep_0, keep_1], [send_0, send_1])
    grad_attended, *late.got = tied(grad_attended, *late.got)
    late.step()
    first_half = attention_back(doc_split, qkv, grad_attended, attended, lse, heads, blk, 0)
    grad_attended, first_half, *late.got = tied(grad_attended, first_half, *late.got)
    late.step()
    last_half = attention_back(doc_split, qkv, grad_attended, attended, lse, heads, blk, 1)
    last_half, *late.got = tied(last_half, *late.got)
    late.step()
    dq, dk, dv = (jnp.concatenate(pair, 1) for pair in zip(first_half, last_half))
    grad_tokens, last_sums = finish(tokens, dq, dk, dv, grad_middle, w_qkv, vec)
    vec_grads = jnp.concatenate([last_sums[:4], sums[4:n_vec]], 0)
    grad_heads_local = jnp.sum(sums[n_vec].reshape(heads, -1), axis=1)
    hid_grads = hid_sums[:n_hid]
    vec_cols = jnp.concatenate(
        [
            vec_grads.T,
            hid_grads.reshape(n_hid, width, per_row)
            .transpose(1, 0, 2)
            .reshape(width, n_hid * per_row),
            jnp.broadcast_to(grad_heads_local, (width, heads)),
        ],
        1,
    )
    used = vec_cols.shape[1]
    vec_cols = jnp.pad(vec_cols, ((0, 0), (0, 128 - used))).astype(bf16)
    first_t = by_group(first_t)
    keep_b, send_b = grads(tables[1], [(first_t, 0, dv, both)])
    keep_a, send_a = grads(
        tables[0],
        [(first_t, 0, dq, both), (first_t, 0, dk, both)],
        vec_cols.reshape(plan.ways, width // plan.ways, 128),
    )
    last = Scatter(plan, [0, 1], [keep_a, keep_b], [send_a, send_b])
    sum_0, sum_1 = late.finish()
    sent_a, sent_b = last.finish()
    sent_qkv = split_low(plan, jnp.concatenate([sent_a[:, :cut], sent_b], 1))
    sent_fc1 = split_low(plan, sum_0[:, :hidden])
    sent_out = split_low(plan, sum_1[:, half_q * width :])
    row_blocks = [sum_0[:, hidden + q * width : hidden + (q + 1) * width] for q in range(half_q)]
    row_blocks += [sum_1[:, q * width : (q + 1) * width] for q in range(half_q)]
    sent_fc2 = split_low(plan, jnp.concatenate(row_blocks, 0))
    sent_vec = split_low(plan, sent_a[:, cut:])
    sent_vecd = sent_vec[:, :n_vec].T
    mid = n_vec + n_hid * per_row
    sent_vecff = (
        sent_vec[:, n_vec:mid]
        .reshape(shard, n_hid, per_row)
        .transpose(1, 0, 2)
        .reshape(n_hid, shard * per_row)
    )
    grad_heads = sent_vec[0, mid : mid + heads]
    return (
        output,
        grad_tokens,
        grad_heads,
        sent_qkv,
        sent_out,
        sent_fc1,
        sent_fc2,
        sent_vecd,
        sent_vecff,
    )


def solution(mesh):
    rows = P(AXES, None)
    columns = P(None, AXES)
    return jax.shard_map(
        functools.partial(local, Plan(mesh)),
        mesh=mesh,
        in_specs=(rows, P(AXES), P(), rows, rows, rows, rows, columns, columns, rows),
        out_specs=(rows, rows, P(), rows, rows, rows, rows, columns, columns),
        check_vma=False,
    )
```

```python
import functools

import jax
import jax.numpy as jnp
from jax import lax
from jax.experimental import pallas as pl
from jax.experimental.pallas import tpu as pltpu
from jax.sharding import PartitionSpec as P

epsilon = 1e-05
AXES = ("dp", "fsdp")
f32 = jnp.float32
bf16 = jnp.bfloat16
NEG = -1e30
VMEM_LIMIT = 56 << 20
MIDDLE_LIMIT = 62 << 20


class Plan:
    def __init__(self, mesh):
        n_dp, n_fs = mesh.shape["dp"], mesh.shape["fsdp"]
        self.count = n_dp * n_fs
        self.ways = min(self.count, 32)
        self.low = self.count // self.ways
        self.core = max(1, n_fs // self.low)
        self.dims = [1 << b for b in range(self.ways.bit_length() - 1) if 1 << b != self.core]
        self.half = self.ways // 2
        self.steps = len(self.dims)

    def order(self, core_bit, part, gathers):
        near, far = self.dims[:-1], self.dims[-1:]
        shift = (core_bit if part == 0 else 2) % len(near)
        near = near[shift:] + near[:shift]
        return far + near if gathers else near + far

    def pairs(self, part, step, gathers):
        out = []
        for i in range(self.count):
            group = i // self.low
            mask = self.order(int(bool(group & self.core)), part, gathers)[step]
            out.append((i, i ^ (mask * self.low)))
        return out

    def core_pairs(self):
        return [(i, i ^ (self.core * self.low)) for i in range(self.count)]

    def low_groups(self):
        return [[g * self.low + i for i in range(self.low)] for g in range(self.ways)]

    def table(self, part, gathers):
        me = (lax.axis_index("dp") * lax.axis_size("fsdp") + lax.axis_index("fsdp")) // self.low
        rows = []
        for core_bit in (0, 1):
            row = []
            for other in (0, 1):
                masks = self.order(core_bit ^ other, part, gathers)
                for r in range(self.half):
                    x = self.core if other else 0
                    for k in range(self.steps):
                        bit = k if gathers else self.steps - 1 - k
                        if (r >> bit) & 1:
                            x ^= masks[k]
                    row.append(x)
            rows.append(row)
        mine = ((me & self.core) != 0).astype(jnp.int32)
        masks = jnp.where(mine == 1, jnp.array(rows[1], jnp.int32), jnp.array(rows[0], jnp.int32))
        return jnp.bitwise_xor(me.astype(jnp.int32), masks)


def tied(*values):
    return lax.optimization_barrier(values)


class Gather:
    def __init__(self, plan, pieces):
        self.plan = plan
        self.held = [piece[None] for piece in pieces]
        self.fresh = None
        self.at = 0

    def step(self):
        if self.fresh is not None:
            self.held = [jnp.concatenate(pair, 0) for pair in zip(self.held, self.fresh)]
        self.fresh = [
            lax.ppermute(h, AXES, self.plan.pairs(part, self.at, True)) for part, h in enumerate(self.held)
        ]
        self.at += 1

    def after(self, other):
        if self.fresh is None:
            *self.held, _ = tied(*self.held, other)
        else:
            *self.fresh, _ = tied(*self.fresh, other)

    def cross_held(self):
        self.far_held = [lax.ppermute(h, AXES, self.plan.core_pairs()) for h in self.held]

    def cross_fresh(self):
        self.far_fresh = [lax.ppermute(h, AXES, self.plan.core_pairs()) for h in self.fresh]

    def blocks(self):
        return [list(b) for b in zip(self.held, self.fresh, self.far_held, self.far_fresh)]


def join_low(plan, piece, axis=0):
    if plan.low == 1:
        return piece
    return lax.all_gather(piece, AXES, axis=axis, tiled=True, axis_index_groups=plan.low_groups())


def fetch(action, table_ref, sources, lines, sem):
    for number, part, column, width, place in lines:
        for b in range(4):
            source = sources[4 * part + b]
            count = source.shape[0]

            def one(r, _, source=source, number=number, part=part, b=b, count=count):
                at = b * count + r
                copy = pltpu.make_async_copy(
                    source.at[r, :, pl.ds(column, width)],
                    place(table_ref[part, at]),
                    sem.at[number, at],
                )
                getattr(copy, action)()
                return _

            lax.fori_loop(0, count, one, 0)


def block_operands(plan, gathered):
    blocks = gathered.blocks()
    table = jnp.stack([plan.table(part, True) for part in range(len(blocks))])
    flat = [b for part in blocks for b in part]
    specs = [pl.BlockSpec(memory_space=pltpu.SMEM)] + [pl.BlockSpec(memory_space=pl.ANY)] * len(flat)
    return [table, *flat], specs


def plus(a, b):
    return a.astype(f32) + b.astype(f32)


class Scatter:
    def __init__(self, plan, part, going, keep):
        self.plan, self.part, self.keep, self.at = plan, part, keep, 0
        self.send(going)

    def send(self, going):
        self.got = lax.ppermute(going, AXES, self.plan.pairs(self.part, self.at, False))
        self.at += 1

    def step(self):
        half = self.keep.shape[0] // 2
        kind = self.keep.dtype
        keep, got = self.keep, self.got
        self.send(plus(keep[half:], got[half:]).astype(kind))
        self.keep = plus(keep[:half], got[:half]).astype(kind)

    def after(self, *others):
        self.got, *others = tied(self.got, *others)
        return others if len(others) > 1 else others[0]

    def total(self):
        while self.at < self.plan.steps:
            self.step()
        return plus(self.keep[0], self.got[0])


def to_other_core(plan, values):
    return lax.ppermute(values, AXES, plan.core_pairs())


def split_low(plan, total, axis=0):
    if plan.low == 1:
        return total
    return lax.psum_scatter(
        total, AXES, scatter_dimension=axis, tiled=True, axis_index_groups=plan.low_groups()
    )


def dot_nt(a, b):
    return lax.dot_general(a, b, (((1,), (1,)), ((), ())), preferred_element_type=f32)


def dot_nn(a, b):
    return lax.dot_general(a, b, (((1,), (0,)), ((), ())), preferred_element_type=f32)


def transposed(a):
    return a.astype(f32).T.astype(a.dtype)


def allowed_block(i, j, split, blk):
    key_pos = j * blk + lax.broadcasted_iota(jnp.int32, (blk, blk), 0)
    query_row = i * blk + lax.broadcasted_iota(jnp.int32, (1, blk), 1)
    allowed = key_pos >= jnp.where(query_row >= split, split, 0)
    if i == j:
        allowed &= key_pos <= i * blk + lax.broadcasted_iota(jnp.int32, (blk, blk), 1)
    return allowed


def attention_kernel(split_ref, q_ref, k_ref, v_ref, o_ref, lse_ref, *, seq, hd, blk):
    split = split_ref[0]
    v_t = transposed(v_ref[...])
    lane = lax.broadcasted_iota(jnp.int32, (blk, 2 * hd), 1)
    for i in range(seq // blk):
        rows = slice(i * blk, (i + 1) * blk)
        outs = []
        for h in (0, 1):
            q = jnp.where((lane >= hd) if h else (lane < hd), q_ref[rows, :], 0) * bf16(hd**-0.5)
            scores = []
            for j in range(i + 1):
                s = dot_nt(k_ref[j * blk : (j + 1) * blk, :], q)
                scores.append(jnp.where(allowed_block(i, j, split, blk), s, NEG))
            peak = scores[0].max(0, keepdims=True)
            for s in scores[1:]:
                peak = jnp.maximum(peak, s.max(0, keepdims=True))
            total = jnp.zeros((1, blk), f32)
            mixed = jnp.zeros((hd, blk), f32)
            for j, s in enumerate(scores):
                e = jnp.exp(s - peak)
                total += e.sum(0, keepdims=True)
                mixed += dot_nn(
                    v_t[h * hd : (h + 1) * hd, j * blk : (j + 1) * blk], e.astype(bf16)
                )
            outs.append(mixed / total)
            lse_ref[0, h : h + 1, rows] = peak + jnp.log(total)
        o_ref[rows, :] = jnp.concatenate(outs, 0).T


def attention(split, qkv, heads, blk):
    seq, width = qkv.shape[0], qkv.shape[1] // 3
    hd, pairs = width // heads, heads // 2
    w = 2 * hd
    count, start = pairs, 0
    return pl.pallas_call(
        functools.partial(attention_kernel, seq=seq, hd=hd, blk=blk),
        grid=(count,),
        in_specs=[
            pl.BlockSpec(memory_space=pltpu.SMEM),
            pl.BlockSpec((seq, w), lambda p: (0, p + start)),
            pl.BlockSpec((seq, w), lambda p: (0, p + start + pairs)),
            pl.BlockSpec((seq, w), lambda p: (0, p + start + 2 * pairs)),
        ],
        out_specs=[
            pl.BlockSpec((seq, w), lambda p: (0, p)),
            pl.BlockSpec((1, 2, seq), lambda p: (p, 0, 0)),
        ],
        out_shape=[
            jax.ShapeDtypeStruct((seq, width), f32),
            jax.ShapeDtypeStruct((count, 2, seq), f32),
        ],
        compiler_params=pltpu.CompilerParams(vmem_limit_bytes=VMEM_LIMIT),
        cost_estimate=pl.CostEstimate(
            flops=12 * seq * seq * width,
            bytes_accessed=seq * width * 5,
            transcendentals=heads * seq * seq // 2,
        ),
        name="attention",
    )(split, qkv, qkv, qkv)


def attention_back_kernel(
    split_ref, q_ref, k_ref, v_ref, da_ref, o_ref, lse_ref, dq_ref, dk_ref, dv_ref, dk_acc, dv_acc,
    *, seq, hd, blk,
):
    split = split_ref[0]
    k_t = transposed(k_ref[...])
    lane = lax.broadcasted_iota(jnp.int32, (blk, 2 * hd), 1)
    for i in range(seq // blk):
        rows = slice(i * blk, (i + 1) * blk)
        q_full, da_full = q_ref[rows, :], da_ref[rows, :]
        inner = (da_full.astype(f32) * o_ref[rows, :]).T
        dqs = []
        for h in (0, 1):
            mine = (lane >= hd) if h else (lane < hd)
            q = jnp.where(mine, q_full, 0) * bf16(hd**-0.5)
            da = jnp.where(mine, da_full, 0)
            row_inner = inner[h * hd : (h + 1) * hd].sum(0, keepdims=True)
            lse = lse_ref[0, h : h + 1, rows]
            dq = jnp.zeros((hd, blk), f32)
            for j in range(i + 1):
                keys = slice(j * blk, (j + 1) * blk)
                s = dot_nt(k_ref[keys, :], q)
                s = jnp.where(allowed_block(i, j, split, blk), s, NEG)
                p = jnp.exp(s - lse)
                dp = dot_nt(v_ref[keys, :], da)
                ds = (p * (dp - row_inner)).astype(bf16)
                dv = dot_nn(p.astype(bf16), da)
                dk = dot_nn(ds, q)
                if i == j and h == 0:
                    dv_acc[keys, :] = dv
                    dk_acc[keys, :] = dk
                else:
                    dv_acc[keys, :] += dv
                    dk_acc[keys, :] += dk
                dq += dot_nn(k_t[h * hd : (h + 1) * hd, keys], ds)
            dqs.append(dq)
        dq_ref[rows, :] = (jnp.concatenate(dqs, 0).T * (hd**-0.5)).astype(bf16)
    dk_ref[...] = dk_acc[...].astype(bf16)
    dv_ref[...] = dv_acc[...].astype(bf16)


def attention_back(split, qkv, da, attended, lse, heads, blk, start, count):
    seq, width = qkv.shape[0], qkv.shape[1] // 3
    hd, pairs = width // heads, heads // 2
    w = 2 * hd
    column = pl.BlockSpec((seq, w), lambda p: (0, p + start))
    out = pl.BlockSpec((seq, w), lambda p: (0, p))
    return pl.pallas_call(
        functools.partial(attention_back_kernel, seq=seq, hd=hd, blk=blk),
        grid=(count,),
        in_specs=[
            pl.BlockSpec(memory_space=pltpu.SMEM),
            column,
            pl.BlockSpec((seq, w), lambda p: (0, p + start + pairs)),
            pl.BlockSpec((seq, w), lambda p: (0, p + start + 2 * pairs)),
            column,
            column,
            pl.BlockSpec((1, 2, seq), lambda p: (p + start, 0, 0)),
        ],
        out_specs=[out, out, out],
        out_shape=[jax.ShapeDtypeStruct((seq, count * w), bf16)] * 3,
        scratch_shapes=[pltpu.VMEM((seq, w), f32)] * 2,
        compiler_params=pltpu.CompilerParams(vmem_limit_bytes=VMEM_LIMIT),
        cost_estimate=pl.CostEstimate(
            flops=20 * seq * seq * w * count,
            bytes_accessed=seq * w * count * 20,
            transcendentals=heads * seq * seq // 2,
        ),
        name="attention_back",
    )(split, qkv, qkv, qkv, da, attended, lse)


def grads_kernel(table_ref, place_ref, *refs, runs, n_left, n_right, adds):
    lefts, rights, rest = refs[:n_left], refs[n_left : n_left + n_right], refs[n_left + n_right :]
    left = rest[-1]
    ways, rows, tokens = left.shape
    step = pl.program_id(0)
    for first, last, l, r in runs:

        @pl.when(step == first)
        def _():
            for w in range(ways):
                left[w] = lefts[l][table_ref[w], 0]

        @pl.when((step >= first) & (step < last))
        def _():
            product = dot_nn(left[...].reshape(ways * rows, tokens), rights[r][...])
            product = product.reshape(ways, rows, product.shape[1])
            if adds:
                got_ref, going_ref, keep_ref, _ = rest
                product = (product + got_ref[...].astype(f32)).astype(bf16)
                keep_ref[...] = product[: ways // 2]
                going_ref[...] = product[ways // 2 :]
            else:
                rest[0][...] = product.astype(bf16)


def grads(table, jobs, tile, got=None):
    groups, _, rows, tokens = jobs[0][0].shape
    ways = table.shape[0]
    lefts, rights, runs, places = [], [], [], []
    at = 0
    for left, q, right, numbers in jobs:
        for known, one in ((lefts, left), (rights, right)):
            if not any(one is k for k in known):
                known.append(one)
        l = next(i for i, k in enumerate(lefts) if k is left)
        r = next(i for i, k in enumerate(rights) if k is right)
        runs.append((at, at + len(numbers), l, r))
        for n in numbers:
            places.append((l, q, r, n))
        at += len(numbers)

    def held(which, entry, count):
        lines = []
        for k in range(count):
            used = [(s, p[entry]) for s, p in enumerate(places) if p[which] == k]
            lines.append([next((v for s, v in used if s >= i), used[-1][1]) for i in range(at)])
        return lines

    place = jnp.array(held(0, 1, len(lefts)) + held(2, 3, len(rights)), jnp.int32)

    def left_spec(k):
        return pl.BlockSpec((groups, 1, rows, tokens), lambda i, t, p: (0, p[k, i], 0, 0))

    def right_spec(k):
        return pl.BlockSpec((tokens, tile), lambda i, t, p: (0, p[len(lefts) + k, i]))

    def block(count):
        return pl.BlockSpec((count, rows, tile), lambda i, t, p: (0, 0, i))

    def shape(count):
        return jax.ShapeDtypeStruct((count, rows, at * tile), bf16)

    half = ways // 2
    adds = got is not None
    return pl.pallas_call(
        functools.partial(
            grads_kernel, runs=runs, n_left=len(lefts), n_right=len(rights), adds=adds
        ),
        grid_spec=pltpu.PrefetchScalarGridSpec(
            num_scalar_prefetch=2,
            grid=(at,),
            in_specs=[left_spec(k) for k in range(len(lefts))]
            + [right_spec(k) for k in range(len(rights))]
            + [block(ways)] * adds,
            out_specs=[block(half), block(half)] if adds else block(ways),
            scratch_shapes=[pltpu.VMEM((ways, rows, tokens), bf16)],
        ),
        out_shape=[shape(half), shape(half)] if adds else shape(ways),
        compiler_params=pltpu.CompilerParams(vmem_limit_bytes=VMEM_LIMIT),
        cost_estimate=pl.CostEstimate(
            flops=2 * tokens * ways * rows * tile * at,
            bytes_accessed=2 * rows * (tokens * groups * (len(lefts) + 1) + 2 * ways * tile * at),
            transcendentals=0,
        ),
        name="grads_keep" if adds else "grads_send",
    )(table, place, *lefts, *rights, *([got] if adds else []))


def normalized(values):
    center = values - jnp.mean(values, axis=-1, keepdims=True)
    rate = lax.rsqrt(jnp.mean(center * center, axis=-1, keepdims=True) + epsilon)
    return center * rate, rate


def norm_back(grad, unit, rate):
    inner = jnp.mean(grad * unit, axis=-1, keepdims=True)
    return rate * (grad - jnp.mean(grad, axis=-1, keepdims=True) - unit * inner)


def column_sum(values):
    return jnp.sum(values, axis=0, keepdims=True)


def resident(shape):
    return pl.BlockSpec(shape, lambda i: (0,) * len(shape), pipeline_mode=pl.Buffered(1))


def by_rows(blk, width):
    return pl.BlockSpec((blk, width), lambda i: (i, 0))


def by_columns(height, blk):
    return pl.BlockSpec((height, blk), lambda i: (0, i))


def weight_lines(w, cut, group, first=0):
    def rows(g):
        return pl.ds(pl.multiple_of(g * group, group), group)

    rest = w.shape[1] - cut
    return [
        (first, 0, 0, cut, lambda g: w.at[rows(g), pl.ds(0, cut)]),
        (first + 1, 1, 0, rest, lambda g: w.at[rows(g), pl.ds(cut, rest)]),
    ]


def project_kernel(table_ref, x_ref, *refs, cut):
    sources = refs[:8]
    qkv_ref, left_t_ref, vec_ref, hid_ref, w, raw, sem = refs[8:]
    ways, group, lanes = raw.shape
    width = x_ref.shape[1]

    @pl.when(pl.program_id(0) == 0)
    def _():
        vec_lines = [(2, 0, cut, lanes, lambda g: raw.at[g])]
        lines = weight_lines(w, cut, group)
        fetch("start", table_ref, sources, vec_lines, sem)
        fetch("start", table_ref, sources, lines, sem)
        fetch("wait", table_ref, sources, vec_lines, sem)
        per = lanes // group
        for k in range(0, ways, per):
            row = [raw[k + j][:16, :group].astype(f32) for j in range(per)]
            vec_ref[:, k * group : (k + per) * group] = jnp.concatenate(row, 1)
        for k in range(ways):
            hid_ref[:, k * lanes : (k + 1) * lanes] = raw[k][:16].astype(f32)
        fetch("wait", table_ref, sources, lines, sem)

    unit, _ = normalized(x_ref[...].astype(f32))
    left = (unit * vec_ref[0:1, :] + vec_ref[1:2, :]).astype(bf16)
    left_t_ref[...] = transposed(left)
    for part, bias in ((0, 2), (1, None), (2, 3)):
        cols = slice(part * width, (part + 1) * width)
        rows = dot_nn(left, w[:, cols])
        if bias is not None:
            rows += vec_ref[bias : bias + 1, :]
        qkv_ref[:, cols] = rows.astype(bf16)


def project(plan, tokens, gathered, cut, hidden, blk=256):
    seq, width = tokens.shape
    blk = min(blk, seq)
    (table, *blocks), (table_spec, *specs) = block_operands(plan, gathered)
    return pl.pallas_call(
        functools.partial(project_kernel, cut=cut),
        grid=(seq // blk,),
        in_specs=[table_spec, by_rows(blk, width), *specs],
        out_specs=[
            by_rows(blk, 3 * width),
            by_columns(width, blk),
            pl.BlockSpec((16, width), lambda i: (0, 0)),
            pl.BlockSpec((16, hidden), lambda i: (0, 0)),
        ],
        out_shape=[
            jax.ShapeDtypeStruct((seq, 3 * width), bf16),
            jax.ShapeDtypeStruct((width, seq), bf16),
            jax.ShapeDtypeStruct((16, width), f32),
            jax.ShapeDtypeStruct((16, hidden), f32),
        ],
        scratch_shapes=[
            pltpu.VMEM((width, 3 * width), bf16),
            pltpu.VMEM((plan.ways, width // plan.ways, hidden // plan.ways), bf16),
            pltpu.SemaphoreType.DMA((3, plan.ways)),
        ],
        compiler_params=pltpu.CompilerParams(vmem_limit_bytes=VMEM_LIMIT),
        cost_estimate=pl.CostEstimate(
            flops=6 * seq * width * width, bytes_accessed=18 * seq * width, transcendentals=seq
        ),
        name="project",
    )(table, tokens, *blocks)


def middle_kernel(
    table_ref, x_ref, att_ref, c_ref, vec_ref, hid_ref, scale_ref, *refs, chunk, half_q
):
    sources, refs = refs[:8], refs[8:]
    out_ref, z_t_ref, a2_t_ref, m_t_ref, df_ref, dy_ref, da_ref, dx_ref, sums_ref, hid_sums_ref = refs[:10]
    wo_ref, w1_ref, w2_ref, gate, slope, dm_keep, acc, sem = refs[10:]
    width, hidden = w1_ref.shape
    group = sources[0].shape[1]
    n_q = hidden // width

    def rows(g, stride, first=0):
        return pl.ds(pl.multiple_of(g * stride + first, group), group)

    def quarter(q):
        column = hidden * (q < half_q) + q % half_q * width
        return (2 + q, q // half_q, column, width, lambda g: w2_ref.at[rows(g, n_q * group, q * group)])

    out_lines = [(0, 1, half_q * width, width, lambda g: wo_ref.at[rows(g, group)])]
    fc1_lines = [(1, 0, 0, hidden, lambda g: w1_ref.at[rows(g, group)])]
    fc2_lines = [quarter(q) for q in range(n_q)]

    def arrived(lines):
        @pl.when(pl.program_id(0) == 0)
        def _():
            fetch("wait", table_ref, sources, lines, sem)

    chunks = [slice(k, k + chunk) for k in range(0, hidden, chunk)]

    @pl.when(pl.program_id(0) == 0)
    def _():
        for lines in (out_lines, fc1_lines, fc2_lines):
            fetch("start", table_ref, sources, lines, sem)
        sums_ref[...] = jnp.zeros_like(sums_ref)
        hid_sums_ref[...] = jnp.zeros_like(hid_sums_ref)

    def vec(row):
        return vec_ref[row : row + 1, :]

    def add_sum(row, values):
        sums_ref[row : row + 1, :] += column_sum(values)

    z = (att_ref[...] * scale_ref[...]).astype(bf16)
    z_t_ref[...] = transposed(z)
    arrived(out_lines)
    unit_1, rate_1 = normalized(dot_nn(z, wo_ref[...]) + vec(4))
    x2 = x_ref[...].astype(f32) + (unit_1 * vec(5) + vec(6))
    unit_2, rate_2 = normalized(x2)
    a2 = (unit_2 * vec(7) + vec(8)).astype(bf16)
    a2_t_ref[...] = transposed(a2)
    arrived(fc1_lines)

    total = 0.0
    root = (2.0 / jnp.pi) ** 0.5
    for ch in chunks:
        f = dot_nn(a2, w1_ref[:, ch]) + hid_ref[10:11, ch]
        square = f * f
        t = jnp.tanh(f * (root + (root * 0.044715) * square))
        half = 0.5 + 0.5 * t
        g = f * half
        gate[:, ch] = g
        slope[:, ch] = half + g * (1.0 - t) * (root + (3 * root * 0.044715) * square)
        total += jnp.sum(g, axis=-1, keepdims=True)
    mean = total / hidden
    spread = 0.0
    for ch in chunks:
        center = gate[:, ch] - mean
        spread += jnp.sum(center * center, axis=-1, keepdims=True)
    rate = lax.rsqrt(spread / hidden + epsilon)

    arrived(fc2_lines)
    grad_sum = 0.0
    grad_inner = 0.0
    for ch in chunks:
        unit = (gate[:, ch] - mean) * rate
        gate[:, ch] = unit
        gain = hid_ref[11:12, ch]
        m = (unit * gain + hid_ref[12:13, ch]).astype(bf16)
        m_t_ref[ch, :] = transposed(m)
        y = dot_nn(m, w2_ref[ch, :])
        if ch.start == 0:
            acc[...] = y
        else:
            acc[...] += y
        dm = dot_nt(c_ref[...], w2_ref[ch, :]).astype(bf16)
        dm_keep[:, ch] = dm
        dm = dm.astype(f32)
        hid_sums_ref[1:2, ch] += column_sum(dm * unit)
        hid_sums_ref[2:3, ch] += column_sum(dm)
        grad = dm * gain
        grad_sum += jnp.sum(grad, axis=-1, keepdims=True)
        grad_inner += jnp.sum(grad * unit, axis=-1, keepdims=True)
    out_ref[...] = (x2 + (acc[...] + vec(9))).astype(bf16)

    grad_sum = grad_sum / hidden
    grad_inner = grad_inner / hidden
    for ch in chunks:
        grad = dm_keep[:, ch].astype(f32) * hid_ref[11:12, ch]
        grad = rate * (grad - grad_sum - gate[:, ch] * grad_inner)
        df = (slope[:, ch] * grad).astype(bf16)
        df_ref[:, ch] = df
        hid_sums_ref[0:1, ch] += column_sum(df.astype(f32))
        back = dot_nt(df, w1_ref[:, ch])
        if ch.start == 0:
            acc[...] = back
        else:
            acc[...] += back

    upstream = c_ref[...].astype(f32)
    da2 = acc[...]
    add_sum(9, upstream)
    add_sum(7, da2 * unit_2)
    add_sum(8, da2)
    dx2 = upstream + norm_back(da2 * vec(7), unit_2, rate_2)
    dx_ref[...] = dx2
    add_sum(5, dx2 * unit_1)
    add_sum(6, dx2)
    dy = norm_back(dx2 * vec(5), unit_1, rate_1).astype(bf16)
    dy_ref[...] = dy
    add_sum(4, dy.astype(f32))
    dz = dot_nt(dy, wo_ref[...]).astype(bf16).astype(f32)
    add_sum(10, dz * att_ref[...])
    da_ref[...] = (dz * scale_ref[...]).astype(bf16)


def middle(plan, tokens, attended, cotangent, gathered, vec, hid, scale, half_q, blk=256, chunk=256):
    seq, width = tokens.shape
    hidden = hid.shape[1]
    (table, *blocks), (table_spec, *specs) = block_operands(plan, gathered)
    blk = min(blk, seq)
    row, col = by_rows(blk, width), by_columns(width, blk)
    sums = pl.BlockSpec((16, width), lambda i: (0, 0))
    hid_sums = pl.BlockSpec((8, hidden), lambda i: (0, 0))
    shape = jax.ShapeDtypeStruct
    return pl.pallas_call(
        functools.partial(middle_kernel, chunk=chunk, half_q=half_q),
        grid=(seq // blk,),
        in_specs=[table_spec, row, row, row, *(resident(a.shape) for a in (vec, hid, scale)), *specs],
        out_specs=[
            row, col, col, by_columns(hidden, blk), by_rows(blk, hidden), row, row, row, sums, hid_sums,
        ],
        out_shape=[
            shape((seq, width), bf16),
            shape((width, seq), bf16),
            shape((width, seq), bf16),
            shape((hidden, seq), bf16),
            shape((seq, hidden), bf16),
            shape((seq, width), bf16),
            shape((seq, width), bf16),
            shape((seq, width), f32),
            shape((16, width), f32),
            shape((8, hidden), f32),
        ],
        scratch_shapes=[
            pltpu.VMEM((width, width), bf16),
            pltpu.VMEM((width, hidden), bf16),
            pltpu.VMEM((hidden, width), bf16),
            pltpu.VMEM((blk, hidden), f32),
            pltpu.VMEM((blk, hidden), f32),
            pltpu.VMEM((blk, hidden), bf16),
            pltpu.VMEM((blk, width), f32),
            pltpu.SemaphoreType.DMA((2 + hidden // width, plan.ways)),
        ],
        compiler_params=pltpu.CompilerParams(vmem_limit_bytes=MIDDLE_LIMIT),
        cost_estimate=pl.CostEstimate(
            flops=4 * seq * width * (width + 2 * hidden),
            bytes_accessed=2 * width * (width + 2 * hidden) + 40 * seq * width,
            transcendentals=seq * hidden,
        ),
        name="middle",
    )(table, tokens, attended, cotangent, vec, hid, scale, *blocks)


def finish_kernel(table_ref, x_ref, dx_ref, vec_ref, *refs, cut, n_parts):
    grads_in, sources = refs[: 3 * n_parts], refs[3 * n_parts : 3 * n_parts + 8]
    out_ref, sums_ref, w, sem = refs[3 * n_parts + 8 :]
    width = x_ref.shape[1]

    @pl.when(pl.program_id(0) == 0)
    def _():
        lines = weight_lines(w, cut, sources[0].shape[1])
        fetch("start", table_ref, sources, lines, sem)
        sums_ref[...] = jnp.zeros_like(sums_ref)
        fetch("wait", table_ref, sources, lines, sem)

    da1 = 0.0
    column = 0
    for part in range(n_parts):
        wide = grads_in[3 * part].shape[1]
        for k in range(3):
            grad = grads_in[3 * part + k][...]
            da1 += dot_nt(grad, w[:, k * width + column : k * width + column + wide])
            if k != 1:
                row = 2 + k // 2
                sums_ref[row : row + 1, column : column + wide] += column_sum(grad.astype(f32))
        column += wide
    unit, rate = normalized(x_ref[...].astype(f32))
    sums_ref[0:1, :] += column_sum(da1 * unit)
    sums_ref[1:2, :] += column_sum(da1)
    out_ref[...] = dx_ref[...] + norm_back(da1 * vec_ref[0:1, :], unit, rate)


def finish(plan, tokens, dx2, vec, parts, gathered, cut, blk=256):
    seq, width = tokens.shape
    blk = min(blk, seq)
    row = by_rows(blk, width)
    (table, *blocks), (table_spec, *specs) = block_operands(plan, gathered)
    grads_in = [g for part in parts for g in part]
    return pl.pallas_call(
        functools.partial(finish_kernel, cut=cut, n_parts=len(parts)),
        grid=(seq // blk,),
        in_specs=[table_spec, row, row, resident(vec.shape)]
        + [by_rows(blk, g.shape[1]) for g in grads_in]
        + specs,
        out_specs=[row, pl.BlockSpec((8, width), lambda i: (0, 0))],
        out_shape=[
            jax.ShapeDtypeStruct((seq, width), f32),
            jax.ShapeDtypeStruct((8, width), f32),
        ],
        scratch_shapes=[
            pltpu.VMEM((width, 3 * width), bf16),
            pltpu.SemaphoreType.DMA((2, plan.ways)),
        ],
        compiler_params=pltpu.CompilerParams(vmem_limit_bytes=VMEM_LIMIT),
        cost_estimate=pl.CostEstimate(
            flops=6 * seq * width * width, bytes_accessed=24 * seq * width, transcendentals=seq
        ),
        name="finish",
    )(table, tokens, dx2, vec, *grads_in, *blocks)


def local(
    plan,
    tokens,
    doc_split,
    head_scale,
    query_key_value_weight,
    output_weight,
    first_weight,
    second_weight,
    model_vectors,
    hidden_vectors,
    cotangent,
):
    seq, width = tokens.shape
    hidden = first_weight.shape[1]
    heads = head_scale.shape[0]
    blk = min(256, seq)
    ways, half = plan.ways, plan.half
    n_vec, n_hid = model_vectors.shape[0], hidden_vectors.shape[0]

    cut = 2 * width
    group, lanes = width // ways, hidden // ways
    qkv_rows = join_low(plan, query_key_value_weight)
    vec_rows = jnp.concatenate(
        [
            jnp.pad(join_low(plan, model_vectors, 1), ((0, 0), (0, lanes - group))),
            join_low(plan, hidden_vectors, 1),
            jnp.zeros((group - n_vec - n_hid, lanes), bf16),
        ],
        0,
    )
    fc1_rows = join_low(plan, first_weight)
    fc2_rows = join_low(plan, second_weight)
    out_rows = join_low(plan, output_weight)
    quarters = [fc2_rows[q * group : (q + 1) * group] for q in range(hidden // width)]
    half_q = len(quarters) // 2
    first = Gather(plan, [jnp.concatenate([qkv_rows[:, :cut], vec_rows], 1), qkv_rows[:, cut:]])
    second = Gather(
        plan,
        [
            jnp.concatenate([fc1_rows, *quarters[:half_q]], 1),
            jnp.concatenate([*quarters[half_q:], out_rows], 1),
        ],
    )
    first.step()
    second.after(first.fresh[0])
    second.step()
    while first.at < plan.steps - 1:
        first.step()
    second.after(first.fresh[0])
    second.step()
    first.step()
    first.cross_held()
    first.cross_fresh()
    tokens_in, *second.fresh = tied(tokens, *second.fresh)
    second.step()

    qkv, first_t, vec, hid = project(plan, tokens_in, first, cut, hidden)
    qkv, *second.fresh = tied(qkv, *second.fresh)
    second.step()
    second.cross_held()
    attended, lse = attention(doc_split, qkv, heads, blk)
    attended, *second.fresh = tied(attended, *second.fresh)
    second.cross_fresh()

    scale_row = jnp.repeat(head_scale, width // heads)[None]
    output, scaled_t, second_t, hidden_t, grad_pre, grad_branch, grad_attended, grad_middle, sums, hid_sums = (
        middle(plan, tokens, attended, cotangent, second, vec, hid, scale_row, half_q)
    )
    tables = [plan.table(part, False) for part in (0, 1)]

    def by_group(left_t):
        return left_t.reshape(ways, -1, group, seq)

    hidden_t = by_group(hidden_t)
    jobs = [
        [(by_group(second_t), 0, grad_pre, range(hidden // width))]
        + [(hidden_t, q, cotangent, [0]) for q in range(half_q)],
        [(hidden_t, q, cotangent, [0]) for q in range(half_q, 2 * half_q)]
        + [(by_group(scaled_t), 0, grad_branch, [0])],
    ]
    sent = [grads(tables[part][half:], jobs[part], width) for part in (0, 1)]
    got = [to_other_core(plan, v) for v in sent]
    late = []
    for part in (0, 1):
        going, keep = grads(tables[part][:half], jobs[part], width, got[part])
        late.append(Scatter(plan, part, going, keep))

    first_t = by_group(first_t)
    pairs = heads // 2
    counts = [pairs - pairs // 4, pairs // 4]
    parts, last = [], []
    for part, count in enumerate(counts):
        start = sum(counts[:part])
        parts.append(
            attention_back(doc_split, qkv, grad_attended, attended, lse, heads, blk, start, count)
        )
        if part == 0:
            for one in late:
                parts[0] = one.after(*parts[0])
                one.step()
        tile = parts[part][0].shape[1]
        last_jobs = [(first_t, 0, grad, [0]) for grad in parts[part]]
        got = to_other_core(plan, grads(tables[part][half:], last_jobs, tile))
        going, keep = grads(tables[part][:half], last_jobs, tile, got)
        last.append(Scatter(plan, part, going, keep))
        if part == 0:
            grad_attended, going = tied(grad_attended, going)
    for one in late:
        parts[1] = one.after(*parts[1])
        one.step()
    grad_tokens, last_sums = finish(plan, tokens, grad_middle, vec, parts, first, cut)

    vec_grads = jnp.concatenate([last_sums[:4], sums[4:n_vec]], 0)
    head_sums = jnp.sum(sums[n_vec].reshape(heads, -1), axis=1)
    vec_blocks = jnp.concatenate(
        [
            jnp.pad(
                vec_grads.reshape(n_vec, ways, group).transpose(1, 0, 2),
                ((0, 0), (0, 0), (0, lanes - group)),
            ),
            hid_sums[:n_hid].reshape(n_hid, ways, lanes).transpose(1, 0, 2),
            jnp.broadcast_to(jnp.pad(head_sums, (0, lanes - heads)), (ways, 1, lanes)),
            jnp.zeros((ways, 15 - n_vec - n_hid, lanes), f32),
        ],
        1,
    )
    got = to_other_core(plan, vec_blocks[tables[0][half:]])
    mine = vec_blocks[tables[0][:half]] + got
    last_vec = Scatter(plan, 0, mine[half // 2 :], mine[: half // 2])

    sum_0, sum_1 = (one.total() for one in late)
    sent_a, sent_b = (one.total() for one in last)
    sent_vec = last_vec.total()
    wide = [count * 2 * width // heads for count in counts]
    columns = [
        total[:, k * w : (k + 1) * w] for k in range(3) for total, w in zip((sent_a, sent_b), wide)
    ]
    sent_qkv = split_low(plan, jnp.concatenate(columns, 1))
    sent_fc1 = split_low(plan, sum_0[:, :hidden])
    sent_out = split_low(plan, sum_1[:, half_q * width :])
    row_blocks = [sum_0[:, hidden + q * width : hidden + (q + 1) * width] for q in range(half_q)]
    row_blocks += [sum_1[:, q * width : (q + 1) * width] for q in range(half_q)]
    sent_fc2 = split_low(plan, jnp.concatenate(row_blocks, 0))
    sent_vecd = split_low(plan, sent_vec[:n_vec, :group], 1)
    sent_vecff = split_low(plan, sent_vec[n_vec : n_vec + n_hid], 1)
    grad_heads = sent_vec[n_vec + n_hid, :heads]
    if plan.low > 1:
        grad_heads = lax.psum(grad_heads, AXES, axis_index_groups=plan.low_groups())
    return (
        output,
        grad_tokens,
        grad_heads,
        sent_qkv,
        sent_out,
        sent_fc1,
        sent_fc2,
        sent_vecd,
        sent_vecff,
    )


def solution(mesh):
    rows = P(AXES, None)
    columns = P(None, AXES)
    return jax.shard_map(
        functools.partial(local, Plan(mesh)),
        mesh=mesh,
        in_specs=(rows, P(AXES), P(), rows, rows, rows, rows, columns, columns, rows),
        out_specs=(rows, rows, P(), rows, rows, rows, rows, columns, columns),
        check_vma=False,
    )
```

```python
import functools

import jax
import jax.numpy as jnp
from jax import lax
from jax.experimental import pallas as pl
from jax.experimental.pallas import tpu as pltpu
from jax.sharding import PartitionSpec as P

epsilon = 1e-05
AXES = ("dp", "fsdp")
f32 = jnp.float32
bf16 = jnp.bfloat16
NEG = -1e30
VMEM_LIMIT = 56 << 20
ROWS_LIMIT = 62 << 20


class Plan:
    def __init__(self, mesh):
        n_dp, n_fs = mesh.shape["dp"], mesh.shape["fsdp"]
        self.count = n_dp * n_fs
        self.ways = min(self.count, 32)
        self.low = self.count // self.ways
        self.core = max(1, n_fs // self.low)
        self.dims = [1 << b for b in range(self.ways.bit_length() - 1) if 1 << b != self.core]
        self.half = self.ways // 2
        self.steps = len(self.dims)

    def order(self, core_bit, part, gathers):
        near, far = self.dims[:-1], self.dims[-1:]
        shift = (core_bit + part if part != 1 else 2) % len(near)
        near = near[shift:] + near[:shift]
        return far + near if gathers else near + far

    def pairs(self, part, step, gathers):
        out = []
        for i in range(self.count):
            group = i // self.low
            mask = self.order(int(bool(group & self.core)), part, gathers)[step]
            out.append((i, i ^ (mask * self.low)))
        return out

    def core_pairs(self):
        return [(i, i ^ (self.core * self.low)) for i in range(self.count)]

    def low_groups(self):
        return [[g * self.low + i for i in range(self.low)] for g in range(self.ways)]

    def table(self, part, gathers):
        me = (lax.axis_index("dp") * lax.axis_size("fsdp") + lax.axis_index("fsdp")) // self.low
        rows = []
        for core_bit in (0, 1):
            row = []
            for other in (0, 1):
                masks = self.order(core_bit ^ other, part, gathers)
                for r in range(self.half):
                    x = self.core if other else 0
                    for k in range(self.steps):
                        bit = k if gathers else self.steps - 1 - k
                        if (r >> bit) & 1:
                            x ^= masks[k]
                    row.append(x)
            rows.append(row)
        mine = ((me & self.core) != 0).astype(jnp.int32)
        masks = jnp.where(mine == 1, jnp.array(rows[1], jnp.int32), jnp.array(rows[0], jnp.int32))
        return jnp.bitwise_xor(me.astype(jnp.int32), masks)


def tied(*values):
    return lax.optimization_barrier(values)


class Gather:
    def __init__(self, plan, pieces):
        self.plan = plan
        self.held = [piece[None] for piece in pieces]
        self.fresh = None
        self.at = 0

    def step(self):
        if self.fresh is not None:
            self.held = [jnp.concatenate(pair, 0) for pair in zip(self.held, self.fresh)]
        self.fresh = [
            lax.ppermute(h, AXES, self.plan.pairs(part, self.at, True)) for part, h in enumerate(self.held)
        ]
        self.at += 1

    def after(self, other):
        if self.fresh is None:
            *self.held, _ = tied(*self.held, other)
        else:
            *self.fresh, _ = tied(*self.fresh, other)

    def cross_held(self):
        self.far_held = [lax.ppermute(h, AXES, self.plan.core_pairs()) for h in self.held]

    def cross_fresh(self):
        self.far_fresh = [lax.ppermute(h, AXES, self.plan.core_pairs()) for h in self.fresh]

    def blocks(self):
        return [list(b) for b in zip(self.held, self.fresh, self.far_held, self.far_fresh)]


def join_low(plan, piece, axis=0):
    if plan.low == 1:
        return piece
    return lax.all_gather(piece, AXES, axis=axis, tiled=True, axis_index_groups=plan.low_groups())


def fetch(action, table_ref, sources, lines, sem):
    for number, part, column, width, place in lines:
        for b in range(4):
            source = sources[4 * part + b]
            count = source.shape[0]

            def one(r, _, source=source, number=number, part=part, b=b, count=count):
                at = b * count + r
                copy = pltpu.make_async_copy(
                    source.at[r, :, pl.ds(column, width)],
                    place(table_ref[part, at]),
                    sem.at[number, at],
                )
                getattr(copy, action)()
                return _

            lax.fori_loop(0, count, one, 0)


def block_operands(plan, gathered):
    blocks = gathered.blocks()
    table = jnp.stack([plan.table(part, True) for part in range(len(blocks))])
    flat = [b for part in blocks for b in part]
    specs = [pl.BlockSpec(memory_space=pltpu.SMEM)] + [pl.BlockSpec(memory_space=pl.ANY)] * len(flat)
    return [table, *flat], specs


def plus(a, b):
    return a.astype(f32) + b.astype(f32)


class Scatter:
    def __init__(self, plan, part, going, keep):
        self.plan, self.part, self.keep, self.at = plan, part, keep, 0
        self.send(going)

    def send(self, going):
        self.got = lax.ppermute(going, AXES, self.plan.pairs(self.part, self.at, False))
        self.at += 1

    def step(self, lead=None):
        half = self.keep.shape[0] // 2
        kind = self.keep.dtype
        keep, got = self.keep, self.got
        if lead is not None:
            got, lead = tied(got, lead)
        going = plus(keep[half:], got[half:]).astype(kind)
        if lead is not None:
            going, lead = tied(going, lead)
        self.send(going)
        self.keep = plus(keep[:half], got[:half]).astype(kind)
        return lead

    def total(self):
        while self.at < self.plan.steps:
            self.step()
        return plus(self.keep[0], self.got[0])


def to_other_core(plan, values):
    return lax.ppermute(values, AXES, plan.core_pairs())


def split_low(plan, total, axis=0):
    if plan.low == 1:
        return total
    return lax.psum_scatter(
        total, AXES, scatter_dimension=axis, tiled=True, axis_index_groups=plan.low_groups()
    )


def dot_nt(a, b):
    return lax.dot_general(a, b, (((1,), (1,)), ((), ())), preferred_element_type=f32)


def dot_nn(a, b):
    return lax.dot_general(a, b, (((1,), (0,)), ((), ())), preferred_element_type=f32)


def transposed(a):
    return a.astype(f32).T.astype(a.dtype)


def allowed_block(i, j, split, blk):
    key_pos = j * blk + lax.broadcasted_iota(jnp.int32, (blk, blk), 0)
    query_row = i * blk + lax.broadcasted_iota(jnp.int32, (1, blk), 1)
    allowed = key_pos >= jnp.where(query_row >= split, split, 0)
    if i == j:
        allowed &= key_pos <= i * blk + lax.broadcasted_iota(jnp.int32, (blk, blk), 1)
    return allowed


def attention_kernel(split_ref, q_ref, k_ref, v_ref, *refs, seq, hd, blk):
    o_ref, lse_ref = refs[-2:]
    split = split_ref[0]
    v_t = transposed(v_ref[...])
    lane = lax.broadcasted_iota(jnp.int32, (blk, 2 * hd), 1)
    for i in range(seq // blk):
        rows = slice(i * blk, (i + 1) * blk)
        outs = []
        for h in (0, 1):
            q = jnp.where((lane >= hd) if h else (lane < hd), q_ref[rows, :], 0) * bf16(hd**-0.5)
            scores = []
            for j in range(i + 1):
                s = dot_nt(k_ref[j * blk : (j + 1) * blk, :], q)
                scores.append(jnp.where(allowed_block(i, j, split, blk), s, NEG))
            peak = scores[0].max(0, keepdims=True)
            for s in scores[1:]:
                peak = jnp.maximum(peak, s.max(0, keepdims=True))
            total = jnp.zeros((1, blk), f32)
            mixed = jnp.zeros((hd, blk), f32)
            for j, s in enumerate(scores):
                e = jnp.exp(s - peak)
                total += e.sum(0, keepdims=True)
                mixed += dot_nn(
                    v_t[h * hd : (h + 1) * hd, j * blk : (j + 1) * blk], e.astype(bf16)
                )
            outs.append(mixed / total)
            lse_ref[0, h : h + 1, rows] = peak + jnp.log(total)
        o_ref[rows, :] = jnp.concatenate(outs, 0).T


def attention(split, qkv, heads, blk, start, count, into=None):
    seq, width = qkv.shape[0], qkv.shape[1] // 3
    hd, pairs = width // heads, heads // 2
    w = 2 * hd
    more = [] if into is None else list(into)
    return pl.pallas_call(
        functools.partial(attention_kernel, seq=seq, hd=hd, blk=blk),
        grid=(count,),
        in_specs=[
            pl.BlockSpec(memory_space=pltpu.SMEM),
            pl.BlockSpec((seq, w), lambda p: (0, p + start)),
            pl.BlockSpec((seq, w), lambda p: (0, p + start + pairs)),
            pl.BlockSpec((seq, w), lambda p: (0, p + start + 2 * pairs)),
        ]
        + [pl.BlockSpec(memory_space=pl.ANY)] * len(more),
        out_specs=[
            pl.BlockSpec((seq, w), lambda p: (0, p + start)),
            pl.BlockSpec((1, 2, seq), lambda p: (p + start, 0, 0)),
        ],
        out_shape=[
            jax.ShapeDtypeStruct((seq, width), f32),
            jax.ShapeDtypeStruct((pairs, 2, seq), f32),
        ],
        compiler_params=pltpu.CompilerParams(vmem_limit_bytes=VMEM_LIMIT),
        cost_estimate=pl.CostEstimate(
            flops=12 * seq * seq * w * count,
            bytes_accessed=seq * w * count * 10,
            transcendentals=2 * count * seq * seq,
        ),
        input_output_aliases={4 + k: k for k in range(len(more))},
        name="attention",
    )(split, qkv, qkv, qkv, *more)


def attention_back_kernel(
    split_ref, q_ref, k_ref, v_ref, da_ref, o_ref, lse_ref, dq_ref, dk_ref, dv_ref, dk_acc, dv_acc,
    *, seq, hd, blk,
):
    split = split_ref[0]
    k_t = transposed(k_ref[...])
    lane = lax.broadcasted_iota(jnp.int32, (blk, 2 * hd), 1)
    for i in range(seq // blk):
        rows = slice(i * blk, (i + 1) * blk)
        q_full, da_full = q_ref[rows, :], da_ref[rows, :]
        inner = (da_full.astype(f32) * o_ref[rows, :]).T
        dqs = []
        for h in (0, 1):
            mine = (lane >= hd) if h else (lane < hd)
            q = jnp.where(mine, q_full, 0) * bf16(hd**-0.5)
            da = jnp.where(mine, da_full, 0)
            row_inner = inner[h * hd : (h + 1) * hd].sum(0, keepdims=True)
            lse = lse_ref[0, h : h + 1, rows]
            dq = jnp.zeros((hd, blk), f32)
            for j in range(i + 1):
                keys = slice(j * blk, (j + 1) * blk)
                s = dot_nt(k_ref[keys, :], q)
                s = jnp.where(allowed_block(i, j, split, blk), s, NEG)
                p = jnp.exp(s - lse)
                dp = dot_nt(v_ref[keys, :], da)
                ds = (p * (dp - row_inner)).astype(bf16)
                dv = dot_nn(p.astype(bf16), da)
                dk = dot_nn(ds, q)
                if i == j and h == 0:
                    dv_acc[keys, :] = dv
                    dk_acc[keys, :] = dk
                else:
                    dv_acc[keys, :] += dv
                    dk_acc[keys, :] += dk
                dq += dot_nn(k_t[h * hd : (h + 1) * hd, keys], ds)
            dqs.append(dq)
        dq_ref[rows, :] = (jnp.concatenate(dqs, 0).T * (hd**-0.5)).astype(bf16)
    dk_ref[...] = dk_acc[...].astype(bf16)
    dv_ref[...] = dv_acc[...].astype(bf16)


def attention_back(split, qkv, da, attended, lse, heads, blk, start, count):
    seq, width = qkv.shape[0], qkv.shape[1] // 3
    hd, pairs = width // heads, heads // 2
    w = 2 * hd
    column = pl.BlockSpec((seq, w), lambda p: (0, p + start))
    out = pl.BlockSpec((seq, w), lambda p: (0, p))
    return pl.pallas_call(
        functools.partial(attention_back_kernel, seq=seq, hd=hd, blk=blk),
        grid=(count,),
        in_specs=[
            pl.BlockSpec(memory_space=pltpu.SMEM),
            column,
            pl.BlockSpec((seq, w), lambda p: (0, p + start + pairs)),
            pl.BlockSpec((seq, w), lambda p: (0, p + start + 2 * pairs)),
            column,
            column,
            pl.BlockSpec((1, 2, seq), lambda p: (p + start, 0, 0)),
        ],
        out_specs=[out, out, out],
        out_shape=[jax.ShapeDtypeStruct((seq, count * w), bf16)] * 3,
        scratch_shapes=[pltpu.VMEM((seq, w), f32)] * 2,
        compiler_params=pltpu.CompilerParams(vmem_limit_bytes=VMEM_LIMIT),
        cost_estimate=pl.CostEstimate(
            flops=20 * seq * seq * w * count,
            bytes_accessed=seq * w * count * 20,
            transcendentals=heads * seq * seq // 2,
        ),
        name="attention_back",
    )(split, qkv, qkv, qkv, da, attended, lse)


def grads_kernel(table_ref, place_ref, *refs, runs, n_left, n_right, adds):
    lefts, rights, rest = refs[:n_left], refs[n_left : n_left + n_right], refs[n_left + n_right :]
    left = rest[-1]
    ways, rows, tokens = left.shape
    step = pl.program_id(0)
    for first, last, l, r in runs:

        @pl.when(step == first)
        def _():
            for w in range(ways):
                left[w] = lefts[l][table_ref[w], 0]

        @pl.when((step >= first) & (step < last))
        def _():
            product = dot_nn(left[...].reshape(ways * rows, tokens), rights[r][...])
            product = product.reshape(ways, rows, product.shape[1])
            if adds:
                got_ref, going_ref, keep_ref, _ = rest
                product = (product + got_ref[...].astype(f32)).astype(bf16)
                keep_ref[...] = product[: ways // 2]
                going_ref[...] = product[ways // 2 :]
            else:
                rest[0][...] = product.astype(bf16)


def grads(table, jobs, tile, got=None):
    groups, _, rows, tokens = jobs[0][0].shape
    ways = table.shape[0]
    lefts, rights, runs, places = [], [], [], []
    at = 0
    for left, q, right, numbers in jobs:
        for known, one in ((lefts, left), (rights, right)):
            if not any(one is k for k in known):
                known.append(one)
        l = next(i for i, k in enumerate(lefts) if k is left)
        r = next(i for i, k in enumerate(rights) if k is right)
        runs.append((at, at + len(numbers), l, r))
        for n in numbers:
            places.append((l, q, r, n))
        at += len(numbers)

    def held(which, entry, count):
        lines = []
        for k in range(count):
            used = [(s, p[entry]) for s, p in enumerate(places) if p[which] == k]
            lines.append([next((v for s, v in used if s >= i), used[-1][1]) for i in range(at)])
        return lines

    place = jnp.array(held(0, 1, len(lefts)) + held(2, 3, len(rights)), jnp.int32)

    def left_spec(k):
        return pl.BlockSpec((groups, 1, rows, tokens), lambda i, t, p: (0, p[k, i], 0, 0))

    def right_spec(k):
        return pl.BlockSpec((tokens, tile), lambda i, t, p: (0, p[len(lefts) + k, i]))

    def block(count):
        return pl.BlockSpec((count, rows, tile), lambda i, t, p: (0, 0, i))

    def shape(count):
        return jax.ShapeDtypeStruct((count, rows, at * tile), bf16)

    half = ways // 2
    adds = got is not None
    return pl.pallas_call(
        functools.partial(
            grads_kernel, runs=runs, n_left=len(lefts), n_right=len(rights), adds=adds
        ),
        grid_spec=pltpu.PrefetchScalarGridSpec(
            num_scalar_prefetch=2,
            grid=(at,),
            in_specs=[left_spec(k) for k in range(len(lefts))]
            + [right_spec(k) for k in range(len(rights))]
            + [block(ways)] * adds,
            out_specs=[block(half), block(half)] if adds else block(ways),
            scratch_shapes=[pltpu.VMEM((ways, rows, tokens), bf16)],
        ),
        out_shape=[shape(half), shape(half)] if adds else shape(ways),
        compiler_params=pltpu.CompilerParams(vmem_limit_bytes=VMEM_LIMIT),
        cost_estimate=pl.CostEstimate(
            flops=2 * tokens * ways * rows * tile * at,
            bytes_accessed=2 * rows * (tokens * groups * (len(lefts) + 1) + 2 * ways * tile * at),
            transcendentals=0,
        ),
        name="grads_keep" if adds else "grads_send",
    )(table, place, *lefts, *rights, *([got] if adds else []))


def normalized(values):
    center = values - jnp.mean(values, axis=-1, keepdims=True)
    rate = lax.rsqrt(jnp.mean(center * center, axis=-1, keepdims=True) + epsilon)
    return center * rate, rate


def norm_back(grad, unit, rate):
    inner = jnp.mean(grad * unit, axis=-1, keepdims=True)
    return rate * (grad - jnp.mean(grad, axis=-1, keepdims=True) - unit * inner)


def column_sum(values):
    return jnp.sum(values, axis=0, keepdims=True)


def resident(shape):
    return pl.BlockSpec(shape, lambda i: (0,) * len(shape), pipeline_mode=pl.Buffered(1))


def by_rows(blk, width):
    return pl.BlockSpec((blk, width), lambda i: (i, 0))


def by_columns(height, blk):
    return pl.BlockSpec((height, blk), lambda i: (0, i))


def weight_lines(w, cut, group, first=0):
    def rows(g):
        return pl.ds(pl.multiple_of(g * group, group), group)

    rest = w.shape[1] - cut
    return [
        (first, 0, 0, cut, lambda g: w.at[rows(g), pl.ds(0, cut)]),
        (first + 1, 1, 0, rest, lambda g: w.at[rows(g), pl.ds(cut, rest)]),
    ]


def project_kernel(table_ref, x_ref, *refs, cut):
    sources = refs[:8]
    qkv_ref, left_t_ref, vec_ref, hid_ref, w, raw, sem = refs[8:]
    ways, group, lanes = raw.shape
    width = x_ref.shape[1]

    @pl.when(pl.program_id(0) == 0)
    def _():
        vec_lines = [(2, 0, cut, lanes, lambda g: raw.at[g])]
        lines = weight_lines(w, cut, group)
        fetch("start", table_ref, sources, vec_lines, sem)
        fetch("start", table_ref, sources, lines, sem)
        fetch("wait", table_ref, sources, vec_lines, sem)
        per = lanes // group
        for k in range(0, ways, per):
            row = [raw[k + j][:16, :group].astype(f32) for j in range(per)]
            vec_ref[:, k * group : (k + per) * group] = jnp.concatenate(row, 1)
        for k in range(ways):
            hid_ref[:, k * lanes : (k + 1) * lanes] = raw[k][:16].astype(f32)
        fetch("wait", table_ref, sources, lines, sem)

    unit, _ = normalized(x_ref[...].astype(f32))
    left = (unit * vec_ref[0:1, :] + vec_ref[1:2, :]).astype(bf16)
    left_t_ref[...] = transposed(left)
    for part, bias in ((0, 2), (1, None), (2, 3)):
        cols = slice(part * width, (part + 1) * width)
        rows = dot_nn(left, w[:, cols])
        if bias is not None:
            rows += vec_ref[bias : bias + 1, :]
        qkv_ref[:, cols] = rows.astype(bf16)


def project(plan, tokens, gathered, cut, hidden, blk=256):
    seq, width = tokens.shape
    blk = min(blk, seq)
    (table, *blocks), (table_spec, *specs) = block_operands(plan, gathered)
    return pl.pallas_call(
        functools.partial(project_kernel, cut=cut),
        grid=(seq // blk,),
        in_specs=[table_spec, by_rows(blk, width), *specs],
        out_specs=[
            by_rows(blk, 3 * width),
            by_columns(width, blk),
            pl.BlockSpec((16, width), lambda i: (0, 0)),
            pl.BlockSpec((16, hidden), lambda i: (0, 0)),
        ],
        out_shape=[
            jax.ShapeDtypeStruct((seq, 3 * width), bf16),
            jax.ShapeDtypeStruct((width, seq), bf16),
            jax.ShapeDtypeStruct((16, width), f32),
            jax.ShapeDtypeStruct((16, hidden), f32),
        ],
        scratch_shapes=[
            pltpu.VMEM((width, 3 * width), bf16),
            pltpu.VMEM((plan.ways, width // plan.ways, hidden // plan.ways), bf16),
            pltpu.SemaphoreType.DMA((3, plan.ways)),
        ],
        compiler_params=pltpu.CompilerParams(vmem_limit_bytes=VMEM_LIMIT),
        cost_estimate=pl.CostEstimate(
            flops=6 * seq * width * width, bytes_accessed=18 * seq * width, transcendentals=seq
        ),
        name="project",
    )(table, tokens, *blocks)


def group_rows(g, group, stride, first=0):
    return pl.ds(pl.multiple_of(g * stride + first, group), group)


def first_weight_lines(wo, w1, group, cut):
    hidden, width = w1.shape[1], wo.shape[1]
    rest = hidden - cut
    return [
        (0, 1, rest, width, lambda g: wo.at[group_rows(g, group, group)]),
        (1, 0, 0, cut, lambda g: w1.at[group_rows(g, group, group), pl.ds(0, cut)]),
        (2, 1, 0, rest, lambda g: w1.at[group_rows(g, group, group), pl.ds(cut, rest)]),
    ]


def second_weight_lines(w2, group, cut, first):
    hidden, width = w2.shape
    count = hidden // width
    lines = []
    for q in range(count):
        for part, low, high in ((0, 0, cut), (1, cut, hidden)):
            start, stop = max(low, q * width), min(high, (q + 1) * width)
            if start < stop:

                def place(g, q=q, start=start, stop=stop):
                    rows = group_rows(g, group, count * group, q * group)
                    return w2.at[rows, pl.ds(start - q * width, stop - start)]

                lines.append((first + len(lines), part, start - low, stop - start, place))
    return lines


def vector(ref, row):
    return ref[row : row + 1, :]


def forward_rows_kernel(table_ref, x_ref, att_ref, vec_ref, hid_ref, scale_ref, *refs, chunk, cut):
    sources = refs[:8]
    y_ref, z_t_ref, a2_t_ref, m_t_ref, unit_ref, slope_ref, rate_ref, wo_ref, w1_ref, sem = refs[8:]
    hidden = w1_ref.shape[1]
    chunks = [slice(k, k + chunk) for k in range(0, hidden, chunk)]

    @pl.when(pl.program_id(0) == 0)
    def _():
        lines = first_weight_lines(wo_ref, w1_ref, sources[0].shape[1], cut)
        fetch("start", table_ref, sources, lines, sem)
        fetch("wait", table_ref, sources, lines, sem)

    z = (att_ref[...] * scale_ref[...]).astype(bf16)
    y = dot_nn(z, wo_ref[...]) + vector(vec_ref, 4)
    y_ref[...] = y
    z_t_ref[...] = transposed(z)
    unit_1, _ = normalized(y)
    x2 = x_ref[...].astype(f32) + (unit_1 * vector(vec_ref, 5) + vector(vec_ref, 6))
    unit_2, _ = normalized(x2)
    a2 = (unit_2 * vector(vec_ref, 7) + vector(vec_ref, 8)).astype(bf16)
    a2_t_ref[...] = transposed(a2)

    total = 0.0
    root = (2.0 / jnp.pi) ** 0.5
    ahead = dot_nn(a2, w1_ref[:, chunks[0]])
    for n, ch in enumerate(chunks):
        f = ahead + hid_ref[10:11, ch]
        if n + 1 < len(chunks):
            ahead = dot_nn(a2, w1_ref[:, chunks[n + 1]])
        square = f * f
        t = jnp.tanh(f * (root + (root * 0.044715) * square))
        half = 0.5 + 0.5 * t
        g = f * half
        unit_ref[:, ch] = g
        slope_ref[:, ch] = half + g * (1.0 - t) * (root + (3 * root * 0.044715) * square)
        total += jnp.sum(g, axis=-1, keepdims=True)
    mean = total / hidden
    spread = 0.0
    for ch in chunks:
        center = unit_ref[:, ch] - mean
        spread += jnp.sum(center * center, axis=-1, keepdims=True)
    rate = lax.rsqrt(spread / hidden + epsilon)
    rate_ref[...] = jnp.broadcast_to(rate, rate_ref.shape)
    for ch in chunks:
        unit = (unit_ref[:, ch] - mean) * rate
        unit_ref[:, ch] = unit
        m_t_ref[ch, :] = transposed((unit * hid_ref[11:12, ch] + hid_ref[12:13, ch]).astype(bf16))


def forward_rows(plan, tokens, attended, gathered, cut, vec, hid, scale, blk=256, chunk=256):
    seq, width = tokens.shape
    hidden = hid.shape[1]
    blk = min(blk, seq)
    (table, *blocks), (table_spec, *specs) = block_operands(plan, gathered)
    row, wide, col = by_rows(blk, width), by_rows(blk, hidden), by_columns(width, blk)
    shape = jax.ShapeDtypeStruct
    return pl.pallas_call(
        functools.partial(forward_rows_kernel, chunk=chunk, cut=cut),
        grid=(seq // blk,),
        in_specs=[table_spec, row, row, *(resident(a.shape) for a in (vec, hid, scale)), *specs],
        out_specs=[row, col, col, by_columns(hidden, blk), wide, wide, by_rows(blk, 128)],
        out_shape=[
            shape((seq, width), f32),
            shape((width, seq), bf16),
            shape((width, seq), bf16),
            shape((hidden, seq), bf16),
            shape((seq, hidden), f32),
            shape((seq, hidden), f32),
            shape((seq, 128), f32),
        ],
        scratch_shapes=[
            pltpu.VMEM((width, width), bf16),
            pltpu.VMEM((width, hidden), bf16),
            pltpu.SemaphoreType.DMA((3, plan.ways)),
        ],
        compiler_params=pltpu.CompilerParams(vmem_limit_bytes=ROWS_LIMIT),
        cost_estimate=pl.CostEstimate(
            flops=2 * seq * width * (width + hidden),
            bytes_accessed=2 * width * (width + hidden) + 50 * seq * width,
            transcendentals=seq * hidden,
        ),
        name="forward_rows",
    )(table, tokens, attended, vec, hid, scale, *blocks)


def back_rows_kernel(
    table_1_ref, table_2_ref, x_ref, att_ref, c_ref, y_ref, unit_ref, slope_ref, rate_ref,
    vec_ref, hid_ref, scale_ref, *refs, chunk, cuts,
):
    sources_1, sources_2, refs = refs[:8], refs[8:16], refs[16:]
    out_ref, df_ref, dy_ref, da_ref, dx_ref, sums_ref, hid_sums_ref = refs[:7]
    wo_ref, w1_ref, w2_ref, m_ref, sem = refs[7:]
    width, hidden = w1_ref.shape
    chunks = [slice(k, k + chunk) for k in range(0, hidden, chunk)]

    @pl.when(pl.program_id(0) == 0)
    def _():
        group = sources_1[0].shape[1]
        lines_1 = first_weight_lines(wo_ref, w1_ref, group, cuts[0])
        lines_2 = second_weight_lines(w2_ref, group, cuts[1], 3)
        fetch("start", table_2_ref, sources_2, lines_2, sem)
        fetch("start", table_1_ref, sources_1, lines_1, sem)
        sums_ref[...] = jnp.zeros_like(sums_ref)
        hid_sums_ref[...] = jnp.zeros_like(hid_sums_ref)
        fetch("wait", table_2_ref, sources_2, lines_2, sem)
        fetch("wait", table_1_ref, sources_1, lines_1, sem)

    def add_sum(row, values):
        sums_ref[row : row + 1, :] += column_sum(values)

    grad_sum = 0.0
    grad_inner = 0.0
    c = c_ref[...]
    ahead = dot_nt(c, w2_ref[chunks[0], :])
    for n, ch in enumerate(chunks):
        dm = ahead.astype(bf16)
        if n + 1 < len(chunks):
            ahead = dot_nt(c, w2_ref[chunks[n + 1], :])
        unit, gain = unit_ref[:, ch], hid_ref[11:12, ch]
        m_ref[:, ch] = (unit * gain + hid_ref[12:13, ch]).astype(bf16)
        df_ref[:, ch] = dm
        dm = dm.astype(f32)
        inner = dm * unit
        hid_sums_ref[1:2, ch] += column_sum(inner)
        hid_sums_ref[2:3, ch] += column_sum(dm)
        grad_sum += jnp.sum(dm * gain, axis=-1, keepdims=True)
        grad_inner += jnp.sum(inner * gain, axis=-1, keepdims=True)
    rate = rate_ref[:, :1]
    grad_sum = grad_sum * (1.0 / hidden)
    grad_inner = grad_inner * (1.0 / hidden)
    result = dot_nn(m_ref[...], w2_ref[...])
    for ch in chunks:
        grad = df_ref[:, ch].astype(f32) * hid_ref[11:12, ch]
        grad = grad - grad_sum - unit_ref[:, ch] * grad_inner
        df = (slope_ref[:, ch] * (rate * grad)).astype(bf16)
        df_ref[:, ch] = df
        hid_sums_ref[0:1, ch] += column_sum(df.astype(f32))
    da2 = dot_nt(df_ref[...], w1_ref[...])

    unit_1, rate_1 = normalized(y_ref[...])
    x2 = x_ref[...].astype(f32) + (unit_1 * vector(vec_ref, 5) + vector(vec_ref, 6))
    unit_2, rate_2 = normalized(x2)
    out_ref[...] = (x2 + (result + vector(vec_ref, 9))).astype(bf16)
    upstream = c.astype(f32)
    add_sum(9, upstream)
    add_sum(7, da2 * unit_2)
    add_sum(8, da2)
    dx2 = upstream + norm_back(da2 * vector(vec_ref, 7), unit_2, rate_2)
    dx_ref[...] = dx2
    add_sum(5, dx2 * unit_1)
    add_sum(6, dx2)
    dy = norm_back(dx2 * vector(vec_ref, 5), unit_1, rate_1).astype(bf16)
    dy_ref[...] = dy
    add_sum(4, dy.astype(f32))
    dz = dot_nt(dy, wo_ref[...]).astype(bf16).astype(f32)
    add_sum(10, dz * att_ref[...])
    da_ref[...] = (dz * scale_ref[...]).astype(bf16)


def back_rows(plan, rows_in, vectors, gathered, cuts, blk=256, chunk=256):
    seq, width = rows_in[0].shape
    hidden = vectors[1].shape[1]
    blk = min(blk, seq)
    (table_1, *blocks_1), (table_spec, *specs) = block_operands(plan, gathered[0])
    (table_2, *blocks_2), _ = block_operands(plan, gathered[1])
    row, wide = by_rows(blk, width), by_rows(blk, hidden)
    shape = jax.ShapeDtypeStruct
    return pl.pallas_call(
        functools.partial(back_rows_kernel, chunk=chunk, cuts=cuts),
        grid=(seq // blk,),
        in_specs=[table_spec, table_spec]
        + [by_rows(blk, a.shape[1]) for a in rows_in]
        + [resident(a.shape) for a in vectors]
        + specs
        + specs,
        out_specs=[
            row, wide, row, row, row,
            pl.BlockSpec((16, width), lambda i: (0, 0)),
            pl.BlockSpec((8, hidden), lambda i: (0, 0)),
        ],
        out_shape=[
            shape((seq, width), bf16),
            shape((seq, hidden), bf16),
            shape((seq, width), bf16),
            shape((seq, width), bf16),
            shape((seq, width), f32),
            shape((16, width), f32),
            shape((8, hidden), f32),
        ],
        scratch_shapes=[
            pltpu.VMEM((width, width), bf16),
            pltpu.VMEM((width, hidden), bf16),
            pltpu.VMEM((hidden, width), bf16),
            pltpu.VMEM((blk, hidden), bf16),
            pltpu.SemaphoreType.DMA((3 + 2 * hidden // width, plan.ways)),
        ],
        compiler_params=pltpu.CompilerParams(vmem_limit_bytes=ROWS_LIMIT),
        cost_estimate=pl.CostEstimate(
            flops=2 * seq * width * (width + 3 * hidden),
            bytes_accessed=2 * width * (width + 2 * hidden) + 60 * seq * width,
            transcendentals=0,
        ),
        name="back_rows",
    )(table_1, table_2, *rows_in, *vectors, *blocks_1, *blocks_2)


def finish_kernel(table_ref, x_ref, dx_ref, vec_ref, *refs, cut, n_parts):
    grads_in, sources = refs[: 3 * n_parts], refs[3 * n_parts : 3 * n_parts + 8]
    out_ref, sums_ref, w, sem = refs[3 * n_parts + 8 :]
    width = x_ref.shape[1]

    @pl.when(pl.program_id(0) == 0)
    def _():
        lines = weight_lines(w, cut, sources[0].shape[1])
        fetch("start", table_ref, sources, lines, sem)
        sums_ref[...] = jnp.zeros_like(sums_ref)
        fetch("wait", table_ref, sources, lines, sem)

    da1 = 0.0
    column = 0
    for part in range(n_parts):
        wide = grads_in[3 * part].shape[1]
        for k in range(3):
            grad = grads_in[3 * part + k][...]
            da1 += dot_nt(grad, w[:, k * width + column : k * width + column + wide])
            if k != 1:
                row = 2 + k // 2
                sums_ref[row : row + 1, column : column + wide] += column_sum(grad.astype(f32))
        column += wide
    unit, rate = normalized(x_ref[...].astype(f32))
    sums_ref[0:1, :] += column_sum(da1 * unit)
    sums_ref[1:2, :] += column_sum(da1)
    out_ref[...] = dx_ref[...] + norm_back(da1 * vec_ref[0:1, :], unit, rate)


def finish(plan, tokens, dx2, vec, parts, gathered, cut, blk=256):
    seq, width = tokens.shape
    blk = min(blk, seq)
    row = by_rows(blk, width)
    (table, *blocks), (table_spec, *specs) = block_operands(plan, gathered)
    grads_in = [g for part in parts for g in part]
    return pl.pallas_call(
        functools.partial(finish_kernel, cut=cut, n_parts=len(parts)),
        grid=(seq // blk,),
        in_specs=[table_spec, row, row, resident(vec.shape)]
        + [by_rows(blk, g.shape[1]) for g in grads_in]
        + specs,
        out_specs=[row, pl.BlockSpec((8, width), lambda i: (0, 0))],
        out_shape=[
            jax.ShapeDtypeStruct((seq, width), f32),
            jax.ShapeDtypeStruct((8, width), f32),
        ],
        scratch_shapes=[
            pltpu.VMEM((width, 3 * width), bf16),
            pltpu.SemaphoreType.DMA((2, plan.ways)),
        ],
        compiler_params=pltpu.CompilerParams(vmem_limit_bytes=VMEM_LIMIT),
        cost_estimate=pl.CostEstimate(
            flops=6 * seq * width * width, bytes_accessed=24 * seq * width, transcendentals=seq
        ),
        name="finish",
    )(table, tokens, dx2, vec, *grads_in, *blocks)


def local(
    plan,
    tokens,
    doc_split,
    head_scale,
    query_key_value_weight,
    output_weight,
    first_weight,
    second_weight,
    model_vectors,
    hidden_vectors,
    cotangent,
):
    seq, width = tokens.shape
    hidden = first_weight.shape[1]
    heads = head_scale.shape[0]
    blk = min(256, seq)
    ways, half = plan.ways, plan.half
    n_vec, n_hid = model_vectors.shape[0], hidden_vectors.shape[0]

    cut = 2 * width
    group, lanes = width // ways, hidden // ways
    qkv_rows = join_low(plan, query_key_value_weight)
    vec_rows = jnp.concatenate(
        [
            jnp.pad(join_low(plan, model_vectors, 1), ((0, 0), (0, lanes - group))),
            join_low(plan, hidden_vectors, 1),
            jnp.zeros((group - n_vec - n_hid, lanes), bf16),
        ],
        0,
    )
    fc1_rows = join_low(plan, first_weight)
    fc2_rows = join_low(plan, second_weight)
    out_rows = join_low(plan, output_weight)
    n_q = hidden // width
    fc2_wide = jnp.concatenate([fc2_rows[q * group : (q + 1) * group] for q in range(n_q)], 1)
    cuts = (hidden * 27 // 32, hidden * 21 // 32)
    first = Gather(plan, [jnp.concatenate([qkv_rows[:, :cut], vec_rows], 1), qkv_rows[:, cut:]])
    second = Gather(
        plan,
        [fc1_rows[:, : cuts[0]], jnp.concatenate([fc1_rows[:, cuts[0] :], out_rows], 1)],
    )
    third = Gather(plan, [fc2_wide[:, : cuts[1]], fc2_wide[:, cuts[1] :]])
    first.step()
    second.after(first.fresh[0])
    second.step()
    first.step()
    first.step()
    second.after(first.fresh[0])
    second.step()
    first.step()
    first.cross_held()
    first.cross_fresh()
    third.after(first.held[0])
    third.step()
    tokens_in, *second.fresh = tied(tokens, *second.fresh)
    second.step()

    qkv, first_t, vec, hid = project(plan, tokens_in, first, cut, hidden)
    qkv, *second.fresh = tied(qkv, *second.fresh)
    second.step()
    second.cross_held()
    qkv, *third.fresh = tied(qkv, *third.fresh)
    third.step()
    pairs = heads // 2
    some = attention(doc_split, qkv, heads, blk, 0, pairs // 2)
    *some, qkv = tied(*some, qkv)
    *second.fresh, qkv = tied(*second.fresh, qkv)
    second.cross_fresh()
    *third.fresh, qkv = tied(*third.fresh, qkv)
    third.step()
    attended, lse = attention(doc_split, qkv, heads, blk, pairs // 2, pairs // 2, some)
    attended, *third.fresh = tied(attended, *third.fresh)
    third.step()
    third.cross_held()

    scale_row = jnp.repeat(head_scale, width // heads)[None]
    branch, scaled_t, second_t, hidden_t, unit, slope, rate = forward_rows(
        plan, tokens, attended, second, cuts[0], vec, hid, scale_row
    )
    hidden_t, *third.fresh = tied(hidden_t, *third.fresh)
    third.cross_fresh()
    tables = {part: plan.table(part, False) for part in range(3)}

    def by_group(left_t):
        return left_t.reshape(ways, -1, group, seq)

    def summed(lead, jobs, parts):
        got, sums = [], []
        for part, job in zip(parts, jobs):
            left, q, right, numbers = job[0]
            left, lead = tied(left, lead)
            tile = min(width, right.shape[1])
            lead = grads(tables[part][half:], [(left, q, right, numbers), *job[1:]], tile)
            got.append(to_other_core(plan, lead))
        for part, job, theirs in zip(parts, jobs, got):
            left, q, right, numbers = job[0]
            left, lead = tied(left, lead)
            tile = min(width, right.shape[1])
            going, lead = grads(
                tables[part][:half], [(left, q, right, numbers), *job[1:]], tile, theirs
            )
            going, lead = tied(going, lead)
            sums.append(Scatter(plan, part, going, lead))
        return lead, sums

    hidden_t = by_group(hidden_t)
    lead, fc2_sums = summed(
        hidden_t[:1, :1, :8, :128],
        [[(hidden_t, q, cotangent, [0]) for q in qs] for qs in (range(n_q - 1), [n_q - 1])],
        (0, 1),
    )
    branch, lead = tied(branch, lead)
    output, grad_pre, grad_branch, grad_attended, grad_middle, sums, hid_sums = back_rows(
        plan,
        (tokens, attended, cotangent, branch, unit, slope, rate),
        (vec, hid, scale_row),
        (second, third),
        cuts,
    )
    for one in fc2_sums:
        grad_pre = one.step(grad_pre)
    lead, fc1_sums = summed(
        grad_branch,
        [
            [(by_group(second_t), 0, grad_pre, range(n_q))],
            [(by_group(scaled_t), 0, grad_branch, [0])],
        ],
        (0, 1),
    )
    for one in fc2_sums:
        grad_attended = one.step(grad_attended)
    grad_attended, lead = tied(grad_attended, lead)

    first_t = by_group(first_t)
    counts = [pairs - pairs // 4, pairs // 4]
    first_part = attention_back(doc_split, qkv, grad_attended, attended, lse, heads, blk, 0, counts[0])
    dq = first_part[0]
    for one in (*fc1_sums, *fc2_sums):
        dq = one.step(dq)
    first_part = [dq, *first_part[1:]]
    lead, sums_a = summed(dq, [[(first_t, 0, grad, [0]) for grad in first_part]], (0,))
    for one in fc1_sums:
        lead = one.step(lead)
    grad_attended, lead = tied(grad_attended, lead)
    last_part = attention_back(
        doc_split, qkv, grad_attended, attended, lse, heads, blk, counts[0], counts[1]
    )
    dq = last_part[0]
    for one in (*sums_a, *fc1_sums):
        dq = one.step(dq)
    last_part = [dq, *last_part[1:]]
    lead, sums_b = summed(dq, [[(first_t, 0, grad, [0]) for grad in last_part]], (2,))
    for one in sums_a:
        lead = one.step(lead)
    grad_middle, lead = tied(grad_middle, lead)
    grad_tokens, last_sums = finish(
        plan, tokens, grad_middle, vec, (first_part, last_part), first, cut
    )

    vec_grads = jnp.concatenate([last_sums[:4], sums[4:n_vec]], 0)
    head_sums = jnp.sum(sums[n_vec].reshape(heads, -1), axis=1)
    vec_blocks = jnp.concatenate(
        [
            jnp.pad(
                vec_grads.reshape(n_vec, ways, group).transpose(1, 0, 2),
                ((0, 0), (0, 0), (0, lanes - group)),
            ),
            hid_sums[:n_hid].reshape(n_hid, ways, lanes).transpose(1, 0, 2),
            jnp.broadcast_to(jnp.pad(head_sums, (0, lanes - heads)), (ways, 1, lanes)),
            jnp.zeros((ways, 15 - n_vec - n_hid, lanes), f32),
        ],
        1,
    )
    got = to_other_core(plan, vec_blocks[tables[0][half:]])
    mine = vec_blocks[tables[0][:half]] + got
    last_vec = Scatter(plan, 0, mine[half // 2 :], mine[: half // 2])

    sent_vec = last_vec.total()
    sent_a, sent_b = (one.total() for one in (*sums_a, *sums_b))
    sum_fc2 = [one.total() for one in fc2_sums]
    sum_fc1, sum_out = (one.total() for one in fc1_sums)
    wide = [count * 2 * width // heads for count in counts]
    columns = [
        total[:, k * w : (k + 1) * w] for k in range(3) for total, w in zip((sent_a, sent_b), wide)
    ]
    sent_qkv = split_low(plan, jnp.concatenate(columns, 1))
    sent_fc1 = split_low(plan, sum_fc1)
    sent_out = split_low(plan, sum_out)
    row_blocks = [
        total[:, k : k + width] for total in sum_fc2 for k in range(0, total.shape[1], width)
    ]
    sent_fc2 = split_low(plan, jnp.concatenate(row_blocks, 0))
    sent_vecd = split_low(plan, sent_vec[:n_vec, :group], 1)
    sent_vecff = split_low(plan, sent_vec[n_vec : n_vec + n_hid], 1)
    grad_heads = sent_vec[n_vec + n_hid, :heads]
    if plan.low > 1:
        grad_heads = lax.psum(grad_heads, AXES, axis_index_groups=plan.low_groups())
    return (
        output,
        grad_tokens,
        grad_heads,
        sent_qkv,
        sent_out,
        sent_fc1,
        sent_fc2,
        sent_vecd,
        sent_vecff,
    )


def solution(mesh):
    rows = P(AXES, None)
    columns = P(None, AXES)
    return jax.shard_map(
        functools.partial(local, Plan(mesh)),
        mesh=mesh,
        in_specs=(rows, P(AXES), P(), rows, rows, rows, rows, columns, columns, rows),
        out_specs=(rows, rows, P(), rows, rows, rows, rows, columns, columns),
        check_vma=False,
    )
```

```python
import functools

import jax
import jax.numpy as jnp
from jax import lax
from jax.experimental import pallas as pl
from jax.experimental.pallas import tpu as pltpu
from jax.sharding import PartitionSpec as P

epsilon = 1e-05
AXES = ("dp", "fsdp")
f32 = jnp.float32
bf16 = jnp.bfloat16
NEG = -1e30
VMEM_LIMIT = 56 << 20
ROWS_LIMIT = 62 << 20


def launch(
    kernel, args, *, in_specs, out_specs, out_shape, name, after=(), grid=(), scratch_shapes=(),
    prefetch=0, limit=VMEM_LIMIT, aliases=None, cover=False, cost=(1, 1, 0),
):
    after, count = list(after), len(args)

    def body(*refs):
        kernel(*refs[:count], *refs[count + len(after) :])

    return pl.pallas_call(
        body,
        grid_spec=pltpu.PrefetchScalarGridSpec(
            num_scalar_prefetch=prefetch,
            grid=grid,
            in_specs=[*in_specs] + [pl.BlockSpec(memory_space=pltpu.HBM)] * len(after),
            out_specs=out_specs,
            scratch_shapes=scratch_shapes,
        ),
        out_shape=out_shape,
        input_output_aliases=aliases or {},
        compiler_params=pltpu.CompilerParams(vmem_limit_bytes=limit),
        cost_estimate=pl.CostEstimate(
            flops=10**12 if cover else cost[0], bytes_accessed=cost[1], transcendentals=cost[2]
        ),
        name=name,
    )(*args, *after)


def relay(values, after):
    anywhere = pl.BlockSpec(memory_space=pl.ANY)
    return list(
        launch(
            lambda *refs: None,
            values,
            after=after,
            in_specs=[anywhere] * len(values),
            out_specs=[anywhere] * len(values),
            out_shape=[jax.ShapeDtypeStruct(v.shape, v.dtype) for v in values],
            aliases={k: k for k in range(len(values))},
            name="relay",
        )
    )


def in_vmem(value):
    return pltpu.with_memory_space_constraint(value, pltpu.VMEM)


class Plan:
    def __init__(self, mesh):
        n_dp, n_fs = mesh.shape["dp"], mesh.shape["fsdp"]
        self.count = n_dp * n_fs
        self.ways = min(self.count, 32)
        self.low = self.count // self.ways
        self.core = max(1, n_fs // self.low)
        self.dims = [1 << b for b in range(self.ways.bit_length() - 1) if 1 << b != self.core]
        self.half = self.ways // 2
        self.steps = len(self.dims)

    def order(self, core_bit, part, gathers):
        near, far = self.dims[:-1], self.dims[-1:]
        shift = (core_bit + part if part != 1 else 2) % len(near)
        near = near[shift:] + near[:shift]
        return far + near if gathers else near + far

    def pairs(self, part, step, gathers):
        out = []
        for i in range(self.count):
            group = i // self.low
            mask = self.order(int(bool(group & self.core)), part, gathers)[step]
            out.append((i, i ^ (mask * self.low)))
        return out

    def core_pairs(self):
        return [(i, i ^ (self.core * self.low)) for i in range(self.count)]

    def low_groups(self):
        return [[g * self.low + i for i in range(self.low)] for g in range(self.ways)]

    def table(self, part, gathers):
        me = (lax.axis_index("dp") * lax.axis_size("fsdp") + lax.axis_index("fsdp")) // self.low
        rows = []
        for core_bit in (0, 1):
            row = []
            for other in (0, 1):
                masks = self.order(core_bit ^ other, part, gathers)
                for r in range(self.half):
                    x = self.core if other else 0
                    for k in range(self.steps):
                        bit = k if gathers else self.steps - 1 - k
                        if (r >> bit) & 1:
                            x ^= masks[k]
                    row.append(x)
            rows.append(row)
        mine = ((me & self.core) != 0).astype(jnp.int32)
        masks = jnp.where(mine == 1, jnp.array(rows[1], jnp.int32), jnp.array(rows[0], jnp.int32))
        return jnp.bitwise_xor(me.astype(jnp.int32), masks)


class Gather:
    def __init__(self, plan, pieces):
        self.plan = plan
        self.held = [piece[None] for piece in pieces]
        self.fresh = None
        self.at = 0

    def join(self):
        if self.fresh is not None:
            self.held = [jnp.concatenate(pair, 0) for pair in zip(self.held, self.fresh)]
            self.fresh = None

    def step(self):
        self.join()
        self.fresh = [
            lax.ppermute(h, AXES, self.plan.pairs(part, self.at, True)) for part, h in enumerate(self.held)
        ]
        self.at += 1

    def cross_held(self):
        self.far_held = [lax.ppermute(h, AXES, self.plan.core_pairs()) for h in self.held]

    def cross_fresh(self):
        self.far_fresh = [lax.ppermute(h, AXES, self.plan.core_pairs()) for h in self.fresh]

    def blocks(self):
        return [list(b) for b in zip(self.held, self.fresh, self.far_held, self.far_fresh)]


def join_kernel(*refs, count):
    for n in range(count):
        out = refs[2 * count + n]
        half = out.shape[0] // 2
        out[:half] = refs[2 * n][...]
        out[half:] = refs[2 * n + 1][...]


def join_after(gathers, after):
    args = [
        a
        for one in gathers
        for held, fresh in zip(one.held, one.fresh)
        for a in (held, in_vmem(fresh))
    ]
    shapes = [(2 * h.shape[0], *h.shape[1:]) for one in gathers for h in one.held]
    vmem = pl.BlockSpec(memory_space=pltpu.VMEM)
    outs = launch(
        functools.partial(join_kernel, count=len(shapes)),
        args,
        after=after,
        in_specs=[vmem] * len(args),
        out_specs=[vmem] * len(shapes),
        out_shape=[jax.ShapeDtypeStruct(shape, bf16) for shape in shapes],
        name="join",
    )
    for n, one in enumerate(gathers):
        one.held = list(outs[2 * n : 2 * n + 2])
        one.fresh = None


def join_low(plan, piece, axis=0):
    if plan.low == 1:
        return piece
    return lax.all_gather(piece, AXES, axis=axis, tiled=True, axis_index_groups=plan.low_groups())


def fetch(action, table_ref, sources, lines, sem):
    for number, part, column, width, place in lines:
        for b in range(4):
            source = sources[4 * part + b]
            count = source.shape[0]

            def one(r, _, source=source, number=number, part=part, b=b, count=count):
                at = b * count + r
                copy = pltpu.make_async_copy(
                    source.at[r, :, pl.ds(column, width)],
                    place(table_ref[part, at]),
                    sem.at[number, at],
                )
                getattr(copy, action)()
                return _

            lax.fori_loop(0, count, one, 0)


def block_operands(plan, gathered):
    blocks = gathered.blocks()
    table = jnp.stack([plan.table(part, True) for part in range(len(blocks))])
    flat = [b for part in blocks for b in part]
    specs = [pl.BlockSpec(memory_space=pltpu.SMEM)] + [pl.BlockSpec(memory_space=pltpu.HBM)] * len(flat)
    return [table, *flat], specs


def plus(a, b):
    return a.astype(f32) + b.astype(f32)


class Scatter:
    def __init__(self, plan, part, keep, got):
        self.plan, self.part, self.at = plan, part, 0
        self.keep, self.got = keep, got

    @classmethod
    def begun(cls, plan, part, going, keep):
        one = cls(plan, part, None, None)
        one.send(going, keep)
        return one

    def send(self, going, keep):
        self.keep = keep
        self.got = lax.ppermute(going, AXES, self.plan.pairs(self.part, self.at, False))
        self.at += 1

    def total(self):
        return plus(self.keep[0], self.got[0])


def halve_kernel(*refs, count):
    for n in range(count):
        keep_ref, got_ref = refs[2 * n], refs[2 * n + 1]
        going_ref, kept_ref = refs[2 * (count + n)], refs[2 * (count + n) + 1]
        half = keep_ref.shape[0] // 2
        for out, part in ((going_ref, slice(half, 2 * half)), (kept_ref, slice(0, half))):
            out[...] = plus(keep_ref[part], got_ref[part]).astype(out.dtype)


def step_all(scatters, after=(), cover=False):
    args = [
        a
        for one in scatters
        for a in (one.keep, in_vmem(one.got))
    ]
    shapes = [
        jax.ShapeDtypeStruct((one.keep.shape[0] // 2, *one.keep.shape[1:]), one.keep.dtype)
        for one in scatters
        for _ in range(2)
    ]
    outs = launch(
        functools.partial(halve_kernel, count=len(scatters)),
        args,
        after=after,
        in_specs=[pl.BlockSpec(memory_space=pltpu.VMEM)] * len(args),
        out_specs=[pl.BlockSpec(memory_space=pltpu.VMEM)] * len(args),
        out_shape=shapes,
        name="halve",
        cover=cover,
    )
    for n, one in enumerate(scatters):
        one.send(*outs[2 * n : 2 * n + 2])
    return [outs[0]]


def to_other_core(plan, values):
    return lax.ppermute(values, AXES, plan.core_pairs())


def split_low(plan, total, axis=0):
    if plan.low == 1:
        return total
    return lax.psum_scatter(
        total, AXES, scatter_dimension=axis, tiled=True, axis_index_groups=plan.low_groups()
    )


def dot_nt(a, b):
    return lax.dot_general(a, b, (((1,), (1,)), ((), ())), preferred_element_type=f32)


def dot_nn(a, b):
    return lax.dot_general(a, b, (((1,), (0,)), ((), ())), preferred_element_type=f32)


def transposed(a):
    return a.astype(f32).T.astype(a.dtype)


def causal(scores):
    keys = lax.broadcasted_iota(jnp.int32, scores.shape, 0)
    return jnp.where(keys <= lax.broadcasted_iota(jnp.int32, scores.shape, 1), scores, NEG)


def head_lanes(shape, h, hd):
    lane = lax.broadcasted_iota(jnp.int32, shape, 1)
    mine = (lane >= hd) if h else (lane < hd)
    return mine, lane == (0 if h else hd)


def masked_keys(k, h, hd, split):
    mine, spare = head_lanes(k.shape, h, hd)
    early = lax.broadcasted_iota(jnp.int32, k.shape, 0) < split
    return jnp.where(mine, k, jnp.where(spare & early, bf16(NEG), bf16(0)))


def masked_queries(q, h, hd, split, start):
    mine, spare = head_lanes(q.shape, h, hd)
    late = lax.broadcasted_iota(jnp.int32, q.shape, 0) + start >= split
    alone = jnp.where(mine, q, bf16(0)) * bf16(hd**-0.5)
    return alone, jnp.where(spare & late, bf16(1), alone)


def attention_kernel(split_ref, q_ref, k_ref, v_ref, *refs, seq, hd, blk):
    o_ref, lse_ref = refs[-2:]
    split = split_ref[0]
    v_t = transposed(v_ref[...])
    keys = [masked_keys(k_ref[...], h, hd, split) for h in (0, 1)]
    for i in range(seq // blk):
        rows = slice(i * blk, (i + 1) * blk)
        outs = []
        for h in (0, 1):
            _, q = masked_queries(q_ref[rows, :], h, hd, split, i * blk)
            scores = [dot_nt(keys[h][j * blk : (j + 1) * blk], q) for j in range(i + 1)]
            scores[i] = causal(scores[i])
            peak = scores[0].max(0, keepdims=True)
            for s in scores[1:]:
                peak = jnp.maximum(peak, s.max(0, keepdims=True))
            total = jnp.zeros((1, blk), f32)
            mixed = jnp.zeros((hd, blk), f32)
            for j, s in enumerate(scores):
                low = []
                for r in strips(blk, 64):
                    e = jnp.exp(s[r] - peak)
                    total += e.sum(0, keepdims=True)
                    low.append(e.astype(bf16))
                mixed += dot_nn(
                    v_t[h * hd : (h + 1) * hd, j * blk : (j + 1) * blk], jnp.concatenate(low, 0)
                )
            outs.append(mixed / total)
            lse_ref[0, h : h + 1, rows] = peak + jnp.log(total)
        o_ref[rows, :] = jnp.concatenate(outs, 0).T


def attention(split, qkv, heads, blk, start, count, into=(), after=()):
    seq, width = qkv.shape[0], qkv.shape[1] // 3
    hd, pairs = width // heads, heads // 2
    w = 2 * hd
    return launch(
        functools.partial(attention_kernel, seq=seq, hd=hd, blk=blk),
        [split, qkv, qkv, qkv, *into],
        after=after,
        grid=(count,),
        in_specs=[
            pl.BlockSpec(memory_space=pltpu.SMEM),
            pl.BlockSpec((seq, w), lambda p: (0, p + start)),
            pl.BlockSpec((seq, w), lambda p: (0, p + start + pairs)),
            pl.BlockSpec((seq, w), lambda p: (0, p + start + 2 * pairs)),
        ]
        + [pl.BlockSpec(memory_space=pl.ANY)] * len(into),
        out_specs=[
            pl.BlockSpec((seq, w), lambda p: (0, p + start)),
            pl.BlockSpec((1, 2, seq), lambda p: (p + start, 0, 0)),
        ],
        out_shape=[
            jax.ShapeDtypeStruct((seq, width), f32),
            jax.ShapeDtypeStruct((pairs, 2, seq), f32),
        ],
        aliases={4 + k: k for k in range(len(into))},
        name="attention",
        cost=(12 * seq * seq * w * count, seq * w * count * 10, 2 * count * seq * seq),
    )


def attention_back_kernel(
    split_ref, q_ref, k_ref, v_ref, da_ref, o_ref, lse_ref, dq_ref, dk_ref, dv_ref, dk_acc, dv_acc,
    *, seq, hd, blk,
):
    split = split_ref[0]
    k_t = transposed(k_ref[...])
    keys_of = [masked_keys(k_ref[...], h, hd, split) for h in (0, 1)]
    for i in range(seq // blk):
        rows = slice(i * blk, (i + 1) * blk)
        q_full, da_full = q_ref[rows, :], da_ref[rows, :]
        inner = (da_full.astype(f32) * o_ref[rows, :]).T
        dqs = []
        for h in (0, 1):
            q, q_marked = masked_queries(q_full, h, hd, split, i * blk)
            da = jnp.where(head_lanes(da_full.shape, h, hd)[0], da_full, bf16(0))
            row_inner = inner[h * hd : (h + 1) * hd].sum(0, keepdims=True)
            lse = lse_ref[0, h : h + 1, rows]
            dq = jnp.zeros((hd, blk), f32)
            for j in range(i + 1):
                keys = slice(j * blk, (j + 1) * blk)
                s = dot_nt(keys_of[h][keys], q_marked)
                if i == j:
                    s = causal(s)
                dp = dot_nt(v_ref[keys, :], da)
                p_low, ds = [], []
                for r in strips(blk, 64):
                    p = jnp.exp(s[r] - lse)
                    p_low.append(p.astype(bf16))
                    ds.append((p * (dp[r] - row_inner)).astype(bf16))
                ds = jnp.concatenate(ds, 0)
                dv = dot_nn(jnp.concatenate(p_low, 0), da)
                dk = dot_nn(ds, q)
                if i == j and h == 0:
                    dv_acc[keys, :] = dv
                    dk_acc[keys, :] = dk
                else:
                    dv_acc[keys, :] += dv
                    dk_acc[keys, :] += dk
                dq += dot_nn(k_t[h * hd : (h + 1) * hd, keys], ds)
            dqs.append(dq)
        dq_ref[rows, :] = (jnp.concatenate(dqs, 0).T * (hd**-0.5)).astype(bf16)
    dk_ref[...] = dk_acc[...].astype(bf16)
    dv_ref[...] = dv_acc[...].astype(bf16)


def attention_back(split, qkv, da, attended, lse, heads, blk, start, count, after=()):
    seq, width = qkv.shape[0], qkv.shape[1] // 3
    hd, pairs = width // heads, heads // 2
    w = 2 * hd
    column = pl.BlockSpec((seq, w), lambda p: (0, p + start))
    out = pl.BlockSpec((seq, w), lambda p: (0, p))
    return launch(
        functools.partial(attention_back_kernel, seq=seq, hd=hd, blk=blk),
        [split, qkv, qkv, qkv, da, attended, lse],
        after=after,
        grid=(count,),
        in_specs=[
            pl.BlockSpec(memory_space=pltpu.SMEM),
            column,
            pl.BlockSpec((seq, w), lambda p: (0, p + start + pairs)),
            pl.BlockSpec((seq, w), lambda p: (0, p + start + 2 * pairs)),
            column,
            column,
            pl.BlockSpec((1, 2, seq), lambda p: (p + start, 0, 0)),
        ],
        out_specs=[out, out, out],
        out_shape=[jax.ShapeDtypeStruct((seq, count * w), bf16)] * 3,
        scratch_shapes=[pltpu.VMEM((seq, w), f32)] * 2,
        name="attention_back",
    )


def grads_kernel(table_ref, place_ref, *refs, runs, n_left, n_right, begins, adds):
    lefts, rights, rest = refs[:n_left], refs[n_left : n_left + n_right], refs[n_left + n_right :]
    left = rest[-1]
    ways, rows, tokens = left.shape
    step = pl.program_id(0)
    for first, last, l, r, part in runs:

        @pl.when(step == first)
        def _():
            for w in range(ways):
                left[w] = lefts[l][table_ref[part, w], 0]

        @pl.when((step >= first) & (step < last))
        def _():
            product = [dot_nn(left[...].reshape(ways * rows, tokens), rights[k][...]) for k in r]
            product = jnp.concatenate(product, 1) if len(r) > 1 else product[0]
            product = product.reshape(ways, rows, product.shape[1])
            if adds:
                n_parts = len(begins)
                got_ref = rest[part]
                at = pl.multiple_of((step - begins[part]) * product.shape[2], 128)
                theirs = got_ref[:, :, pl.ds(at, product.shape[2])]
                going_ref, keep_ref = rest[n_parts + 2 * part : n_parts + 2 * part + 2]
                product = (product + theirs.astype(f32)).astype(bf16)
                keep_ref[...] = product[: ways // 2]
                going_ref[...] = product[ways // 2 :]
            else:
                rest[part][...] = product.astype(bf16)


def grads(tables, parts, tile, got=None, after=(), cover=False):
    groups, _, rows, tokens = parts[0][0][0].shape
    ways = tables[0].shape[0]
    lefts, rights, runs, places, spans = [], [], [], [], []
    at = 0
    for part, jobs in enumerate(parts):
        begin = at
        for left, q, group, numbers in jobs:
            for known, one in ((lefts, left), *((rights, right) for right in group)):
                if not any(one is k for k in known):
                    known.append(one)
            l = next(i for i, k in enumerate(lefts) if k is left)
            r = [next(i for i, k in enumerate(rights) if k is right) for right in group]
            runs.append((at, at + len(numbers), l, r, part))
            for n in numbers:
                places.append(([l], q, r, n))
            at += len(numbers)
        spans.append((begin, at - begin))

    def held(which, entry, count):
        lines = []
        for k in range(count):
            used = [(s, p[entry]) for s, p in enumerate(places) if k in p[which]]
            lines.append([next((v for s, v in used if s >= i), used[-1][1]) for i in range(at)])
        return lines

    place = jnp.array(held(0, 1, len(lefts)) + held(2, 3, len(rights)), jnp.int32)

    def left_spec(k):
        return pl.BlockSpec((groups, 1, rows, tokens), lambda i, t, p: (0, p[k, i], 0, 0))

    def right_spec(k):
        return pl.BlockSpec((tokens, share), lambda i, t, p: (0, p[len(lefts) + k, i]))

    def block(count, span):
        begin, steps = span
        return pl.BlockSpec(
            (count, rows, tile), lambda i, t, p: (0, 0, jnp.clip(i - begin, 0, steps - 1))
        )

    def shape(count, span):
        return jax.ShapeDtypeStruct((count, rows, span[1] * tile), bf16)

    share = tile // len(parts[0][0][2])
    adds = got is not None
    each = [ways // 2] * 2 if adds else [ways]
    return launch(
        functools.partial(
            grads_kernel,
            runs=runs,
            n_left=len(lefts),
            n_right=len(rights),
            begins=[span[0] for span in spans],
            adds=adds,
        ),
        [jnp.stack(tables), place, *lefts, *rights, *(map(in_vmem, got) if adds else [])],
        after=after,
        prefetch=2,
        grid=(at,),
        in_specs=[left_spec(k) for k in range(len(lefts))]
        + [right_spec(k) for k in range(len(rights))]
        + [pl.BlockSpec(memory_space=pltpu.VMEM)] * (len(parts) * adds),
        out_specs=[block(count, span) for span in spans for count in each],
        out_shape=[shape(count, span) for span in spans for count in each],
        scratch_shapes=[pltpu.VMEM((ways, rows, tokens), bf16)],
        name="grads_keep" if adds else "grads_send",
        cover=cover,
    )


def normalized(values):
    center = values - jnp.mean(values, axis=-1, keepdims=True)
    rate = lax.rsqrt(jnp.mean(center * center, axis=-1, keepdims=True) + epsilon)
    return center * rate, rate


def norm_back(grad, unit, rate):
    inner = jnp.mean(grad * unit, axis=-1, keepdims=True)
    return rate * (grad - jnp.mean(grad, axis=-1, keepdims=True) - unit * inner)


def by_lanes(values):
    total = values[:, :128]
    for k in range(128, values.shape[1], 128):
        total += values[:, k : k + 128]
    return total


def by_sublanes(values):
    total = values[:8]
    for k in range(8, values.shape[0], 8):
        total += values[k : k + 8]
    return total


def column_sum(values):
    return jnp.sum(values, axis=0, keepdims=True)


def resident(shape):
    return pl.BlockSpec(shape, lambda i: (0,) * len(shape), pipeline_mode=pl.Buffered(1))


def by_rows(blk, width):
    return pl.BlockSpec((blk, width), lambda i: (i, 0))


def by_columns(height, blk):
    return pl.BlockSpec((height, blk), lambda i: (0, i))


def weight_lines(w, cut, group, first=0):
    def rows(g):
        return pl.ds(pl.multiple_of(g * group, group), group)

    rest = w.shape[1] - cut
    return [
        (first, 0, 0, cut, lambda g: w.at[rows(g), pl.ds(0, cut)]),
        (first + 1, 1, 0, rest, lambda g: w.at[rows(g), pl.ds(cut, rest)]),
    ]


def project_kernel(table_ref, x_ref, *refs, cut):
    sources = refs[:8]
    qkv_ref, left_t_ref, vec_ref, hid_ref, w, raw, left_ref, sem = refs[8:]
    ways, group, lanes = raw.shape
    width = x_ref.shape[1]

    @pl.when(pl.program_id(0) == 0)
    def _():
        vec_lines = [(2, 0, cut, lanes, lambda g: raw.at[g])]
        lines = weight_lines(w, cut, group)
        fetch("start", table_ref, sources, vec_lines, sem)
        fetch("start", table_ref, sources, lines, sem)
        fetch("wait", table_ref, sources, vec_lines, sem)
        per = lanes // group
        for k in range(0, ways, per):
            row = [raw[k + j][:16, :group].astype(f32) for j in range(per)]
            vec_ref[:, k * group : (k + per) * group] = jnp.concatenate(row, 1)
        for k in range(ways):
            hid_ref[:, k * lanes : (k + 1) * lanes] = raw[k][:16].astype(f32)
        fetch("wait", table_ref, sources, lines, sem)

    for r in strips(x_ref.shape[0], 16):
        unit, _ = normalized(x_ref[r, :].astype(f32))
        left_ref[r, :] = (unit * vec_ref[0:1, :] + vec_ref[1:2, :]).astype(bf16)
    left = left_ref[...]
    left_t_ref[...] = transposed(left)
    for part, bias in ((0, 2), (1, None), (2, 3)):
        cols = slice(part * width, (part + 1) * width)
        rows = dot_nn(left, w[:, cols])
        if bias is not None:
            rows += vec_ref[bias : bias + 1, :]
        qkv_ref[:, cols] = rows.astype(bf16)


def project(plan, tokens, gathered, cut, hidden, after=(), blk=256):
    seq, width = tokens.shape
    blk = min(blk, seq)
    (table, *blocks), (table_spec, *specs) = block_operands(plan, gathered)
    return launch(
        functools.partial(project_kernel, cut=cut),
        [table, tokens, *blocks],
        after=after,
        grid=(seq // blk,),
        in_specs=[table_spec, by_rows(blk, width), *specs],
        out_specs=[
            by_rows(blk, 3 * width),
            by_columns(width, blk),
            pl.BlockSpec((16, width), lambda i: (0, 0)),
            pl.BlockSpec((16, hidden), lambda i: (0, 0)),
        ],
        out_shape=[
            jax.ShapeDtypeStruct((seq, 3 * width), bf16),
            jax.ShapeDtypeStruct((width, seq), bf16),
            jax.ShapeDtypeStruct((16, width), f32),
            jax.ShapeDtypeStruct((16, hidden), f32),
        ],
        scratch_shapes=[
            pltpu.VMEM((width, 3 * width), bf16),
            pltpu.VMEM((plan.ways, width // plan.ways, hidden // plan.ways), bf16),
            pltpu.VMEM((blk, width), bf16),
            pltpu.SemaphoreType.DMA((3, plan.ways)),
        ],
        name="project",
        cost=(6 * seq * width * width, 18 * seq * width, seq),
    )


def group_rows(g, group, stride, first=0):
    return pl.ds(pl.multiple_of(g * stride + first, group), group)


def vector(ref, row):
    return ref[row : row + 1, :]


def strips(rows, height):
    return [slice(r, r + height) for r in range(0, rows, height)]


def middle_kernel(
    table_ref, x_ref, att_ref, c_ref, vec_ref, hid_ref, scale_ref, *refs, chunk, half_q
):
    sources, refs = refs[:8], refs[8:]
    out_ref, z_t_ref, a2_t_ref, m_t_ref, df_ref, dy_ref, da_ref, dx_ref, sums_ref, hid_sums_ref = refs[:10]
    wo_ref, w1_ref, w2_ref, gate, slope, dm_keep, acc, sem = refs[10:]
    width, hidden = w1_ref.shape
    group = sources[0].shape[1]
    n_q = hidden // width

    def rows(g, stride, first=0):
        return pl.ds(pl.multiple_of(g * stride + first, group), group)

    def quarter(q):
        column = hidden * (q < half_q) + q % half_q * width
        return (2 + q, q // half_q, column, width, lambda g: w2_ref.at[rows(g, n_q * group, q * group)])

    out_lines = [(0, 1, half_q * width, width, lambda g: wo_ref.at[rows(g, group)])]
    fc1_lines = [(1, 0, 0, hidden, lambda g: w1_ref.at[rows(g, group)])]
    fc2_lines = [quarter(q) for q in range(n_q)]

    def arrived(lines):
        @pl.when(pl.program_id(0) == 0)
        def _():
            fetch("wait", table_ref, sources, lines, sem)

    chunks = [slice(k, k + chunk) for k in range(0, hidden, chunk)]

    @pl.when(pl.program_id(0) == 0)
    def _():
        for lines in (out_lines, fc1_lines, fc2_lines):
            fetch("start", table_ref, sources, lines, sem)
        sums_ref[...] = jnp.zeros_like(sums_ref)
        hid_sums_ref[...] = jnp.zeros_like(hid_sums_ref)

    def vec(row):
        return vec_ref[row : row + 1, :]

    def add_sum(row, values):
        sums_ref[row : row + 1, :] += column_sum(values)

    z = (att_ref[...] * scale_ref[...]).astype(bf16)
    z_t_ref[...] = transposed(z)
    arrived(out_lines)
    unit_1, rate_1 = normalized(dot_nn(z, wo_ref[...]) + vec(4))
    x2 = x_ref[...].astype(f32) + (unit_1 * vec(5) + vec(6))
    unit_2, rate_2 = normalized(x2)
    a2 = (unit_2 * vec(7) + vec(8)).astype(bf16)
    a2_t_ref[...] = transposed(a2)
    arrived(fc1_lines)

    total = 0.0
    root = (2.0 / jnp.pi) ** 0.5
    for ch in chunks:
        f = dot_nn(a2, w1_ref[:, ch]) + hid_ref[10:11, ch]
        square = f * f
        t = jnp.tanh(f * (root + (root * 0.044715) * square))
        half = 0.5 + 0.5 * t
        g = f * half
        gate[:, ch] = g
        slope[:, ch] = half + g * (1.0 - t) * (root + (3 * root * 0.044715) * square)
        total += jnp.sum(g, axis=-1, keepdims=True)
    mean = total / hidden
    spread = 0.0
    for ch in chunks:
        center = gate[:, ch] - mean
        spread += jnp.sum(center * center, axis=-1, keepdims=True)
    rate = lax.rsqrt(spread / hidden + epsilon)

    arrived(fc2_lines)
    grad_sum = 0.0
    grad_inner = 0.0
    for ch in chunks:
        unit = (gate[:, ch] - mean) * rate
        gate[:, ch] = unit
        gain = hid_ref[11:12, ch]
        m = (unit * gain + hid_ref[12:13, ch]).astype(bf16)
        m_t_ref[ch, :] = transposed(m)
        y = dot_nn(m, w2_ref[ch, :])
        if ch.start == 0:
            acc[...] = y
        else:
            acc[...] += y
        dm = dot_nt(c_ref[...], w2_ref[ch, :]).astype(bf16)
        dm_keep[:, ch] = dm
        dm = dm.astype(f32)
        hid_sums_ref[1:2, ch] += column_sum(dm * unit)
        hid_sums_ref[2:3, ch] += column_sum(dm)
        grad = dm * gain
        grad_sum += jnp.sum(grad, axis=-1, keepdims=True)
        grad_inner += jnp.sum(grad * unit, axis=-1, keepdims=True)
    out_ref[...] = (x2 + (acc[...] + vec(9))).astype(bf16)

    grad_sum = grad_sum / hidden
    grad_inner = grad_inner / hidden
    for ch in chunks:
        grad = dm_keep[:, ch].astype(f32) * hid_ref[11:12, ch]
        grad = rate * (grad - grad_sum - gate[:, ch] * grad_inner)
        df = (slope[:, ch] * grad).astype(bf16)
        df_ref[:, ch] = df
        hid_sums_ref[0:1, ch] += column_sum(df.astype(f32))
        back = dot_nt(df, w1_ref[:, ch])
        if ch.start == 0:
            acc[...] = back
        else:
            acc[...] += back

    upstream = c_ref[...].astype(f32)
    da2 = acc[...]
    add_sum(9, upstream)
    add_sum(7, da2 * unit_2)
    add_sum(8, da2)
    dx2 = upstream + norm_back(da2 * vec(7), unit_2, rate_2)
    dx_ref[...] = dx2
    add_sum(5, dx2 * unit_1)
    add_sum(6, dx2)
    dy = norm_back(dx2 * vec(5), unit_1, rate_1).astype(bf16)
    dy_ref[...] = dy
    add_sum(4, dy.astype(f32))
    dz = dot_nt(dy, wo_ref[...]).astype(bf16).astype(f32)
    add_sum(10, dz * att_ref[...])
    da_ref[...] = (dz * scale_ref[...]).astype(bf16)


def middle(plan, tokens, attended, cotangent, gathered, vec, hid, scale, half_q, after=(), blk=256, chunk=256):
    seq, width = tokens.shape
    hidden = hid.shape[1]
    blk = min(blk, seq)
    (table, *blocks), (table_spec, *specs) = block_operands(plan, gathered)
    row, col, wide = by_rows(blk, width), by_columns(width, blk), by_rows(blk, hidden)
    shape = jax.ShapeDtypeStruct
    return launch(
        functools.partial(middle_kernel, chunk=chunk, half_q=half_q),
        [table, tokens, attended, cotangent, vec, hid, scale, *blocks],
        after=after,
        grid=(seq // blk,),
        in_specs=[table_spec, row, row, row, *(resident(a.shape) for a in (vec, hid, scale)), *specs],
        out_specs=[
            row, col, col, by_columns(hidden, blk), wide, row, row, row,
            pl.BlockSpec((16, width), lambda i: (0, 0)),
            pl.BlockSpec((8, hidden), lambda i: (0, 0)),
        ],
        out_shape=[
            shape((seq, width), bf16),
            shape((width, seq), bf16),
            shape((width, seq), bf16),
            shape((hidden, seq), bf16),
            shape((seq, hidden), bf16),
            shape((seq, width), bf16),
            shape((seq, width), bf16),
            shape((seq, width), f32),
            shape((16, width), f32),
            shape((8, hidden), f32),
        ],
        scratch_shapes=[
            pltpu.VMEM((width, width), bf16),
            pltpu.VMEM((width, hidden), bf16),
            pltpu.VMEM((hidden, width), bf16),
            pltpu.VMEM((blk, hidden), f32),
            pltpu.VMEM((blk, hidden), f32),
            pltpu.VMEM((blk, hidden), bf16),
            pltpu.VMEM((blk, width), f32),
            pltpu.SemaphoreType.DMA((2 + hidden // width, plan.ways)),
        ],
        limit=ROWS_LIMIT,
        name="middle",
        cost=(
            4 * seq * width * (width + 2 * hidden),
            2 * width * (width + 2 * hidden) + 40 * seq * width,
            seq * hidden,
        ),
    )


def finish_kernel(table_ref, x_ref, dx_ref, vec_ref, *refs, cut, n_parts):
    grads_in, sources = refs[: 3 * n_parts], refs[3 * n_parts : 3 * n_parts + 8]
    out_ref, sums_ref, w, acc, sem = refs[3 * n_parts + 8 :]
    width = x_ref.shape[1]

    @pl.when(pl.program_id(0) == 0)
    def _():
        lines = weight_lines(w, cut, sources[0].shape[1])
        fetch("start", table_ref, sources, lines, sem)
        sums_ref[...] = jnp.zeros_like(sums_ref)
        acc[...] = jnp.zeros_like(acc)
        fetch("wait", table_ref, sources, lines, sem)

    da1 = 0.0
    column = 0
    for part in range(n_parts):
        wide = grads_in[3 * part].shape[1]
        for k in range(3):
            grad = grads_in[3 * part + k][...]
            da1 += dot_nt(grad, w[:, k * width + column : k * width + column + wide])
            if k != 1:
                row = 2 + k // 2
                sums_ref[row : row + 1, column : column + wide] += column_sum(grad.astype(f32))
        column += wide
    for r in strips(x_ref.shape[0], 16):
        grad = da1[r]
        unit, rate = normalized(x_ref[r, :].astype(f32))
        acc[:8] += by_sublanes(grad * unit)
        acc[8:] += by_sublanes(grad)
        out_ref[r, :] = dx_ref[r, :] + norm_back(grad * vec_ref[0:1, :], unit, rate)

    @pl.when(pl.program_id(0) == pl.num_programs(0) - 1)
    def _():
        sums_ref[0:1, :] = column_sum(acc[:8])
        sums_ref[1:2, :] = column_sum(acc[8:])


def finish(plan, tokens, dx2, vec, parts, gathered, cut, after=(), blk=256):
    seq, width = tokens.shape
    blk = min(blk, seq)
    row = by_rows(blk, width)
    (table, *blocks), (table_spec, *specs) = block_operands(plan, gathered)
    grads_in = [g for part in parts for g in part]
    return launch(
        functools.partial(finish_kernel, cut=cut, n_parts=len(parts)),
        [table, tokens, dx2, vec, *grads_in, *blocks],
        after=after,
        grid=(seq // blk,),
        in_specs=[table_spec, row, row, resident(vec.shape)]
        + [by_rows(blk, g.shape[1]) for g in grads_in]
        + specs,
        out_specs=[row, pl.BlockSpec((8, width), lambda i: (0, 0))],
        out_shape=[
            jax.ShapeDtypeStruct((seq, width), f32),
            jax.ShapeDtypeStruct((8, width), f32),
        ],
        scratch_shapes=[
            pltpu.VMEM((width, 3 * width), bf16),
            pltpu.VMEM((16, width), f32),
            pltpu.SemaphoreType.DMA((2, plan.ways)),
        ],
        name="finish",
    )


def local(
    plan,
    tokens,
    doc_split,
    head_scale,
    query_key_value_weight,
    output_weight,
    first_weight,
    second_weight,
    model_vectors,
    hidden_vectors,
    cotangent,
):
    seq, width = tokens.shape
    hidden = first_weight.shape[1]
    heads = head_scale.shape[0]
    blk = min(256, seq)
    ways, half = plan.ways, plan.half
    n_vec, n_hid = model_vectors.shape[0], hidden_vectors.shape[0]

    cut = 2 * width
    group, lanes = width // ways, hidden // ways
    qkv_rows = join_low(plan, query_key_value_weight)
    vec_rows = jnp.concatenate(
        [
            jnp.pad(join_low(plan, model_vectors, 1), ((0, 0), (0, lanes - group))),
            join_low(plan, hidden_vectors, 1),
            jnp.zeros((group - n_vec - n_hid, lanes), bf16),
        ],
        0,
    )
    fc1_rows = join_low(plan, first_weight)
    fc2_rows = join_low(plan, second_weight)
    out_rows = join_low(plan, output_weight)
    n_q = hidden // width
    half_q = n_q // 2
    quarters = [fc2_rows[q * group : (q + 1) * group] for q in range(n_q)]
    first = Gather(plan, [jnp.concatenate([qkv_rows[:, :cut], vec_rows], 1), qkv_rows[:, cut:]])
    second = Gather(
        plan,
        [
            jnp.concatenate([fc1_rows, *quarters[:half_q]], 1),
            jnp.concatenate([*quarters[half_q:], out_rows], 1),
        ],
    )
    first.step()
    second.step()
    while first.at < plan.steps:
        first.step()
    first.cross_held()
    first.cross_fresh()
    while second.at < plan.steps - 1:
        second.step()

    qkv, first_t, vec, hid = project(plan, tokens, first, cut, hidden, second.held)
    join_after([second], [vec])
    second.step()
    second.cross_held()
    pairs = heads // 2
    attended, lse = attention(doc_split, qkv, heads, blk, 0, pairs, after=second.held)
    second.fresh = relay(second.fresh, [lse])
    second.cross_fresh()

    scale_row = jnp.repeat(head_scale, width // heads)[None]
    output, scaled_t, second_t, hidden_t, grad_pre, grad_branch, grad_attended, grad_middle, sums, hid_sums = (
        middle(plan, tokens, attended, cotangent, second, vec, hid, scale_row, half_q)
    )
    table = plan.table(0, False)

    def by_group(left_t):
        return left_t.reshape(ways, -1, group, seq)

    def send_grads(jobs, tile, after=(), cover=False):
        sent = grads([table[half:]], [jobs], tile, None, after, cover)
        return list(sent), to_other_core(plan, sent[0])

    def keep_grads(jobs, tile, got, after=(), cover=False):
        outs = grads([table[:half]], [jobs], tile, [got], after, cover)
        return list(outs[:1]), Scatter.begun(plan, 0, *outs)

    hidden_t = by_group(hidden_t)
    fc2_jobs = [(hidden_t, q, [cotangent], [0]) for q in range(n_q)]
    fc1_jobs = [
        (by_group(second_t), 0, [grad_pre], range(n_q)),
        (by_group(scaled_t), 0, [grad_branch], [0]),
    ]
    done, got_2 = send_grads(fc2_jobs, width)
    done, got_1 = send_grads(fc1_jobs, width, done, True)
    done, fc2_sum = keep_grads(fc2_jobs, width, got_2, done, True)
    done, fc1_sum = keep_grads(fc1_jobs, width, got_1, done)

    first_t = by_group(first_t)

    def back(start, count, after):
        out = attention_back(doc_split, qkv, grad_attended, attended, lse, heads, blk, start, count, after)
        return list(out[:1]), list(out)

    some = pairs * 3 // 8
    done, part_a = back(0, some, done)
    done = step_all([fc2_sum], done)
    done, part_b = back(some, some, done)
    size = part_a[0].shape[1]
    jobs = [(first_t, 0, part, [0]) for part in (part_a, part_b)]
    done, got = send_grads(jobs, 3 * size, done)
    done = step_all([fc2_sum, fc1_sum], done, True)
    done, sum_a = keep_grads(jobs, 3 * size, got, done)
    done, part_c = back(2 * some, pairs - 2 * some, done)
    rest = part_c[0].shape[1]
    jobs = [(first_t, 0, part_c, [0])]
    done, got = send_grads(jobs, 3 * rest, done)
    done = step_all([fc2_sum, fc1_sum, sum_a], done, True)
    done, sum_b = keep_grads(jobs, 3 * rest, got, done)
    grad_tokens, last_sums = finish(
        plan, tokens, grad_middle, vec, (part_a, part_b, part_c), first, cut, done
    )
    done = step_all([fc1_sum, sum_a, sum_b], [last_sums])

    vec_grads = jnp.concatenate([last_sums[:4], sums[4:n_vec]], 0)
    head_sums = jnp.sum(sums[n_vec].reshape(heads, -1), axis=1)
    vec_blocks = jnp.concatenate(
        [
            jnp.pad(
                vec_grads.reshape(n_vec, ways, group).transpose(1, 0, 2),
                ((0, 0), (0, 0), (0, lanes - group)),
            ),
            hid_sums[:n_hid].reshape(n_hid, ways, lanes).transpose(1, 0, 2),
            jnp.broadcast_to(jnp.pad(head_sums, (0, lanes - heads)), (ways, 1, lanes)),
            jnp.zeros((ways, 15 - n_vec - n_hid, lanes), f32),
        ],
        1,
    )
    got = to_other_core(plan, vec_blocks[table[half:]])
    vec_sum = Scatter(plan, 0, vec_blocks[table[:half]], got)
    done = step_all([sum_a, sum_b, vec_sum], done)
    done = step_all([sum_b, vec_sum], done)
    while vec_sum.at < plan.steps:
        done = step_all([vec_sum], done)
    sent_vec = vec_sum.total()
    sent_a, sent_b = sum_a.total(), sum_b.total()
    sum_fc2, sum_fc1 = fc2_sum.total(), fc1_sum.total()
    columns = []
    for k in range(3):
        columns += [sent_a[:, k * size : (k + 1) * size], sent_a[:, (3 + k) * size : (4 + k) * size]]
        columns.append(sent_b[:, k * rest : (k + 1) * rest])
    sent_qkv = split_low(plan, jnp.concatenate(columns, 1))
    sent_fc1 = split_low(plan, sum_fc1[:, :hidden])
    sent_out = split_low(plan, sum_fc1[:, hidden:])
    row_blocks = [sum_fc2[:, k : k + width] for k in range(0, hidden, width)]
    sent_fc2 = split_low(plan, jnp.concatenate(row_blocks, 0))
    sent_vecd = split_low(plan, sent_vec[:n_vec, :group], 1)
    sent_vecff = split_low(plan, sent_vec[n_vec : n_vec + n_hid], 1)
    grad_heads = sent_vec[n_vec + n_hid, :heads]
    if plan.low > 1:
        grad_heads = lax.psum(grad_heads, AXES, axis_index_groups=plan.low_groups())
    return (
        output,
        grad_tokens,
        grad_heads,
        sent_qkv,
        sent_out,
        sent_fc1,
        sent_fc2,
        sent_vecd,
        sent_vecff,
    )


def solution(mesh):
    rows = P(AXES, None)
    columns = P(None, AXES)
    return jax.shard_map(
        functools.partial(local, Plan(mesh)),
        mesh=mesh,
        in_specs=(rows, P(AXES), P(), rows, rows, rows, rows, columns, columns, rows),
        out_specs=(rows, rows, P(), rows, rows, rows, rows, columns, columns),
        check_vma=False,
    )
```

```python
import functools

import jax
import jax.numpy as jnp
from jax import lax
from jax.experimental import pallas as pl
from jax.experimental.pallas import tpu as pltpu
from jax.sharding import PartitionSpec as P

epsilon = 1e-05
AXES = ("dp", "fsdp")
f32 = jnp.float32
bf16 = jnp.bfloat16
NEG = -1e30
VMEM_LIMIT = 56 << 20
ROWS_LIMIT = 62 << 20


def launch(
    kernel, args, *, in_specs, out_specs, out_shape, name, after=(), grid=(), scratch_shapes=(),
    prefetch=0, limit=VMEM_LIMIT, aliases=None, cover=False, cost=(1, 1, 0),
):
    after, count = list(after), len(args)

    def body(*refs):
        kernel(*refs[:count], *refs[count + len(after) :])

    return pl.pallas_call(
        body,
        grid_spec=pltpu.PrefetchScalarGridSpec(
            num_scalar_prefetch=prefetch,
            grid=grid,
            in_specs=[*in_specs] + [pl.BlockSpec(memory_space=pltpu.HBM)] * len(after),
            out_specs=out_specs,
            scratch_shapes=scratch_shapes,
        ),
        out_shape=out_shape,
        input_output_aliases=aliases or {},
        compiler_params=pltpu.CompilerParams(vmem_limit_bytes=limit),
        cost_estimate=pl.CostEstimate(
            flops=10**12 if cover else cost[0], bytes_accessed=cost[1], transcendentals=cost[2]
        ),
        name=name,
    )(*args, *after)


def relay(values, after):
    anywhere = pl.BlockSpec(memory_space=pl.ANY)
    return list(
        launch(
            lambda *refs: None,
            values,
            after=after,
            in_specs=[anywhere] * len(values),
            out_specs=[anywhere] * len(values),
            out_shape=[jax.ShapeDtypeStruct(v.shape, v.dtype) for v in values],
            aliases={k: k for k in range(len(values))},
            name="relay",
        )
    )


def in_vmem(value):
    return pltpu.with_memory_space_constraint(value, pltpu.VMEM)


class Plan:
    def __init__(self, mesh):
        n_dp, n_fs = mesh.shape["dp"], mesh.shape["fsdp"]
        self.count = n_dp * n_fs
        self.ways = min(self.count, 32)
        self.low = self.count // self.ways
        self.core = max(1, n_fs // self.low)
        self.dims = [1 << b for b in range(self.ways.bit_length() - 1) if 1 << b != self.core]
        self.half = self.ways // 2
        self.steps = len(self.dims)

    def order(self, core_bit, part, gathers):
        near, far = self.dims[:-1], self.dims[-1:]
        shift = (core_bit + part if part != 1 else 2) % len(near)
        near = near[shift:] + near[:shift]
        return far + near if gathers else near + far

    def pairs(self, part, step, gathers):
        out = []
        for i in range(self.count):
            group = i // self.low
            mask = self.order(int(bool(group & self.core)), part, gathers)[step]
            out.append((i, i ^ (mask * self.low)))
        return out

    def core_pairs(self):
        return [(i, i ^ (self.core * self.low)) for i in range(self.count)]

    def low_groups(self):
        return [[g * self.low + i for i in range(self.low)] for g in range(self.ways)]

    def table(self, part, gathers):
        me = (lax.axis_index("dp") * lax.axis_size("fsdp") + lax.axis_index("fsdp")) // self.low
        rows = []
        for core_bit in (0, 1):
            row = []
            for other in (0, 1):
                masks = self.order(core_bit ^ other, part, gathers)
                for r in range(self.half):
                    x = self.core if other else 0
                    for k in range(self.steps):
                        bit = k if gathers else self.steps - 1 - k
                        if (r >> bit) & 1:
                            x ^= masks[k]
                    row.append(x)
            rows.append(row)
        mine = ((me & self.core) != 0).astype(jnp.int32)
        masks = jnp.where(mine == 1, jnp.array(rows[1], jnp.int32), jnp.array(rows[0], jnp.int32))
        return jnp.bitwise_xor(me.astype(jnp.int32), masks)


class Gather:
    def __init__(self, plan, pieces):
        self.plan = plan
        self.held = [piece[None] for piece in pieces]
        self.fresh = None
        self.at = 0

    def join(self):
        if self.fresh is not None:
            self.held = [jnp.concatenate(pair, 0) for pair in zip(self.held, self.fresh)]
            self.fresh = None

    def step(self):
        self.join()
        self.fresh = [
            lax.ppermute(h, AXES, self.plan.pairs(part, self.at, True)) for part, h in enumerate(self.held)
        ]
        self.at += 1

    def cross_held(self):
        self.far_held = [lax.ppermute(h, AXES, self.plan.core_pairs()) for h in self.held]

    def cross_fresh(self):
        self.far_fresh = [lax.ppermute(h, AXES, self.plan.core_pairs()) for h in self.fresh]

    def blocks(self):
        return [list(b) for b in zip(self.held, self.fresh, self.far_held, self.far_fresh)]


def join_kernel(*refs, count):
    for n in range(count):
        out = refs[2 * count + n]
        half = out.shape[0] // 2
        out[:half] = refs[2 * n][...]
        out[half:] = refs[2 * n + 1][...]


def join_after(gathers, after=()):
    args = [
        a
        for one in gathers
        for held, fresh in zip(one.held, one.fresh)
        for a in (held, in_vmem(fresh))
    ]
    shapes = [(2 * h.shape[0], *h.shape[1:]) for one in gathers for h in one.held]
    vmem = pl.BlockSpec(memory_space=pltpu.VMEM)
    outs = launch(
        functools.partial(join_kernel, count=len(shapes)),
        args,
        after=after,
        in_specs=[vmem] * len(args),
        out_specs=[vmem] * len(shapes),
        out_shape=[jax.ShapeDtypeStruct(shape, bf16) for shape in shapes],
        name="join",
    )
    for n, one in enumerate(gathers):
        one.held = list(outs[2 * n : 2 * n + 2])
        one.fresh = None


def join_low(plan, piece, axis=0):
    if plan.low == 1:
        return piece
    return lax.all_gather(piece, AXES, axis=axis, tiled=True, axis_index_groups=plan.low_groups())


def fetch(action, table_ref, sources, lines, sem):
    for number, part, column, width, place in lines:
        for b in range(4):
            source = sources[4 * part + b]
            count = source.shape[0]

            def one(r, _, source=source, number=number, part=part, b=b, count=count):
                at = b * count + r
                copy = pltpu.make_async_copy(
                    source.at[r, :, pl.ds(column, width)],
                    place(table_ref[part, at]),
                    sem.at[number, at],
                )
                getattr(copy, action)()
                return _

            lax.fori_loop(0, count, one, 0)


def block_operands(plan, gathered):
    blocks = gathered.blocks()
    table = jnp.stack([plan.table(part, True) for part in range(len(blocks))])
    flat = [b for part in blocks for b in part]
    specs = [pl.BlockSpec(memory_space=pltpu.SMEM)] + [pl.BlockSpec(memory_space=pltpu.HBM)] * len(flat)
    return [table, *flat], specs


def plus(a, b):
    return a.astype(f32) + b.astype(f32)


class Scatter:
    def __init__(self, plan, part, keep, got):
        self.plan, self.part, self.at = plan, part, 0
        self.keep, self.got = keep, got

    @classmethod
    def begun(cls, plan, part, going, keep):
        one = cls(plan, part, None, None)
        one.send(going, keep)
        return one

    def send(self, going, keep):
        self.keep = keep
        self.got = lax.ppermute(going, AXES, self.plan.pairs(self.part, self.at, False))
        self.at += 1

    def total(self):
        return plus(self.keep[0], self.got[0])


def halve_kernel(*refs, count):
    for n in range(count):
        keep_ref, got_ref = refs[2 * n], refs[2 * n + 1]
        going_ref, kept_ref = refs[2 * (count + n)], refs[2 * (count + n) + 1]
        half = keep_ref.shape[0] // 2
        for out, part in ((going_ref, slice(half, 2 * half)), (kept_ref, slice(0, half))):
            out[...] = plus(keep_ref[part], got_ref[part]).astype(out.dtype)


def step_all(scatters, after=(), cover=False):
    args = [
        a
        for one in scatters
        for a in (one.keep, in_vmem(one.got))
    ]
    shapes = [
        jax.ShapeDtypeStruct((one.keep.shape[0] // 2, *one.keep.shape[1:]), one.keep.dtype)
        for one in scatters
        for _ in range(2)
    ]
    outs = launch(
        functools.partial(halve_kernel, count=len(scatters)),
        args,
        after=after,
        in_specs=[pl.BlockSpec(memory_space=pltpu.VMEM)] * len(args),
        out_specs=[pl.BlockSpec(memory_space=pltpu.VMEM)] * len(args),
        out_shape=shapes,
        name="halve",
        cover=cover,
    )
    for n, one in enumerate(scatters):
        one.send(*outs[2 * n : 2 * n + 2])
    return [outs[0]]


def to_other_core(plan, values):
    return lax.ppermute(values, AXES, plan.core_pairs())


def split_low(plan, total, axis=0):
    if plan.low == 1:
        return total
    return lax.psum_scatter(
        total, AXES, scatter_dimension=axis, tiled=True, axis_index_groups=plan.low_groups()
    )


def dot_nt(a, b):
    return lax.dot_general(a, b, (((1,), (1,)), ((), ())), preferred_element_type=f32)


def dot_nn(a, b):
    return lax.dot_general(a, b, (((1,), (0,)), ((), ())), preferred_element_type=f32)


def transposed(a):
    return a.astype(f32).T.astype(a.dtype)


def causal(scores):
    keys = lax.broadcasted_iota(jnp.int32, scores.shape, 0)
    return jnp.where(keys <= lax.broadcasted_iota(jnp.int32, scores.shape, 1), scores, NEG)


def head_lanes(shape, h, hd):
    lane = lax.broadcasted_iota(jnp.int32, shape, 1)
    mine = (lane >= hd) if h else (lane < hd)
    return mine, lane == (0 if h else hd)


def masked_keys(k, h, hd, split):
    mine, spare = head_lanes(k.shape, h, hd)
    early = lax.broadcasted_iota(jnp.int32, k.shape, 0) < split
    return jnp.where(mine, k, jnp.where(spare & early, bf16(NEG), bf16(0)))


def masked_queries(q, h, hd, split, start):
    mine, spare = head_lanes(q.shape, h, hd)
    late = lax.broadcasted_iota(jnp.int32, q.shape, 0) + start >= split
    alone = jnp.where(mine, q, bf16(0)) * bf16(hd**-0.5)
    return alone, jnp.where(spare & late, bf16(1), alone)


def attention_kernel(split_ref, q_ref, k_ref, v_ref, *refs, seq, hd, blk):
    o_ref, lse_ref = refs[-2:]
    split = split_ref[0]
    v_t = transposed(v_ref[...])
    keys = [masked_keys(k_ref[...], h, hd, split) for h in (0, 1)]
    for i in range(seq // blk):
        rows = slice(i * blk, (i + 1) * blk)
        outs = []
        for h in (0, 1):
            _, q = masked_queries(q_ref[rows, :], h, hd, split, i * blk)
            scores = [dot_nt(keys[h][j * blk : (j + 1) * blk], q) for j in range(i + 1)]
            scores[i] = causal(scores[i])
            peak = scores[0].max(0, keepdims=True)
            for s in scores[1:]:
                peak = jnp.maximum(peak, s.max(0, keepdims=True))
            total = jnp.zeros((1, blk), f32)
            mixed = jnp.zeros((hd, blk), f32)
            for j, s in enumerate(scores):
                low = []
                for r in strips(blk, 64):
                    e = jnp.exp(s[r] - peak)
                    total += e.sum(0, keepdims=True)
                    low.append(e.astype(bf16))
                mixed += dot_nn(
                    v_t[h * hd : (h + 1) * hd, j * blk : (j + 1) * blk], jnp.concatenate(low, 0)
                )
            outs.append(mixed / total)
            lse_ref[0, h : h + 1, rows] = peak + jnp.log(total)
        o_ref[rows, :] = jnp.concatenate(outs, 0).T


def attention(split, qkv, heads, blk, start, count, into=(), after=()):
    seq, width = qkv.shape[0], qkv.shape[1] // 3
    hd, pairs = width // heads, heads // 2
    w = 2 * hd
    return launch(
        functools.partial(attention_kernel, seq=seq, hd=hd, blk=blk),
        [split, qkv, qkv, qkv, *into],
        after=after,
        grid=(count,),
        in_specs=[
            pl.BlockSpec(memory_space=pltpu.SMEM),
            pl.BlockSpec((seq, w), lambda p: (0, p + start)),
            pl.BlockSpec((seq, w), lambda p: (0, p + start + pairs)),
            pl.BlockSpec((seq, w), lambda p: (0, p + start + 2 * pairs)),
        ]
        + [pl.BlockSpec(memory_space=pl.ANY)] * len(into),
        out_specs=[
            pl.BlockSpec((seq, w), lambda p: (0, p + start)),
            pl.BlockSpec((1, 2, seq), lambda p: (p + start, 0, 0)),
        ],
        out_shape=[
            jax.ShapeDtypeStruct((seq, width), f32),
            jax.ShapeDtypeStruct((pairs, 2, seq), f32),
        ],
        aliases={4 + k: k for k in range(len(into))},
        name="attention",
        cost=(12 * seq * seq * w * count, seq * w * count * 10, 2 * count * seq * seq),
    )


def attention_back_kernel(
    split_ref, q_ref, k_ref, v_ref, da_ref, o_ref, lse_ref, dq_ref, dk_ref, dv_ref, dk_acc, dv_acc,
    *, seq, hd, blk,
):
    split = split_ref[0]
    k_t = transposed(k_ref[...])
    keys_of = [masked_keys(k_ref[...], h, hd, split) for h in (0, 1)]
    for i in range(seq // blk):
        rows = slice(i * blk, (i + 1) * blk)
        q_full, da_full = q_ref[rows, :], da_ref[rows, :]
        inner = (da_full.astype(f32) * o_ref[rows, :]).T
        dqs = []
        for h in (0, 1):
            q, q_marked = masked_queries(q_full, h, hd, split, i * blk)
            da = jnp.where(head_lanes(da_full.shape, h, hd)[0], da_full, bf16(0))
            row_inner = inner[h * hd : (h + 1) * hd].sum(0, keepdims=True)
            lse = lse_ref[0, h : h + 1, rows]
            dq = jnp.zeros((hd, blk), f32)
            for j in range(i + 1):
                keys = slice(j * blk, (j + 1) * blk)
                s = dot_nt(keys_of[h][keys], q_marked)
                if i == j:
                    s = causal(s)
                dp = dot_nt(v_ref[keys, :], da)
                p_low, ds = [], []
                for r in strips(blk, 64):
                    p = jnp.exp(s[r] - lse)
                    p_low.append(p.astype(bf16))
                    ds.append((p * (dp[r] - row_inner)).astype(bf16))
                ds = jnp.concatenate(ds, 0)
                dv = dot_nn(jnp.concatenate(p_low, 0), da)
                dk = dot_nn(ds, q)
                if i == j and h == 0:
                    dv_acc[keys, :] = dv
                    dk_acc[keys, :] = dk
                else:
                    dv_acc[keys, :] += dv
                    dk_acc[keys, :] += dk
                dq += dot_nn(k_t[h * hd : (h + 1) * hd, keys], ds)
            dqs.append(dq)
        dq_ref[rows, :] = (jnp.concatenate(dqs, 0).T * (hd**-0.5)).astype(bf16)
    dk_ref[...] = dk_acc[...].astype(bf16)
    dv_ref[...] = dv_acc[...].astype(bf16)


def attention_back(split, qkv, da, attended, lse, heads, blk, start, count, after=()):
    seq, width = qkv.shape[0], qkv.shape[1] // 3
    hd, pairs = width // heads, heads // 2
    w = 2 * hd
    column = pl.BlockSpec((seq, w), lambda p: (0, p + start))
    out = pl.BlockSpec((seq, w), lambda p: (0, p))
    return launch(
        functools.partial(attention_back_kernel, seq=seq, hd=hd, blk=blk),
        [split, qkv, qkv, qkv, da, attended, lse],
        after=after,
        grid=(count,),
        in_specs=[
            pl.BlockSpec(memory_space=pltpu.SMEM),
            column,
            pl.BlockSpec((seq, w), lambda p: (0, p + start + pairs)),
            pl.BlockSpec((seq, w), lambda p: (0, p + start + 2 * pairs)),
            column,
            column,
            pl.BlockSpec((1, 2, seq), lambda p: (p + start, 0, 0)),
        ],
        out_specs=[out, out, out],
        out_shape=[jax.ShapeDtypeStruct((seq, count * w), bf16)] * 3,
        scratch_shapes=[pltpu.VMEM((seq, w), f32)] * 2,
        name="attention_back",
    )


def grads_kernel(table_ref, place_ref, *refs, runs, n_left, n_right, begins, adds):
    lefts, rights, rest = refs[:n_left], refs[n_left : n_left + n_right], refs[n_left + n_right :]
    left = rest[-1]
    ways, rows, tokens = left.shape
    step = pl.program_id(0)
    for first, last, l, r, part in runs:

        @pl.when(step == first)
        def _():
            for w in range(ways):
                left[w] = lefts[l][table_ref[part, w], 0]

        @pl.when((step >= first) & (step < last))
        def _():
            product = [dot_nn(left[...].reshape(ways * rows, tokens), rights[k][...]) for k in r]
            product = jnp.concatenate(product, 1) if len(r) > 1 else product[0]
            product = product.reshape(ways, rows, product.shape[1])
            if adds:
                n_parts = len(begins)
                got_ref = rest[part]
                at = pl.multiple_of((step - begins[part]) * product.shape[2], 128)
                theirs = got_ref[:, :, pl.ds(at, product.shape[2])]
                going_ref, keep_ref = rest[n_parts + 2 * part : n_parts + 2 * part + 2]
                product = (product + theirs.astype(f32)).astype(bf16)
                keep_ref[...] = product[: ways // 2]
                going_ref[...] = product[ways // 2 :]
            else:
                rest[part][...] = product.astype(bf16)


def grads(tables, parts, tile, got=None, after=(), cover=False):
    groups, _, rows, tokens = parts[0][0][0].shape
    ways = tables[0].shape[0]
    lefts, rights, runs, places, spans = [], [], [], [], []
    at = 0
    for part, jobs in enumerate(parts):
        begin = at
        for left, q, group, numbers in jobs:
            for known, one in ((lefts, left), *((rights, right) for right in group)):
                if not any(one is k for k in known):
                    known.append(one)
            l = next(i for i, k in enumerate(lefts) if k is left)
            r = [next(i for i, k in enumerate(rights) if k is right) for right in group]
            runs.append((at, at + len(numbers), l, r, part))
            for n in numbers:
                places.append(([l], q, r, n))
            at += len(numbers)
        spans.append((begin, at - begin))

    def held(which, entry, count):
        lines = []
        for k in range(count):
            used = [(s, p[entry]) for s, p in enumerate(places) if k in p[which]]
            lines.append([next((v for s, v in used if s >= i), used[-1][1]) for i in range(at)])
        return lines

    place = jnp.array(held(0, 1, len(lefts)) + held(2, 3, len(rights)), jnp.int32)

    def left_spec(k):
        return pl.BlockSpec((groups, 1, rows, tokens), lambda i, t, p: (0, p[k, i], 0, 0))

    def right_spec(k):
        return pl.BlockSpec((tokens, share), lambda i, t, p: (0, p[len(lefts) + k, i]))

    def block(count, span):
        begin, steps = span
        return pl.BlockSpec(
            (count, rows, tile), lambda i, t, p: (0, 0, jnp.clip(i - begin, 0, steps - 1))
        )

    def shape(count, span):
        return jax.ShapeDtypeStruct((count, rows, span[1] * tile), bf16)

    share = tile // len(parts[0][0][2])
    adds = got is not None
    each = [ways // 2] * 2 if adds else [ways]
    return launch(
        functools.partial(
            grads_kernel,
            runs=runs,
            n_left=len(lefts),
            n_right=len(rights),
            begins=[span[0] for span in spans],
            adds=adds,
        ),
        [jnp.stack(tables), place, *lefts, *rights, *(map(in_vmem, got) if adds else [])],
        after=after,
        prefetch=2,
        grid=(at,),
        in_specs=[left_spec(k) for k in range(len(lefts))]
        + [right_spec(k) for k in range(len(rights))]
        + [pl.BlockSpec(memory_space=pltpu.VMEM)] * (len(parts) * adds),
        out_specs=[block(count, span) for span in spans for count in each],
        out_shape=[shape(count, span) for span in spans for count in each],
        scratch_shapes=[pltpu.VMEM((ways, rows, tokens), bf16)],
        name="grads_keep" if adds else "grads_send",
        cover=cover,
    )


def normalized(values):
    center = values - jnp.mean(values, axis=-1, keepdims=True)
    rate = lax.rsqrt(jnp.mean(center * center, axis=-1, keepdims=True) + epsilon)
    return center * rate, rate


def norm_back(grad, unit, rate):
    inner = jnp.mean(grad * unit, axis=-1, keepdims=True)
    return rate * (grad - jnp.mean(grad, axis=-1, keepdims=True) - unit * inner)


def by_lanes(values):
    total = values[:, :128]
    for k in range(128, values.shape[1], 128):
        total += values[:, k : k + 128]
    return total


def by_sublanes(values):
    total = values[:8]
    for k in range(8, values.shape[0], 8):
        total += values[k : k + 8]
    return total


def column_sum(values):
    return jnp.sum(values, axis=0, keepdims=True)


def resident(shape):
    return pl.BlockSpec(shape, lambda i: (0,) * len(shape), pipeline_mode=pl.Buffered(1))


def by_rows(blk, width):
    return pl.BlockSpec((blk, width), lambda i: (i, 0))


def by_columns(height, blk):
    return pl.BlockSpec((height, blk), lambda i: (0, i))


def weight_lines(w, cut, group, first=0):
    def rows(g):
        return pl.ds(pl.multiple_of(g * group, group), group)

    rest = w.shape[1] - cut
    return [
        (first, 0, 0, cut, lambda g: w.at[rows(g), pl.ds(0, cut)]),
        (first + 1, 1, 0, rest, lambda g: w.at[rows(g), pl.ds(cut, rest)]),
    ]


def project_kernel(table_ref, x_ref, *refs, cut):
    sources = refs[:8]
    qkv_ref, left_t_ref, vec_ref, hid_ref, w, raw, left_ref, sem = refs[8:]
    ways, group, lanes = raw.shape
    width = x_ref.shape[1]

    @pl.when(pl.program_id(0) == 0)
    def _():
        vec_lines = [(2, 0, cut, lanes, lambda g: raw.at[g])]
        lines = weight_lines(w, cut, group)
        fetch("start", table_ref, sources, vec_lines, sem)
        fetch("start", table_ref, sources, lines, sem)
        fetch("wait", table_ref, sources, vec_lines, sem)
        per = lanes // group
        for k in range(0, ways, per):
            row = [raw[k + j][:16, :group].astype(f32) for j in range(per)]
            vec_ref[:, k * group : (k + per) * group] = jnp.concatenate(row, 1)
        for k in range(ways):
            hid_ref[:, k * lanes : (k + 1) * lanes] = raw[k][:16].astype(f32)
        fetch("wait", table_ref, sources, lines, sem)

    for r in strips(x_ref.shape[0], 16):
        unit, _ = normalized(x_ref[r, :].astype(f32))
        left_ref[r, :] = (unit * vec_ref[0:1, :] + vec_ref[1:2, :]).astype(bf16)
    left = left_ref[...]
    left_t_ref[...] = transposed(left)
    for part, bias in ((0, 2), (1, None), (2, 3)):
        cols = slice(part * width, (part + 1) * width)
        rows = dot_nn(left, w[:, cols])
        if bias is not None:
            rows += vec_ref[bias : bias + 1, :]
        qkv_ref[:, cols] = rows.astype(bf16)


def project(plan, tokens, gathered, cut, hidden, after=(), blk=256):
    seq, width = tokens.shape
    blk = min(blk, seq)
    (table, *blocks), (table_spec, *specs) = block_operands(plan, gathered)
    return launch(
        functools.partial(project_kernel, cut=cut),
        [table, tokens, *blocks],
        after=after,
        grid=(seq // blk,),
        in_specs=[table_spec, by_rows(blk, width), *specs],
        out_specs=[
            by_rows(blk, 3 * width),
            by_columns(width, blk),
            pl.BlockSpec((16, width), lambda i: (0, 0)),
            pl.BlockSpec((16, hidden), lambda i: (0, 0)),
        ],
        out_shape=[
            jax.ShapeDtypeStruct((seq, 3 * width), bf16),
            jax.ShapeDtypeStruct((width, seq), bf16),
            jax.ShapeDtypeStruct((16, width), f32),
            jax.ShapeDtypeStruct((16, hidden), f32),
        ],
        scratch_shapes=[
            pltpu.VMEM((width, 3 * width), bf16),
            pltpu.VMEM((plan.ways, width // plan.ways, hidden // plan.ways), bf16),
            pltpu.VMEM((blk, width), bf16),
            pltpu.SemaphoreType.DMA((3, plan.ways)),
        ],
        name="project",
        cost=(6 * seq * width * width, 18 * seq * width, seq),
    )


def group_rows(g, group, stride, first=0):
    return pl.ds(pl.multiple_of(g * stride + first, group), group)


def vector(ref, row):
    return ref[row : row + 1, :]


def strips(rows, height):
    return [slice(r, r + height) for r in range(0, rows, height)]


def middle_kernel(
    table_ref, x_ref, att_ref, c_ref, vec_ref, hid_ref, scale_ref, *refs, chunk, half_q
):
    sources, refs = refs[:8], refs[8:]
    out_ref, z_t_ref, a2_t_ref, m_t_ref, df_ref, dy_ref, da_ref, dx_ref, sums_ref, hid_sums_ref = refs[:10]
    wo_ref, w1_ref, w2_ref, gate, slope, dm_keep, acc, sem = refs[10:]
    width, hidden = w1_ref.shape
    group = sources[0].shape[1]
    n_q = hidden // width

    def rows(g, stride, first=0):
        return pl.ds(pl.multiple_of(g * stride + first, group), group)

    def quarter(q):
        column = hidden * (q < half_q) + q % half_q * width
        return (2 + q, q // half_q, column, width, lambda g: w2_ref.at[rows(g, n_q * group, q * group)])

    out_lines = [(0, 1, half_q * width, width, lambda g: wo_ref.at[rows(g, group)])]
    fc1_lines = [(1, 0, 0, hidden, lambda g: w1_ref.at[rows(g, group)])]
    fc2_lines = [quarter(q) for q in range(n_q)]

    def arrived(lines):
        @pl.when(pl.program_id(0) == 0)
        def _():
            fetch("wait", table_ref, sources, lines, sem)

    chunks = [slice(k, k + chunk) for k in range(0, hidden, chunk)]

    @pl.when(pl.program_id(0) == 0)
    def _():
        for lines in (out_lines, fc1_lines, fc2_lines):
            fetch("start", table_ref, sources, lines, sem)
        sums_ref[...] = jnp.zeros_like(sums_ref)
        hid_sums_ref[...] = jnp.zeros_like(hid_sums_ref)

    def vec(row):
        return vec_ref[row : row + 1, :]

    def add_sum(row, values):
        sums_ref[row : row + 1, :] += column_sum(values)

    z = (att_ref[...] * scale_ref[...]).astype(bf16)
    z_t_ref[...] = transposed(z)
    arrived(out_lines)
    unit_1, rate_1 = normalized(dot_nn(z, wo_ref[...]) + vec(4))
    x2 = x_ref[...].astype(f32) + (unit_1 * vec(5) + vec(6))
    unit_2, rate_2 = normalized(x2)
    a2 = (unit_2 * vec(7) + vec(8)).astype(bf16)
    a2_t_ref[...] = transposed(a2)
    arrived(fc1_lines)

    total = 0.0
    root = (2.0 / jnp.pi) ** 0.5
    for ch in chunks:
        f = dot_nn(a2, w1_ref[:, ch]) + hid_ref[10:11, ch]
        square = f * f
        t = jnp.tanh(f * (root + (root * 0.044715) * square))
        half = 0.5 + 0.5 * t
        g = f * half
        gate[:, ch] = g
        slope[:, ch] = half + g * (1.0 - t) * (root + (3 * root * 0.044715) * square)
        total += jnp.sum(g, axis=-1, keepdims=True)
    mean = total / hidden
    spread = 0.0
    for ch in chunks:
        center = gate[:, ch] - mean
        spread += jnp.sum(center * center, axis=-1, keepdims=True)
    rate = lax.rsqrt(spread / hidden + epsilon)

    arrived(fc2_lines)
    grad_sum = 0.0
    grad_inner = 0.0
    for ch in chunks:
        unit = (gate[:, ch] - mean) * rate
        gate[:, ch] = unit
        gain = hid_ref[11:12, ch]
        m = (unit * gain + hid_ref[12:13, ch]).astype(bf16)
        m_t_ref[ch, :] = transposed(m)
        y = dot_nn(m, w2_ref[ch, :])
        if ch.start == 0:
            acc[...] = y
        else:
            acc[...] += y
        dm = dot_nt(c_ref[...], w2_ref[ch, :]).astype(bf16)
        dm_keep[:, ch] = dm
        dm = dm.astype(f32)
        hid_sums_ref[1:2, ch] += column_sum(dm * unit)
        hid_sums_ref[2:3, ch] += column_sum(dm)
        grad = dm * gain
        grad_sum += jnp.sum(grad, axis=-1, keepdims=True)
        grad_inner += jnp.sum(grad * unit, axis=-1, keepdims=True)
    out_ref[...] = (x2 + (acc[...] + vec(9))).astype(bf16)

    grad_sum = grad_sum / hidden
    grad_inner = grad_inner / hidden
    for ch in chunks:
        grad = dm_keep[:, ch].astype(f32) * hid_ref[11:12, ch]
        grad = rate * (grad - grad_sum - gate[:, ch] * grad_inner)
        df = (slope[:, ch] * grad).astype(bf16)
        df_ref[:, ch] = df
        hid_sums_ref[0:1, ch] += column_sum(df.astype(f32))
        back = dot_nt(df, w1_ref[:, ch])
        if ch.start == 0:
            acc[...] = back
        else:
            acc[...] += back

    upstream = c_ref[...].astype(f32)
    da2 = acc[...]
    add_sum(9, upstream)
    add_sum(7, da2 * unit_2)
    add_sum(8, da2)
    dx2 = upstream + norm_back(da2 * vec(7), unit_2, rate_2)
    dx_ref[...] = dx2
    add_sum(5, dx2 * unit_1)
    add_sum(6, dx2)
    dy = norm_back(dx2 * vec(5), unit_1, rate_1).astype(bf16)
    dy_ref[...] = dy
    add_sum(4, dy.astype(f32))
    dz = dot_nt(dy, wo_ref[...]).astype(bf16).astype(f32)
    add_sum(10, dz * att_ref[...])
    da_ref[...] = (dz * scale_ref[...]).astype(bf16)


def middle(plan, tokens, attended, cotangent, gathered, vec, hid, scale, half_q, after=(), blk=256, chunk=256):
    seq, width = tokens.shape
    hidden = hid.shape[1]
    blk = min(blk, seq)
    (table, *blocks), (table_spec, *specs) = block_operands(plan, gathered)
    row, col, wide = by_rows(blk, width), by_columns(width, blk), by_rows(blk, hidden)
    shape = jax.ShapeDtypeStruct
    return launch(
        functools.partial(middle_kernel, chunk=chunk, half_q=half_q),
        [table, tokens, attended, cotangent, vec, hid, scale, *blocks],
        after=after,
        grid=(seq // blk,),
        in_specs=[table_spec, row, row, row, *(resident(a.shape) for a in (vec, hid, scale)), *specs],
        out_specs=[
            row, col, col, by_columns(hidden, blk), wide, row, row, row,
            pl.BlockSpec((16, width), lambda i: (0, 0)),
            pl.BlockSpec((8, hidden), lambda i: (0, 0)),
        ],
        out_shape=[
            shape((seq, width), bf16),
            shape((width, seq), bf16),
            shape((width, seq), bf16),
            shape((hidden, seq), bf16),
            shape((seq, hidden), bf16),
            shape((seq, width), bf16),
            shape((seq, width), bf16),
            shape((seq, width), f32),
            shape((16, width), f32),
            shape((8, hidden), f32),
        ],
        scratch_shapes=[
            pltpu.VMEM((width, width), bf16),
            pltpu.VMEM((width, hidden), bf16),
            pltpu.VMEM((hidden, width), bf16),
            pltpu.VMEM((blk, hidden), f32),
            pltpu.VMEM((blk, hidden), f32),
            pltpu.VMEM((blk, hidden), bf16),
            pltpu.VMEM((blk, width), f32),
            pltpu.SemaphoreType.DMA((2 + hidden // width, plan.ways)),
        ],
        limit=ROWS_LIMIT,
        name="middle",
        cost=(
            4 * seq * width * (width + 2 * hidden),
            2 * width * (width + 2 * hidden) + 40 * seq * width,
            seq * hidden,
        ),
    )


def finish_kernel(
    table_ref, order_ref, x_ref, dx_ref, vec_ref, sums_ref, hid_sums_ref, heads_ref, *refs,
    cut, n_parts, n_vec, n_hid,
):
    grads_in, sources = refs[: 3 * n_parts], refs[3 * n_parts : 3 * n_parts + 8]
    out_ref, keep_ref, send_ref, w, acc, rows, packed, sem = refs[3 * n_parts + 8 :]
    width = x_ref.shape[1]

    @pl.when(pl.program_id(0) == 0)
    def _():
        lines = weight_lines(w, cut, sources[0].shape[1])
        fetch("start", table_ref, sources, lines, sem)
        rows[...] = jnp.zeros_like(rows)
        acc[...] = jnp.zeros_like(acc)
        fetch("wait", table_ref, sources, lines, sem)

    ordered = [grads_in[3 * part + k][...] for k in range(3) for part in range(n_parts)]
    grad = jnp.concatenate(ordered, 1)
    da1 = dot_nt(grad, w[...])
    for row, columns in ((2, slice(0, width)), (3, slice(2 * width, 3 * width))):
        rows[row : row + 1, :] += column_sum(grad[:, columns].astype(f32))
    for r in strips(x_ref.shape[0], 16):
        grad = da1[r]
        unit, rate = normalized(x_ref[r, :].astype(f32))
        acc[:8] += by_sublanes(grad * unit)
        acc[8:] += by_sublanes(grad)
        out_ref[r, :] = dx_ref[r, :] + norm_back(grad * vec_ref[0:1, :], unit, rate)

    @pl.when(pl.program_id(0) == pl.num_programs(0) - 1)
    def _():
        rows[0:1, :] = column_sum(acc[:8])
        rows[1:2, :] = column_sum(acc[8:])
        rows[4:n_vec, :] = sums_ref[4:n_vec, :]
        ways, _, lanes = packed.shape
        group = width // ways
        packed[...] = jnp.zeros_like(packed)
        for g in range(ways):
            packed[g, :n_vec, :group] = rows[:n_vec, g * group : (g + 1) * group]
            packed[g, n_vec : n_vec + n_hid, :] = hid_sums_ref[:n_hid, g * lanes : (g + 1) * lanes]
            packed[g, n_vec + n_hid : n_vec + n_hid + 1, :] = heads_ref[0:1, :]
        for k in range(ways // 2):
            keep_ref[k] = packed[order_ref[k]]
            send_ref[k] = packed[order_ref[ways // 2 + k]]


def finish(plan, order, tokens, dx2, vec, sums, parts, gathered, cut, n_vec, n_hid, after=(), blk=256):
    seq, width = tokens.shape
    blk = min(blk, seq)
    row = by_rows(blk, width)
    (table, *blocks), (table_spec, *specs) = block_operands(plan, gathered)
    grads_in = [g for part in parts for g in part]
    lanes = sums[1].shape[1] // plan.ways
    packed = jax.ShapeDtypeStruct((plan.half, 16, lanes), f32)
    packed_spec = pl.BlockSpec(packed.shape, lambda i: (0, 0, 0))
    return launch(
        functools.partial(finish_kernel, cut=cut, n_parts=len(parts), n_vec=n_vec, n_hid=n_hid),
        [table, order, tokens, dx2, vec, *sums, *grads_in, *blocks],
        after=after,
        grid=(seq // blk,),
        in_specs=[table_spec, table_spec, row, row, *(resident(a.shape) for a in (vec, *sums))]
        + [by_rows(blk, g.shape[1]) for g in grads_in]
        + specs,
        out_specs=[row, packed_spec, packed_spec],
        out_shape=[jax.ShapeDtypeStruct((seq, width), f32), packed, packed],
        scratch_shapes=[
            pltpu.VMEM((width, 3 * width), bf16),
            pltpu.VMEM((16, width), f32),
            pltpu.VMEM((16, width), f32),
            pltpu.VMEM((plan.ways, 16, lanes), f32),
            pltpu.SemaphoreType.DMA((2, plan.ways)),
        ],
        name="finish",
    )


def local(
    plan,
    tokens,
    doc_split,
    head_scale,
    query_key_value_weight,
    output_weight,
    first_weight,
    second_weight,
    model_vectors,
    hidden_vectors,
    cotangent,
):
    seq, width = tokens.shape
    hidden = first_weight.shape[1]
    heads = head_scale.shape[0]
    blk = min(256, seq)
    ways, half = plan.ways, plan.half
    n_vec, n_hid = model_vectors.shape[0], hidden_vectors.shape[0]

    cut = 2 * width
    group, lanes = width // ways, hidden // ways
    qkv_rows = join_low(plan, query_key_value_weight)
    vec_rows = jnp.concatenate(
        [
            jnp.pad(join_low(plan, model_vectors, 1), ((0, 0), (0, lanes - group))),
            join_low(plan, hidden_vectors, 1),
            jnp.zeros((group - n_vec - n_hid, lanes), bf16),
        ],
        0,
    )
    fc1_rows = join_low(plan, first_weight)
    fc2_rows = join_low(plan, second_weight)
    out_rows = join_low(plan, output_weight)
    n_q = hidden // width
    half_q = n_q // 2
    quarters = [fc2_rows[q * group : (q + 1) * group] for q in range(n_q)]
    first = Gather(plan, [jnp.concatenate([qkv_rows[:, :cut], vec_rows], 1), qkv_rows[:, cut:]])
    second = Gather(
        plan,
        [
            jnp.concatenate([fc1_rows, *quarters[:half_q]], 1),
            jnp.concatenate([*quarters[half_q:], out_rows], 1),
        ],
    )
    first.step()
    join_after([first])
    first.step()
    second.held = relay(second.held, first.held[:1])
    second.step()
    while first.at < plan.steps:
        join_after([first])
        first.step()
    first.cross_held()
    while second.at < plan.steps - 2:
        second.step()
    second.fresh = relay(second.fresh, first.fresh)
    second.step()
    first.cross_fresh()

    qkv, first_t, vec, hid = project(plan, tokens, first, cut, hidden)
    join_after([second], [vec])
    second.step()
    second.cross_held()
    pairs = heads // 2
    attended, lse = attention(doc_split, qkv, heads, blk, 0, pairs, after=second.held)
    second.fresh = relay(second.fresh, [lse])
    second.cross_fresh()

    scale_row = jnp.repeat(head_scale, width // heads)[None]
    output, scaled_t, second_t, hidden_t, grad_pre, grad_branch, grad_attended, grad_middle, sums, hid_sums = (
        middle(plan, tokens, attended, cotangent, second, vec, hid, scale_row, half_q)
    )
    table = plan.table(0, False)

    def by_group(left_t):
        return left_t.reshape(ways, -1, group, seq)

    def send_grads(jobs, tile, after=(), cover=False):
        sent = grads([table[half:]], [jobs], tile, None, after, cover)
        return list(sent), to_other_core(plan, sent[0])

    def keep_grads(jobs, tile, got, after=(), cover=False):
        outs = grads([table[:half]], [jobs], tile, [got], after, cover)
        return list(outs[:1]), Scatter.begun(plan, 0, *outs)

    hidden_t = by_group(hidden_t)
    fc2_jobs = [(hidden_t, q, [cotangent], [0]) for q in range(n_q)]
    fc1_jobs = [
        (by_group(second_t), 0, [grad_pre], range(n_q)),
        (by_group(scaled_t), 0, [grad_branch], [0]),
    ]
    done, got_2 = send_grads(fc2_jobs, width)
    done, got_1 = send_grads(fc1_jobs, width, done, True)
    done, fc2_sum = keep_grads(fc2_jobs, width, got_2, done, True)
    done, fc1_sum = keep_grads(fc1_jobs, width, got_1, done)

    first_t = by_group(first_t)

    def back(start, count, after):
        out = attention_back(doc_split, qkv, grad_attended, attended, lse, heads, blk, start, count, after)
        return list(out[:1]), list(out)

    some = pairs * 3 // 8
    done, part_a = back(0, some, done)
    done = step_all([fc2_sum], done)
    done, part_b = back(some, some, done)
    size = part_a[0].shape[1]
    jobs = [(first_t, 0, part, [0]) for part in (part_a, part_b)]
    done, got = send_grads(jobs, 3 * size, done)
    done = step_all([fc2_sum, fc1_sum], done, True)
    done, sum_a = keep_grads(jobs, 3 * size, got, done)
    done, part_c = back(2 * some, pairs - 2 * some, done)
    rest = part_c[0].shape[1]
    jobs = [(first_t, 0, part_c, [0])]
    done, got = send_grads(jobs, 3 * rest, done)
    done = step_all([fc2_sum, fc1_sum, sum_a], done, True)
    done, sum_b = keep_grads(jobs, 3 * rest, got, done)
    head_sums = jnp.sum(sums[n_vec].reshape(heads, -1), axis=1)
    head_row = jnp.broadcast_to(jnp.pad(head_sums, (0, lanes - heads)), (8, lanes))
    grad_tokens, vec_keep, vec_send = finish(
        plan,
        table,
        tokens,
        grad_middle,
        vec,
        (sums, hid_sums, head_row),
        (part_a, part_b, part_c),
        first,
        cut,
        n_vec,
        n_hid,
        done,
    )
    vec_sum = Scatter(plan, 0, vec_keep, to_other_core(plan, vec_send))
    done = step_all([fc1_sum, sum_a, sum_b], [vec_keep], True)
    done = step_all([vec_sum], done)
    while vec_sum.at < plan.steps:
        done = step_all([one for one in (sum_a, sum_b, vec_sum) if one.at < plan.steps], done)
    sent_vec = vec_sum.total()
    sent_a, sent_b = sum_a.total(), sum_b.total()
    sum_fc2, sum_fc1 = fc2_sum.total(), fc1_sum.total()
    columns = []
    for k in range(3):
        columns += [sent_a[:, k * size : (k + 1) * size], sent_a[:, (3 + k) * size : (4 + k) * size]]
        columns.append(sent_b[:, k * rest : (k + 1) * rest])
    sent_qkv = split_low(plan, jnp.concatenate(columns, 1))
    sent_fc1 = split_low(plan, sum_fc1[:, :hidden])
    sent_out = split_low(plan, sum_fc1[:, hidden:])
    row_blocks = [sum_fc2[:, k : k + width] for k in range(0, hidden, width)]
    sent_fc2 = split_low(plan, jnp.concatenate(row_blocks, 0))
    sent_vecd = split_low(plan, sent_vec[:n_vec, :group], 1)
    sent_vecff = split_low(plan, sent_vec[n_vec : n_vec + n_hid], 1)
    grad_heads = sent_vec[n_vec + n_hid, :heads]
    if plan.low > 1:
        grad_heads = lax.psum(grad_heads, AXES, axis_index_groups=plan.low_groups())
    return (
        output,
        grad_tokens,
        grad_heads,
        sent_qkv,
        sent_out,
        sent_fc1,
        sent_fc2,
        sent_vecd,
        sent_vecff,
    )


def solution(mesh):
    rows = P(AXES, None)
    columns = P(None, AXES)
    return jax.shard_map(
        functools.partial(local, Plan(mesh)),
        mesh=mesh,
        in_specs=(rows, P(AXES), P(), rows, rows, rows, rows, columns, columns, rows),
        out_specs=(rows, rows, P(), rows, rows, rows, rows, columns, columns),
        check_vma=False,
    )
```

```python
import functools

import jax
import jax.numpy as jnp
from jax import lax
from jax.experimental import pallas as pl
from jax.experimental.pallas import tpu as pltpu
from jax.sharding import PartitionSpec as P

epsilon = 1e-05
AXES = ("dp", "fsdp")
f32 = jnp.float32
bf16 = jnp.bfloat16
NEG = -1e30
VMEM_LIMIT = 56 << 20
ROWS_LIMIT = 62 << 20


def launch(
    kernel, args, *, in_specs, out_specs, out_shape, name, after=(), grid=(), scratch_shapes=(),
    prefetch=0, limit=VMEM_LIMIT, aliases=None, cover=False, cost=(1, 1, 0),
):
    after, count = list(after), len(args)

    def body(*refs):
        kernel(*refs[:count], *refs[count + len(after) :])

    return pl.pallas_call(
        body,
        grid_spec=pltpu.PrefetchScalarGridSpec(
            num_scalar_prefetch=prefetch,
            grid=grid,
            in_specs=[*in_specs] + [pl.BlockSpec(memory_space=pltpu.HBM)] * len(after),
            out_specs=out_specs,
            scratch_shapes=scratch_shapes,
        ),
        out_shape=out_shape,
        input_output_aliases=aliases or {},
        compiler_params=pltpu.CompilerParams(vmem_limit_bytes=limit),
        cost_estimate=pl.CostEstimate(
            flops=10**12 if cover else cost[0], bytes_accessed=cost[1], transcendentals=cost[2]
        ),
        name=name,
    )(*args, *after)


def relay(values, after):
    anywhere = pl.BlockSpec(memory_space=pl.ANY)
    return list(
        launch(
            lambda *refs: None,
            values,
            after=after,
            in_specs=[anywhere] * len(values),
            out_specs=[anywhere] * len(values),
            out_shape=[jax.ShapeDtypeStruct(v.shape, v.dtype) for v in values],
            aliases={k: k for k in range(len(values))},
            name="relay",
        )
    )


def in_vmem(value):
    return pltpu.with_memory_space_constraint(value, pltpu.VMEM)


class Plan:
    def __init__(self, mesh):
        n_dp, n_fs = mesh.shape["dp"], mesh.shape["fsdp"]
        self.count = n_dp * n_fs
        self.ways = min(self.count, 32)
        self.low = self.count // self.ways
        self.core = max(1, n_fs // self.low)
        self.dims = [1 << b for b in range(self.ways.bit_length() - 1) if 1 << b != self.core]
        self.half = self.ways // 2
        self.steps = len(self.dims)

    def order(self, core_bit, part, gathers):
        near, far = self.dims[:-1], self.dims[-1:]
        shift = (core_bit + part if part != 1 else 2) % len(near)
        near = near[shift:] + near[:shift]
        return far + near if gathers else near + far

    def pairs(self, part, step, gathers):
        out = []
        for i in range(self.count):
            group = i // self.low
            mask = self.order(int(bool(group & self.core)), part, gathers)[step]
            out.append((i, i ^ (mask * self.low)))
        return out

    def core_pairs(self):
        return [(i, i ^ (self.core * self.low)) for i in range(self.count)]

    def corner_pairs(self, part):
        out = []
        for i in range(self.count):
            group = i // self.low
            mask = self.core ^ self.order(int(not group & self.core), part, False)[0]
            out.append((i, i ^ (mask * self.low)))
        return out

    def low_groups(self):
        return [[g * self.low + i for i in range(self.low)] for g in range(self.ways)]

    def table(self, part, gathers):
        me = (lax.axis_index("dp") * lax.axis_size("fsdp") + lax.axis_index("fsdp")) // self.low
        rows = []
        for core_bit in (0, 1):
            row = []
            for other in (0, 1):
                masks = self.order(core_bit ^ other, part, gathers)
                for r in range(self.half):
                    x = self.core if other else 0
                    for k in range(self.steps):
                        bit = k if gathers else self.steps - 1 - k
                        if (r >> bit) & 1:
                            x ^= masks[k]
                    row.append(x)
            rows.append(row)
        mine = ((me & self.core) != 0).astype(jnp.int32)
        masks = jnp.where(mine == 1, jnp.array(rows[1], jnp.int32), jnp.array(rows[0], jnp.int32))
        return jnp.bitwise_xor(me.astype(jnp.int32), masks)


class Gather:
    def __init__(self, plan, pieces):
        self.plan = plan
        self.held = [piece[None] for piece in pieces]
        self.fresh = None
        self.at = 0

    def join(self):
        if self.fresh is not None:
            self.held = [jnp.concatenate(pair, 0) for pair in zip(self.held, self.fresh)]
            self.fresh = None

    def step(self):
        self.join()
        self.fresh = [
            lax.ppermute(h, AXES, self.plan.pairs(part, self.at, True)) for part, h in enumerate(self.held)
        ]
        self.at += 1

    def cross_held(self):
        self.far_held = [lax.ppermute(h, AXES, self.plan.core_pairs()) for h in self.held]

    def cross_fresh(self):
        self.far_fresh = [lax.ppermute(h, AXES, self.plan.core_pairs()) for h in self.fresh]

    def blocks(self):
        return [list(b) for b in zip(self.held, self.fresh, self.far_held, self.far_fresh)]


def join_kernel(*refs, count):
    for n in range(count):
        out = refs[2 * count + n]
        half = out.shape[0] // 2
        out[:half] = refs[2 * n][...]
        out[half:] = refs[2 * n + 1][...]


def join_after(gathers, after=()):
    args = [
        a
        for one in gathers
        for held, fresh in zip(one.held, one.fresh)
        for a in (held, in_vmem(fresh))
    ]
    shapes = [(2 * h.shape[0], *h.shape[1:]) for one in gathers for h in one.held]
    vmem = pl.BlockSpec(memory_space=pltpu.VMEM)
    outs = launch(
        functools.partial(join_kernel, count=len(shapes)),
        args,
        after=after,
        in_specs=[vmem] * len(args),
        out_specs=[vmem] * len(shapes),
        out_shape=[jax.ShapeDtypeStruct(shape, bf16) for shape in shapes],
        name="join",
    )
    for n, one in enumerate(gathers):
        one.held = list(outs[2 * n : 2 * n + 2])
        one.fresh = None


def join_low(plan, piece, axis=0):
    if plan.low == 1:
        return piece
    return lax.all_gather(piece, AXES, axis=axis, tiled=True, axis_index_groups=plan.low_groups())


def fetch(action, table_ref, sources, lines, sem):
    for number, part, column, width, place in lines:
        for b in range(4):
            source = sources[4 * part + b]
            count = source.shape[0]

            def one(r, _, source=source, number=number, part=part, b=b, count=count):
                at = b * count + r
                copy = pltpu.make_async_copy(
                    source.at[r, :, pl.ds(column, width)],
                    place(table_ref[part, at]),
                    sem.at[number, at],
                )
                getattr(copy, action)()
                return _

            lax.fori_loop(0, count, one, 0)


def block_operands(plan, gathered):
    blocks = gathered.blocks()
    table = jnp.stack([plan.table(part, True) for part in range(len(blocks))])
    flat = [b for part in blocks for b in part]
    specs = [pl.BlockSpec(memory_space=pltpu.SMEM)] + [pl.BlockSpec(memory_space=pltpu.HBM)] * len(flat)
    return [table, *flat], specs


def plus(a, b):
    return a.astype(f32) + b.astype(f32)


class Scatter:
    def __init__(self, plan, part, keep, got):
        self.plan, self.part, self.at = plan, part, 0
        self.keep, self.got = keep, got

    @classmethod
    def begun(cls, plan, part, going, keep):
        one = cls(plan, part, None, None)
        one.send(going, keep)
        return one

    def send(self, going, keep):
        self.keep = keep
        self.got = lax.ppermute(going, AXES, self.plan.pairs(self.part, self.at, False))
        self.at += 1

    def total(self):
        return plus(self.keep[0], self.got[0])


def halve_kernel(*refs, count):
    for n in range(count):
        keep_ref, got_ref = refs[2 * n], refs[2 * n + 1]
        going_ref, kept_ref = refs[2 * (count + n)], refs[2 * (count + n) + 1]
        half = keep_ref.shape[0] // 2
        for out, part in ((going_ref, slice(half, 2 * half)), (kept_ref, slice(0, half))):
            out[...] = plus(keep_ref[part], got_ref[part]).astype(out.dtype)


def step_all(scatters, after=(), cover=False):
    args = [
        a
        for one in scatters
        for a in (one.keep, in_vmem(one.got))
    ]
    shapes = [
        jax.ShapeDtypeStruct((one.keep.shape[0] // 2, *one.keep.shape[1:]), one.keep.dtype)
        for one in scatters
        for _ in range(2)
    ]
    outs = launch(
        functools.partial(halve_kernel, count=len(scatters)),
        args,
        after=after,
        in_specs=[pl.BlockSpec(memory_space=pltpu.VMEM)] * len(args),
        out_specs=[pl.BlockSpec(memory_space=pltpu.VMEM)] * len(args),
        out_shape=shapes,
        name="halve",
        cover=cover,
    )
    for n, one in enumerate(scatters):
        one.send(*outs[2 * n : 2 * n + 2])
    return [outs[0]]


def to_other_core(plan, values):
    return lax.ppermute(values, AXES, plan.core_pairs())


def split_low(plan, total, axis=0):
    if plan.low == 1:
        return total
    return lax.psum_scatter(
        total, AXES, scatter_dimension=axis, tiled=True, axis_index_groups=plan.low_groups()
    )


def dot_nt(a, b):
    return lax.dot_general(a, b, (((1,), (1,)), ((), ())), preferred_element_type=f32)


def dot_nn(a, b):
    return lax.dot_general(a, b, (((1,), (0,)), ((), ())), preferred_element_type=f32)


def transposed(a):
    return a.astype(f32).T.astype(a.dtype)


def causal(scores):
    keys = lax.broadcasted_iota(jnp.int32, scores.shape, 0)
    return jnp.where(keys <= lax.broadcasted_iota(jnp.int32, scores.shape, 1), scores, NEG)


def head_lanes(shape, h, hd):
    lane = lax.broadcasted_iota(jnp.int32, shape, 1)
    mine = (lane >= hd) if h else (lane < hd)
    return mine, lane == (0 if h else hd)


def masked_keys(k, h, hd, split):
    mine, spare = head_lanes(k.shape, h, hd)
    early = lax.broadcasted_iota(jnp.int32, k.shape, 0) < split
    return jnp.where(mine, k, jnp.where(spare & early, bf16(NEG), bf16(0)))


def masked_queries(q, h, hd, split, start):
    mine, spare = head_lanes(q.shape, h, hd)
    late = lax.broadcasted_iota(jnp.int32, q.shape, 0) + start >= split
    alone = jnp.where(mine, q, bf16(0)) * bf16(hd**-0.5)
    return alone, jnp.where(spare & late, bf16(1), alone)


def attention_kernel(split_ref, q_ref, k_ref, v_ref, *refs, seq, hd, blk):
    o_ref, lse_ref = refs[-2:]
    split = split_ref[0]
    v_t = transposed(v_ref[...])
    keys = [masked_keys(k_ref[...], h, hd, split) for h in (0, 1)]
    for i in range(seq // blk):
        rows = slice(i * blk, (i + 1) * blk)
        outs = []
        for h in (0, 1):
            _, q = masked_queries(q_ref[rows, :], h, hd, split, i * blk)
            scores = [dot_nt(keys[h][j * blk : (j + 1) * blk], q) for j in range(i + 1)]
            scores[i] = causal(scores[i])
            peak = scores[0].max(0, keepdims=True)
            for s in scores[1:]:
                peak = jnp.maximum(peak, s.max(0, keepdims=True))
            total = jnp.zeros((1, blk), f32)
            mixed = jnp.zeros((hd, blk), f32)
            for j, s in enumerate(scores):
                low = []
                for r in strips(blk, 64):
                    e = jnp.exp(s[r] - peak)
                    total += e.sum(0, keepdims=True)
                    low.append(e.astype(bf16))
                mixed += dot_nn(
                    v_t[h * hd : (h + 1) * hd, j * blk : (j + 1) * blk], jnp.concatenate(low, 0)
                )
            outs.append(mixed / total)
            lse_ref[0, h : h + 1, rows] = peak + jnp.log(total)
        o_ref[rows, :] = jnp.concatenate(outs, 0).T


def attention(split, qkv, heads, blk, start, count, into=(), after=()):
    seq, width = qkv.shape[0], qkv.shape[1] // 3
    hd, pairs = width // heads, heads // 2
    w = 2 * hd
    return launch(
        functools.partial(attention_kernel, seq=seq, hd=hd, blk=blk),
        [split, qkv, qkv, qkv, *into],
        after=after,
        grid=(count,),
        in_specs=[
            pl.BlockSpec(memory_space=pltpu.SMEM),
            pl.BlockSpec((seq, w), lambda p: (0, p + start)),
            pl.BlockSpec((seq, w), lambda p: (0, p + start + pairs)),
            pl.BlockSpec((seq, w), lambda p: (0, p + start + 2 * pairs)),
        ]
        + [pl.BlockSpec(memory_space=pl.ANY)] * len(into),
        out_specs=[
            pl.BlockSpec((seq, w), lambda p: (0, p + start)),
            pl.BlockSpec((1, 2, seq), lambda p: (p + start, 0, 0)),
        ],
        out_shape=[
            jax.ShapeDtypeStruct((seq, width), f32),
            jax.ShapeDtypeStruct((pairs, 2, seq), f32),
        ],
        aliases={4 + k: k for k in range(len(into))},
        name="attention",
        cost=(12 * seq * seq * w * count, seq * w * count * 10, 2 * count * seq * seq),
    )


def attention_back_kernel(
    split_ref, q_ref, k_ref, v_ref, da_ref, o_ref, lse_ref, dq_ref, dk_ref, dv_ref, dk_acc, dv_acc,
    *, seq, hd, blk,
):
    split = split_ref[0]
    k_t = transposed(k_ref[...])
    keys_of = [masked_keys(k_ref[...], h, hd, split) for h in (0, 1)]
    for i in range(seq // blk):
        rows = slice(i * blk, (i + 1) * blk)
        q_full, da_full = q_ref[rows, :], da_ref[rows, :]
        inner = (da_full.astype(f32) * o_ref[rows, :]).T
        dqs = []
        for h in (0, 1):
            q, q_marked = masked_queries(q_full, h, hd, split, i * blk)
            da = jnp.where(head_lanes(da_full.shape, h, hd)[0], da_full, bf16(0))
            row_inner = inner[h * hd : (h + 1) * hd].sum(0, keepdims=True)
            lse = lse_ref[0, h : h + 1, rows]
            dq = jnp.zeros((hd, blk), f32)
            for j in range(i + 1):
                keys = slice(j * blk, (j + 1) * blk)
                s = dot_nt(keys_of[h][keys], q_marked)
                if i == j:
                    s = causal(s)
                dp = dot_nt(v_ref[keys, :], da)
                p_low, ds = [], []
                for r in strips(blk, 64):
                    p = jnp.exp(s[r] - lse)
                    p_low.append(p.astype(bf16))
                    ds.append((p * (dp[r] - row_inner)).astype(bf16))
                ds = jnp.concatenate(ds, 0)
                dv = dot_nn(jnp.concatenate(p_low, 0), da)
                dk = dot_nn(ds, q)
                if i == j and h == 0:
                    dv_acc[keys, :] = dv
                    dk_acc[keys, :] = dk
                else:
                    dv_acc[keys, :] += dv
                    dk_acc[keys, :] += dk
                dq += dot_nn(k_t[h * hd : (h + 1) * hd, keys], ds)
            dqs.append(dq)
        dq_ref[rows, :] = (jnp.concatenate(dqs, 0).T * (hd**-0.5)).astype(bf16)
    dk_ref[...] = dk_acc[...].astype(bf16)
    dv_ref[...] = dv_acc[...].astype(bf16)


def attention_back(split, qkv, da, attended, lse, heads, blk, start, count, after=()):
    seq, width = qkv.shape[0], qkv.shape[1] // 3
    hd, pairs = width // heads, heads // 2
    w = 2 * hd
    column = pl.BlockSpec((seq, w), lambda p: (0, p + start))
    out = pl.BlockSpec((seq, w), lambda p: (0, p))
    return launch(
        functools.partial(attention_back_kernel, seq=seq, hd=hd, blk=blk),
        [split, qkv, qkv, qkv, da, attended, lse],
        after=after,
        grid=(count,),
        in_specs=[
            pl.BlockSpec(memory_space=pltpu.SMEM),
            column,
            pl.BlockSpec((seq, w), lambda p: (0, p + start + pairs)),
            pl.BlockSpec((seq, w), lambda p: (0, p + start + 2 * pairs)),
            column,
            column,
            pl.BlockSpec((1, 2, seq), lambda p: (p + start, 0, 0)),
        ],
        out_specs=[out, out, out],
        out_shape=[jax.ShapeDtypeStruct((seq, count * w), bf16)] * 3,
        scratch_shapes=[pltpu.VMEM((seq, w), f32)] * 2,
        name="attention_back",
    )


def grads_kernel(table_ref, place_ref, *refs, runs, n_left, n_right, begins, adds):
    lefts, rights, rest = refs[:n_left], refs[n_left : n_left + n_right], refs[n_left + n_right :]
    left = rest[-1]
    ways, rows, tokens = left.shape
    step = pl.program_id(0)
    for first, last, l, r, part in runs:

        @pl.when(step == first)
        def _():
            for w in range(ways):
                left[w] = lefts[l][table_ref[part, w], 0]

        @pl.when((step >= first) & (step < last))
        def _():
            product = [dot_nn(left[...].reshape(ways * rows, tokens), rights[k][...]) for k in r]
            product = jnp.concatenate(product, 1) if len(r) > 1 else product[0]
            product = product.reshape(ways, rows, product.shape[1])
            if adds:
                n_parts = len(begins)
                got_ref = rest[part]
                at = pl.multiple_of((step - begins[part]) * product.shape[2], 128)
                theirs = got_ref[:, :, pl.ds(at, product.shape[2])]
                going_ref, keep_ref = rest[n_parts + 2 * part : n_parts + 2 * part + 2]
                product = (product + theirs.astype(f32)).astype(bf16)
                keep_ref[...] = product[: ways // 2]
                going_ref[...] = product[ways // 2 :]
            else:
                rest[part][...] = product.astype(bf16)


def grads(tables, parts, tile, got=None, after=(), cover=False):
    groups, _, rows, tokens = parts[0][0][0].shape
    ways = tables[0].shape[0]
    lefts, rights, runs, places, spans = [], [], [], [], []
    at = 0
    for part, jobs in enumerate(parts):
        begin = at
        for left, q, group, numbers in jobs:
            for known, one in ((lefts, left), *((rights, right) for right in group)):
                if not any(one is k for k in known):
                    known.append(one)
            l = next(i for i, k in enumerate(lefts) if k is left)
            r = [next(i for i, k in enumerate(rights) if k is right) for right in group]
            runs.append((at, at + len(numbers), l, r, part))
            for n in numbers:
                places.append(([l], q, r, n))
            at += len(numbers)
        spans.append((begin, at - begin))

    def held(which, entry, count):
        lines = []
        for k in range(count):
            used = [(s, p[entry]) for s, p in enumerate(places) if k in p[which]]
            lines.append([next((v for s, v in used if s >= i), used[-1][1]) for i in range(at)])
        return lines

    place = jnp.array(held(0, 1, len(lefts)) + held(2, 3, len(rights)), jnp.int32)

    def left_spec(k):
        return pl.BlockSpec((groups, 1, rows, tokens), lambda i, t, p: (0, p[k, i], 0, 0))

    def right_spec(k):
        return pl.BlockSpec((tokens, share), lambda i, t, p: (0, p[len(lefts) + k, i]))

    def block(count, span):
        begin, steps = span
        return pl.BlockSpec(
            (count, rows, tile), lambda i, t, p: (0, 0, jnp.clip(i - begin, 0, steps - 1))
        )

    def shape(count, span):
        return jax.ShapeDtypeStruct((count, rows, span[1] * tile), bf16)

    share = tile // len(parts[0][0][2])
    adds = got is not None
    each = [ways // 2] * 2 if adds else [ways]
    return launch(
        functools.partial(
            grads_kernel,
            runs=runs,
            n_left=len(lefts),
            n_right=len(rights),
            begins=[span[0] for span in spans],
            adds=adds,
        ),
        [jnp.stack(tables), place, *lefts, *rights, *(map(in_vmem, got) if adds else [])],
        after=after,
        prefetch=2,
        grid=(at,),
        in_specs=[left_spec(k) for k in range(len(lefts))]
        + [right_spec(k) for k in range(len(rights))]
        + [pl.BlockSpec(memory_space=pltpu.VMEM)] * (len(parts) * adds),
        out_specs=[block(count, span) for span in spans for count in each],
        out_shape=[shape(count, span) for span in spans for count in each],
        scratch_shapes=[pltpu.VMEM((ways, rows, tokens), bf16)],
        name="grads_keep" if adds else "grads_send",
        cover=cover,
    )


def normalized(values):
    center = values - jnp.mean(values, axis=-1, keepdims=True)
    rate = lax.rsqrt(jnp.mean(center * center, axis=-1, keepdims=True) + epsilon)
    return center * rate, rate


def norm_back(grad, unit, rate):
    inner = jnp.mean(grad * unit, axis=-1, keepdims=True)
    return rate * (grad - jnp.mean(grad, axis=-1, keepdims=True) - unit * inner)


def by_lanes(values):
    total = values[:, :128]
    for k in range(128, values.shape[1], 128):
        total += values[:, k : k + 128]
    return total


def by_sublanes(values):
    total = values[:8]
    for k in range(8, values.shape[0], 8):
        total += values[k : k + 8]
    return total


def column_sum(values):
    return jnp.sum(values, axis=0, keepdims=True)


def resident(shape):
    return pl.BlockSpec(shape, lambda i: (0,) * len(shape), pipeline_mode=pl.Buffered(1))


def by_rows(blk, width):
    return pl.BlockSpec((blk, width), lambda i: (i, 0))


def by_columns(height, blk):
    return pl.BlockSpec((height, blk), lambda i: (0, i))


def weight_lines(w, cut, group, first=0):
    def rows(g):
        return pl.ds(pl.multiple_of(g * group, group), group)

    rest = w.shape[1] - cut
    return [
        (first, 0, 0, cut, lambda g: w.at[rows(g), pl.ds(0, cut)]),
        (first + 1, 1, 0, rest, lambda g: w.at[rows(g), pl.ds(cut, rest)]),
    ]


def project_kernel(table_ref, x_ref, *refs, cut):
    sources = refs[:8]
    qkv_ref, left_t_ref, vec_ref, hid_ref, w, raw, left_ref, sem = refs[8:]
    ways, group, lanes = raw.shape
    width = x_ref.shape[1]

    @pl.when(pl.program_id(0) == 0)
    def _():
        vec_lines = [(2, 0, cut, lanes, lambda g: raw.at[g])]
        lines = weight_lines(w, cut, group)
        fetch("start", table_ref, sources, vec_lines, sem)
        fetch("start", table_ref, sources, lines, sem)
        fetch("wait", table_ref, sources, vec_lines, sem)
        per = lanes // group
        for k in range(0, ways, per):
            row = [raw[k + j][:16, :group].astype(f32) for j in range(per)]
            vec_ref[:, k * group : (k + per) * group] = jnp.concatenate(row, 1)
        for k in range(ways):
            hid_ref[:, k * lanes : (k + 1) * lanes] = raw[k][:16].astype(f32)
        fetch("wait", table_ref, sources, lines, sem)

    for r in strips(x_ref.shape[0], 16):
        unit, _ = normalized(x_ref[r, :].astype(f32))
        left_ref[r, :] = (unit * vec_ref[0:1, :] + vec_ref[1:2, :]).astype(bf16)
    left = left_ref[...]
    left_t_ref[...] = transposed(left)
    for part, bias in ((0, 2), (1, None), (2, 3)):
        cols = slice(part * width, (part + 1) * width)
        rows = dot_nn(left, w[:, cols])
        if bias is not None:
            rows += vec_ref[bias : bias + 1, :]
        qkv_ref[:, cols] = rows.astype(bf16)


def project(plan, tokens, gathered, cut, hidden, after=(), blk=256):
    seq, width = tokens.shape
    blk = min(blk, seq)
    (table, *blocks), (table_spec, *specs) = block_operands(plan, gathered)
    return launch(
        functools.partial(project_kernel, cut=cut),
        [table, tokens, *blocks],
        after=after,
        grid=(seq // blk,),
        in_specs=[table_spec, by_rows(blk, width), *specs],
        out_specs=[
            by_rows(blk, 3 * width),
            by_columns(width, blk),
            pl.BlockSpec((16, width), lambda i: (0, 0)),
            pl.BlockSpec((16, hidden), lambda i: (0, 0)),
        ],
        out_shape=[
            jax.ShapeDtypeStruct((seq, 3 * width), bf16),
            jax.ShapeDtypeStruct((width, seq), bf16),
            jax.ShapeDtypeStruct((16, width), f32),
            jax.ShapeDtypeStruct((16, hidden), f32),
        ],
        scratch_shapes=[
            pltpu.VMEM((width, 3 * width), bf16),
            pltpu.VMEM((plan.ways, width // plan.ways, hidden // plan.ways), bf16),
            pltpu.VMEM((blk, width), bf16),
            pltpu.SemaphoreType.DMA((3, plan.ways)),
        ],
        name="project",
        cost=(6 * seq * width * width, 18 * seq * width, seq),
    )


def group_rows(g, group, stride, first=0):
    return pl.ds(pl.multiple_of(g * stride + first, group), group)


def vector(ref, row):
    return ref[row : row + 1, :]


def strips(rows, height):
    return [slice(r, r + height) for r in range(0, rows, height)]


def middle_kernel(
    table_ref, x_ref, att_ref, c_ref, vec_ref, hid_ref, scale_ref, *refs, chunk, half_q
):
    sources, refs = refs[:8], refs[8:]
    out_ref, z_t_ref, a2_t_ref, m_t_ref, df_ref, dy_ref, da_ref, dx_ref, sums_ref, hid_sums_ref = refs[:10]
    wo_ref, w1_ref, w2_ref, gate, slope, dm_keep, acc, sem = refs[10:]
    width, hidden = w1_ref.shape
    group = sources[0].shape[1]
    n_q = hidden // width

    def rows(g, stride, first=0):
        return pl.ds(pl.multiple_of(g * stride + first, group), group)

    def quarter(q):
        column = hidden * (q < half_q) + q % half_q * width
        return (2 + q, q // half_q, column, width, lambda g: w2_ref.at[rows(g, n_q * group, q * group)])

    out_lines = [(0, 1, half_q * width, width, lambda g: wo_ref.at[rows(g, group)])]
    fc1_lines = [(1, 0, 0, hidden, lambda g: w1_ref.at[rows(g, group)])]
    fc2_lines = [quarter(q) for q in range(n_q)]

    def arrived(lines):
        @pl.when(pl.program_id(0) == 0)
        def _():
            fetch("wait", table_ref, sources, lines, sem)

    chunks = [slice(k, k + chunk) for k in range(0, hidden, chunk)]

    @pl.when(pl.program_id(0) == 0)
    def _():
        for lines in (out_lines, fc1_lines, fc2_lines):
            fetch("start", table_ref, sources, lines, sem)
        sums_ref[...] = jnp.zeros_like(sums_ref)
        hid_sums_ref[...] = jnp.zeros_like(hid_sums_ref)

    def vec(row):
        return vec_ref[row : row + 1, :]

    def add_sum(row, values):
        sums_ref[row : row + 1, :] += column_sum(values)

    z = (att_ref[...] * scale_ref[...]).astype(bf16)
    z_t_ref[...] = transposed(z)
    arrived(out_lines)
    unit_1, rate_1 = normalized(dot_nn(z, wo_ref[...]) + vec(4))
    x2 = x_ref[...].astype(f32) + (unit_1 * vec(5) + vec(6))
    unit_2, rate_2 = normalized(x2)
    a2 = (unit_2 * vec(7) + vec(8)).astype(bf16)
    a2_t_ref[...] = transposed(a2)
    arrived(fc1_lines)

    total = 0.0
    root = (2.0 / jnp.pi) ** 0.5
    for ch in chunks:
        f = dot_nn(a2, w1_ref[:, ch]) + hid_ref[10:11, ch]
        square = f * f
        t = jnp.tanh(f * (root + (root * 0.044715) * square))
        half = 0.5 + 0.5 * t
        g = f * half
        gate[:, ch] = g
        slope[:, ch] = half + g * (1.0 - t) * (root + (3 * root * 0.044715) * square)
        total += jnp.sum(g, axis=-1, keepdims=True)
    mean = total / hidden
    spread = 0.0
    for ch in chunks:
        center = gate[:, ch] - mean
        spread += jnp.sum(center * center, axis=-1, keepdims=True)
    rate = lax.rsqrt(spread / hidden + epsilon)

    arrived(fc2_lines)
    grad_sum = 0.0
    grad_inner = 0.0
    for ch in chunks:
        unit = (gate[:, ch] - mean) * rate
        gate[:, ch] = unit
        gain = hid_ref[11:12, ch]
        m = (unit * gain + hid_ref[12:13, ch]).astype(bf16)
        m_t_ref[ch, :] = transposed(m)
        y = dot_nn(m, w2_ref[ch, :])
        if ch.start == 0:
            acc[...] = y
        else:
            acc[...] += y
        dm = dot_nt(c_ref[...], w2_ref[ch, :]).astype(bf16)
        dm_keep[:, ch] = dm
        dm = dm.astype(f32)
        hid_sums_ref[1:2, ch] += column_sum(dm * unit)
        hid_sums_ref[2:3, ch] += column_sum(dm)
        grad = dm * gain
        grad_sum += jnp.sum(grad, axis=-1, keepdims=True)
        grad_inner += jnp.sum(grad * unit, axis=-1, keepdims=True)
    out_ref[...] = (x2 + (acc[...] + vec(9))).astype(bf16)

    grad_sum = grad_sum / hidden
    grad_inner = grad_inner / hidden
    for ch in chunks:
        grad = dm_keep[:, ch].astype(f32) * hid_ref[11:12, ch]
        grad = rate * (grad - grad_sum - gate[:, ch] * grad_inner)
        df = (slope[:, ch] * grad).astype(bf16)
        df_ref[:, ch] = df
        hid_sums_ref[0:1, ch] += column_sum(df.astype(f32))
        back = dot_nt(df, w1_ref[:, ch])
        if ch.start == 0:
            acc[...] = back
        else:
            acc[...] += back

    upstream = c_ref[...].astype(f32)
    da2 = acc[...]
    add_sum(9, upstream)
    add_sum(7, da2 * unit_2)
    add_sum(8, da2)
    dx2 = upstream + norm_back(da2 * vec(7), unit_2, rate_2)
    dx_ref[...] = dx2
    add_sum(5, dx2 * unit_1)
    add_sum(6, dx2)
    dy = norm_back(dx2 * vec(5), unit_1, rate_1).astype(bf16)
    dy_ref[...] = dy
    add_sum(4, dy.astype(f32))
    dz = dot_nt(dy, wo_ref[...]).astype(bf16).astype(f32)
    add_sum(10, dz * att_ref[...])
    da_ref[...] = (dz * scale_ref[...]).astype(bf16)


def middle(plan, tokens, attended, cotangent, gathered, vec, hid, scale, half_q, after=(), blk=256, chunk=256):
    seq, width = tokens.shape
    hidden = hid.shape[1]
    blk = min(blk, seq)
    (table, *blocks), (table_spec, *specs) = block_operands(plan, gathered)
    row, col, wide = by_rows(blk, width), by_columns(width, blk), by_rows(blk, hidden)
    shape = jax.ShapeDtypeStruct
    return launch(
        functools.partial(middle_kernel, chunk=chunk, half_q=half_q),
        [table, tokens, attended, cotangent, vec, hid, scale, *blocks],
        after=after,
        grid=(seq // blk,),
        in_specs=[table_spec, row, row, row, *(resident(a.shape) for a in (vec, hid, scale)), *specs],
        out_specs=[
            row, col, col, by_columns(hidden, blk), wide, row, row, row,
            pl.BlockSpec((16, width), lambda i: (0, 0)),
            pl.BlockSpec((8, hidden), lambda i: (0, 0)),
        ],
        out_shape=[
            shape((seq, width), bf16),
            shape((width, seq), bf16),
            shape((width, seq), bf16),
            shape((hidden, seq), bf16),
            shape((seq, hidden), bf16),
            shape((seq, width), bf16),
            shape((seq, width), bf16),
            shape((seq, width), f32),
            shape((16, width), f32),
            shape((8, hidden), f32),
        ],
        scratch_shapes=[
            pltpu.VMEM((width, width), bf16),
            pltpu.VMEM((width, hidden), bf16),
            pltpu.VMEM((hidden, width), bf16),
            pltpu.VMEM((blk, hidden), f32),
            pltpu.VMEM((blk, hidden), f32),
            pltpu.VMEM((blk, hidden), bf16),
            pltpu.VMEM((blk, width), f32),
            pltpu.SemaphoreType.DMA((2 + hidden // width, plan.ways)),
        ],
        limit=ROWS_LIMIT,
        name="middle",
        cost=(
            4 * seq * width * (width + 2 * hidden),
            2 * width * (width + 2 * hidden) + 40 * seq * width,
            seq * hidden,
        ),
    )


def finish_kernel(
    table_ref, order_ref, x_ref, dx_ref, vec_ref, sums_ref, hid_sums_ref, heads_ref, *refs,
    cut, n_parts, n_vec, n_hid,
):
    grads_in, sources = refs[: 3 * n_parts], refs[3 * n_parts : 3 * n_parts + 8]
    out_ref, *quarters, w, acc, rows, packed, sem = refs[3 * n_parts + 8 :]
    width = x_ref.shape[1]

    @pl.when(pl.program_id(0) == 0)
    def _():
        lines = weight_lines(w, cut, sources[0].shape[1])
        fetch("start", table_ref, sources, lines, sem)
        rows[...] = jnp.zeros_like(rows)
        acc[...] = jnp.zeros_like(acc)
        fetch("wait", table_ref, sources, lines, sem)

    ordered = [grads_in[3 * part + k][...] for k in range(3) for part in range(n_parts)]
    grad = jnp.concatenate(ordered, 1)
    da1 = dot_nt(grad, w[...])
    for row, columns in ((2, slice(0, width)), (3, slice(2 * width, 3 * width))):
        rows[row : row + 1, :] += column_sum(grad[:, columns].astype(f32))
    for r in strips(x_ref.shape[0], 16):
        grad = da1[r]
        unit, rate = normalized(x_ref[r, :].astype(f32))
        acc[:8] += by_sublanes(grad * unit)
        acc[8:] += by_sublanes(grad)
        out_ref[r, :] = dx_ref[r, :] + norm_back(grad * vec_ref[0:1, :], unit, rate)

    @pl.when(pl.program_id(0) == pl.num_programs(0) - 1)
    def _():
        rows[0:1, :] = column_sum(acc[:8])
        rows[1:2, :] = column_sum(acc[8:])
        rows[4:n_vec, :] = sums_ref[4:n_vec, :]
        ways, _, lanes = packed.shape
        group = width // ways
        packed[...] = jnp.zeros_like(packed)
        for g in range(ways):
            packed[g, :n_vec, :group] = rows[:n_vec, g * group : (g + 1) * group]
            packed[g, n_vec : n_vec + n_hid, :] = hid_sums_ref[:n_hid, g * lanes : (g + 1) * lanes]
            packed[g, n_vec + n_hid : n_vec + n_hid + 1, :] = heads_ref[0:1, :]
        for k in range(ways):
            quarters[4 * k // ways][k % (ways // 4)] = packed[order_ref[k]]


def finish(plan, order, tokens, dx2, vec, sums, parts, gathered, cut, n_vec, n_hid, after=(), blk=256):
    seq, width = tokens.shape
    blk = min(blk, seq)
    row = by_rows(blk, width)
    (table, *blocks), (table_spec, *specs) = block_operands(plan, gathered)
    grads_in = [g for part in parts for g in part]
    lanes = sums[1].shape[1] // plan.ways
    packed = jax.ShapeDtypeStruct((plan.ways // 4, 16, lanes), f32)
    packed_spec = pl.BlockSpec(packed.shape, lambda i: (0, 0, 0))
    return launch(
        functools.partial(finish_kernel, cut=cut, n_parts=len(parts), n_vec=n_vec, n_hid=n_hid),
        [table, order, tokens, dx2, vec, *sums, *grads_in, *blocks],
        after=after,
        grid=(seq // blk,),
        in_specs=[table_spec, table_spec, row, row, *(resident(a.shape) for a in (vec, *sums))]
        + [by_rows(blk, g.shape[1]) for g in grads_in]
        + specs,
        out_specs=[row] + [packed_spec] * 4,
        out_shape=[jax.ShapeDtypeStruct((seq, width), f32)] + [packed] * 4,
        scratch_shapes=[
            pltpu.VMEM((width, 3 * width), bf16),
            pltpu.VMEM((16, width), f32),
            pltpu.VMEM((16, width), f32),
            pltpu.VMEM((plan.ways, 16, lanes), f32),
            pltpu.SemaphoreType.DMA((2, plan.ways)),
        ],
        name="finish",
    )


def local(
    plan,
    tokens,
    doc_split,
    head_scale,
    query_key_value_weight,
    output_weight,
    first_weight,
    second_weight,
    model_vectors,
    hidden_vectors,
    cotangent,
):
    seq, width = tokens.shape
    hidden = first_weight.shape[1]
    heads = head_scale.shape[0]
    blk = min(512, seq)
    ways, half = plan.ways, plan.half
    n_vec, n_hid = model_vectors.shape[0], hidden_vectors.shape[0]

    cut = 2 * width
    group, lanes = width // ways, hidden // ways
    qkv_rows = join_low(plan, query_key_value_weight)
    vec_rows = jnp.concatenate(
        [
            jnp.pad(join_low(plan, model_vectors, 1), ((0, 0), (0, lanes - group))),
            join_low(plan, hidden_vectors, 1),
            jnp.zeros((group - n_vec - n_hid, lanes), bf16),
        ],
        0,
    )
    fc1_rows = join_low(plan, first_weight)
    fc2_rows = join_low(plan, second_weight)
    out_rows = join_low(plan, output_weight)
    n_q = hidden // width
    half_q = n_q // 2
    quarters = [fc2_rows[q * group : (q + 1) * group] for q in range(n_q)]
    first = Gather(plan, [jnp.concatenate([qkv_rows[:, :cut], vec_rows], 1), qkv_rows[:, cut:]])
    second = Gather(
        plan,
        [
            jnp.concatenate([fc1_rows, *quarters[:half_q]], 1),
            jnp.concatenate([*quarters[half_q:], out_rows], 1),
        ],
    )
    first.step()
    join_after([first])
    first.step()
    second.held = relay(second.held, first.held[:1])
    second.step()
    while first.at < plan.steps:
        join_after([first])
        first.step()
    first.cross_held()
    while second.at < plan.steps - 2:
        second.step()
    second.fresh = relay(second.fresh, first.fresh)
    second.step()
    first.cross_fresh()

    qkv, first_t, vec, hid = project(plan, tokens, first, cut, hidden)
    join_after([second], [vec])
    second.step()
    second.cross_held()
    pairs = heads // 2
    attended, lse = attention(doc_split, qkv, heads, blk, 0, pairs, after=second.held)
    second.fresh = relay(second.fresh, [lse])
    second.cross_fresh()

    scale_row = jnp.repeat(head_scale, width // heads)[None]
    output, scaled_t, second_t, hidden_t, grad_pre, grad_branch, grad_attended, grad_middle, sums, hid_sums = (
        middle(plan, tokens, attended, cotangent, second, vec, hid, scale_row, half_q)
    )
    table = plan.table(0, False)

    def by_group(left_t):
        return left_t.reshape(ways, -1, group, seq)

    def send_grads(jobs, tile, after=(), cover=False):
        sent = grads([table[half:]], [jobs], tile, None, after, cover)
        return list(sent), to_other_core(plan, sent[0])

    def keep_grads(jobs, tile, got, after=(), cover=False):
        outs = grads([table[:half]], [jobs], tile, [got], after, cover)
        return list(outs[:1]), Scatter.begun(plan, 0, *outs)

    hidden_t = by_group(hidden_t)
    fc2_jobs = [(hidden_t, q, [cotangent], [0]) for q in range(n_q)]
    fc1_jobs = [
        (by_group(second_t), 0, [grad_pre], range(n_q)),
        (by_group(scaled_t), 0, [grad_branch], [0]),
    ]
    done, got_2 = send_grads(fc2_jobs, width)
    done, got_1 = send_grads(fc1_jobs, width, done, True)
    done, fc2_sum = keep_grads(fc2_jobs, width, got_2, done, True)
    done, fc1_sum = keep_grads(fc1_jobs, width, got_1, done)

    first_t = by_group(first_t)

    def back(start, count, after):
        out = attention_back(doc_split, qkv, grad_attended, attended, lse, heads, blk, start, count, after)
        return list(out[:1]), list(out)

    some = pairs * 3 // 8
    done, part_a = back(0, some, done)
    done = step_all([fc2_sum], done)
    done, part_b = back(some, some, done)
    size = part_a[0].shape[1]
    jobs = [(first_t, 0, part, [0]) for part in (part_a, part_b)]
    done, got = send_grads(jobs, 3 * size, done)
    done = step_all([fc2_sum, fc1_sum], done, True)
    done, sum_a = keep_grads(jobs, 3 * size, got, done)
    done, part_c = back(2 * some, pairs - 2 * some, done)
    rest = part_c[0].shape[1]
    jobs = [(first_t, 0, part_c, [0])]
    done, got = send_grads(jobs, 3 * rest, done)
    done = step_all([fc2_sum, fc1_sum, sum_a], done, True)
    done, sum_b = keep_grads(jobs, 3 * rest, got, done)
    head_sums = jnp.sum(sums[n_vec].reshape(heads, -1), axis=1)
    head_row = jnp.broadcast_to(jnp.pad(head_sums, (0, lanes - heads)), (8, lanes))
    grad_tokens, *vec_parts = finish(
        plan,
        table,
        tokens,
        grad_middle,
        vec,
        (sums, hid_sums, head_row),
        (part_a, part_b, part_c),
        first,
        cut,
        n_vec,
        n_hid,
        done,
    )
    done = step_all([fc1_sum, sum_a, sum_b], [grad_tokens])
    ways_out = (plan.pairs(0, 0, False), plan.core_pairs(), plan.corner_pairs(0))
    vec_all = vec_parts[0]
    for one, pairs_of in zip(relay(vec_parts[1:], done), ways_out):
        vec_all += lax.ppermute(one, AXES, pairs_of)
    vec_sum = Scatter(plan, 0, None, None)
    vec_sum.at = 1
    vec_sum.send(vec_all[half // 4 :], vec_all[: half // 4])
    done = step_all([sum_a, sum_b, vec_sum], done)
    step_all([sum_b, vec_sum], done)
    sent_vec = vec_sum.total()
    sent_a, sent_b = sum_a.total(), sum_b.total()
    sum_fc2, sum_fc1 = fc2_sum.total(), fc1_sum.total()
    columns = []
    for k in range(3):
        columns += [sent_a[:, k * size : (k + 1) * size], sent_a[:, (3 + k) * size : (4 + k) * size]]
        columns.append(sent_b[:, k * rest : (k + 1) * rest])
    sent_qkv = split_low(plan, jnp.concatenate(columns, 1))
    sent_fc1 = split_low(plan, sum_fc1[:, :hidden])
    sent_out = split_low(plan, sum_fc1[:, hidden:])
    row_blocks = [sum_fc2[:, k : k + width] for k in range(0, hidden, width)]
    sent_fc2 = split_low(plan, jnp.concatenate(row_blocks, 0))
    sent_vecd = split_low(plan, sent_vec[:n_vec, :group], 1)
    sent_vecff = split_low(plan, sent_vec[n_vec : n_vec + n_hid], 1)
    grad_heads = sent_vec[n_vec + n_hid, :heads]
    if plan.low > 1:
        grad_heads = lax.psum(grad_heads, AXES, axis_index_groups=plan.low_groups())
    return (
        output,
        grad_tokens,
        grad_heads,
        sent_qkv,
        sent_out,
        sent_fc1,
        sent_fc2,
        sent_vecd,
        sent_vecff,
    )


def solution(mesh):
    rows = P(AXES, None)
    columns = P(None, AXES)
    return jax.shard_map(
        functools.partial(local, Plan(mesh)),
        mesh=mesh,
        in_specs=(rows, P(AXES), P(), rows, rows, rows, rows, columns, columns, rows),
        out_specs=(rows, rows, P(), rows, rows, rows, rows, columns, columns),
        check_vma=False,
    )
```

```python
import functools

import jax
import jax.numpy as jnp
from jax import lax
from jax.experimental import pallas as pl
from jax.experimental.pallas import tpu as pltpu
from jax.sharding import PartitionSpec as P

epsilon = 1e-05
AXES = ("dp", "fsdp")
f32 = jnp.float32
bf16 = jnp.bfloat16
NEG = -1e30
VMEM_LIMIT = 56 << 20
ROWS_LIMIT = 62 << 20


def launch(
    kernel, args, *, in_specs, out_specs, out_shape, name, after=(), grid=(), scratch_shapes=(),
    prefetch=0, limit=VMEM_LIMIT, aliases=None, cover=False, cost=(1, 1, 0),
):
    after, count = list(after), len(args)

    def body(*refs):
        kernel(*refs[:count], *refs[count + len(after) :])

    return pl.pallas_call(
        body,
        grid_spec=pltpu.PrefetchScalarGridSpec(
            num_scalar_prefetch=prefetch,
            grid=grid,
            in_specs=[*in_specs] + [pl.BlockSpec(memory_space=pltpu.HBM)] * len(after),
            out_specs=out_specs,
            scratch_shapes=scratch_shapes,
        ),
        out_shape=out_shape,
        input_output_aliases=aliases or {},
        compiler_params=pltpu.CompilerParams(vmem_limit_bytes=limit),
        cost_estimate=pl.CostEstimate(
            flops=10**12 if cover else cost[0], bytes_accessed=cost[1], transcendentals=cost[2]
        ),
        name=name,
    )(*args, *after)


def relay(values, after):
    anywhere = pl.BlockSpec(memory_space=pl.ANY)
    return list(
        launch(
            lambda *refs: None,
            values,
            after=after,
            in_specs=[anywhere] * len(values),
            out_specs=[anywhere] * len(values),
            out_shape=[jax.ShapeDtypeStruct(v.shape, v.dtype) for v in values],
            aliases={k: k for k in range(len(values))},
            name="relay",
        )
    )


def in_vmem(value):
    return pltpu.with_memory_space_constraint(value, pltpu.VMEM)


class Plan:
    def __init__(self, mesh):
        n_dp, n_fs = mesh.shape["dp"], mesh.shape["fsdp"]
        self.count = n_dp * n_fs
        self.ways = min(self.count, 32)
        self.low = self.count // self.ways
        self.core = max(1, n_fs // self.low)
        self.dims = [1 << b for b in range(self.ways.bit_length() - 1) if 1 << b != self.core]
        self.half = self.ways // 2
        self.steps = len(self.dims)

    def order(self, core_bit, part, gathers):
        near, far = self.dims[:-1], self.dims[-1:]
        shift = (core_bit + part if part != 1 else 2) % len(near)
        near = near[shift:] + near[:shift]
        return far + near if gathers else near + far

    def pairs(self, part, step, gathers):
        out = []
        for i in range(self.count):
            group = i // self.low
            mask = self.order(int(bool(group & self.core)), part, gathers)[step]
            out.append((i, i ^ (mask * self.low)))
        return out

    def core_pairs(self):
        return [(i, i ^ (self.core * self.low)) for i in range(self.count)]

    def corner_pairs(self, part):
        out = []
        for i in range(self.count):
            group = i // self.low
            mask = self.core ^ self.order(int(not group & self.core), part, False)[0]
            out.append((i, i ^ (mask * self.low)))
        return out

    def low_groups(self):
        return [[g * self.low + i for i in range(self.low)] for g in range(self.ways)]

    def table(self, part, gathers):
        me = (lax.axis_index("dp") * lax.axis_size("fsdp") + lax.axis_index("fsdp")) // self.low
        rows = []
        for core_bit in (0, 1):
            row = []
            for other in (0, 1):
                masks = self.order(core_bit ^ other, part, gathers)
                for r in range(self.half):
                    x = self.core if other else 0
                    for k in range(self.steps):
                        bit = k if gathers else self.steps - 1 - k
                        if (r >> bit) & 1:
                            x ^= masks[k]
                    row.append(x)
            rows.append(row)
        mine = ((me & self.core) != 0).astype(jnp.int32)
        masks = jnp.where(mine == 1, jnp.array(rows[1], jnp.int32), jnp.array(rows[0], jnp.int32))
        return jnp.bitwise_xor(me.astype(jnp.int32), masks)


class Gather:
    def __init__(self, plan, pieces):
        self.plan = plan
        self.held = [piece[None] for piece in pieces]
        self.fresh = None
        self.at = 0

    def join(self):
        if self.fresh is not None:
            self.held = [jnp.concatenate(pair, 0) for pair in zip(self.held, self.fresh)]
            self.fresh = None

    def step(self):
        self.join()
        self.fresh = [
            lax.ppermute(h, AXES, self.plan.pairs(part, self.at, True)) for part, h in enumerate(self.held)
        ]
        self.at += 1

    def cross_held(self):
        self.far_held = [lax.ppermute(h, AXES, self.plan.core_pairs()) for h in self.held]

    def cross_fresh(self):
        self.far_fresh = [lax.ppermute(h, AXES, self.plan.core_pairs()) for h in self.fresh]

    def blocks(self):
        return [list(b) for b in zip(self.held, self.fresh, self.far_held, self.far_fresh)]


def join_kernel(*refs, count):
    for n in range(count):
        out = refs[2 * count + n]
        half = out.shape[0] // 2
        out[:half] = refs[2 * n][...]
        out[half:] = refs[2 * n + 1][...]


def join_after(gathers, after=()):
    args = [
        a
        for one in gathers
        for held, fresh in zip(one.held, one.fresh)
        for a in (held, in_vmem(fresh))
    ]
    shapes = [(2 * h.shape[0], *h.shape[1:]) for one in gathers for h in one.held]
    vmem = pl.BlockSpec(memory_space=pltpu.VMEM)
    outs = launch(
        functools.partial(join_kernel, count=len(shapes)),
        args,
        after=after,
        in_specs=[vmem] * len(args),
        out_specs=[vmem] * len(shapes),
        out_shape=[jax.ShapeDtypeStruct(shape, bf16) for shape in shapes],
        name="join",
    )
    for n, one in enumerate(gathers):
        one.held = list(outs[2 * n : 2 * n + 2])
        one.fresh = None


def join_low(plan, piece, axis=0):
    if plan.low == 1:
        return piece
    return lax.all_gather(piece, AXES, axis=axis, tiled=True, axis_index_groups=plan.low_groups())


def fetch(action, table_ref, sources, lines, sem):
    for number, part, column, width, place in lines:
        for b in range(4):
            source = sources[4 * part + b]
            count = source.shape[0]

            def one(r, _, source=source, number=number, part=part, b=b, count=count):
                at = b * count + r
                copy = pltpu.make_async_copy(
                    source.at[r, :, pl.ds(column, width)],
                    place(table_ref[part, at]),
                    sem.at[number, at],
                )
                getattr(copy, action)()
                return _

            lax.fori_loop(0, count, one, 0)


def block_operands(plan, gathered):
    blocks = gathered.blocks()
    table = jnp.stack([plan.table(part, True) for part in range(len(blocks))])
    flat = [b for part in blocks for b in part]
    specs = [pl.BlockSpec(memory_space=pltpu.SMEM)] + [pl.BlockSpec(memory_space=pltpu.HBM)] * len(flat)
    return [table, *flat], specs


def plus(a, b):
    return a.astype(f32) + b.astype(f32)


class Scatter:
    def __init__(self, plan, part, keep, got):
        self.plan, self.part, self.at = plan, part, 0
        self.keep, self.got = keep, got

    @classmethod
    def begun(cls, plan, part, going, keep):
        one = cls(plan, part, None, None)
        one.send(going, keep)
        return one

    def send(self, going, keep):
        self.keep = keep
        self.got = lax.ppermute(going, AXES, self.plan.pairs(self.part, self.at, False))
        self.at += 1

    def total(self):
        return plus(self.keep[0], self.got[0])


def halve_kernel(*refs, count):
    for n in range(count):
        keep_ref, got_ref = refs[2 * n], refs[2 * n + 1]
        going_ref, kept_ref = refs[2 * (count + n)], refs[2 * (count + n) + 1]
        half = keep_ref.shape[0] // 2
        for out, part in ((going_ref, slice(half, 2 * half)), (kept_ref, slice(0, half))):
            out[...] = plus(keep_ref[part], got_ref[part]).astype(out.dtype)


def step_all(scatters, after=(), cover=False):
    args = [
        a
        for one in scatters
        for a in (one.keep, in_vmem(one.got))
    ]
    shapes = [
        jax.ShapeDtypeStruct((one.keep.shape[0] // 2, *one.keep.shape[1:]), one.keep.dtype)
        for one in scatters
        for _ in range(2)
    ]
    outs = launch(
        functools.partial(halve_kernel, count=len(scatters)),
        args,
        after=after,
        in_specs=[pl.BlockSpec(memory_space=pltpu.VMEM)] * len(args),
        out_specs=[pl.BlockSpec(memory_space=pltpu.VMEM)] * len(args),
        out_shape=shapes,
        name="halve",
        cover=cover,
    )
    for n, one in enumerate(scatters):
        one.send(*outs[2 * n : 2 * n + 2])
    return [outs[0]]


def to_other_core(plan, values):
    return lax.ppermute(values, AXES, plan.core_pairs())


def split_low(plan, total, axis=0):
    if plan.low == 1:
        return total
    return lax.psum_scatter(
        total, AXES, scatter_dimension=axis, tiled=True, axis_index_groups=plan.low_groups()
    )


def dot_nt(a, b):
    return lax.dot_general(a, b, (((1,), (1,)), ((), ())), preferred_element_type=f32)


def dot_nn(a, b):
    return lax.dot_general(a, b, (((1,), (0,)), ((), ())), preferred_element_type=f32)


def transposed(a):
    return a.astype(f32).T.astype(a.dtype)


def causal(scores):
    keys = lax.broadcasted_iota(jnp.int32, scores.shape, 0)
    return jnp.where(keys <= lax.broadcasted_iota(jnp.int32, scores.shape, 1), scores, NEG)


def head_lanes(shape, h, hd):
    lane = lax.broadcasted_iota(jnp.int32, shape, 1)
    mine = (lane >= hd) if h else (lane < hd)
    return mine, lane == (0 if h else hd)


def masked_keys(k, h, hd, split):
    mine, spare = head_lanes(k.shape, h, hd)
    early = lax.broadcasted_iota(jnp.int32, k.shape, 0) < split
    return jnp.where(mine, k, jnp.where(spare & early, bf16(NEG), bf16(0)))


def masked_queries(q, h, hd, split, start):
    mine, spare = head_lanes(q.shape, h, hd)
    late = lax.broadcasted_iota(jnp.int32, q.shape, 0) + start >= split
    alone = jnp.where(mine, q, bf16(0)) * bf16(hd**-0.5)
    return alone, jnp.where(spare & late, bf16(1), alone)


def key_pieces(i, blk):
    half = blk // 2
    whole = [(j * blk, blk, 0) for j in range(i)]
    return whole + [(i * blk, half, 0), (i * blk + half, half, half)]


def added(total, more, first):
    if not first:
        return total + more
    return jnp.concatenate([total[:, :first], total[:, first:] + more], 1)


def attention_kernel(split_ref, q_ref, k_ref, v_ref, *refs, seq, hd, blk):
    o_ref, lse_ref = refs[-2:]
    split = split_ref[0]
    v_t = transposed(v_ref[...])
    keys = [masked_keys(k_ref[...], h, hd, split) for h in (0, 1)]
    for i in range(seq // blk):
        rows = slice(i * blk, (i + 1) * blk)
        outs = []
        for h in (0, 1):
            _, q = masked_queries(q_ref[rows, :], h, hd, split, i * blk)
            pieces = key_pieces(i, blk)
            scores = [dot_nt(keys[h][at : at + count], q[first:]) for at, count, first in pieces]
            scores[i:] = [causal(s) for s in scores[i:]]
            peak = scores[0].max(0, keepdims=True)
            for s in scores[1:-1]:
                peak = jnp.maximum(peak, s.max(0, keepdims=True))
            first = pieces[-1][2]
            late = jnp.maximum(peak[:, first:], scores[-1].max(0, keepdims=True))
            peak = jnp.concatenate([peak[:, :first], late], 1)
            total = jnp.zeros((1, blk), f32)
            mixed = jnp.zeros((hd, blk), f32)
            for (at, count, first), s in zip(pieces, scores):
                low = []
                for r in strips(count, 64):
                    e = jnp.exp(s[r] - peak[:, first:])
                    total = added(total, e.sum(0, keepdims=True), first)
                    low.append(e.astype(bf16))
                low = jnp.concatenate(low, 0)
                values = v_t[h * hd : (h + 1) * hd, at : at + count]
                mixed = added(mixed, dot_nn(values, low), first)
            outs.append(mixed / total)
            lse_ref[0, h : h + 1, rows] = peak + jnp.log(total)
        o_ref[rows, :] = jnp.concatenate(outs, 0).T


def attention(split, qkv, heads, blk, start, count, into=(), after=()):
    seq, width = qkv.shape[0], qkv.shape[1] // 3
    hd, pairs = width // heads, heads // 2
    w = 2 * hd
    return launch(
        functools.partial(attention_kernel, seq=seq, hd=hd, blk=blk),
        [split, qkv, qkv, qkv, *into],
        after=after,
        grid=(count,),
        in_specs=[
            pl.BlockSpec(memory_space=pltpu.SMEM),
            pl.BlockSpec((seq, w), lambda p: (0, p + start)),
            pl.BlockSpec((seq, w), lambda p: (0, p + start + pairs)),
            pl.BlockSpec((seq, w), lambda p: (0, p + start + 2 * pairs)),
        ]
        + [pl.BlockSpec(memory_space=pl.ANY)] * len(into),
        out_specs=[
            pl.BlockSpec((seq, w), lambda p: (0, p + start)),
            pl.BlockSpec((1, 2, seq), lambda p: (p + start, 0, 0)),
        ],
        out_shape=[
            jax.ShapeDtypeStruct((seq, width), f32),
            jax.ShapeDtypeStruct((pairs, 2, seq), f32),
        ],
        aliases={4 + k: k for k in range(len(into))},
        name="attention",
        cost=(12 * seq * seq * w * count, seq * w * count * 10, 2 * count * seq * seq),
    )


def attention_back_kernel(
    split_ref, q_ref, k_ref, v_ref, da_ref, o_ref, lse_ref, dq_ref, dk_ref, dv_ref, dk_acc, dv_acc,
    *, seq, hd, blk,
):
    split = split_ref[0]
    k_t = transposed(k_ref[...])
    keys_of = [masked_keys(k_ref[...], h, hd, split) for h in (0, 1)]
    for i in range(seq // blk):
        rows = slice(i * blk, (i + 1) * blk)
        q_full, da_full = q_ref[rows, :], da_ref[rows, :]
        inner = (da_full.astype(f32) * o_ref[rows, :]).T
        dqs = []
        for h in (0, 1):
            q, q_marked = masked_queries(q_full, h, hd, split, i * blk)
            da = jnp.where(head_lanes(da_full.shape, h, hd)[0], da_full, bf16(0))
            row_inner = inner[h * hd : (h + 1) * hd].sum(0, keepdims=True)
            lse = lse_ref[0, h : h + 1, rows]
            dq = jnp.zeros((hd, blk), f32)
            for at, count, first in key_pieces(i, blk):
                keys = slice(at, at + count)
                diagonal = at >= i * blk
                s = dot_nt(keys_of[h][keys], q_marked[first:])
                if diagonal:
                    s = causal(s)
                dp = dot_nt(v_ref[keys, :], da[first:])
                p_low, ds = [], []
                for r in strips(count, 64):
                    p = jnp.exp(s[r] - lse[:, first:])
                    p_low.append(p.astype(bf16))
                    ds.append((p * (dp[r] - row_inner[:, first:])).astype(bf16))
                ds = jnp.concatenate(ds, 0)
                dv = dot_nn(jnp.concatenate(p_low, 0), da[first:])
                dk = dot_nn(ds, q[first:])
                if diagonal and h == 0:
                    dv_acc[keys, :] = dv
                    dk_acc[keys, :] = dk
                else:
                    dv_acc[keys, :] += dv
                    dk_acc[keys, :] += dk
                dq = added(dq, dot_nn(k_t[h * hd : (h + 1) * hd, keys], ds), first)
            dqs.append(dq)
        dq_ref[rows, :] = (jnp.concatenate(dqs, 0).T * (hd**-0.5)).astype(bf16)
    dk_ref[...] = dk_acc[...].astype(bf16)
    dv_ref[...] = dv_acc[...].astype(bf16)


def attention_back(split, qkv, da, attended, lse, heads, blk, start, count, after=()):
    seq, width = qkv.shape[0], qkv.shape[1] // 3
    hd, pairs = width // heads, heads // 2
    w = 2 * hd
    column = pl.BlockSpec((seq, w), lambda p: (0, p + start))
    out = pl.BlockSpec((seq, w), lambda p: (0, p))
    return launch(
        functools.partial(attention_back_kernel, seq=seq, hd=hd, blk=blk),
        [split, qkv, qkv, qkv, da, attended, lse],
        after=after,
        grid=(count,),
        in_specs=[
            pl.BlockSpec(memory_space=pltpu.SMEM),
            column,
            pl.BlockSpec((seq, w), lambda p: (0, p + start + pairs)),
            pl.BlockSpec((seq, w), lambda p: (0, p + start + 2 * pairs)),
            column,
            column,
            pl.BlockSpec((1, 2, seq), lambda p: (p + start, 0, 0)),
        ],
        out_specs=[out, out, out],
        out_shape=[jax.ShapeDtypeStruct((seq, count * w), bf16)] * 3,
        scratch_shapes=[pltpu.VMEM((seq, w), f32)] * 2,
        name="attention_back",
    )


def grads_kernel(table_ref, place_ref, *refs, runs, n_left, n_right, begins, adds):
    lefts, rights, rest = refs[:n_left], refs[n_left : n_left + n_right], refs[n_left + n_right :]
    left = rest[-1]
    ways, rows, tokens = left.shape
    step = pl.program_id(0)
    for first, last, l, r, part in runs:

        @pl.when(step == first)
        def _():
            for w in range(ways):
                left[w] = lefts[l][table_ref[part, w], 0]

        @pl.when((step >= first) & (step < last))
        def _():
            product = [dot_nn(left[...].reshape(ways * rows, tokens), rights[k][...]) for k in r]
            product = jnp.concatenate(product, 1) if len(r) > 1 else product[0]
            product = product.reshape(ways, rows, product.shape[1])
            if adds:
                n_parts = len(begins)
                got_ref = rest[part]
                at = pl.multiple_of((step - begins[part]) * product.shape[2], 128)
                theirs = got_ref[:, :, pl.ds(at, product.shape[2])]
                going_ref, keep_ref = rest[n_parts + 2 * part : n_parts + 2 * part + 2]
                product = (product + theirs.astype(f32)).astype(bf16)
                keep_ref[...] = product[: ways // 2]
                going_ref[...] = product[ways // 2 :]
            else:
                rest[part][...] = product.astype(bf16)


def grads(tables, parts, tile, got=None, after=(), cover=False):
    groups, _, rows, tokens = parts[0][0][0].shape
    ways = tables[0].shape[0]
    lefts, rights, runs, places, spans = [], [], [], [], []
    at = 0
    for part, jobs in enumerate(parts):
        begin = at
        for left, q, group, numbers in jobs:
            for known, one in ((lefts, left), *((rights, right) for right in group)):
                if not any(one is k for k in known):
                    known.append(one)
            l = next(i for i, k in enumerate(lefts) if k is left)
            r = [next(i for i, k in enumerate(rights) if k is right) for right in group]
            runs.append((at, at + len(numbers), l, r, part))
            for n in numbers:
                places.append(([l], q, r, n))
            at += len(numbers)
        spans.append((begin, at - begin))

    def held(which, entry, count):
        lines = []
        for k in range(count):
            used = [(s, p[entry]) for s, p in enumerate(places) if k in p[which]]
            lines.append([next((v for s, v in used if s >= i), used[-1][1]) for i in range(at)])
        return lines

    place = jnp.array(held(0, 1, len(lefts)) + held(2, 3, len(rights)), jnp.int32)

    def left_spec(k):
        return pl.BlockSpec((groups, 1, rows, tokens), lambda i, t, p: (0, p[k, i], 0, 0))

    def right_spec(k):
        return pl.BlockSpec((tokens, share), lambda i, t, p: (0, p[len(lefts) + k, i]))

    def block(count, span):
        begin, steps = span
        return pl.BlockSpec(
            (count, rows, tile), lambda i, t, p: (0, 0, jnp.clip(i - begin, 0, steps - 1))
        )

    def shape(count, span):
        return jax.ShapeDtypeStruct((count, rows, span[1] * tile), bf16)

    share = tile // len(parts[0][0][2])
    adds = got is not None
    each = [ways // 2] * 2 if adds else [ways]
    return launch(
        functools.partial(
            grads_kernel,
            runs=runs,
            n_left=len(lefts),
            n_right=len(rights),
            begins=[span[0] for span in spans],
            adds=adds,
        ),
        [jnp.stack(tables), place, *lefts, *rights, *(map(in_vmem, got) if adds else [])],
        after=after,
        prefetch=2,
        grid=(at,),
        in_specs=[left_spec(k) for k in range(len(lefts))]
        + [right_spec(k) for k in range(len(rights))]
        + [pl.BlockSpec(memory_space=pltpu.VMEM)] * (len(parts) * adds),
        out_specs=[block(count, span) for span in spans for count in each],
        out_shape=[shape(count, span) for span in spans for count in each],
        scratch_shapes=[pltpu.VMEM((ways, rows, tokens), bf16)],
        name="grads_keep" if adds else "grads_send",
        cover=cover,
    )


def normalized(values):
    center = values - jnp.mean(values, axis=-1, keepdims=True)
    rate = lax.rsqrt(jnp.mean(center * center, axis=-1, keepdims=True) + epsilon)
    return center * rate, rate


def norm_back(grad, unit, rate):
    inner = jnp.mean(grad * unit, axis=-1, keepdims=True)
    return rate * (grad - jnp.mean(grad, axis=-1, keepdims=True) - unit * inner)


def by_lanes(values):
    total = values[:, :128]
    for k in range(128, values.shape[1], 128):
        total += values[:, k : k + 128]
    return total


def by_sublanes(values):
    total = values[:8]
    for k in range(8, values.shape[0], 8):
        total += values[k : k + 8]
    return total


def column_sum(values):
    return jnp.sum(values, axis=0, keepdims=True)


def resident(shape):
    return pl.BlockSpec(shape, lambda i: (0,) * len(shape), pipeline_mode=pl.Buffered(1))


def by_rows(blk, width):
    return pl.BlockSpec((blk, width), lambda i: (i, 0))


def by_columns(height, blk):
    return pl.BlockSpec((height, blk), lambda i: (0, i))


def weight_lines(w, cut, group, first=0):
    def rows(g):
        return pl.ds(pl.multiple_of(g * group, group), group)

    rest = w.shape[1] - cut
    return [
        (first, 0, 0, cut, lambda g: w.at[rows(g), pl.ds(0, cut)]),
        (first + 1, 1, 0, rest, lambda g: w.at[rows(g), pl.ds(cut, rest)]),
    ]


def project_kernel(table_ref, x_ref, *refs, cut):
    sources = refs[:8]
    qkv_ref, left_t_ref, vec_ref, hid_ref, w, raw, left_ref, sem = refs[8:]
    ways, group, lanes = raw.shape
    width = x_ref.shape[1]

    @pl.when(pl.program_id(0) == 0)
    def _():
        vec_lines = [(2, 0, cut, lanes, lambda g: raw.at[g])]
        lines = weight_lines(w, cut, group)
        fetch("start", table_ref, sources, vec_lines, sem)
        fetch("start", table_ref, sources, lines, sem)
        fetch("wait", table_ref, sources, vec_lines, sem)
        per = lanes // group
        for k in range(0, ways, per):
            row = [raw[k + j][:16, :group].astype(f32) for j in range(per)]
            vec_ref[:, k * group : (k + per) * group] = jnp.concatenate(row, 1)
        for k in range(ways):
            hid_ref[:, k * lanes : (k + 1) * lanes] = raw[k][:16].astype(f32)
        fetch("wait", table_ref, sources, lines, sem)

    for r in strips(x_ref.shape[0], 16):
        unit, _ = normalized(x_ref[r, :].astype(f32))
        left_ref[r, :] = (unit * vec_ref[0:1, :] + vec_ref[1:2, :]).astype(bf16)
    left = left_ref[...]
    left_t_ref[...] = transposed(left)
    for part, bias in ((0, 2), (1, None), (2, 3)):
        cols = slice(part * width, (part + 1) * width)
        rows = dot_nn(left, w[:, cols])
        if bias is not None:
            rows += vec_ref[bias : bias + 1, :]
        qkv_ref[:, cols] = rows.astype(bf16)


def project(plan, tokens, gathered, cut, hidden, after=(), blk=256):
    seq, width = tokens.shape
    blk = min(blk, seq)
    (table, *blocks), (table_spec, *specs) = block_operands(plan, gathered)
    return launch(
        functools.partial(project_kernel, cut=cut),
        [table, tokens, *blocks],
        after=after,
        grid=(seq // blk,),
        in_specs=[table_spec, by_rows(blk, width), *specs],
        out_specs=[
            by_rows(blk, 3 * width),
            by_columns(width, blk),
            pl.BlockSpec((16, width), lambda i: (0, 0)),
            pl.BlockSpec((16, hidden), lambda i: (0, 0)),
        ],
        out_shape=[
            jax.ShapeDtypeStruct((seq, 3 * width), bf16),
            jax.ShapeDtypeStruct((width, seq), bf16),
            jax.ShapeDtypeStruct((16, width), f32),
            jax.ShapeDtypeStruct((16, hidden), f32),
        ],
        scratch_shapes=[
            pltpu.VMEM((width, 3 * width), bf16),
            pltpu.VMEM((plan.ways, width // plan.ways, hidden // plan.ways), bf16),
            pltpu.VMEM((blk, width), bf16),
            pltpu.SemaphoreType.DMA((3, plan.ways)),
        ],
        name="project",
        cost=(6 * seq * width * width, 18 * seq * width, seq),
    )


def group_rows(g, group, stride, first=0):
    return pl.ds(pl.multiple_of(g * stride + first, group), group)


def vector(ref, row):
    return ref[row : row + 1, :]


def strips(rows, height):
    return [slice(r, r + height) for r in range(0, rows, height)]


def middle_kernel(
    table_ref, x_ref, att_ref, c_ref, vec_ref, hid_ref, scale_ref, *refs, chunk, half_q
):
    sources, refs = refs[:8], refs[8:]
    out_ref, z_t_ref, a2_t_ref, m_t_ref, df_ref, dy_ref, da_ref, dx_ref, sums_ref, hid_sums_ref = refs[:10]
    wo_ref, w1_ref, w2_ref, gate, slope, dm_keep, acc, sem = refs[10:]
    width, hidden = w1_ref.shape
    group = sources[0].shape[1]
    n_q = hidden // width

    def rows(g, stride, first=0):
        return pl.ds(pl.multiple_of(g * stride + first, group), group)

    def quarter(q):
        column = hidden * (q < half_q) + q % half_q * width
        return (2 + q, q // half_q, column, width, lambda g: w2_ref.at[rows(g, n_q * group, q * group)])

    out_lines = [(0, 1, half_q * width, width, lambda g: wo_ref.at[rows(g, group)])]
    fc1_lines = [(1, 0, 0, hidden, lambda g: w1_ref.at[rows(g, group)])]
    fc2_lines = [quarter(q) for q in range(n_q)]

    def arrived(lines):
        @pl.when(pl.program_id(0) == 0)
        def _():
            fetch("wait", table_ref, sources, lines, sem)

    chunks = [slice(k, k + chunk) for k in range(0, hidden, chunk)]

    @pl.when(pl.program_id(0) == 0)
    def _():
        for lines in (out_lines, fc1_lines, fc2_lines):
            fetch("start", table_ref, sources, lines, sem)
        sums_ref[...] = jnp.zeros_like(sums_ref)
        hid_sums_ref[...] = jnp.zeros_like(hid_sums_ref)

    def vec(row):
        return vec_ref[row : row + 1, :]

    def add_sum(row, values):
        sums_ref[row : row + 1, :] += column_sum(values)

    z = (att_ref[...] * scale_ref[...]).astype(bf16)
    z_t_ref[...] = transposed(z)
    arrived(out_lines)
    unit_1, rate_1 = normalized(dot_nn(z, wo_ref[...]) + vec(4))
    x2 = x_ref[...].astype(f32) + (unit_1 * vec(5) + vec(6))
    unit_2, rate_2 = normalized(x2)
    a2 = (unit_2 * vec(7) + vec(8)).astype(bf16)
    a2_t_ref[...] = transposed(a2)
    arrived(fc1_lines)

    total = 0.0
    root = (2.0 / jnp.pi) ** 0.5
    for ch in chunks:
        f = dot_nn(a2, w1_ref[:, ch]) + hid_ref[10:11, ch]
        square = f * f
        t = jnp.tanh(f * (root + (root * 0.044715) * square))
        half = 0.5 + 0.5 * t
        g = f * half
        gate[:, ch] = g
        slope[:, ch] = half + g * (1.0 - t) * (root + (3 * root * 0.044715) * square)
        total += jnp.sum(g, axis=-1, keepdims=True)
    mean = total / hidden
    spread = 0.0
    for ch in chunks:
        center = gate[:, ch] - mean
        spread += jnp.sum(center * center, axis=-1, keepdims=True)
    rate = lax.rsqrt(spread / hidden + epsilon)

    arrived(fc2_lines)
    grad_sum = 0.0
    grad_inner = 0.0
    for ch in chunks:
        unit = (gate[:, ch] - mean) * rate
        gate[:, ch] = unit
        gain = hid_ref[11:12, ch]
        m = (unit * gain + hid_ref[12:13, ch]).astype(bf16)
        m_t_ref[ch, :] = transposed(m)
        y = dot_nn(m, w2_ref[ch, :])
        if ch.start == 0:
            acc[...] = y
        else:
            acc[...] += y
        dm = dot_nt(c_ref[...], w2_ref[ch, :]).astype(bf16)
        dm_keep[:, ch] = dm
        dm = dm.astype(f32)
        hid_sums_ref[1:2, ch] += column_sum(dm * unit)
        hid_sums_ref[2:3, ch] += column_sum(dm)
        grad = dm * gain
        grad_sum += jnp.sum(grad, axis=-1, keepdims=True)
        grad_inner += jnp.sum(grad * unit, axis=-1, keepdims=True)
    out_ref[...] = (x2 + (acc[...] + vec(9))).astype(bf16)

    grad_sum = grad_sum / hidden
    grad_inner = grad_inner / hidden
    for ch in chunks:
        grad = dm_keep[:, ch].astype(f32) * hid_ref[11:12, ch]
        grad = rate * (grad - grad_sum - gate[:, ch] * grad_inner)
        df = (slope[:, ch] * grad).astype(bf16)
        df_ref[:, ch] = df
        hid_sums_ref[0:1, ch] += column_sum(df.astype(f32))
        back = dot_nt(df, w1_ref[:, ch])
        if ch.start == 0:
            acc[...] = back
        else:
            acc[...] += back

    upstream = c_ref[...].astype(f32)
    da2 = acc[...]
    add_sum(9, upstream)
    add_sum(7, da2 * unit_2)
    add_sum(8, da2)
    dx2 = upstream + norm_back(da2 * vec(7), unit_2, rate_2)
    dx_ref[...] = dx2
    add_sum(5, dx2 * unit_1)
    add_sum(6, dx2)
    dy = norm_back(dx2 * vec(5), unit_1, rate_1).astype(bf16)
    dy_ref[...] = dy
    add_sum(4, dy.astype(f32))
    dz = dot_nt(dy, wo_ref[...]).astype(bf16).astype(f32)
    add_sum(10, dz * att_ref[...])
    da_ref[...] = (dz * scale_ref[...]).astype(bf16)


def middle(plan, tokens, attended, cotangent, gathered, vec, hid, scale, half_q, after=(), blk=256, chunk=256):
    seq, width = tokens.shape
    hidden = hid.shape[1]
    blk = min(blk, seq)
    (table, *blocks), (table_spec, *specs) = block_operands(plan, gathered)
    row, col, wide = by_rows(blk, width), by_columns(width, blk), by_rows(blk, hidden)
    shape = jax.ShapeDtypeStruct
    return launch(
        functools.partial(middle_kernel, chunk=chunk, half_q=half_q),
        [table, tokens, attended, cotangent, vec, hid, scale, *blocks],
        after=after,
        grid=(seq // blk,),
        in_specs=[table_spec, row, row, row, *(resident(a.shape) for a in (vec, hid, scale)), *specs],
        out_specs=[
            row, col, col, by_columns(hidden, blk), wide, row, row, row,
            pl.BlockSpec((16, width), lambda i: (0, 0)),
            pl.BlockSpec((8, hidden), lambda i: (0, 0)),
        ],
        out_shape=[
            shape((seq, width), bf16),
            shape((width, seq), bf16),
            shape((width, seq), bf16),
            shape((hidden, seq), bf16),
            shape((seq, hidden), bf16),
            shape((seq, width), bf16),
            shape((seq, width), bf16),
            shape((seq, width), f32),
            shape((16, width), f32),
            shape((8, hidden), f32),
        ],
        scratch_shapes=[
            pltpu.VMEM((width, width), bf16),
            pltpu.VMEM((width, hidden), bf16),
            pltpu.VMEM((hidden, width), bf16),
            pltpu.VMEM((blk, hidden), f32),
            pltpu.VMEM((blk, hidden), f32),
            pltpu.VMEM((blk, hidden), bf16),
            pltpu.VMEM((blk, width), f32),
            pltpu.SemaphoreType.DMA((2 + hidden // width, plan.ways)),
        ],
        limit=ROWS_LIMIT,
        name="middle",
        cost=(
            4 * seq * width * (width + 2 * hidden),
            2 * width * (width + 2 * hidden) + 40 * seq * width,
            seq * hidden,
        ),
    )


def finish_kernel(
    table_ref, order_ref, x_ref, dx_ref, vec_ref, sums_ref, hid_sums_ref, heads_ref, *refs,
    cut, n_parts, n_vec, n_hid,
):
    grads_in, sources = refs[: 3 * n_parts], refs[3 * n_parts : 3 * n_parts + 8]
    out_ref, *quarters, w, acc, rows, packed, sem = refs[3 * n_parts + 8 :]
    width = x_ref.shape[1]

    @pl.when(pl.program_id(0) == 0)
    def _():
        lines = weight_lines(w, cut, sources[0].shape[1])
        fetch("start", table_ref, sources, lines, sem)
        rows[...] = jnp.zeros_like(rows)
        acc[...] = jnp.zeros_like(acc)
        fetch("wait", table_ref, sources, lines, sem)

    ordered = [grads_in[3 * part + k][...] for k in range(3) for part in range(n_parts)]
    grad = jnp.concatenate(ordered, 1)
    da1 = dot_nt(grad, w[...])
    for row, columns in ((2, slice(0, width)), (3, slice(2 * width, 3 * width))):
        rows[row : row + 1, :] += column_sum(grad[:, columns].astype(f32))
    for r in strips(x_ref.shape[0], 16):
        grad = da1[r]
        unit, rate = normalized(x_ref[r, :].astype(f32))
        acc[:8] += by_sublanes(grad * unit)
        acc[8:] += by_sublanes(grad)
        out_ref[r, :] = dx_ref[r, :] + norm_back(grad * vec_ref[0:1, :], unit, rate)

    @pl.when(pl.program_id(0) == pl.num_programs(0) - 1)
    def _():
        rows[0:1, :] = column_sum(acc[:8])
        rows[1:2, :] = column_sum(acc[8:])
        rows[4:n_vec, :] = sums_ref[4:n_vec, :]
        ways, _, lanes = packed.shape
        group = width // ways
        packed[...] = jnp.zeros_like(packed)
        for g in range(ways):
            packed[g, :n_vec, :group] = rows[:n_vec, g * group : (g + 1) * group]
            packed[g, n_vec : n_vec + n_hid, :] = hid_sums_ref[:n_hid, g * lanes : (g + 1) * lanes]
            packed[g, n_vec + n_hid : n_vec + n_hid + 1, :] = heads_ref[0:1, :]
        for k in range(ways):
            quarters[4 * k // ways][k % (ways // 4)] = packed[order_ref[k]]


def finish(plan, order, tokens, dx2, vec, sums, parts, gathered, cut, n_vec, n_hid, after=(), blk=256):
    seq, width = tokens.shape
    blk = min(blk, seq)
    row = by_rows(blk, width)
    (table, *blocks), (table_spec, *specs) = block_operands(plan, gathered)
    grads_in = [g for part in parts for g in part]
    lanes = sums[1].shape[1] // plan.ways
    packed = jax.ShapeDtypeStruct((plan.ways // 4, 16, lanes), f32)
    packed_spec = pl.BlockSpec(packed.shape, lambda i: (0, 0, 0))
    return launch(
        functools.partial(finish_kernel, cut=cut, n_parts=len(parts), n_vec=n_vec, n_hid=n_hid),
        [table, order, tokens, dx2, vec, *sums, *grads_in, *blocks],
        after=after,
        grid=(seq // blk,),
        in_specs=[table_spec, table_spec, row, row, *(resident(a.shape) for a in (vec, *sums))]
        + [by_rows(blk, g.shape[1]) for g in grads_in]
        + specs,
        out_specs=[row] + [packed_spec] * 4,
        out_shape=[jax.ShapeDtypeStruct((seq, width), f32)] + [packed] * 4,
        scratch_shapes=[
            pltpu.VMEM((width, 3 * width), bf16),
            pltpu.VMEM((16, width), f32),
            pltpu.VMEM((16, width), f32),
            pltpu.VMEM((plan.ways, 16, lanes), f32),
            pltpu.SemaphoreType.DMA((2, plan.ways)),
        ],
        name="finish",
    )


def local(
    plan,
    tokens,
    doc_split,
    head_scale,
    query_key_value_weight,
    output_weight,
    first_weight,
    second_weight,
    model_vectors,
    hidden_vectors,
    cotangent,
):
    seq, width = tokens.shape
    hidden = first_weight.shape[1]
    heads = head_scale.shape[0]
    blk = min(512, seq)
    ways, half = plan.ways, plan.half
    n_vec, n_hid = model_vectors.shape[0], hidden_vectors.shape[0]

    cut = 2 * width
    group, lanes = width // ways, hidden // ways
    qkv_rows = join_low(plan, query_key_value_weight)
    vec_rows = jnp.concatenate(
        [
            jnp.pad(join_low(plan, model_vectors, 1), ((0, 0), (0, lanes - group))),
            join_low(plan, hidden_vectors, 1),
            jnp.zeros((group - n_vec - n_hid, lanes), bf16),
        ],
        0,
    )
    fc1_rows = join_low(plan, first_weight)
    fc2_rows = join_low(plan, second_weight)
    out_rows = join_low(plan, output_weight)
    n_q = hidden // width
    half_q = n_q // 2
    quarters = [fc2_rows[q * group : (q + 1) * group] for q in range(n_q)]
    first = Gather(plan, [jnp.concatenate([qkv_rows[:, :cut], vec_rows], 1), qkv_rows[:, cut:]])
    second = Gather(
        plan,
        [
            jnp.concatenate([fc1_rows, *quarters[:half_q]], 1),
            jnp.concatenate([*quarters[half_q:], out_rows], 1),
        ],
    )
    first.step()
    join_after([first])
    first.step()
    second.held = relay(second.held, first.held[:1])
    second.step()
    while first.at < plan.steps:
        join_after([first])
        first.step()
    first.cross_held()
    while second.at < plan.steps - 2:
        second.step()
    second.fresh = relay(second.fresh, first.fresh)
    second.step()
    first.cross_fresh()

    qkv, first_t, vec, hid = project(plan, tokens, first, cut, hidden)
    join_after([second], [vec])
    second.step()
    second.cross_held()
    pairs = heads // 2
    attended, lse = attention(doc_split, qkv, heads, blk, 0, pairs, after=second.held)
    second.fresh = relay(second.fresh, [lse])
    second.cross_fresh()

    scale_row = jnp.repeat(head_scale, width // heads)[None]
    output, scaled_t, second_t, hidden_t, grad_pre, grad_branch, grad_attended, grad_middle, sums, hid_sums = (
        middle(plan, tokens, attended, cotangent, second, vec, hid, scale_row, half_q)
    )
    table = plan.table(0, False)

    def by_group(left_t):
        return left_t.reshape(ways, -1, group, seq)

    def send_grads(jobs, tile, after=(), cover=False):
        sent = grads([table[half:]], [jobs], tile, None, after, cover)
        return list(sent), to_other_core(plan, sent[0])

    def keep_grads(jobs, tile, got, after=(), cover=False):
        outs = grads([table[:half]], [jobs], tile, [got], after, cover)
        return list(outs[:1]), Scatter.begun(plan, 0, *outs)

    hidden_t = by_group(hidden_t)
    fc2_jobs = [(hidden_t, q, [cotangent], [0]) for q in range(n_q)]
    fc1_jobs = [
        (by_group(second_t), 0, [grad_pre], range(n_q)),
        (by_group(scaled_t), 0, [grad_branch], [0]),
    ]
    done, got_2 = send_grads(fc2_jobs, width)
    done, got_1 = send_grads(fc1_jobs, width, done, True)
    done, fc2_sum = keep_grads(fc2_jobs, width, got_2, done, True)
    done, fc1_sum = keep_grads(fc1_jobs, width, got_1, done)

    first_t = by_group(first_t)

    def back(start, count, after):
        out = attention_back(doc_split, qkv, grad_attended, attended, lse, heads, blk, start, count, after)
        return list(out[:1]), list(out)

    some = pairs * 3 // 8
    done, part_a = back(0, some, done)
    done = step_all([fc2_sum], done)
    done, part_b = back(some, some, done)
    size = part_a[0].shape[1]
    jobs = [(first_t, 0, part, [0]) for part in (part_a, part_b)]
    done, got = send_grads(jobs, 3 * size, done)
    done = step_all([fc2_sum, fc1_sum], done, True)
    done, sum_a = keep_grads(jobs, 3 * size, got, done)
    done, part_c = back(2 * some, pairs - 2 * some, done)
    rest = part_c[0].shape[1]
    jobs = [(first_t, 0, part_c, [0])]
    done, got = send_grads(jobs, 3 * rest, done)
    done = step_all([fc2_sum, fc1_sum, sum_a], done, True)
    done, sum_b = keep_grads(jobs, 3 * rest, got, done)
    head_sums = jnp.sum(sums[n_vec].reshape(heads, -1), axis=1)
    head_row = jnp.broadcast_to(jnp.pad(head_sums, (0, lanes - heads)), (8, lanes))
    grad_tokens, *vec_parts = finish(
        plan,
        table,
        tokens,
        grad_middle,
        vec,
        (sums, hid_sums, head_row),
        (part_a, part_b, part_c),
        first,
        cut,
        n_vec,
        n_hid,
        done,
    )
    done = step_all([fc1_sum, sum_a, sum_b], [grad_tokens])
    ways_out = (plan.pairs(0, 0, False), plan.core_pairs(), plan.corner_pairs(0))
    vec_all = vec_parts[0]
    for one, pairs_of in zip(relay(vec_parts[1:], done), ways_out):
        vec_all += lax.ppermute(one, AXES, pairs_of)
    vec_sum = Scatter(plan, 0, None, None)
    vec_sum.at = 1
    vec_sum.send(vec_all[half // 4 :], vec_all[: half // 4])
    done = step_all([sum_a, sum_b, vec_sum], done)
    step_all([sum_b, vec_sum], done)
    sent_vec = vec_sum.total()
    sent_a, sent_b = sum_a.total(), sum_b.total()
    sum_fc2, sum_fc1 = fc2_sum.total(), fc1_sum.total()
    columns = []
    for k in range(3):
        columns += [sent_a[:, k * size : (k + 1) * size], sent_a[:, (3 + k) * size : (4 + k) * size]]
        columns.append(sent_b[:, k * rest : (k + 1) * rest])
    sent_qkv = split_low(plan, jnp.concatenate(columns, 1))
    sent_fc1 = split_low(plan, sum_fc1[:, :hidden])
    sent_out = split_low(plan, sum_fc1[:, hidden:])
    row_blocks = [sum_fc2[:, k : k + width] for k in range(0, hidden, width)]
    sent_fc2 = split_low(plan, jnp.concatenate(row_blocks, 0))
    sent_vecd = split_low(plan, sent_vec[:n_vec, :group], 1)
    sent_vecff = split_low(plan, sent_vec[n_vec : n_vec + n_hid], 1)
    grad_heads = sent_vec[n_vec + n_hid, :heads]
    if plan.low > 1:
        grad_heads = lax.psum(grad_heads, AXES, axis_index_groups=plan.low_groups())
    return (
        output,
        grad_tokens,
        grad_heads,
        sent_qkv,
        sent_out,
        sent_fc1,
        sent_fc2,
        sent_vecd,
        sent_vecff,
    )


def solution(mesh):
    rows = P(AXES, None)
    columns = P(None, AXES)
    return jax.shard_map(
        functools.partial(local, Plan(mesh)),
        mesh=mesh,
        in_specs=(rows, P(AXES), P(), rows, rows, rows, rows, columns, columns, rows),
        out_specs=(rows, rows, P(), rows, rows, rows, rows, columns, columns),
        check_vma=False,
    )
```

```python
import functools

import jax
import jax.numpy as jnp
from jax import lax
from jax.experimental import pallas as pl
from jax.experimental.pallas import tpu as pltpu
from jax.sharding import PartitionSpec as P

epsilon = 1e-05
AXES = ("dp", "fsdp")
f32 = jnp.float32
bf16 = jnp.bfloat16
NEG = -1e30
VMEM_LIMIT = 56 << 20
ROWS_LIMIT = 62 << 20


def launch(
    kernel, args, *, in_specs, out_specs, out_shape, name, after=(), grid=(), scratch_shapes=(),
    prefetch=0, limit=VMEM_LIMIT, aliases=None, cover=False, cost=(1, 1, 0),
):
    after, count = list(after), len(args)

    def body(*refs):
        kernel(*refs[:count], *refs[count + len(after) :])

    return pl.pallas_call(
        body,
        grid_spec=pltpu.PrefetchScalarGridSpec(
            num_scalar_prefetch=prefetch,
            grid=grid,
            in_specs=[*in_specs] + [pl.BlockSpec(memory_space=pltpu.HBM)] * len(after),
            out_specs=out_specs,
            scratch_shapes=scratch_shapes,
        ),
        out_shape=out_shape,
        input_output_aliases=aliases or {},
        compiler_params=pltpu.CompilerParams(vmem_limit_bytes=limit),
        cost_estimate=pl.CostEstimate(
            flops=10**12 if cover else cost[0], bytes_accessed=cost[1], transcendentals=cost[2]
        ),
        name=name,
    )(*args, *after)


def relay(values, after):
    anywhere = pl.BlockSpec(memory_space=pl.ANY)
    return list(
        launch(
            lambda *refs: None,
            values,
            after=after,
            in_specs=[anywhere] * len(values),
            out_specs=[anywhere] * len(values),
            out_shape=[jax.ShapeDtypeStruct(v.shape, v.dtype) for v in values],
            aliases={k: k for k in range(len(values))},
            name="relay",
        )
    )


def in_vmem(value):
    return pltpu.with_memory_space_constraint(value, pltpu.VMEM)


class Plan:
    def __init__(self, mesh):
        n_dp, n_fs = mesh.shape["dp"], mesh.shape["fsdp"]
        self.count = n_dp * n_fs
        self.ways = min(self.count, 32)
        self.low = self.count // self.ways
        self.core = max(1, n_fs // self.low)
        self.dims = [1 << b for b in range(self.ways.bit_length() - 1) if 1 << b != self.core]
        self.half = self.ways // 2
        self.steps = len(self.dims)

    def order(self, core_bit, part, gathers):
        near, far = self.dims[:-1], self.dims[-1:]
        shift = (core_bit + part if part != 1 else 2) % len(near)
        near = near[shift:] + near[:shift]
        return far + near if gathers else near + far

    def pairs(self, part, step, gathers):
        out = []
        for i in range(self.count):
            group = i // self.low
            mask = self.order(int(bool(group & self.core)), part, gathers)[step]
            out.append((i, i ^ (mask * self.low)))
        return out

    def core_pairs(self):
        return [(i, i ^ (self.core * self.low)) for i in range(self.count)]

    def corner_pairs(self, part):
        out = []
        for i in range(self.count):
            group = i // self.low
            mask = self.core ^ self.order(int(not group & self.core), part, False)[0]
            out.append((i, i ^ (mask * self.low)))
        return out

    def low_groups(self):
        return [[g * self.low + i for i in range(self.low)] for g in range(self.ways)]

    def table(self, part, gathers):
        me = (lax.axis_index("dp") * lax.axis_size("fsdp") + lax.axis_index("fsdp")) // self.low
        rows = []
        for core_bit in (0, 1):
            row = []
            for other in (0, 1):
                masks = self.order(core_bit ^ other, part, gathers)
                for r in range(self.half):
                    x = self.core if other else 0
                    for k in range(self.steps):
                        bit = k if gathers else self.steps - 1 - k
                        if (r >> bit) & 1:
                            x ^= masks[k]
                    row.append(x)
            rows.append(row)
        mine = ((me & self.core) != 0).astype(jnp.int32)
        masks = jnp.where(mine == 1, jnp.array(rows[1], jnp.int32), jnp.array(rows[0], jnp.int32))
        return jnp.bitwise_xor(me.astype(jnp.int32), masks)


class Gather:
    def __init__(self, plan, pieces):
        self.plan = plan
        self.held = [piece[None] for piece in pieces]
        self.fresh = None
        self.at = 0

    def join(self):
        if self.fresh is not None:
            self.held = [jnp.concatenate(pair, 0) for pair in zip(self.held, self.fresh)]
            self.fresh = None

    def step(self):
        self.join()
        self.fresh = [
            lax.ppermute(h, AXES, self.plan.pairs(part, self.at, True)) for part, h in enumerate(self.held)
        ]
        self.at += 1

    def cross_held(self):
        self.far_held = [lax.ppermute(h, AXES, self.plan.core_pairs()) for h in self.held]

    def cross_fresh(self):
        self.far_fresh = [lax.ppermute(h, AXES, self.plan.core_pairs()) for h in self.fresh]

    def blocks(self):
        return [list(b) for b in zip(self.held, self.fresh, self.far_held, self.far_fresh)]


def join_kernel(*refs, count):
    for n in range(count):
        out = refs[2 * count + n]
        half = out.shape[0] // 2
        out[:half] = refs[2 * n][...]
        out[half:] = refs[2 * n + 1][...]


def join_after(gathers, after=()):
    args = [
        a
        for one in gathers
        for held, fresh in zip(one.held, one.fresh)
        for a in (held, in_vmem(fresh))
    ]
    shapes = [(2 * h.shape[0], *h.shape[1:]) for one in gathers for h in one.held]
    vmem = pl.BlockSpec(memory_space=pltpu.VMEM)
    outs = launch(
        functools.partial(join_kernel, count=len(shapes)),
        args,
        after=after,
        in_specs=[vmem] * len(args),
        out_specs=[vmem] * len(shapes),
        out_shape=[jax.ShapeDtypeStruct(shape, bf16) for shape in shapes],
        name="join",
    )
    for n, one in enumerate(gathers):
        one.held = list(outs[2 * n : 2 * n + 2])
        one.fresh = None


def join_low(plan, piece, axis=0):
    if plan.low == 1:
        return piece
    return lax.all_gather(piece, AXES, axis=axis, tiled=True, axis_index_groups=plan.low_groups())


def fetch(action, table_ref, sources, lines, sem):
    for number, part, column, width, place in lines:
        for b in range(4):
            source = sources[4 * part + b]
            count = source.shape[0]

            def one(r, _, source=source, number=number, part=part, b=b, count=count):
                at = b * count + r
                copy = pltpu.make_async_copy(
                    source.at[r, :, pl.ds(column, width)],
                    place(table_ref[part, at]),
                    sem.at[number, at],
                )
                getattr(copy, action)()
                return _

            lax.fori_loop(0, count, one, 0)


def block_operands(plan, gathered):
    blocks = gathered.blocks()
    table = jnp.stack([plan.table(part, True) for part in range(len(blocks))])
    flat = [b for part in blocks for b in part]
    specs = [pl.BlockSpec(memory_space=pltpu.SMEM)] + [pl.BlockSpec(memory_space=pltpu.HBM)] * len(flat)
    return [table, *flat], specs


def plus(a, b):
    return a.astype(f32) + b.astype(f32)


class Scatter:
    def __init__(self, plan, part, keep, got):
        self.plan, self.part, self.at = plan, part, 0
        self.keep, self.got = keep, got

    @classmethod
    def begun(cls, plan, part, going, keep):
        one = cls(plan, part, None, None)
        one.send(going, keep)
        return one

    def send(self, going, keep):
        self.keep = keep
        self.got = lax.ppermute(going, AXES, self.plan.pairs(self.part, self.at, False))
        self.at += 1

    def total(self):
        return plus(self.keep[0], self.got[0])


def halve_kernel(*refs, count):
    for n in range(count):
        keep_ref, got_ref = refs[2 * n], refs[2 * n + 1]
        going_ref, kept_ref = refs[2 * (count + n)], refs[2 * (count + n) + 1]
        half = keep_ref.shape[0] // 2
        for out, part in ((going_ref, slice(half, 2 * half)), (kept_ref, slice(0, half))):
            out[...] = plus(keep_ref[part], got_ref[part]).astype(out.dtype)


def step_all(scatters, after=(), cover=False):
    args = [
        a
        for one in scatters
        for a in (one.keep, in_vmem(one.got))
    ]
    shapes = [
        jax.ShapeDtypeStruct((one.keep.shape[0] // 2, *one.keep.shape[1:]), one.keep.dtype)
        for one in scatters
        for _ in range(2)
    ]
    outs = launch(
        functools.partial(halve_kernel, count=len(scatters)),
        args,
        after=after,
        in_specs=[pl.BlockSpec(memory_space=pltpu.VMEM)] * len(args),
        out_specs=[pl.BlockSpec(memory_space=pltpu.VMEM)] * len(args),
        out_shape=shapes,
        name="halve",
        cover=cover,
    )
    for n, one in enumerate(scatters):
        one.send(*outs[2 * n : 2 * n + 2])
    return [outs[0]]


def to_other_core(plan, values):
    return lax.ppermute(values, AXES, plan.core_pairs())


def split_low(plan, total, axis=0):
    if plan.low == 1:
        return total
    return lax.psum_scatter(
        total, AXES, scatter_dimension=axis, tiled=True, axis_index_groups=plan.low_groups()
    )


def dot_nt(a, b):
    return lax.dot_general(a, b, (((1,), (1,)), ((), ())), preferred_element_type=f32)


def dot_nn(a, b):
    return lax.dot_general(a, b, (((1,), (0,)), ((), ())), preferred_element_type=f32)


def transposed(a):
    return a.astype(f32).T.astype(a.dtype)


def causal(scores):
    keys = lax.broadcasted_iota(jnp.int32, scores.shape, 0)
    return jnp.where(keys <= lax.broadcasted_iota(jnp.int32, scores.shape, 1), scores, NEG)


def head_lanes(shape, h, hd):
    lane = lax.broadcasted_iota(jnp.int32, shape, 1)
    mine = (lane >= hd) if h else (lane < hd)
    return mine, lane == (0 if h else hd)


def masked_keys(k, h, hd, split):
    mine, spare = head_lanes(k.shape, h, hd)
    early = lax.broadcasted_iota(jnp.int32, k.shape, 0) < split
    return jnp.where(mine, k, jnp.where(spare & early, bf16(NEG), bf16(0)))


def masked_queries(q, h, hd, split, start):
    mine, spare = head_lanes(q.shape, h, hd)
    late = lax.broadcasted_iota(jnp.int32, q.shape, 0) + start >= split
    alone = jnp.where(mine, q, bf16(0)) * bf16(hd**-0.5)
    return alone, jnp.where(spare & late, bf16(1), alone)


def key_pieces(i, blk):
    half = blk // 2
    whole = [(j * blk, blk, 0) for j in range(i)]
    return whole + [(i * blk, half, 0), (i * blk + half, half, half)]


def added(total, more, first):
    if not first:
        return total + more
    return jnp.concatenate([total[:, :first], total[:, first:] + more], 1)


def attention_kernel(split_ref, q_ref, k_ref, v_ref, *refs, seq, hd, blk):
    o_ref, lse_ref = refs[-2:]
    split = split_ref[0]
    v_t = transposed(v_ref[...])
    keys = [masked_keys(k_ref[...], h, hd, split) for h in (0, 1)]
    for i in range(seq // blk):
        rows = slice(i * blk, (i + 1) * blk)
        outs = []
        for h in (0, 1):
            _, q = masked_queries(q_ref[rows, :], h, hd, split, i * blk)
            pieces = key_pieces(i, blk)
            scores = [dot_nt(keys[h][at : at + count], q[first:]) for at, count, first in pieces]
            scores[i:] = [causal(s) for s in scores[i:]]
            peak = scores[0].max(0, keepdims=True)
            for s in scores[1:-1]:
                peak = jnp.maximum(peak, s.max(0, keepdims=True))
            first = pieces[-1][2]
            late = jnp.maximum(peak[:, first:], scores[-1].max(0, keepdims=True))
            peak = jnp.concatenate([peak[:, :first], late], 1)
            total = jnp.zeros((1, blk), f32)
            mixed = jnp.zeros((hd, blk), f32)
            for (at, count, first), s in zip(pieces, scores):
                low = []
                for r in strips(count, 64):
                    e = jnp.exp(s[r] - peak[:, first:])
                    total = added(total, e.sum(0, keepdims=True), first)
                    low.append(e.astype(bf16))
                low = jnp.concatenate(low, 0)
                values = v_t[h * hd : (h + 1) * hd, at : at + count]
                mixed = added(mixed, dot_nn(values, low), first)
            outs.append(mixed / total)
            lse_ref[0, h : h + 1, rows] = peak + jnp.log(total)
        o_ref[rows, :] = jnp.concatenate(outs, 0).T


def attention(split, qkv, heads, blk, start, count, into=(), after=()):
    seq, width = qkv.shape[0], qkv.shape[1] // 3
    hd, pairs = width // heads, heads // 2
    w = 2 * hd
    return launch(
        functools.partial(attention_kernel, seq=seq, hd=hd, blk=blk),
        [split, qkv, qkv, qkv, *into],
        after=after,
        grid=(count,),
        in_specs=[
            pl.BlockSpec(memory_space=pltpu.SMEM),
            pl.BlockSpec((seq, w), lambda p: (0, p + start)),
            pl.BlockSpec((seq, w), lambda p: (0, p + start + pairs)),
            pl.BlockSpec((seq, w), lambda p: (0, p + start + 2 * pairs)),
        ]
        + [pl.BlockSpec(memory_space=pl.ANY)] * len(into),
        out_specs=[
            pl.BlockSpec((seq, w), lambda p: (0, p + start)),
            pl.BlockSpec((1, 2, seq), lambda p: (p + start, 0, 0)),
        ],
        out_shape=[
            jax.ShapeDtypeStruct((seq, width), f32),
            jax.ShapeDtypeStruct((pairs, 2, seq), f32),
        ],
        aliases={4 + k: k for k in range(len(into))},
        name="attention",
        cost=(12 * seq * seq * w * count, seq * w * count * 10, 2 * count * seq * seq),
    )


def attention_back_kernel(
    split_ref, q_ref, k_ref, v_ref, da_ref, o_ref, lse_ref, dq_ref, dk_ref, dv_ref, dk_acc, dv_acc,
    *, seq, hd, blk,
):
    split = split_ref[0]
    k_t = transposed(k_ref[...])
    keys_of = [masked_keys(k_ref[...], h, hd, split) for h in (0, 1)]
    for i in range(seq // blk):
        rows = slice(i * blk, (i + 1) * blk)
        q_full, da_full = q_ref[rows, :], da_ref[rows, :]
        inner = (da_full.astype(f32) * o_ref[rows, :]).T
        dqs = []
        for h in (0, 1):
            q, q_marked = masked_queries(q_full, h, hd, split, i * blk)
            da = jnp.where(head_lanes(da_full.shape, h, hd)[0], da_full, bf16(0))
            row_inner = inner[h * hd : (h + 1) * hd].sum(0, keepdims=True)
            lse = lse_ref[0, h : h + 1, rows]
            dq = jnp.zeros((hd, blk), f32)
            for at, count, first in key_pieces(i, blk):
                keys = slice(at, at + count)
                diagonal = at >= i * blk
                s = dot_nt(keys_of[h][keys], q_marked[first:])
                if diagonal:
                    s = causal(s)
                dp = dot_nt(v_ref[keys, :], da[first:])
                p_low, ds = [], []
                for r in strips(count, 64):
                    p = jnp.exp(s[r] - lse[:, first:])
                    p_low.append(p.astype(bf16))
                    ds.append((p * (dp[r] - row_inner[:, first:])).astype(bf16))
                ds = jnp.concatenate(ds, 0)
                dv = dot_nn(jnp.concatenate(p_low, 0), da[first:])
                dk = dot_nn(ds, q[first:])
                if diagonal and h == 0:
                    dv_acc[keys, :] = dv
                    dk_acc[keys, :] = dk
                else:
                    dv_acc[keys, :] += dv
                    dk_acc[keys, :] += dk
                dq = added(dq, dot_nn(k_t[h * hd : (h + 1) * hd, keys], ds), first)
            dqs.append(dq)
        dq_ref[rows, :] = (jnp.concatenate(dqs, 0).T * (hd**-0.5)).astype(bf16)
    dk_ref[...] = dk_acc[...].astype(bf16)
    dv_ref[...] = dv_acc[...].astype(bf16)


def attention_back(split, qkv, da, attended, lse, heads, blk, start, count, after=()):
    seq, width = qkv.shape[0], qkv.shape[1] // 3
    hd, pairs = width // heads, heads // 2
    w = 2 * hd
    column = pl.BlockSpec((seq, w), lambda p: (0, p + start))
    out = pl.BlockSpec((seq, w), lambda p: (0, p))
    return launch(
        functools.partial(attention_back_kernel, seq=seq, hd=hd, blk=blk),
        [split, qkv, qkv, qkv, da, attended, lse],
        after=after,
        grid=(count,),
        in_specs=[
            pl.BlockSpec(memory_space=pltpu.SMEM),
            column,
            pl.BlockSpec((seq, w), lambda p: (0, p + start + pairs)),
            pl.BlockSpec((seq, w), lambda p: (0, p + start + 2 * pairs)),
            column,
            column,
            pl.BlockSpec((1, 2, seq), lambda p: (p + start, 0, 0)),
        ],
        out_specs=[out, out, out],
        out_shape=[jax.ShapeDtypeStruct((seq, count * w), bf16)] * 3,
        scratch_shapes=[pltpu.VMEM((seq, w), f32)] * 2,
        name="attention_back",
    )


def grads_kernel(table_ref, place_ref, *refs, runs, n_left, n_right, begins, adds):
    lefts, rights, rest = refs[:n_left], refs[n_left : n_left + n_right], refs[n_left + n_right :]
    left = rest[-1]
    ways, rows, tokens = left.shape
    step = pl.program_id(0)
    for first, last, l, r, part in runs:

        @pl.when(step == first)
        def _():
            for w in range(ways):
                left[w] = lefts[l][table_ref[part, w], 0]

        @pl.when((step >= first) & (step < last))
        def _():
            product = [dot_nn(left[...].reshape(ways * rows, tokens), rights[k][...]) for k in r]
            product = jnp.concatenate(product, 1) if len(r) > 1 else product[0]
            product = product.reshape(ways, rows, product.shape[1])
            if adds:
                n_parts = len(begins)
                got_ref = rest[part]
                at = pl.multiple_of((step - begins[part]) * product.shape[2], 128)
                theirs = got_ref[:, :, pl.ds(at, product.shape[2])]
                going_ref, keep_ref = rest[n_parts + 2 * part : n_parts + 2 * part + 2]
                product = (product + theirs.astype(f32)).astype(bf16)
                keep_ref[...] = product[: ways // 2]
                going_ref[...] = product[ways // 2 :]
            else:
                rest[part][...] = product.astype(bf16)


def grads(tables, parts, tile, got=None, after=(), cover=False):
    groups, _, rows, tokens = parts[0][0][0].shape
    ways = tables[0].shape[0]
    lefts, rights, runs, places, spans = [], [], [], [], []
    at = 0
    for part, jobs in enumerate(parts):
        begin = at
        for left, q, group, numbers in jobs:
            for known, one in ((lefts, left), *((rights, right) for right in group)):
                if not any(one is k for k in known):
                    known.append(one)
            l = next(i for i, k in enumerate(lefts) if k is left)
            r = [next(i for i, k in enumerate(rights) if k is right) for right in group]
            runs.append((at, at + len(numbers), l, r, part))
            for n in numbers:
                places.append(([l], q, r, n))
            at += len(numbers)
        spans.append((begin, at - begin))

    def held(which, entry, count):
        lines = []
        for k in range(count):
            used = [(s, p[entry]) for s, p in enumerate(places) if k in p[which]]
            lines.append([next((v for s, v in used if s >= i), used[-1][1]) for i in range(at)])
        return lines

    place = jnp.array(held(0, 1, len(lefts)) + held(2, 3, len(rights)), jnp.int32)

    def left_spec(k):
        return pl.BlockSpec((groups, 1, rows, tokens), lambda i, t, p: (0, p[k, i], 0, 0))

    def right_spec(k):
        return pl.BlockSpec((tokens, share), lambda i, t, p: (0, p[len(lefts) + k, i]))

    def block(count, span):
        begin, steps = span
        return pl.BlockSpec(
            (count, rows, tile), lambda i, t, p: (0, 0, jnp.clip(i - begin, 0, steps - 1))
        )

    def shape(count, span):
        return jax.ShapeDtypeStruct((count, rows, span[1] * tile), bf16)

    share = tile // len(parts[0][0][2])
    adds = got is not None
    each = [ways // 2] * 2 if adds else [ways]
    return launch(
        functools.partial(
            grads_kernel,
            runs=runs,
            n_left=len(lefts),
            n_right=len(rights),
            begins=[span[0] for span in spans],
            adds=adds,
        ),
        [jnp.stack(tables), place, *lefts, *rights, *(map(in_vmem, got) if adds else [])],
        after=after,
        prefetch=2,
        grid=(at,),
        in_specs=[left_spec(k) for k in range(len(lefts))]
        + [right_spec(k) for k in range(len(rights))]
        + [pl.BlockSpec(memory_space=pltpu.VMEM)] * (len(parts) * adds),
        out_specs=[block(count, span) for span in spans for count in each],
        out_shape=[shape(count, span) for span in spans for count in each],
        scratch_shapes=[pltpu.VMEM((ways, rows, tokens), bf16)],
        name="grads_keep" if adds else "grads_send",
        cover=cover,
    )


def normalized(values):
    center = values - jnp.mean(values, axis=-1, keepdims=True)
    rate = lax.rsqrt(jnp.mean(center * center, axis=-1, keepdims=True) + epsilon)
    return center * rate, rate


def norm_back(grad, unit, rate):
    inner = jnp.mean(grad * unit, axis=-1, keepdims=True)
    return rate * (grad - jnp.mean(grad, axis=-1, keepdims=True) - unit * inner)


def by_lanes(values):
    total = values[:, :128]
    for k in range(128, values.shape[1], 128):
        total += values[:, k : k + 128]
    return total


def by_sublanes(values):
    total = values[:8]
    for k in range(8, values.shape[0], 8):
        total += values[k : k + 8]
    return total


def column_sum(values):
    return jnp.sum(values, axis=0, keepdims=True)


def resident(shape):
    return pl.BlockSpec(shape, lambda i: (0,) * len(shape), pipeline_mode=pl.Buffered(1))


def by_rows(blk, width):
    return pl.BlockSpec((blk, width), lambda i: (i, 0))


def by_columns(height, blk):
    return pl.BlockSpec((height, blk), lambda i: (0, i))


def weight_lines(w, cut, group, first=0):
    def rows(g):
        return pl.ds(pl.multiple_of(g * group, group), group)

    rest = w.shape[1] - cut
    return [
        (first, 0, 0, cut, lambda g: w.at[rows(g), pl.ds(0, cut)]),
        (first + 1, 1, 0, rest, lambda g: w.at[rows(g), pl.ds(cut, rest)]),
    ]


def project_kernel(table_ref, x_ref, *refs, cut):
    sources = refs[:8]
    qkv_ref, left_t_ref, vec_ref, hid_ref, w, raw, left_ref, sem = refs[8:]
    ways, group, lanes = raw.shape
    width = x_ref.shape[1]

    @pl.when(pl.program_id(0) == 0)
    def _():
        vec_lines = [(2, 0, cut, lanes, lambda g: raw.at[g])]
        lines = weight_lines(w, cut, group)
        fetch("start", table_ref, sources, vec_lines, sem)
        fetch("start", table_ref, sources, lines, sem)
        fetch("wait", table_ref, sources, vec_lines, sem)
        per = lanes // group
        for k in range(0, ways, per):
            row = [raw[k + j][:16, :group].astype(f32) for j in range(per)]
            vec_ref[:, k * group : (k + per) * group] = jnp.concatenate(row, 1)
        for k in range(ways):
            hid_ref[:, k * lanes : (k + 1) * lanes] = raw[k][:16].astype(f32)
        fetch("wait", table_ref, sources, lines, sem)

    for r in strips(x_ref.shape[0], 16):
        unit, _ = normalized(x_ref[r, :].astype(f32))
        left_ref[r, :] = (unit * vec_ref[0:1, :] + vec_ref[1:2, :]).astype(bf16)
    left = left_ref[...]
    left_t_ref[...] = transposed(left)
    for part, bias in ((0, 2), (1, None), (2, 3)):
        cols = slice(part * width, (part + 1) * width)
        rows = dot_nn(left, w[:, cols])
        if bias is not None:
            rows += vec_ref[bias : bias + 1, :]
        qkv_ref[:, cols] = rows.astype(bf16)


def project(plan, tokens, gathered, cut, hidden, after=(), blk=256):
    seq, width = tokens.shape
    blk = min(blk, seq)
    (table, *blocks), (table_spec, *specs) = block_operands(plan, gathered)
    return launch(
        functools.partial(project_kernel, cut=cut),
        [table, tokens, *blocks],
        after=after,
        grid=(seq // blk,),
        in_specs=[table_spec, by_rows(blk, width), *specs],
        out_specs=[
            by_rows(blk, 3 * width),
            by_columns(width, blk),
            pl.BlockSpec((16, width), lambda i: (0, 0)),
            pl.BlockSpec((16, hidden), lambda i: (0, 0)),
        ],
        out_shape=[
            jax.ShapeDtypeStruct((seq, 3 * width), bf16),
            jax.ShapeDtypeStruct((width, seq), bf16),
            jax.ShapeDtypeStruct((16, width), f32),
            jax.ShapeDtypeStruct((16, hidden), f32),
        ],
        scratch_shapes=[
            pltpu.VMEM((width, 3 * width), bf16),
            pltpu.VMEM((plan.ways, width // plan.ways, hidden // plan.ways), bf16),
            pltpu.VMEM((blk, width), bf16),
            pltpu.SemaphoreType.DMA((3, plan.ways)),
        ],
        name="project",
        cost=(6 * seq * width * width, 18 * seq * width, seq),
    )


def group_rows(g, group, stride, first=0):
    return pl.ds(pl.multiple_of(g * stride + first, group), group)


def vector(ref, row):
    return ref[row : row + 1, :]


def strips(rows, height):
    return [slice(r, r + height) for r in range(0, rows, height)]


def middle_kernel(
    table_ref, x_ref, att_ref, c_ref, vec_ref, hid_ref, scale_ref, *refs, chunk, half_q
):
    sources, refs = refs[:8], refs[8:]
    out_ref, z_t_ref, a2_t_ref, m_t_ref, df_ref, dy_ref, da_ref, dx_ref, sums_ref, hid_sums_ref = refs[:10]
    wo_ref, w1_ref, w2_ref, gate, slope, dm_keep, acc, sem = refs[10:]
    width, hidden = w1_ref.shape
    group = sources[0].shape[1]
    n_q = hidden // width

    def rows(g, stride, first=0):
        return pl.ds(pl.multiple_of(g * stride + first, group), group)

    def quarter(q):
        column = hidden * (q < half_q) + q % half_q * width
        return (2 + q, q // half_q, column, width, lambda g: w2_ref.at[rows(g, n_q * group, q * group)])

    out_lines = [(0, 1, half_q * width, width, lambda g: wo_ref.at[rows(g, group)])]
    fc1_lines = [(1, 0, 0, hidden, lambda g: w1_ref.at[rows(g, group)])]
    fc2_lines = [quarter(q) for q in range(n_q)]

    def arrived(lines):
        @pl.when(pl.program_id(0) == 0)
        def _():
            fetch("wait", table_ref, sources, lines, sem)

    chunks = [slice(k, k + chunk) for k in range(0, hidden, chunk)]

    @pl.when(pl.program_id(0) == 0)
    def _():
        for lines in (out_lines, fc1_lines, fc2_lines):
            fetch("start", table_ref, sources, lines, sem)
        sums_ref[...] = jnp.zeros_like(sums_ref)
        hid_sums_ref[...] = jnp.zeros_like(hid_sums_ref)

    def vec(row):
        return vec_ref[row : row + 1, :]

    def add_sum(row, values):
        sums_ref[row : row + 1, :] += column_sum(values)

    z = (att_ref[...] * scale_ref[...]).astype(bf16)
    z_t_ref[...] = transposed(z)
    arrived(out_lines)
    unit_1, rate_1 = normalized(dot_nn(z, wo_ref[...]) + vec(4))
    x2 = x_ref[...].astype(f32) + (unit_1 * vec(5) + vec(6))
    unit_2, rate_2 = normalized(x2)
    a2 = (unit_2 * vec(7) + vec(8)).astype(bf16)
    a2_t_ref[...] = transposed(a2)
    arrived(fc1_lines)

    total = 0.0
    root = (2.0 / jnp.pi) ** 0.5
    for ch in chunks:
        f = dot_nn(a2, w1_ref[:, ch]) + hid_ref[10:11, ch]
        square = f * f
        t = jnp.tanh(f * (root + (root * 0.044715) * square))
        half = 0.5 + 0.5 * t
        g = f * half
        gate[:, ch] = g
        slope[:, ch] = half + g * (1.0 - t) * (root + (3 * root * 0.044715) * square)
        total += jnp.sum(g, axis=-1, keepdims=True)
    mean = total / hidden
    spread = 0.0
    for ch in chunks:
        center = gate[:, ch] - mean
        spread += jnp.sum(center * center, axis=-1, keepdims=True)
    rate = lax.rsqrt(spread / hidden + epsilon)

    arrived(fc2_lines)
    grad_sum = 0.0
    grad_inner = 0.0
    for ch in chunks:
        unit = (gate[:, ch] - mean) * rate
        gate[:, ch] = unit
        gain = hid_ref[11:12, ch]
        m = (unit * gain + hid_ref[12:13, ch]).astype(bf16)
        m_t_ref[ch, :] = transposed(m)
        y = dot_nn(m, w2_ref[ch, :])
        if ch.start == 0:
            acc[...] = y
        else:
            acc[...] += y
        dm = dot_nt(c_ref[...], w2_ref[ch, :]).astype(bf16)
        dm_keep[:, ch] = dm
        dm = dm.astype(f32)
        hid_sums_ref[1:2, ch] += column_sum(dm * unit)
        hid_sums_ref[2:3, ch] += column_sum(dm)
        grad = dm * gain
        grad_sum += jnp.sum(grad, axis=-1, keepdims=True)
        grad_inner += jnp.sum(grad * unit, axis=-1, keepdims=True)
    out_ref[...] = (x2 + (acc[...] + vec(9))).astype(bf16)

    grad_sum = grad_sum / hidden
    grad_inner = grad_inner / hidden
    for ch in chunks:
        grad = dm_keep[:, ch].astype(f32) * hid_ref[11:12, ch]
        grad = rate * (grad - grad_sum - gate[:, ch] * grad_inner)
        df = (slope[:, ch] * grad).astype(bf16)
        df_ref[:, ch] = df
        hid_sums_ref[0:1, ch] += column_sum(df.astype(f32))
        back = dot_nt(df, w1_ref[:, ch])
        if ch.start == 0:
            acc[...] = back
        else:
            acc[...] += back

    upstream = c_ref[...].astype(f32)
    da2 = acc[...]
    add_sum(9, upstream)
    add_sum(7, da2 * unit_2)
    add_sum(8, da2)
    dx2 = upstream + norm_back(da2 * vec(7), unit_2, rate_2)
    dx_ref[...] = dx2
    add_sum(5, dx2 * unit_1)
    add_sum(6, dx2)
    dy = norm_back(dx2 * vec(5), unit_1, rate_1).astype(bf16)
    dy_ref[...] = dy
    add_sum(4, dy.astype(f32))
    dz = dot_nt(dy, wo_ref[...]).astype(bf16).astype(f32)
    add_sum(10, dz * att_ref[...])
    da_ref[...] = (dz * scale_ref[...]).astype(bf16)


def middle(plan, tokens, attended, cotangent, gathered, vec, hid, scale, half_q, after=(), blk=256, chunk=256):
    seq, width = tokens.shape
    hidden = hid.shape[1]
    blk = min(blk, seq)
    (table, *blocks), (table_spec, *specs) = block_operands(plan, gathered)
    row, col, wide = by_rows(blk, width), by_columns(width, blk), by_rows(blk, hidden)
    shape = jax.ShapeDtypeStruct
    return launch(
        functools.partial(middle_kernel, chunk=chunk, half_q=half_q),
        [table, tokens, attended, cotangent, vec, hid, scale, *blocks],
        after=after,
        grid=(seq // blk,),
        in_specs=[table_spec, row, row, row, *(resident(a.shape) for a in (vec, hid, scale)), *specs],
        out_specs=[
            row, col, col, by_columns(hidden, blk), wide, row, row, row,
            pl.BlockSpec((16, width), lambda i: (0, 0)),
            pl.BlockSpec((8, hidden), lambda i: (0, 0)),
        ],
        out_shape=[
            shape((seq, width), bf16),
            shape((width, seq), bf16),
            shape((width, seq), bf16),
            shape((hidden, seq), bf16),
            shape((seq, hidden), bf16),
            shape((seq, width), bf16),
            shape((seq, width), bf16),
            shape((seq, width), f32),
            shape((16, width), f32),
            shape((8, hidden), f32),
        ],
        scratch_shapes=[
            pltpu.VMEM((width, width), bf16),
            pltpu.VMEM((width, hidden), bf16),
            pltpu.VMEM((hidden, width), bf16),
            pltpu.VMEM((blk, hidden), f32),
            pltpu.VMEM((blk, hidden), f32),
            pltpu.VMEM((blk, hidden), bf16),
            pltpu.VMEM((blk, width), f32),
            pltpu.SemaphoreType.DMA((2 + hidden // width, plan.ways)),
        ],
        limit=ROWS_LIMIT,
        name="middle",
        cost=(
            4 * seq * width * (width + 2 * hidden),
            2 * width * (width + 2 * hidden) + 40 * seq * width,
            seq * hidden,
        ),
    )


def finish_kernel(
    table_ref, order_ref, x_ref, dx_ref, vec_ref, sums_ref, hid_sums_ref, heads_ref, *refs,
    cut, n_parts, n_vec, n_hid,
):
    grads_in, sources = refs[: 3 * n_parts], refs[3 * n_parts : 3 * n_parts + 8]
    out_ref, *quarters, w, acc, rows, packed, sem = refs[3 * n_parts + 8 :]
    width = x_ref.shape[1]

    @pl.when(pl.program_id(0) == 0)
    def _():
        lines = weight_lines(w, cut, sources[0].shape[1])
        fetch("start", table_ref, sources, lines, sem)
        rows[...] = jnp.zeros_like(rows)
        acc[...] = jnp.zeros_like(acc)
        fetch("wait", table_ref, sources, lines, sem)

    ordered = [grads_in[3 * part + k][...] for k in range(3) for part in range(n_parts)]
    grad = jnp.concatenate(ordered, 1)
    da1 = dot_nt(grad, w[...])
    for row, columns in ((2, slice(0, width)), (3, slice(2 * width, 3 * width))):
        rows[row : row + 1, :] += column_sum(grad[:, columns].astype(f32))
    for r in strips(x_ref.shape[0], 16):
        grad = da1[r]
        unit, rate = normalized(x_ref[r, :].astype(f32))
        acc[:8] += by_sublanes(grad * unit)
        acc[8:] += by_sublanes(grad)
        out_ref[r, :] = dx_ref[r, :] + norm_back(grad * vec_ref[0:1, :], unit, rate)

    @pl.when(pl.program_id(0) == pl.num_programs(0) - 1)
    def _():
        rows[0:1, :] = column_sum(acc[:8])
        rows[1:2, :] = column_sum(acc[8:])
        rows[4:n_vec, :] = sums_ref[4:n_vec, :]
        ways, _, lanes = packed.shape
        group = width // ways
        packed[...] = jnp.zeros_like(packed)
        for g in range(ways):
            packed[g, :n_vec, :group] = rows[:n_vec, g * group : (g + 1) * group]
            packed[g, n_vec : n_vec + n_hid, :] = hid_sums_ref[:n_hid, g * lanes : (g + 1) * lanes]
            packed[g, n_vec + n_hid : n_vec + n_hid + 1, :] = heads_ref[0:1, :]
        for k in range(ways):
            quarters[4 * k // ways][k % (ways // 4)] = packed[order_ref[k]]


def finish(plan, order, tokens, dx2, vec, sums, parts, gathered, cut, n_vec, n_hid, after=(), blk=256):
    seq, width = tokens.shape
    blk = min(blk, seq)
    row = by_rows(blk, width)
    (table, *blocks), (table_spec, *specs) = block_operands(plan, gathered)
    grads_in = [g for part in parts for g in part]
    lanes = sums[1].shape[1] // plan.ways
    packed = jax.ShapeDtypeStruct((plan.ways // 4, 16, lanes), f32)
    packed_spec = pl.BlockSpec(packed.shape, lambda i: (0, 0, 0))
    return launch(
        functools.partial(finish_kernel, cut=cut, n_parts=len(parts), n_vec=n_vec, n_hid=n_hid),
        [table, order, tokens, dx2, vec, *sums, *grads_in, *blocks],
        after=after,
        grid=(seq // blk,),
        in_specs=[table_spec, table_spec, row, row, *(resident(a.shape) for a in (vec, *sums))]
        + [by_rows(blk, g.shape[1]) for g in grads_in]
        + specs,
        out_specs=[row] + [packed_spec] * 4,
        out_shape=[jax.ShapeDtypeStruct((seq, width), f32)] + [packed] * 4,
        scratch_shapes=[
            pltpu.VMEM((width, 3 * width), bf16),
            pltpu.VMEM((16, width), f32),
            pltpu.VMEM((16, width), f32),
            pltpu.VMEM((plan.ways, 16, lanes), f32),
            pltpu.SemaphoreType.DMA((2, plan.ways)),
        ],
        name="finish",
    )


def local(
    plan,
    tokens,
    doc_split,
    head_scale,
    query_key_value_weight,
    output_weight,
    first_weight,
    second_weight,
    model_vectors,
    hidden_vectors,
    cotangent,
):
    seq, width = tokens.shape
    hidden = first_weight.shape[1]
    heads = head_scale.shape[0]
    blk = min(512, seq)
    ways, half = plan.ways, plan.half
    n_vec, n_hid = model_vectors.shape[0], hidden_vectors.shape[0]

    cut = 2 * width
    group, lanes = width // ways, hidden // ways
    qkv_rows = join_low(plan, query_key_value_weight)
    vec_rows = jnp.concatenate(
        [
            jnp.pad(join_low(plan, model_vectors, 1), ((0, 0), (0, lanes - group))),
            join_low(plan, hidden_vectors, 1),
            jnp.zeros((group - n_vec - n_hid, lanes), bf16),
        ],
        0,
    )
    fc1_rows = join_low(plan, first_weight)
    fc2_rows = join_low(plan, second_weight)
    out_rows = join_low(plan, output_weight)
    n_q = hidden // width
    half_q = n_q // 2
    quarters = [fc2_rows[q * group : (q + 1) * group] for q in range(n_q)]
    first = Gather(plan, [jnp.concatenate([qkv_rows[:, :cut], vec_rows], 1), qkv_rows[:, cut:]])
    second = Gather(
        plan,
        [
            jnp.concatenate([fc1_rows, *quarters[:half_q]], 1),
            jnp.concatenate([*quarters[half_q:], out_rows], 1),
        ],
    )
    first.step()
    join_after([first])
    first.step()
    second.held = relay(second.held, first.held[:1])
    second.step()
    while first.at < plan.steps:
        join_after([first])
        first.step()
    first.cross_held()
    while second.at < plan.steps - 2:
        second.step()
    second.fresh = relay(second.fresh, first.fresh)
    second.step()
    first.cross_fresh()

    qkv, first_t, vec, hid = project(plan, tokens, first, cut, hidden)
    join_after([second], [vec])
    second.step()
    second.cross_held()
    pairs = heads // 2
    attended, lse = attention(doc_split, qkv, heads, blk, 0, pairs, after=second.held)
    second.fresh = relay(second.fresh, [lse])
    second.cross_fresh()

    scale_row = jnp.repeat(head_scale, width // heads)[None]
    output, scaled_t, second_t, hidden_t, grad_pre, grad_branch, grad_attended, grad_middle, sums, hid_sums = (
        middle(plan, tokens, attended, cotangent, second, vec, hid, scale_row, half_q)
    )
    table = plan.table(0, False)

    def by_group(left_t):
        return left_t.reshape(ways, -1, group, seq)

    def send_grads(jobs, tile, after=(), cover=False):
        sent = grads([table[half:]], [jobs], tile, None, after, cover)
        return list(sent), to_other_core(plan, sent[0])

    def keep_grads(jobs, tile, got, after=(), cover=False):
        outs = grads([table[:half]], [jobs], tile, [got], after, cover)
        return list(outs[:1]), Scatter.begun(plan, 0, *outs)

    hidden_t = by_group(hidden_t)
    fc2_jobs = [(hidden_t, q, [cotangent], [0]) for q in range(n_q)]
    fc1_jobs = [
        (by_group(second_t), 0, [grad_pre], range(n_q)),
        (by_group(scaled_t), 0, [grad_branch], [0]),
    ]
    done, got_2 = send_grads(fc2_jobs, width)
    done, got_1 = send_grads(fc1_jobs, width, done, True)
    done, fc2_sum = keep_grads(fc2_jobs, width, got_2, done, True)
    done, fc1_sum = keep_grads(fc1_jobs, width, got_1, done)

    first_t = by_group(first_t)

    def back(start, count, after):
        out = attention_back(doc_split, qkv, grad_attended, attended, lse, heads, blk, start, count, after)
        return list(out[:1]), list(out)

    some = pairs * 3 // 8
    done, part_a = back(0, some, done)
    done = step_all([fc2_sum], done)
    done, part_b = back(some, some, done)
    size = part_a[0].shape[1]
    jobs = [(first_t, 0, part, [0]) for part in (part_a, part_b)]
    done, got = send_grads(jobs, 3 * size, done)
    done = step_all([fc2_sum, fc1_sum], done, True)
    done, sum_a = keep_grads(jobs, 3 * size, got, done)
    done, part_c = back(2 * some, pairs - 2 * some, done)
    rest = part_c[0].shape[1]
    jobs = [(first_t, 0, part_c, [0])]
    done, got = send_grads(jobs, 3 * rest, done)
    done = step_all([fc2_sum, fc1_sum, sum_a], done, True)
    done, sum_b = keep_grads(jobs, 3 * rest, got, done)
    head_sums = jnp.sum(sums[n_vec].reshape(heads, -1), axis=1)
    head_row = jnp.broadcast_to(jnp.pad(head_sums, (0, lanes - heads)), (8, lanes))
    grad_tokens, *vec_parts = finish(
        plan,
        table,
        tokens,
        grad_middle,
        vec,
        (sums, hid_sums, head_row),
        (part_a, part_b, part_c),
        first,
        cut,
        n_vec,
        n_hid,
        done,
    )
    done = step_all([sum_a, sum_b], [grad_tokens])
    ways_out = (plan.pairs(0, 0, False), plan.core_pairs(), plan.corner_pairs(0))
    vec_all = vec_parts[0]
    for one, pairs_of in zip(relay(vec_parts[1:], done), ways_out):
        vec_all += lax.ppermute(one, AXES, pairs_of)
    vec_sum = Scatter(plan, 0, None, None)
    vec_sum.at = 1
    vec_sum.send(vec_all[half // 4 :], vec_all[: half // 4])
    done = step_all([fc1_sum, sum_a, sum_b, vec_sum], done)
    step_all([sum_b, vec_sum], done)
    sent_vec = vec_sum.total()
    sent_a, sent_b = sum_a.total(), sum_b.total()
    sum_fc2, sum_fc1 = fc2_sum.total(), fc1_sum.total()
    columns = []
    for k in range(3):
        columns += [sent_a[:, k * size : (k + 1) * size], sent_a[:, (3 + k) * size : (4 + k) * size]]
        columns.append(sent_b[:, k * rest : (k + 1) * rest])
    sent_qkv = split_low(plan, jnp.concatenate(columns, 1))
    sent_fc1 = split_low(plan, sum_fc1[:, :hidden])
    sent_out = split_low(plan, sum_fc1[:, hidden:])
    row_blocks = [sum_fc2[:, k : k + width] for k in range(0, hidden, width)]
    sent_fc2 = split_low(plan, jnp.concatenate(row_blocks, 0))
    sent_vecd = split_low(plan, sent_vec[:n_vec, :group], 1)
    sent_vecff = split_low(plan, sent_vec[n_vec : n_vec + n_hid], 1)
    grad_heads = sent_vec[n_vec + n_hid, :heads]
    if plan.low > 1:
        grad_heads = lax.psum(grad_heads, AXES, axis_index_groups=plan.low_groups())
    return (
        output,
        grad_tokens,
        grad_heads,
        sent_qkv,
        sent_out,
        sent_fc1,
        sent_fc2,
        sent_vecd,
        sent_vecff,
    )


def solution(mesh):
    rows = P(AXES, None)
    columns = P(None, AXES)
    return jax.shard_map(
        functools.partial(local, Plan(mesh)),
        mesh=mesh,
        in_specs=(rows, P(AXES), P(), rows, rows, rows, rows, columns, columns, rows),
        out_specs=(rows, rows, P(), rows, rows, rows, rows, columns, columns),
        check_vma=False,
    )
```
